32 devices in a mesh: seq: 4 (over y, x), blk: 8 (over z, core).
Axes of the slice: x: 2, y: 2, z: 4, core: 2. Of those that a mesh axis runs over, the one named last changes fastest.
Arguments:
- tokens: bfloat16 [4096, 1024], P(('seq', 'blk')), may hold values from -6 to 6
- first_values: bfloat16 [4096, 1024], P(('seq', 'blk')), may hold values from -6 to 6
- doc_lengths: int32 [4, 4], P('seq'), may hold values from 1 to 897, as said below
- attn_gain: float32 [1024], replicated, may hold values from 0.2 to 4.5
- query_weight: bfloat16 [1024, 1024], replicated, may hold values from -0.1875 to 0.1875
- key_weight: bfloat16 [1024, 1024], replicated, may hold values from -0.1875 to 0.1875
- value_weight: bfloat16 [1024, 1024], replicated, may hold values from -0.1875 to 0.1875
- out_weight: bfloat16 [1024, 1024], replicated, may hold values from -3 to 3
- ffn_gain: float32 [1024], replicated, may hold values from 0.2 to 4.5
- gate_weight: bfloat16 [1024, 2816], replicated, may hold values from -0.1875 to 0.1875
- up_weight: bfloat16 [1024, 2816], replicated, may hold values from -0.1875 to 0.1875
- down_weight: bfloat16 [2816, 1024], replicated, may hold values from -0.109375 to 0.109375
- cotangent: bfloat16 [4096, 1024], P(('seq', 'blk')), may hold values from -6 to 6
Outputs:
- layer_output: float32 [4096, 1024], P(('seq', 'blk'))
- grad_tokens: float32 [4096, 1024], P(('seq', 'blk'))
- grad_first: float32 [4096, 1024], P(('seq', 'blk'))
- grad_attn_gain: float32 [1024], P('blk')
- grad_query: float32 [1024, 1024], P('blk')
- grad_key: float32 [1024, 1024], P('blk')
- grad_value: float32 [1024, 1024], P('blk')
- grad_out_weight: float32 [1024, 1024], P('blk')
- grad_ffn_gain: float32 [1024], P('blk')
- grad_gate: float32 [1024, 2816], P('blk')
- grad_up: float32 [1024, 2816], P('blk')
- grad_down: float32 [2816, 1024], P('blk')
The draws below stay inside these ranges and needn't reach their ends.
Inputs may be any that keep to these rules, and one draw needn't show every extreme that they name: `doc_lengths`: each row sums to 1024.
All inputs are finite; a program needn't handle non-finite values.
Results may differ from the reference program's by a relative error of at most 0.022.
Values may be sent and summed in bfloat16 or wider, within the bound.
A program may use at most 256 MiB of HBM per device.

```python
import math
import jax
import jax.numpy as jnp
from jax import lax

D = 1024
HEADS = 16
HEAD_DIM = 64
FF = 2816
TOK_DEV = 128
GROUP_TOK = 1024
GROUPS = 4
TOKENS = 4096
N_BLK = 8


def draw_doc_lengths(key, part):
    key = jax.random.fold_in(key, 11)
    first_key, second_key, pick_key, cut_key = jax.random.split(key, 4)
    first = jax.random.randint(first_key, (GROUPS,), 1, TOK_DEV - 2)
    second = jax.random.randint(second_key, (GROUPS,), first + 1, TOK_DEV - 1)
    longest = jnp.full((GROUPS,), TOK_DEV * N_BLK - TOK_DEV + 1, jnp.int32)
    spanning = jnp.stack([first, longest, second - first, TOK_DEV - 1 - second], axis=1)
    eighth = GROUP_TOK // 8
    cuts = jax.random.randint(cut_key, (GROUPS, 3), -eighth, eighth) + jnp.array([2, 4, 6], jnp.int32)[None, :] * eighth
    spread = jnp.stack([cuts[:, 0], cuts[:, 1] - cuts[:, 0], cuts[:, 2] - cuts[:, 1], GROUP_TOK - cuts[:, 2]], axis=1)
    chosen = jax.random.randint(pick_key, (), 0, GROUPS)
    picked = (jnp.arange(GROUPS, dtype=jnp.int32) == chosen)[:, None]
    return jnp.where(picked, spanning, spread).astype(jnp.int32)


def spread_gain(key, low_end, high_end):
    rough = jax.random.uniform(key, (D,), jnp.float32, 0.7, 1.4)
    ramp = jnp.arange(D).astype(jnp.float32) / D
    return low_end * (high_end / low_end) ** ramp * rough


def draw_attn_gain(key, part):
    key = jax.random.fold_in(key, 21)
    return spread_gain(key, 0.4, 2.5)


def draw_ffn_gain(key, part):
    key = jax.random.fold_in(key, 23)
    return spread_gain(key, 0.4, 2.5)


def spiked(values, own_key, source, target, parts, factor):
    owner, partner = [(jnp.arange(values.shape[dim]) // (values.shape[dim] // parts)).reshape([-1 if axis == dim else 1 for axis in range(values.ndim)]) for dim in (source, target)]
    chosen = jax.random.permutation(own_key, parts)[partner]
    strong = (owner == chosen) | (owner == (partner + parts // 2) % parts)
    return jnp.where(strong, factor * values, values)


def steps_of(stream_key, dims, cuts, least, largest):
    level, own = 1.0, jax.random.fold_in(stream_key, 6)
    for axis_at, shards_of in cuts:
        draws = jnp.exp(jax.random.uniform(jax.random.fold_in(own, axis_at), (shards_of,), jnp.float32, least / len(cuts), largest / len(cuts)))
        level = level * jnp.repeat(draws, dims[axis_at] // shards_of).reshape([-1 if axis == axis_at else 1 for axis in range(len(dims))])
    return level


def scatter_about(own_key, dims, deviation, limit, cuts=(), held_as=jnp.bfloat16):
    values = jax.random.normal(own_key, dims, jnp.float32) * deviation
    if len(cuts) > 0:
        values = steps_of(own_key, dims, cuts, -0.22, 0.18) * values
    return jnp.clip(values, min=-limit, max=limit).astype(held_as)


def heavy_noise(key, dims, width, most, cuts, heavy, held_as=jnp.bfloat16):
    drawn = width * jax.random.normal(key, dims, jnp.float32)
    if cuts:
        drawn = drawn * steps_of(key, dims, cuts, -0.22, 0.18)
    return jnp.clip(spiked(drawn, jax.random.fold_in(key, 3), *heavy), -most, most).astype(held_as)


def setup_inputs(seed: int = 0) -> dict:
    streams_of = jax.random.split(jax.random.key(seed), 14)
    tokens = heavy_noise(streams_of[0], (TOKENS, D), 1.0, 6.0, ((0, 32),), (0, 1, 32, 2.75))
    first_values = scatter_about(streams_of[1], (TOKENS, D), 1.0, 6.0, ((0, 32),))
    doc_lengths = draw_doc_lengths(jax.random.fold_in(streams_of[13], 71), 0)
    attn_gain = draw_attn_gain(jax.random.fold_in(streams_of[13], 71), 0)
    query_weight = scatter_about(streams_of[4], (D, D), D ** -0.5, 0.1875)
    key_weight = scatter_about(streams_of[5], (D, D), D ** -0.5, 0.1875)
    value_weight = scatter_about(streams_of[6], (D, D), D ** -0.5, 0.1875)
    out_weight = scatter_about(streams_of[7], (D, D), (max(1, 4 * D // (TOK_DEV * N_BLK))) ** -0.5, 3.0)
    ffn_gain = draw_ffn_gain(jax.random.fold_in(streams_of[13], 71), 0)
    gate_weight = scatter_about(streams_of[9], (D, FF), D ** -0.5, 0.1875)
    up_weight = scatter_about(streams_of[10], (D, FF), D ** -0.5, 0.1875)
    down_weight = scatter_about(streams_of[11], (FF, D), FF ** -0.5, 0.109375)
    cotangent = scatter_about(streams_of[12], (TOKENS, D), 1.0, 6.0, ((0, 32),))
    return dict(tokens=tokens, first_values=first_values, doc_lengths=doc_lengths, attn_gain=attn_gain, query_weight=query_weight, key_weight=key_weight, value_weight=value_weight, out_weight=out_weight, ffn_gain=ffn_gain, gate_weight=gate_weight, up_weight=up_weight, down_weight=down_weight, cotangent=cotangent)


EPS = 1e-05
THETA = 10000.0
MIX = 0.5
NEG = -1e+30
HIGH = lax.Precision.HIGHEST

@jax.custom_vjp
def low(v):
    return lax.optimization_barrier(v.astype(jnp.bfloat16)).astype(jnp.float32)

@jax.custom_vjp
def low_back(v):
    return v

def low_keep(v):
    return (low(v), None)

def low_pass(kept, grad):
    return (grad,)

def back_keep(v):
    return (v, None)

def back_low(kept, grad):
    return (low(grad),)
low.defvjp(low_keep, low_pass)
low_back.defvjp(back_keep, back_low)

def matmul(left, right):
    return jnp.dot(left, right, precision=HIGH, preferred_element_type=jnp.float32)

def norm_rows(values, gain):
    inverse = lax.rsqrt(lax.optimization_barrier(jnp.mean(values * values, axis=-1, keepdims=True)) + EPS)
    return values * inverse * gain

def doc_layout(lengths, index):
    ends = jnp.cumsum(lengths, axis=-1)
    past = (index[:, None] >= ends).astype(jnp.int32)
    return (lax.optimization_barrier(jnp.sum(past, axis=1)), index - lax.optimization_barrier(jnp.sum(past * lengths, axis=1)))

def tables(position):
    half = HEAD_DIM // 2
    freq = THETA ** (-(jnp.arange(half).astype(jnp.float32) * 2.0 / HEAD_DIM))
    angle = position.astype(jnp.float32)[:, None] * freq[None, :]
    return (jnp.cos(angle)[:, None, :], jnp.sin(angle)[:, None, :])

def rotate(values, cosine, sine):
    half = values.shape[-1] // 2
    first = values[..., :half]
    second = values[..., half:]
    return jnp.concatenate([first * cosine - second * sine, second * cosine + first * sine], axis=-1)

def attend_group(queries, keys, mixed, docs):
    scale = HEAD_DIM ** (-0.5)
    block = math.gcd(GROUP_TOK, 512)
    count = GROUP_TOK // block
    index = jnp.arange(GROUP_TOK, dtype=jnp.int32)

    def one_block(inputs):
        query_block, query_index, query_doc = inputs
        score = low_back(jnp.einsum('qhd,khd->hqk', query_block, keys, precision=HIGH) * scale)
        allowed = (query_doc[:, None] == docs[None, :]) & (index[None, :] <= query_index[:, None])
        score = jnp.where(allowed[None], score, NEG)
        top = lax.optimization_barrier(jnp.max(score, axis=-1, keepdims=True))
        weight = jnp.exp(score - top)
        prob = weight / lax.optimization_barrier(jnp.sum(weight, axis=-1, keepdims=True))
        return jnp.einsum('hqk,khd->qhd', low(prob), mixed, precision=HIGH)
    result = lax.map(jax.checkpoint(one_block), (queries.reshape(count, block, HEADS, HEAD_DIM), index.reshape(count, block), docs.reshape(count, block)))
    return result.reshape(GROUP_TOK, HEADS, HEAD_DIM)

def reference(tokens, first_values, doc_lengths, attn_gain, query_weight, key_weight, value_weight, out_weight, ffn_gain, gate_weight, up_weight, down_weight, cotangent):
    rows_all = jnp.arange(TOKENS, dtype=jnp.int32)
    inside = rows_all % GROUP_TOK
    owner = rows_all // GROUP_TOK
    docs, position = doc_layout(doc_lengths[owner], inside)
    cosine, sine = tables(position)
    shape = (GROUPS, GROUP_TOK, HEADS, HEAD_DIM)
    cosine = cosine.reshape(GROUPS, GROUP_TOK, 1, HEAD_DIM // 2)
    sine = sine.reshape(GROUPS, GROUP_TOK, 1, HEAD_DIM // 2)
    group_docs = docs.reshape(GROUPS, GROUP_TOK)

    def forward(source, first, gain_one, wq, wk, wv, wo, gain_two, wg, wu, wd):
        normed = low(norm_rows(source, gain_one))
        q_pre = low_back(matmul(normed, wq))
        k_pre = low_back(matmul(normed, wk))
        v_pre = matmul(normed, wv)
        queries = low(low_back(rotate(q_pre.reshape(shape), cosine, sine)))
        keys = low(low_back(rotate(k_pre.reshape(shape), cosine, sine)))
        mixed = low(low_back(MIX * v_pre + MIX * first)).reshape(shape)
        attended = lax.map(lambda group: attend_group(group[0], group[1], group[2], group[3]), (queries, keys, mixed, group_docs))
        attended_b = low(low_back(attended.reshape(TOKENS, D)))
        mid = source + low_back(matmul(attended_b, wo))
        normed_two = low(norm_rows(mid, gain_two))
        gate = low_back(matmul(normed_two, wg))
        up = low_back(matmul(normed_two, wu))
        act = low(jax.nn.silu(gate) * up)
        return mid + low_back(matmul(act, wd))
    inputs = (tokens.astype(jnp.float32), first_values.astype(jnp.float32), attn_gain, query_weight.astype(jnp.float32), key_weight.astype(jnp.float32), value_weight.astype(jnp.float32), out_weight.astype(jnp.float32), ffn_gain, gate_weight.astype(jnp.float32), up_weight.astype(jnp.float32), down_weight.astype(jnp.float32))
    layer_output, pull = jax.vjp(forward, *inputs)
    grads = pull(cotangent.astype(jnp.float32))
    return (layer_output, grads[0], grads[1], grads[2], grads[3], grads[4], grads[5], grads[6], grads[7], grads[8], grads[9], grads[10])
```

```python
import functools
import math

import jax
import jax.numpy as jnp
from jax import lax
from jax.experimental import pallas as pl
from jax.experimental.pallas import tpu as pltpu
from jax.sharding import PartitionSpec as P

HEAD_DIM = 64


EPS = 1e-05
THETA = 10000.0
MIX = 0.5
NEG = -1e30


def doc_layout(lengths, index):
    ends = jnp.cumsum(lengths, axis=-1)
    past = (index[:, None] >= ends).astype(jnp.int32)
    return (jnp.sum(past, axis=1), index - jnp.sum(past * lengths, axis=1))


def tables(position):
    half = HEAD_DIM // 2
    freq = THETA ** (-(jnp.arange(half).astype(jnp.float32) * 2.0 / HEAD_DIM))
    angle = position.astype(jnp.float32)[:, None] * freq[None, :]
    return (jnp.cos(angle)[:, None, :], jnp.sin(angle)[:, None, :])


def rotate(values, cosine, sine):
    half = values.shape[-1] // 2
    first = values[..., :half]
    second = values[..., half:]
    return jnp.concatenate(
        [first * cosine - second * sine, second * cosine + first * sine], axis=-1
    )


def by_blocks(step, carry, pieces, start):
    rows = pieces[0].shape[0]
    size = math.gcd(rows, 1024)
    count = rows // size
    if count == 1:
        return step(carry, pieces, start)
    stacked = tuple((piece.reshape((count, size) + piece.shape[1:]) for piece in pieces))
    offsets = jnp.arange(count, dtype=jnp.int32) * size

    def turn(state, inputs):
        return (step(state, inputs[1], start + inputs[0]), None)

    result, unused = lax.scan(turn, carry, (offsets, stacked))
    return result


def outer(left, right):
    return lax.dot_general(
        left, right, (((0,), (0,)), ((), ())), preferred_element_type=jnp.float32
    )


def back(left, weight):
    return lax.dot_general(
        left, weight, (((1,), (1,)), ((), ())), preferred_element_type=jnp.float32
    )


TILE = 256
MESH = pl.DeviceIdType.MESH
F32 = jnp.float32
BF16 = jnp.bfloat16


def remote(src, dst, send, recv, where):
    return pltpu.make_async_remote_copy(
        src_ref=src, dst_ref=dst, send_sem=send, recv_sem=recv, device_id=where, device_id_type=MESH
    )


def multiple(value, unit):
    return pl.multiple_of(value, unit)


class Reducer:
    def __init__(self, rows, ff, n_seq, n_blk):
        self.rows, self.ff, self.n_seq, self.n_blk = rows, ff, n_seq, n_blk
        self.seq = lax.axis_index("seq")
        self.blk = lax.axis_index("blk")
        self.core = lax.rem(self.blk, 2)
        self.chip = lax.div(self.blk, 2)
        self.chips = n_blk // 2

    def give(self, owner, kind, src, dst, send, recv):
        here = dst.at[pl.ds(multiple(self.seq * self.rows, self.rows), self.rows)]

        @pl.when(self.seq != owner)
        def _():
            remote(src, here, send.at[kind, owner], recv.at[kind, self.seq], {"seq": owner}).start()

        @pl.when(self.seq == owner)
        def _():
            pltpu.make_async_copy(src, here, recv.at[kind, self.seq]).start()

    def given(self, owner, kind, src, dst, send, recv):
        for other in range(self.n_seq):
            there = dst.at[pl.ds(other * self.rows, self.rows)]
            if other == owner:
                pltpu.make_async_copy(src, there, recv.at[kind, other]).wait()
            else:
                remote(src, there, send.at[kind, other], recv.at[kind, other], {"seq": other}).wait_recv()

    def sent(self, owner, kind, src, dst, send, recv):
        here = dst.at[pl.ds(multiple(self.seq * self.rows, self.rows), self.rows)]

        @pl.when(self.seq != owner)
        def _():
            remote(src, here, send.at[kind, owner], recv.at[kind, self.seq], {"seq": owner}).wait_send()

    def turned(self, step):
        return lax.rem(self.chip + step, self.chips)

    def swap(self, part, size, chip, got, send, recv):
        src = part.at[pl.ds(multiple((2 * chip + 1 - self.core) * size, 32), size)]
        dst = got.at[pl.ds(multiple(chip * size, 32), size)]
        return remote(src, dst, send.at[chip], recv.at[chip], {"blk": 2 * self.chip + 1 - self.core})

    def forward(self, part, size, step, got, send, recv):
        chip = self.turned(step)
        src = part.at[pl.ds(multiple((2 * chip + self.core) * size, 32), size)]
        dst = got.at[pl.ds(multiple((step - 1) * size, 32), size)]
        return remote(src, dst, send.at[step - 1], recv.at[step - 1], {"blk": 2 * chip + self.core})

    def reduce_begin(self, part, size, cgot, zgot, sems):
        csend, crecv, zsend, zrecv = sems

        def one(step, unused):
            chip = self.turned(step)
            self.swap(part, size, chip, cgot, csend, crecv).wait()
            mine = (2 * chip + self.core) * size

            def add(group, unused):
                at = pl.ds(multiple(mine + group * 32, 32), 32)
                other = pl.ds(multiple(chip * size + group * 32, 32), 32)
                part[at, :] = (part[at, :].astype(F32) + cgot[other, :].astype(F32)).astype(BF16)
                return unused

            lax.fori_loop(0, size // 32, add, 0)
            self.forward(part, size, step, zgot, zsend, zrecv).start()
            return unused

        lax.fori_loop(1, self.chips, one, 0)
        self.swap(part, size, self.chip, cgot, csend, crecv).wait()

    def reduce_end(self, part, size, cgot, zgot, total, sems):
        csend, crecv, zsend, zrecv = sems

        def arrived(step, unused):
            self.forward(part, size, step, zgot, zsend, zrecv).wait()
            return unused

        lax.fori_loop(1, self.chips, arrived, 0)
        mine = self.blk * size

        def add(group, unused):
            at = pl.ds(multiple(mine + group * 32, 32), 32)
            other = pl.ds(multiple(self.chip * size + group * 32, 32), 32)
            value = part[at, :].astype(F32) + cgot[other, :].astype(F32)
            for step in range(1, self.chips):
                there = pl.ds(multiple((step - 1) * size + group * 32, 32), 32)
                value = value + zgot[there, :].astype(F32)
            total[pl.ds(multiple(group * 32, 32), 32), :] = value.astype(BF16)
            return unused

        lax.fori_loop(0, size // 32, add, 0)

    def spread(self, owner_static, src, dst, kind, send, recv, local):
        for other in range(self.n_seq):
            if other != owner_static:
                remote(src, dst, send.at[kind, other], recv.at[kind], {"seq": other}).start()
        pltpu.make_async_copy(src, dst, local.at[kind]).start()

    def spread_wait(self, owner, src, dst, kind, send, recv, local):
        @pl.when(self.seq == owner)
        def _():
            for other in range(self.n_seq):
                if other != owner:
                    remote(src, dst, send.at[kind, other], recv.at[kind], {"seq": other}).wait_send()
            pltpu.make_async_copy(src, dst, local.at[kind]).wait()

        @pl.when(self.seq != owner)
        def _():
            remote(src, dst, send.at[kind, owner], recv.at[kind], {"seq": owner}).wait_recv()


def outer_tiles(lhs, rhs, part, turned, chip, tiles, part_at):
    turned[...] = lhs[:, pl.ds(multiple(chip * TILE, TILE), TILE)].T

    def tile(index, unused):
        value = jnp.dot(turned[...], rhs[:, pl.ds(multiple(index * TILE, TILE), TILE)], preferred_element_type=F32)
        part[pl.ds(multiple(chip * TILE, TILE), TILE), pl.ds(multiple(part_at + index * TILE, TILE), TILE)] = (
            value.astype(BF16)
        )
        return unused

    lax.fori_loop(0, tiles, tile, 0)


def grad_kernel(
    sizes,
    normed, q_grad, k_grad, v_grad, att, mid, two, gate_up, act, cot, gains,
    out_gu, out_down, out_out, out_query, out_key, out_value, out_gain,
    buf_a, buf_b, buf_att, buf_mid, buf_n, buf_t,
    turned, part, part_down, part_tail, cgot, cgot_down, cgot_tail, zgot, zgot_down, zgot_tail,
    total, total_down, total_tail, gain_got, gain_sum,
    xsend, xrecv, csend, crecv, zsend, zrecv, csend_t, crecv_t, zsend_t, zrecv_t,
    gsend, grecv, glocal, hsend, hrecv, isend, irecv,
):
    rows, width, ff, n_seq, n_blk, split = sizes
    run = Reducer(rows, ff, n_seq, n_blk)
    barrier = pltpu.get_barrier_semaphore()
    for step in range(1, n_seq):
        pl.semaphore_signal(barrier, inc=1, device_id={"seq": lax.rem(run.seq + step, n_seq)}, device_id_type=MESH)
    for step in range(1, n_blk):
        pl.semaphore_signal(barrier, inc=1, device_id={"blk": lax.rem(run.blk + step, n_blk)}, device_id_type=MESH)
    pl.semaphore_wait(barrier, n_seq + n_blk - 2)

    cuts = [0]
    for tiles in split:
        cuts.append(cuts[-1] + tiles * TILE)
    wide = max(split) * TILE
    chunk = width // n_blk
    down = ff // n_blk
    first = [
        [(0, two, buf_a), (1, gate_up.at[:, cuts[0] : cuts[1]], buf_b.at[:, : cuts[1] - cuts[0]])],
        [(0, two, buf_a), (1, gate_up.at[:, cuts[1] : cuts[2]], buf_b.at[:, : cuts[2] - cuts[1]])],
        [
            (0, two, buf_a),
            (1, gate_up.at[:, cuts[2] : cuts[3]], buf_b.at[:, : cuts[3] - cuts[2]]),
            (2, att, buf_att),
            (3, mid, buf_mid),
        ],
        [(0, cot, buf_a), (1, act, buf_b)],
    ]
    last = [
        [(4, normed, buf_n), (5, q_grad, buf_t)],
        [(4, normed, buf_n), (5, k_grad, buf_t)],
        [(4, normed, buf_n), (5, v_grad, buf_t)],
        [],
    ]
    for owner in range(n_seq):
        for kind, src, dst in first[owner]:
            run.give(owner, kind, src, dst, xsend, xrecv)
    for owner in range(n_seq):
        for kind, src, dst in last[owner]:
            run.give(owner, kind, src, dst, xsend, xrecv)

    for step in range(1, n_blk):
        other = lax.rem(run.blk + step, n_blk)
        remote(gains.at[other], gain_got.at[step - 1], hsend.at[step - 1], hrecv.at[step - 1], {"blk": other}).start()

    sems = (csend, crecv, zsend, zrecv)
    tail_sems = (csend_t, crecv_t, zsend_t, zrecv_t)

    for owner in range(n_seq):

        @pl.when(run.seq == owner)
        def _(owner=owner):
            for kind, src, dst in first[owner]:
                run.given(owner, kind, src, dst, xsend, xrecv)

    @pl.when(run.seq < 3)
    def _():
        def one(step, unused):
            chip = run.turned(step)

            @pl.when(run.seq < 2)
            def _():
                outer_tiles(buf_a, buf_b, part, turned, chip, split[0], 0)

            @pl.when(run.seq == 2)
            def _():
                spare = wide - split[2] * TILE - width
                if spare:
                    part[pl.ds(multiple(chip * TILE, TILE), TILE), wide - spare :] = jnp.zeros((TILE, spare), BF16)
                outer_tiles(buf_a, buf_b, part, turned, chip, split[2], 0)
                outer_tiles(buf_att, buf_mid, part, turned, chip, width // TILE, split[2] * TILE)

            run.swap(part, chunk, chip, cgot, csend, crecv).start()
            return unused

        lax.fori_loop(1, run.chips + 1, one, 0)

    @pl.when(run.seq == 3)
    def _():
        def one(index, unused):
            at = pl.ds(multiple(index * TILE, TILE), TILE)
            turned[...] = buf_b[:, at].T
            part_down[at, :] = jnp.dot(turned[...], buf_a[...], preferred_element_type=F32).astype(BF16)
            return unused

        lax.fori_loop(0, ff // TILE, one, 0)

        def swaps(step, unused):
            run.swap(part_down, down, run.turned(step), cgot_down, csend, crecv).start()
            return unused

        lax.fori_loop(1, run.chips + 1, swaps, 0)

    @pl.when(run.seq < 3)
    def _():
        run.reduce_begin(part, chunk, cgot, zgot, sems)

    @pl.when(run.seq == 3)
    def _():
        run.reduce_begin(part_down, down, cgot_down, zgot_down, sems)

    for owner in range(n_seq - 1):

        @pl.when(run.seq == owner)
        def _(owner=owner):
            for kind, src, dst in last[owner]:
                run.given(owner, kind, src, dst, xsend, xrecv)

    @pl.when(run.seq < 3)
    def _():
        def one(step, unused):
            chip = run.turned(step)
            outer_tiles(buf_n, buf_t, part_tail, turned, chip, width // TILE, 0)
            run.swap(part_tail, chunk, chip, cgot_tail, csend_t, crecv_t).start()
            return unused

        lax.fori_loop(1, run.chips + 1, one, 0)
        run.reduce_begin(part_tail, chunk, cgot_tail, zgot_tail, tail_sems)

    spreads = [
        (0, total.at[:, : cuts[1] - cuts[0]], out_gu.at[:, cuts[0] : cuts[1]], 0),
        (1, total.at[:, : cuts[2] - cuts[1]], out_gu.at[:, cuts[1] : cuts[2]], 1),
        (2, total.at[:, : cuts[3] - cuts[2]], out_gu.at[:, cuts[2] : cuts[3]], 2),
        (2, total.at[:, cuts[3] - cuts[2] : cuts[3] - cuts[2] + width], out_out, 3),
        (3, total_down, out_down, 4),
    ]
    tails = [
        (0, total_tail, out_query, 5),
        (1, total_tail, out_key, 6),
        (2, total_tail, out_value, 7),
    ]

    @pl.when(run.seq < 3)
    def _():
        run.reduce_end(part, chunk, cgot, zgot, total, sems)

    @pl.when(run.seq == 3)
    def _():
        run.reduce_end(part_down, down, cgot_down, zgot_down, total_down, sems)

    for owner, src, dst, kind in spreads:

        @pl.when(run.seq == owner)
        def _(owner=owner, src=src, dst=dst, kind=kind):
            run.spread(owner, src, dst, kind, gsend, grecv, glocal)

    value = gains[run.blk]
    for step in range(1, n_blk):
        other = lax.rem(run.blk + step, n_blk)
        copy = remote(gains.at[other], gain_got.at[step - 1], hsend.at[step - 1], hrecv.at[step - 1], {"blk": other})
        copy.wait()
        value = value + gain_got[step - 1]
    gain_sum[run.seq] = value
    for step in range(1, n_seq):
        other = lax.rem(run.seq + step, n_seq)
        remote(gain_sum.at[run.seq], gain_sum.at[run.seq], isend.at[step - 1], irecv.at[run.seq], {"seq": other}).start()

    @pl.when(run.seq < 3)
    def _():
        run.reduce_end(part_tail, chunk, cgot_tail, zgot_tail, total_tail, tail_sems)

    for owner, src, dst, kind in tails:

        @pl.when(run.seq == owner)
        def _(owner=owner, src=src, dst=dst, kind=kind):
            run.spread(owner, src, dst, kind, gsend, grecv, glocal)

    for step in range(1, n_seq):
        other = lax.rem(run.seq + step, n_seq)
        remote(gain_sum.at[other], gain_sum.at[other], isend.at[step - 1], irecv.at[other], {"seq": other}).wait()
    value = gain_sum[0]
    for group in range(1, n_seq):
        value = value + gain_sum[group]
    half = value.shape[0] // 2
    out_gain[...] = jnp.concatenate(
        [
            jnp.broadcast_to(jnp.sum(value[:half], axis=0, keepdims=True), (half, value.shape[1])),
            jnp.broadcast_to(jnp.sum(value[half:], axis=0, keepdims=True), (half, value.shape[1])),
        ],
        axis=0,
    )

    for owner, src, dst, kind in spreads + tails:
        run.spread_wait(owner, src, dst, kind, gsend, grecv, glocal)
    for owner in range(n_seq):
        for kind, src, dst in first[owner] + last[owner]:
            run.sent(owner, kind, src, dst, xsend, xrecv)


def reduce_grads(sizes, operands):
    rows, width, ff, n_seq, n_blk, split = sizes
    wide = max(split) * TILE
    chunk, down = width // n_blk, ff // n_blk
    all_rows = n_seq * rows
    chips = n_blk // 2
    vmem = pl.BlockSpec(memory_space=pltpu.VMEM)
    hbm = pl.BlockSpec(memory_space=pl.ANY)
    shape = jax.ShapeDtypeStruct
    dma = pltpu.SemaphoreType.DMA
    return pl.pallas_call(
        functools.partial(grad_kernel, sizes),
        out_shape=(
            shape((chunk, 2 * ff), BF16),
            shape((down, width), BF16),
            shape((chunk, width), BF16),
            shape((chunk, width), BF16),
            shape((chunk, width), BF16),
            shape((chunk, width), BF16),
            shape((16, chunk), F32),
        ),
        in_specs=[vmem] * len(operands),
        out_specs=(hbm,) * 6 + (vmem,),
        scratch_shapes=[
            pltpu.VMEM((all_rows, width), BF16),
            pltpu.VMEM((all_rows, ff), BF16),
            pltpu.VMEM((all_rows, width), BF16),
            pltpu.VMEM((all_rows, width), BF16),
            pltpu.VMEM((all_rows, width), BF16),
            pltpu.VMEM((all_rows, width), BF16),
            pltpu.VMEM((TILE, all_rows), BF16),
            pltpu.VMEM((width, wide), BF16),
            pltpu.VMEM((ff, width), BF16),
            pltpu.VMEM((width, width), BF16),
            pltpu.VMEM((chips * chunk, wide), BF16),
            pltpu.VMEM((chips * down, width), BF16),
            pltpu.VMEM((chips * chunk, width), BF16),
            pltpu.VMEM(((chips - 1) * chunk, wide), BF16),
            pltpu.VMEM(((chips - 1) * down, width), BF16),
            pltpu.VMEM(((chips - 1) * chunk, width), BF16),
            pltpu.VMEM((chunk, wide), BF16),
            pltpu.VMEM((down, width), BF16),
            pltpu.VMEM((chunk, width), BF16),
            pltpu.VMEM((n_blk - 1, 16, chunk), F32),
            pltpu.VMEM((n_seq, 16, chunk), F32),
            dma((6, n_seq)), dma((6, n_seq)),
            dma((chips,)), dma((chips,)), dma((chips - 1,)), dma((chips - 1,)),
            dma((chips,)), dma((chips,)), dma((chips - 1,)), dma((chips - 1,)),
            dma((8, n_seq)), dma((8,)), dma((8,)),
            dma((n_blk - 1,)), dma((n_blk - 1,)),
            dma((n_seq - 1,)), dma((n_seq,)),
        ],
        compiler_params=pltpu.CompilerParams(
            collective_id=0, has_side_effects=True, vmem_limit_bytes=60 * 1024 * 1024
        ),
        name="weight_grads",
    )(*operands)


def eighths(values, n_blk):
    rows, width = values.shape
    part = jnp.sum(values.reshape(rows // 8, 8, width), axis=0)
    return part.reshape(8, n_blk, width // n_blk).transpose(1, 0, 2)


def tile_split(width, ff):
    tiles, more = 2 * ff // TILE, width // TILE
    each = -(-(tiles + more) // 3)
    return (each, each, tiles - 2 * each)


def fits(n_seq, n_blk, rows, width, ff):
    return (
        n_seq == 4
        and n_blk % 2 == 0
        and n_blk * 128 == width
        and rows == 128
        and ff % TILE == 0
        and (ff // n_blk) % 32 == 0
    )


def local(
    tokens,
    first_values,
    doc_lengths,
    attn_gain,
    query_weight,
    key_weight,
    value_weight,
    out_weight,
    ffn_gain,
    gate_weight,
    up_weight,
    down_weight,
    cotangent,
):
    rows, width = tokens.shape
    heads = width // HEAD_DIM
    scale = HEAD_DIM ** (-0.5)
    shape3 = (rows, heads, HEAD_DIM)
    my_start = lax.axis_index("blk") * rows
    my_index = my_start + jnp.arange(rows, dtype=jnp.int32)
    my_doc, my_pos = doc_layout(doc_lengths, my_index)
    cosine, sine = tables(my_pos)
    source = tokens.astype(jnp.float32)
    inv_first = lax.rsqrt(jnp.mean(source * source, axis=-1, keepdims=True) + EPS)
    normed = (source * inv_first * attn_gain).astype(jnp.bfloat16)
    query_pre = jnp.dot(normed, query_weight, preferred_element_type=jnp.float32)
    key_pre = jnp.dot(normed, key_weight, preferred_element_type=jnp.float32)
    value_pre = jnp.dot(normed, value_weight, preferred_element_type=jnp.float32)
    queries = rotate(query_pre.reshape(shape3), cosine, sine).astype(jnp.bfloat16)
    keys = rotate(key_pre.reshape(shape3), cosine, sine).astype(jnp.bfloat16).reshape(rows, width)
    mixed = (MIX * value_pre + MIX * first_values.astype(jnp.float32)).astype(jnp.bfloat16)
    keys_local = keys.reshape(shape3)
    mixed_local = mixed.reshape(shape3)

    def allowed_mask(query_index, query_doc, key_index, key_doc):
        return (query_doc[:, None] == key_doc[None, :]) & (
            key_index[None, :] <= query_index[:, None]
        )

    def forward_step(state, pieces, start):
        count = pieces[0].shape[0]
        keys_piece = pieces[0].reshape(count, heads, HEAD_DIM)
        values_piece = pieces[1].reshape(count, heads, HEAD_DIM)
        key_index = start + jnp.arange(count, dtype=jnp.int32)

        def forward_compute(state):
            high, total, accum = state
            key_doc, unused = doc_layout(doc_lengths, key_index)
            allowed = allowed_mask(my_index, my_doc, key_index, key_doc)[None]
            score = (
                jnp.einsum("qhd,khd->hqk", queries, keys_piece, preferred_element_type=jnp.float32)
                * scale
            )
            score = jnp.where(allowed, score, NEG)
            new_high = jnp.maximum(high, jnp.max(score, axis=-1))
            weight = jnp.where(allowed, jnp.exp(score - new_high[:, :, None]), 0.0)
            factor = jnp.exp(high - new_high)
            total = total * factor + jnp.sum(weight, axis=-1)
            accum = accum * factor.T[:, :, None] + jnp.einsum(
                "hqk,khd->qhd",
                weight.astype(jnp.bfloat16),
                values_piece,
                preferred_element_type=jnp.float32,
            )
            return (new_high, total, accum)

        return lax.cond(start <= my_index[-1], forward_compute, lambda kept: kept, state)

    def query_grad_step(grad_q, pieces, start):
        count = pieces[0].shape[0]
        keys_piece = pieces[0].reshape(count, heads, HEAD_DIM)
        values_piece = pieces[1].reshape(count, heads, HEAD_DIM)
        key_index = start + jnp.arange(count, dtype=jnp.int32)

        def query_compute(grad_q):
            key_doc, unused = doc_layout(doc_lengths, key_index)
            allowed = allowed_mask(my_index, my_doc, key_index, key_doc)[None]
            score = (
                jnp.einsum("qhd,khd->hqk", queries, keys_piece, preferred_element_type=jnp.float32)
                * scale
            )
            prob = jnp.where(allowed, jnp.exp(score - logsum[:, :, None]), 0.0)
            prob_grad = jnp.einsum(
                "qhd,khd->hqk", outgrad_local, values_piece, preferred_element_type=jnp.float32
            )
            score_grad = (prob * (prob_grad - delta[:, :, None])).astype(jnp.bfloat16)
            return (
                grad_q
                + jnp.einsum(
                    "hqk,khd->qhd", score_grad, keys_piece, preferred_element_type=jnp.float32
                )
                * scale
            )

        return lax.cond(start <= my_index[-1], query_compute, lambda kept: kept, grad_q)

    init = (
        jnp.full((heads, rows), NEG, jnp.float32),
        jnp.zeros((heads, rows), jnp.float32),
        jnp.zeros(shape3, jnp.float32),
    )
    state = by_blocks(
        forward_step,
        init,
        (
            lax.all_gather(keys, "blk", axis=0, tiled=True),
            lax.all_gather(mixed, "blk", axis=0, tiled=True),
        ),
        jnp.int32(0),
    )
    high, total, accum = state
    logsum = high + jnp.log(total)
    attended = accum / total.T[:, :, None]
    attended_b = attended.astype(jnp.bfloat16).reshape(rows, width)
    mid = source + jnp.dot(attended_b, out_weight, preferred_element_type=jnp.float32)
    inv_second = lax.rsqrt(jnp.mean(mid * mid, axis=-1, keepdims=True) + EPS)
    normed_two = (mid * inv_second * ffn_gain).astype(jnp.bfloat16)
    gate = jnp.dot(normed_two, gate_weight, preferred_element_type=jnp.float32)
    up = jnp.dot(normed_two, up_weight, preferred_element_type=jnp.float32)
    act = (jax.nn.silu(gate) * up).astype(jnp.bfloat16)
    layer_output = mid + jnp.dot(act, down_weight, preferred_element_type=jnp.float32)
    cot_float = cotangent.astype(jnp.float32)
    grad_down = outer(act, cotangent)
    act_grad = back(cotangent, down_weight)
    sigma = jax.nn.sigmoid(gate)
    gate_grad = (act_grad * up * sigma * (1.0 + gate * (1.0 - sigma))).astype(jnp.bfloat16)
    up_grad = (act_grad * gate * sigma).astype(jnp.bfloat16)
    grad_gate = outer(normed_two, gate_grad)
    grad_up = outer(normed_two, up_grad)
    normed_two_grad = back(gate_grad, gate_weight) + back(up_grad, up_weight)
    grad_ffn_gain = jnp.sum(normed_two_grad * mid * inv_second, axis=0)
    scaled_two = normed_two_grad * ffn_gain
    mid_grad = (
        cot_float
        + inv_second * scaled_two
        - mid * inv_second**3 * jnp.mean(scaled_two * mid, axis=-1, keepdims=True)
    )
    mid_grad_b = mid_grad.astype(jnp.bfloat16)
    grad_out_weight = outer(attended_b, mid_grad_b)
    attended_grad = back(mid_grad_b, out_weight).astype(jnp.bfloat16)
    outgrad_local = attended_grad.reshape(shape3)
    delta = jnp.sum(outgrad_local.astype(jnp.float32) * attended, axis=-1).T
    zeros3 = jnp.zeros(shape3, jnp.float32)
    grad_q = by_blocks(
        query_grad_step,
        zeros3,
        (
            lax.all_gather(keys, "blk", axis=0, tiled=True),
            lax.all_gather(mixed, "blk", axis=0, tiled=True),
        ),
        jnp.int32(0),
    )
    all_logsum, all_delta = (
        lax.all_gather(logsum.T, "blk", axis=0, tiled=True),
        lax.all_gather(delta.T, "blk", axis=0, tiled=True),
    )

    def key_grad_step(state, pieces, start):
        count = pieces[0].shape[0]
        query_piece = pieces[0].reshape(count, heads, HEAD_DIM)
        outgrad_piece = pieces[1].reshape(count, heads, HEAD_DIM)
        query_index = start + jnp.arange(count, dtype=jnp.int32)

        def key_compute(state):
            grad_k, grad_v = state
            logsum_piece = lax.dynamic_slice_in_dim(all_logsum, start, count, 0).T
            delta_piece = lax.dynamic_slice_in_dim(all_delta, start, count, 0).T
            query_doc, unused = doc_layout(doc_lengths, query_index)
            allowed = allowed_mask(query_index, query_doc, my_index, my_doc)[None]
            score = (
                jnp.einsum(
                    "qhd,khd->hqk", query_piece, keys_local, preferred_element_type=jnp.float32
                )
                * scale
            )
            prob = jnp.where(allowed, jnp.exp(score - logsum_piece[:, :, None]), 0.0)
            grad_v = grad_v + jnp.einsum(
                "hqk,qhd->khd",
                prob.astype(jnp.bfloat16),
                outgrad_piece,
                preferred_element_type=jnp.float32,
            )
            prob_grad = jnp.einsum(
                "qhd,khd->hqk", outgrad_piece, mixed_local, preferred_element_type=jnp.float32
            )
            score_grad = (prob * (prob_grad - delta_piece[:, :, None])).astype(jnp.bfloat16)
            grad_k = (
                grad_k
                + jnp.einsum(
                    "hqk,qhd->khd", score_grad, query_piece, preferred_element_type=jnp.float32
                )
                * scale
            )
            return (grad_k, grad_v)

        return lax.cond(query_index[-1] >= my_start, key_compute, lambda kept: kept, state)

    grad_k, grad_v = by_blocks(
        key_grad_step,
        (zeros3, zeros3),
        (
            lax.all_gather(queries.reshape(rows, width), "blk", axis=0, tiled=True),
            lax.all_gather(attended_grad, "blk", axis=0, tiled=True),
        ),
        jnp.int32(0),
    )
    queries_grad = grad_q.astype(jnp.bfloat16)
    keys_grad = grad_k.astype(jnp.bfloat16)
    mixed_grad = grad_v.astype(jnp.bfloat16).reshape(rows, width)
    q_pre_grad = (
        rotate(queries_grad.astype(jnp.float32), cosine, -sine)
        .astype(jnp.bfloat16)
        .reshape(rows, width)
    )
    k_pre_grad = (
        rotate(keys_grad.astype(jnp.float32), cosine, -sine)
        .astype(jnp.bfloat16)
        .reshape(rows, width)
    )
    grad_first = MIX * mixed_grad.astype(jnp.float32)
    value_grad = grad_first.astype(jnp.bfloat16)
    grad_query = outer(normed, q_pre_grad)
    grad_key = outer(normed, k_pre_grad)
    grad_value = outer(normed, value_grad)
    normed_grad = (
        back(q_pre_grad, query_weight)
        + back(k_pre_grad, key_weight)
        + back(value_grad, value_weight)
    )
    grad_attn_gain = jnp.sum(normed_grad * source * inv_first, axis=0)
    scaled_one = normed_grad * attn_gain
    grad_tokens = (
        mid_grad
        + inv_first * scaled_one
        - source * inv_first**3 * jnp.mean(scaled_one * source, axis=-1, keepdims=True)
    )
    summed = (
        lax.psum_scatter(grad_attn_gain, "blk", scatter_dimension=0, tiled=True),
        lax.psum_scatter(grad_query, "blk", scatter_dimension=0, tiled=True),
        lax.psum_scatter(grad_key, "blk", scatter_dimension=0, tiled=True),
        lax.psum_scatter(grad_value, "blk", scatter_dimension=0, tiled=True),
        lax.psum_scatter(grad_out_weight, "blk", scatter_dimension=0, tiled=True),
        lax.psum_scatter(grad_ffn_gain, "blk", scatter_dimension=0, tiled=True),
        lax.psum_scatter(grad_gate, "blk", scatter_dimension=0, tiled=True),
        lax.psum_scatter(grad_up, "blk", scatter_dimension=0, tiled=True),
        lax.psum_scatter(grad_down, "blk", scatter_dimension=0, tiled=True),
    )
    summed = (
        lax.psum(summed[0].astype(jnp.bfloat16), "seq").astype(jnp.float32),
        lax.psum(summed[1].astype(jnp.bfloat16), "seq").astype(jnp.float32),
        lax.psum(summed[2].astype(jnp.bfloat16), "seq").astype(jnp.float32),
        lax.psum(summed[3].astype(jnp.bfloat16), "seq").astype(jnp.float32),
        lax.psum(summed[4].astype(jnp.bfloat16), "seq").astype(jnp.float32),
        lax.psum(summed[5].astype(jnp.bfloat16), "seq").astype(jnp.float32),
        lax.psum(summed[6].astype(jnp.bfloat16), "seq").astype(jnp.float32),
        lax.psum(summed[7].astype(jnp.bfloat16), "seq").astype(jnp.float32),
        lax.psum(summed[8].astype(jnp.bfloat16), "seq").astype(jnp.float32),
    )
    return (
        layer_output,
        grad_tokens,
        grad_first,
        summed[0],
        summed[1],
        summed[2],
        summed[3],
        summed[4],
        summed[5],
        summed[6],
        summed[7],
        summed[8],
    )


def local_fast(
    n_seq,
    n_blk,
    tokens,
    first_values,
    doc_lengths,
    attn_gain,
    query_weight,
    key_weight,
    value_weight,
    out_weight,
    ffn_gain,
    gate_weight,
    up_weight,
    down_weight,
    cotangent,
):
    rows, width = tokens.shape
    heads = width // HEAD_DIM
    scale = HEAD_DIM ** (-0.5)
    shape3 = (rows, heads, HEAD_DIM)
    my_start = lax.axis_index("blk") * rows
    my_index = my_start + jnp.arange(rows, dtype=jnp.int32)
    my_doc, my_pos = doc_layout(doc_lengths, my_index)
    cosine, sine = tables(my_pos)
    source = tokens.astype(jnp.float32)
    inv_first = lax.rsqrt(jnp.mean(source * source, axis=-1, keepdims=True) + EPS)
    normed = (source * inv_first * attn_gain).astype(jnp.bfloat16)
    query_pre = jnp.dot(normed, query_weight, preferred_element_type=jnp.float32)
    key_pre = jnp.dot(normed, key_weight, preferred_element_type=jnp.float32)
    value_pre = jnp.dot(normed, value_weight, preferred_element_type=jnp.float32)
    queries = rotate(query_pre.reshape(shape3), cosine, sine).astype(jnp.bfloat16)
    keys = rotate(key_pre.reshape(shape3), cosine, sine).astype(jnp.bfloat16).reshape(rows, width)
    mixed = (MIX * value_pre + MIX * first_values.astype(jnp.float32)).astype(jnp.bfloat16)
    keys_local = keys.reshape(shape3)
    mixed_local = mixed.reshape(shape3)

    def allowed_mask(query_index, query_doc, key_index, key_doc):
        return (query_doc[:, None] == key_doc[None, :]) & (
            key_index[None, :] <= query_index[:, None]
        )

    def forward_step(state, pieces, start):
        count = pieces[0].shape[0]
        keys_piece = pieces[0].reshape(count, heads, HEAD_DIM)
        values_piece = pieces[1].reshape(count, heads, HEAD_DIM)
        key_index = start + jnp.arange(count, dtype=jnp.int32)

        def forward_compute(state):
            high, total, accum = state
            key_doc, unused = doc_layout(doc_lengths, key_index)
            allowed = allowed_mask(my_index, my_doc, key_index, key_doc)[None]
            score = (
                jnp.einsum("qhd,khd->hqk", queries, keys_piece, preferred_element_type=jnp.float32)
                * scale
            )
            score = jnp.where(allowed, score, NEG)
            new_high = jnp.maximum(high, jnp.max(score, axis=-1))
            weight = jnp.where(allowed, jnp.exp(score - new_high[:, :, None]), 0.0)
            factor = jnp.exp(high - new_high)
            total = total * factor + jnp.sum(weight, axis=-1)
            accum = accum * factor.T[:, :, None] + jnp.einsum(
                "hqk,khd->qhd",
                weight.astype(jnp.bfloat16),
                values_piece,
                preferred_element_type=jnp.float32,
            )
            return (new_high, total, accum)

        return lax.cond(start <= my_index[-1], forward_compute, lambda kept: kept, state)

    def query_grad_step(grad_q, pieces, start):
        count = pieces[0].shape[0]
        keys_piece = pieces[0].reshape(count, heads, HEAD_DIM)
        values_piece = pieces[1].reshape(count, heads, HEAD_DIM)
        key_index = start + jnp.arange(count, dtype=jnp.int32)

        def query_compute(grad_q):
            key_doc, unused = doc_layout(doc_lengths, key_index)
            allowed = allowed_mask(my_index, my_doc, key_index, key_doc)[None]
            score = (
                jnp.einsum("qhd,khd->hqk", queries, keys_piece, preferred_element_type=jnp.float32)
                * scale
            )
            prob = jnp.where(allowed, jnp.exp(score - logsum[:, :, None]), 0.0)
            prob_grad = jnp.einsum(
                "qhd,khd->hqk", outgrad_local, values_piece, preferred_element_type=jnp.float32
            )
            score_grad = (prob * (prob_grad - delta[:, :, None])).astype(jnp.bfloat16)
            return (
                grad_q
                + jnp.einsum(
                    "hqk,khd->qhd", score_grad, keys_piece, preferred_element_type=jnp.float32
                )
                * scale
            )

        return lax.cond(start <= my_index[-1], query_compute, lambda kept: kept, grad_q)

    init = (
        jnp.full((heads, rows), NEG, jnp.float32),
        jnp.zeros((heads, rows), jnp.float32),
        jnp.zeros(shape3, jnp.float32),
    )
    state = by_blocks(
        forward_step,
        init,
        (
            lax.all_gather(keys, "blk", axis=0, tiled=True),
            lax.all_gather(mixed, "blk", axis=0, tiled=True),
        ),
        jnp.int32(0),
    )
    high, total, accum = state
    logsum = high + jnp.log(total)
    attended = accum / total.T[:, :, None]
    attended_b = attended.astype(jnp.bfloat16).reshape(rows, width)
    mid = source + jnp.dot(attended_b, out_weight, preferred_element_type=jnp.float32)
    inv_second = lax.rsqrt(jnp.mean(mid * mid, axis=-1, keepdims=True) + EPS)
    normed_two = (mid * inv_second * ffn_gain).astype(jnp.bfloat16)
    gate = jnp.dot(normed_two, gate_weight, preferred_element_type=jnp.float32)
    up = jnp.dot(normed_two, up_weight, preferred_element_type=jnp.float32)
    act = (jax.nn.silu(gate) * up).astype(jnp.bfloat16)
    layer_output = mid + jnp.dot(act, down_weight, preferred_element_type=jnp.float32)
    cot_float = cotangent.astype(jnp.float32)
    act_grad = back(cotangent, down_weight)
    sigma = jax.nn.sigmoid(gate)
    gate_grad = (act_grad * up * sigma * (1.0 + gate * (1.0 - sigma))).astype(jnp.bfloat16)
    up_grad = (act_grad * gate * sigma).astype(jnp.bfloat16)
    normed_two_grad = back(gate_grad, gate_weight) + back(up_grad, up_weight)
    grad_ffn_gain = eighths(normed_two_grad * mid * inv_second, n_blk)
    scaled_two = normed_two_grad * ffn_gain
    mid_grad = (
        cot_float
        + inv_second * scaled_two
        - mid * inv_second**3 * jnp.mean(scaled_two * mid, axis=-1, keepdims=True)
    )
    mid_grad_b = mid_grad.astype(jnp.bfloat16)
    attended_grad = back(mid_grad_b, out_weight).astype(jnp.bfloat16)
    outgrad_local = attended_grad.reshape(shape3)
    delta = jnp.sum(outgrad_local.astype(jnp.float32) * attended, axis=-1).T
    zeros3 = jnp.zeros(shape3, jnp.float32)
    grad_q = by_blocks(
        query_grad_step,
        zeros3,
        (
            lax.all_gather(keys, "blk", axis=0, tiled=True),
            lax.all_gather(mixed, "blk", axis=0, tiled=True),
        ),
        jnp.int32(0),
    )
    all_logsum, all_delta = (
        lax.all_gather(logsum.T, "blk", axis=0, tiled=True),
        lax.all_gather(delta.T, "blk", axis=0, tiled=True),
    )

    def key_grad_step(state, pieces, start):
        count = pieces[0].shape[0]
        query_piece = pieces[0].reshape(count, heads, HEAD_DIM)
        outgrad_piece = pieces[1].reshape(count, heads, HEAD_DIM)
        query_index = start + jnp.arange(count, dtype=jnp.int32)

        def key_compute(state):
            grad_k, grad_v = state
            logsum_piece = lax.dynamic_slice_in_dim(all_logsum, start, count, 0).T
            delta_piece = lax.dynamic_slice_in_dim(all_delta, start, count, 0).T
            query_doc, unused = doc_layout(doc_lengths, query_index)
            allowed = allowed_mask(query_index, query_doc, my_index, my_doc)[None]
            score = (
                jnp.einsum(
                    "qhd,khd->hqk", query_piece, keys_local, preferred_element_type=jnp.float32
                )
                * scale
            )
            prob = jnp.where(allowed, jnp.exp(score - logsum_piece[:, :, None]), 0.0)
            grad_v = grad_v + jnp.einsum(
                "hqk,qhd->khd",
                prob.astype(jnp.bfloat16),
                outgrad_piece,
                preferred_element_type=jnp.float32,
            )
            prob_grad = jnp.einsum(
                "qhd,khd->hqk", outgrad_piece, mixed_local, preferred_element_type=jnp.float32
            )
            score_grad = (prob * (prob_grad - delta_piece[:, :, None])).astype(jnp.bfloat16)
            grad_k = (
                grad_k
                + jnp.einsum(
                    "hqk,qhd->khd", score_grad, query_piece, preferred_element_type=jnp.float32
                )
                * scale
            )
            return (grad_k, grad_v)

        return lax.cond(query_index[-1] >= my_start, key_compute, lambda kept: kept, state)

    grad_k, grad_v = by_blocks(
        key_grad_step,
        (zeros3, zeros3),
        (
            lax.all_gather(queries.reshape(rows, width), "blk", axis=0, tiled=True),
            lax.all_gather(attended_grad, "blk", axis=0, tiled=True),
        ),
        jnp.int32(0),
    )
    queries_grad = grad_q.astype(jnp.bfloat16)
    keys_grad = grad_k.astype(jnp.bfloat16)
    mixed_grad = grad_v.astype(jnp.bfloat16).reshape(rows, width)
    q_pre_grad = (
        rotate(queries_grad.astype(jnp.float32), cosine, -sine)
        .astype(jnp.bfloat16)
        .reshape(rows, width)
    )
    k_pre_grad = (
        rotate(keys_grad.astype(jnp.float32), cosine, -sine)
        .astype(jnp.bfloat16)
        .reshape(rows, width)
    )
    grad_first = MIX * mixed_grad.astype(jnp.float32)
    value_grad = grad_first.astype(jnp.bfloat16)
    normed_grad = (
        back(q_pre_grad, query_weight)
        + back(k_pre_grad, key_weight)
        + back(value_grad, value_weight)
    )
    grad_attn_gain = eighths(normed_grad * source * inv_first, n_blk)
    scaled_one = normed_grad * attn_gain
    grad_tokens = (
        mid_grad
        + inv_first * scaled_one
        - source * inv_first**3 * jnp.mean(scaled_one * source, axis=-1, keepdims=True)
    )
    ff = gate_weight.shape[1]
    sizes = (rows, width, ff, n_seq, n_blk, tile_split(width, ff))
    out_gu, out_down, out_out, out_query, out_key, out_value, out_gain = reduce_grads(
        sizes,
        (
            normed,
            q_pre_grad,
            k_pre_grad,
            value_grad,
            attended_b,
            mid_grad_b,
            normed_two,
            jnp.concatenate([gate_grad, up_grad], axis=1),
            act,
            cotangent,
            jnp.concatenate([grad_attn_gain, grad_ffn_gain], axis=1),
        ),
    )
    return (
        layer_output,
        grad_tokens,
        grad_first,
        out_gain[0],
        out_query.astype(F32),
        out_key.astype(F32),
        out_value.astype(F32),
        out_out.astype(F32),
        out_gain[8],
        out_gu[:, :ff].astype(F32),
        out_gu[:, ff:].astype(F32),
        out_down.astype(F32),
    )


def solution(mesh):
    n_seq, n_blk = mesh.shape["seq"], mesh.shape["blk"]

    def chosen(*args):
        rows, width = args[0].shape
        if fits(n_seq, n_blk, rows, width, args[9].shape[1]):
            return local_fast(n_seq, n_blk, *args)
        return local(*args)

    return jax.shard_map(
        chosen,
        mesh=mesh,
        in_specs=(
            P(("seq", "blk"), None),
            P(("seq", "blk"), None),
            P("seq", None),
            P(),
            P(),
            P(),
            P(),
            P(),
            P(),
            P(),
            P(),
            P(),
            P(("seq", "blk"), None),
        ),
        out_specs=(
            P(("seq", "blk"), None),
            P(("seq", "blk"), None),
            P(("seq", "blk"), None),
            P("blk"),
            P("blk", None),
            P("blk", None),
            P("blk", None),
            P("blk", None),
            P("blk"),
            P("blk", None),
            P("blk", None),
            P("blk", None),
        ),
        check_vma=False,
    )
```

```python
import functools
import math
import types

import jax
import jax.numpy as jnp
from jax import lax
from jax.experimental import pallas as pl
from jax.experimental.pallas import tpu as pltpu
from jax.sharding import PartitionSpec as P

HEAD_DIM = 64


EPS = 1e-05
THETA = 10000.0
MIX = 0.5
NEG = -1e30


def doc_layout(lengths, index):
    ends = jnp.cumsum(lengths, axis=-1)
    past = (index[:, None] >= ends).astype(jnp.int32)
    return (jnp.sum(past, axis=1), index - jnp.sum(past * lengths, axis=1))


def tables(position):
    half = HEAD_DIM // 2
    freq = THETA ** (-(jnp.arange(half).astype(jnp.float32) * 2.0 / HEAD_DIM))
    angle = position.astype(jnp.float32)[:, None] * freq[None, :]
    return (jnp.cos(angle)[:, None, :], jnp.sin(angle)[:, None, :])


def rotate(values, cosine, sine):
    half = values.shape[-1] // 2
    first = values[..., :half]
    second = values[..., half:]
    return jnp.concatenate(
        [first * cosine - second * sine, second * cosine + first * sine], axis=-1
    )


def by_blocks(step, carry, pieces, start):
    rows = pieces[0].shape[0]
    size = math.gcd(rows, 1024)
    count = rows // size
    if count == 1:
        return step(carry, pieces, start)
    stacked = tuple((piece.reshape((count, size) + piece.shape[1:]) for piece in pieces))
    offsets = jnp.arange(count, dtype=jnp.int32) * size

    def turn(state, inputs):
        return (step(state, inputs[1], start + inputs[0]), None)

    result, unused = lax.scan(turn, carry, (offsets, stacked))
    return result


def outer(left, right):
    return lax.dot_general(
        left, right, (((0,), (0,)), ((), ())), preferred_element_type=jnp.float32
    )


def back(left, weight):
    return lax.dot_general(
        left, weight, (((1,), (1,)), ((), ())), preferred_element_type=jnp.float32
    )


TILE = 256
LANES = 128
GROUP = 16
MESH = pl.DeviceIdType.MESH
F32 = jnp.float32
BF16 = jnp.bfloat16


def remote(src, dst, send, recv, where):
    return pltpu.make_async_remote_copy(
        src_ref=src, dst_ref=dst, send_sem=send, recv_sem=recv, device_id=where, device_id_type=MESH
    )


def span(start, size, unit):
    return pl.ds(pl.multiple_of(start, unit), size)


def times(left, right):
    return jnp.dot(left, right, preferred_element_type=F32)


def iota(shape, dim):
    return lax.broadcasted_iota(jnp.int32, shape, dim)


def loop(low, high, body):
    def turn(index, unused):
        body(index)
        return unused

    lax.fori_loop(low, high, turn, 0)


class Trade:
    def __init__(self, blk, n_blk, phase, send, recv, source, place):
        self.blk, self.n_blk = blk, n_blk
        self.send, self.recv = send.at[phase], recv.at[phase]
        self.source, self.place = source, place

    def start(self, peer):
        src, dst = self.source(peer), self.place(self.blk)

        @pl.when(peer != self.blk)
        def _():
            remote(src, dst, self.send.at[peer], self.recv.at[self.blk], {"blk": peer}).start()

        @pl.when(peer == self.blk)
        def _():
            pltpu.make_async_copy(src, dst, self.recv.at[self.blk]).start()

    def arrived(self, peer):
        src, dst = self.source(peer), self.place(peer)

        @pl.when(peer != self.blk)
        def _():
            remote(src, dst, self.send.at[peer], self.recv.at[peer], {"blk": peer}).wait_recv()

        @pl.when(peer == self.blk)
        def _():
            pltpu.make_async_copy(src, dst, self.recv.at[peer]).wait()

    def all_arrived(self):
        loop(0, self.n_blk, self.arrived)

    def all_left(self):
        def left(peer):
            @pl.when(peer != self.blk)
            def _():
                remote(
                    self.source(peer), self.place(self.blk), self.send.at[peer], self.recv.at[self.blk], {"blk": peer}
                ).wait_send()

        loop(0, self.n_blk, left)


class Gift:
    def __init__(self, seq, n_seq, rows, owner, kind, src, dst, send, recv):
        self.seq, self.n_seq, self.rows, self.owner, self.kind = seq, n_seq, rows, owner, kind
        self.src, self.dst, self.send, self.recv = src, dst, send, recv

    def copy(self, other, send):
        dst = self.dst.at[span(other * self.rows, self.rows, self.rows)]
        return remote(self.src, dst, self.send.at[self.kind, send], self.recv.at[self.kind, other], {"seq": send})

    def own(self):
        dst = self.dst.at[pl.ds(self.owner * self.rows, self.rows)]
        return pltpu.make_async_copy(self.src, dst, self.recv.at[self.kind, self.owner])

    def start(self):
        @pl.when(self.seq != self.owner)
        def _():
            self.copy(self.seq, self.owner).start()

        @pl.when(self.seq == self.owner)
        def _():
            self.own().start()

    def arrived(self):
        for other in range(self.n_seq):
            if other == self.owner:
                self.own().wait()
            else:
                self.copy(other, other).wait_recv()

    def left(self):
        @pl.when(self.seq != self.owner)
        def _():
            self.copy(self.seq, self.owner).wait_send()


class Sum:
    def __init__(self, blk, n_blk, size, part, cgot, zgot, total, sems):
        self.blk, self.chips, self.size = blk, n_blk // 2, size
        self.core, self.chip = lax.rem(blk, 2), lax.div(blk, 2)
        self.part, self.cgot, self.zgot, self.total = part, cgot, zgot, total
        self.csend, self.crecv, self.zsend, self.zrecv = sems

    def turned(self, step):
        return lax.rem(self.chip + step, self.chips)

    def chunk(self, index):
        return self.part.at[span(index * self.size, self.size, 32)]

    def swap(self, chip):
        return remote(
            self.chunk(2 * chip + 1 - self.core),
            self.cgot(chip),
            self.csend.at[chip],
            self.crecv.at[chip],
            {"blk": 2 * self.chip + 1 - self.core},
        )

    def forward(self, step):
        chip = self.turned(step)
        return remote(
            self.chunk(2 * chip + self.core),
            self.zgot(step - 1),
            self.zsend.at[step - 1],
            self.zrecv.at[step - 1],
            {"blk": 2 * chip + self.core},
        )

    def begin(self):
        def one(step):
            chip = self.turned(step)
            self.swap(chip).wait()
            mine, other = self.chunk(2 * chip + self.core), self.cgot(chip)

            def add(group):
                at = span(group * 32, 32, 32)
                mine[at, :] = (mine[at, :].astype(F32) + other[at, :].astype(F32)).astype(BF16)

            loop(0, self.size // 32, add)
            self.forward(step).start()

        loop(1, self.chips, one)
        self.swap(self.chip).wait()

    def end(self):
        loop(1, self.chips, lambda step: self.forward(step).wait())
        mine, other = self.chunk(self.blk), self.cgot(self.chip)

        def add(group):
            at = span(group * 32, 32, 32)
            value = mine[at, :].astype(F32) + other[at, :].astype(F32)
            for step in range(1, self.chips):
                value = value + self.zgot(step - 1)[at, :].astype(F32)
            self.total[at, :] = value.astype(BF16)

        loop(0, self.size // 32, add)


class Spread:
    def __init__(self, seq, n_seq, owner, kind, src, dst, send, recv, local):
        self.seq, self.n_seq, self.owner, self.kind, self.src, self.dst = seq, n_seq, owner, kind, src, dst
        self.send, self.recv, self.local = send, recv, local

    def copy(self, other):
        return remote(self.src, self.dst, self.send.at[self.kind, other], self.recv.at[self.kind], {"seq": other})

    def own(self):
        return pltpu.make_async_copy(self.src, self.dst, self.local.at[self.kind])

    def start(self):
        @pl.when(self.seq == self.owner)
        def _():
            for other in range(self.n_seq):
                if other != self.owner:
                    self.copy(other).start()
            self.own().start()

    def finish(self):
        @pl.when(self.seq == self.owner)
        def _():
            for other in range(self.n_seq):
                if other != self.owner:
                    self.copy(other).wait_send()
            self.own().wait()

        @pl.when(self.seq != self.owner)
        def _():
            self.copy(self.owner).wait_recv()


def outer_tiles(lhs, rhs, part, turned, chip, tiles, part_at):
    turned[...] = lhs[:, span(chip * TILE, TILE, TILE)].T

    def tile(index):
        value = times(turned[...], rhs[:, span(index * TILE, TILE, TILE)])
        part[span(chip * TILE, TILE, TILE), span(part_at + index * TILE, TILE, TILE)] = value.astype(BF16)

    loop(0, tiles, tile)


def layer_kernel(
    sizes,
    freq, tokens, first, lengths, attn_gain, ffn_gain, cot,
    h_query, h_key, h_value, h_out, h_gate, h_up, h_down,
    o_layer, o_tokens, o_first, o_gu, o_down, o_out, o_query, o_key, o_value, o_gain,
    v, sem,
):
    rows, width, ff, n_seq, n_blk, split = sizes
    v, sem = types.SimpleNamespace(**v), types.SimpleNamespace(**sem)
    docs = lengths.shape[1]
    chips = n_blk // 2
    scale = HEAD_DIM ** (-0.5)
    seq, blk = lax.axis_index("seq"), lax.axis_index("blk")
    chip_at = lax.div(blk, 2)

    def turned_chip(step):
        return lax.rem(chip_at + step, chips)

    barrier = pltpu.get_barrier_semaphore()
    for step in range(1, n_seq):
        pl.semaphore_signal(barrier, inc=1, device_id={"seq": lax.rem(seq + step, n_seq)}, device_id_type=MESH)
    for step in range(1, n_blk):
        pl.semaphore_signal(barrier, inc=1, device_id={"blk": lax.rem(blk + step, n_blk)}, device_id_type=MESH)

    def load(index, src, dst):
        copy = pltpu.make_async_copy(src, dst, sem.load.at[index])
        copy.start()
        return copy

    load_query = load(0, h_query, v.w_query)
    load_key = load(1, h_key, v.w_key)
    load_value = load(2, h_value, v.w_value)
    load_out = load(3, h_out, v.w_out)
    load_gate = load(4, h_gate, v.w_gate)
    load_up = load(5, h_up, v.w_up)
    load_down = load(6, h_down, v.w_down)

    def norm(group):
        at = span(group * GROUP, GROUP, GROUP)
        x = tokens[at, :].astype(F32)
        inv = lax.rsqrt(jnp.mean(x * x, axis=-1, keepdims=True) + EPS)
        v.normed[at, :] = (x * inv * attn_gain[...]).astype(BF16)
        v.inv_first[at, :] = jnp.broadcast_to(inv, (GROUP, LANES))

    loop(0, rows // GROUP, norm)

    def doc_start(index):
        start, end = jnp.zeros_like(index), jnp.int32(0)
        for doc in range(docs):
            end = end + lengths[0, doc]
            start = jnp.where(index >= end, end, start)
        return start

    my_index = blk * rows + iota((rows, LANES), 0)
    low_half = lax.rem(iota((rows, LANES), 1), HEAD_DIM) < HEAD_DIM // 2
    angle = (my_index - doc_start(my_index)).astype(F32) * freq[...]
    v.cos[...] = jnp.cos(angle)
    sine = jnp.sin(angle)
    v.sin[...] = jnp.where(low_half, -sine, sine)

    def halves_changed(u):
        half = HEAD_DIM // 2
        return jnp.where(low_half, pltpu.roll(u, LANES - half, 1), pltpu.roll(u, half, 1))

    def rotated(u):
        return u * v.cos[...] + halves_changed(u) * v.sin[...]

    def rotated_back(u):
        return u * v.cos[...] - halves_changed(u) * v.sin[...]

    cuts = [0]
    for tiles in split:
        cuts.append(cuts[-1] + tiles * TILE)
    wide = max(split) * TILE

    def gift(owner, kind, src, dst):
        return Gift(seq, n_seq, rows, owner, kind, src, dst, sem.xsend, sem.xrecv)

    gift_cot = gift(3, 0, cot, v.buf_a)
    gifts_two = [gift(owner, 0, v.two, v.buf_a) for owner in range(3)]
    gifts_gu = [
        gift(
            owner,
            1,
            v.gate_up.at[:, cuts[owner] : cuts[owner + 1]],
            v.buf_b.at[:, : cuts[owner + 1] - cuts[owner]],
        )
        for owner in range(3)
    ]
    gift_act = gift(3, 1, v.act, v.buf_b)
    gift_att = gift(2, 2, v.att, v.buf_att)
    gift_mid = gift(2, 3, v.mid_b, v.buf_mid)
    gifts_normed = [gift(owner, 4, v.normed, v.buf_n) for owner in range(3)]
    gifts_pre = [gift(owner, 5, v.pre_grad.at[owner], v.buf_t) for owner in range(3)]

    def trade(phase, source, place):
        return Trade(blk, n_blk, phase, sem.asend, sem.arecv, source, place)

    def block_rows(ref):
        return lambda peer: ref.at[span(peer * rows, rows, rows)]

    def block_columns(ref):
        return lambda peer: ref.at[:, span(peer * LANES, LANES, LANES)]

    give_qkv = trade(0, lambda peer: v.pack.at[peer], lambda peer: v.qkv.at[:, span(peer * rows, rows, rows)])
    give_att = trade(1, block_rows(v.ob), block_columns(v.att))
    give_out = trade(2, lambda peer: v.out_pack.at[peer], block_rows(v.out_grad))
    give_grads = trade(
        3, lambda peer: v.pack.at[peer], lambda peer: v.grads.at[:, :, span(peer * LANES, LANES, LANES)]
    )

    pl.semaphore_wait(barrier, n_seq + n_blk - 2)

    for item in (load_query, load_key, load_value):
        item.wait()

    def project(step):
        chip = turned_chip(step)
        at = span(chip * TILE, TILE, TILE)
        left = v.normed[...]
        q, k, val = times(left, v.w_query[:, at]), times(left, v.w_key[:, at]), times(left, v.w_value[:, at])
        old = first[:, at].astype(F32)
        for core in range(2):
            peer = 2 * chip + core
            cols = slice(core * LANES, (core + 1) * LANES)
            v.pack[peer, 0] = (rotated(q[:, cols]) * scale).astype(BF16)
            v.pack[peer, 1] = rotated(k[:, cols]).astype(BF16)
            v.pack[peer, 2] = (MIX * val[:, cols] + MIX * old[:, cols]).astype(BF16)
            give_qkv.start(peer)

    loop(1, chips + 1, project)
    gift_cot.start()
    for item in gifts_normed:
        item.start()

    first_head = iota((TILE, LANES), 1) < HEAD_DIM

    def stacked(values):
        return jnp.concatenate([jnp.where(first_head, values, 0.0), jnp.where(first_head, 0.0, values)], axis=0)

    def unstacked(values):
        return jnp.where(first_head, values[:TILE], values[TILE:])

    def attend(block):
        for core in range(2):
            give_qkv.arrived(2 * block + core)
        at, both = span(block * TILE, TILE, TILE), span(block * 2 * TILE, 2 * TILE, 2 * TILE)
        v.q2[both, :] = stacked(v.qkv[0, at, :].astype(F32)).astype(BF16)
        index = block * TILE + lax.rem(iota((2 * TILE, 1), 0), TILE)
        start = doc_start(index)
        v.top[...] = jnp.full((2 * TILE, LANES), NEG, F32)

        def scores(tile):
            cols = span(tile * TILE, TILE, TILE)
            score = back(v.q2[both, :], v.qkv[1, cols, :])
            key = tile * TILE + iota((2 * TILE, TILE), 1)
            score = jnp.where((key <= index) & (key >= start), score, NEG)
            v.score[:, cols] = score
            v.top[...] = jnp.maximum(v.top[...], jnp.maximum(score[:, :LANES], score[:, LANES:]))

        loop(0, block + 1, scores)
        top = jnp.max(v.top[...], axis=1, keepdims=True)
        v.top[...] = jnp.zeros((2 * TILE, LANES), F32)
        v.o2[...] = jnp.zeros((2 * TILE, LANES), F32)

        def weights(tile):
            cols = span(tile * TILE, TILE, TILE)
            weight = jnp.exp(v.score[:, cols] - top)
            v.top[...] += weight[:, :LANES] + weight[:, LANES:]
            weight = weight.astype(BF16)
            v.prob[both, cols] = weight
            v.o2[...] += times(weight, v.qkv[2, cols, :])

        loop(0, block + 1, weights)
        inv = 1.0 / jnp.sum(v.top[...], axis=1, keepdims=True)
        v.row[both, :] = jnp.broadcast_to(inv, (2 * TILE, LANES))
        attended = unstacked(v.o2[...] * inv)
        v.o32[at, :] = attended
        v.ob[at, :] = attended.astype(BF16)
        for core in range(2):
            give_att.start(2 * block + core)

    loop(0, chips, attend)
    give_att.all_arrived()
    gift_att.start()

    load_out.wait()

    def middle(tile):
        cols = span(tile * TILE, TILE, TILE)
        value = tokens[:, cols].astype(F32) + times(v.att[...], v.w_out[:, cols])
        v.mid[:, cols] = value
        o_layer[:, cols] = value

    loop(0, width // TILE, middle)

    def norm_two(group):
        at = span(group * GROUP, GROUP, GROUP)
        x = v.mid[at, :]
        inv = lax.rsqrt(jnp.mean(x * x, axis=-1, keepdims=True) + EPS)
        v.two[at, :] = (x * inv * ffn_gain[...]).astype(BF16)
        v.inv_second[at, :] = jnp.broadcast_to(inv, (GROUP, LANES))

    loop(0, rows // GROUP, norm_two)
    for item in gifts_two:
        item.start()

    for item in (load_gate, load_up, load_down):
        item.wait()
    v.two_grad[...] = jnp.zeros((rows, width), F32)

    def feed(tile):
        cols = span(tile * TILE, TILE, TILE)
        gate = times(v.two[...], v.w_gate[:, cols])
        up = times(v.two[...], v.w_up[:, cols])
        act_grad = back(cot[...], v.w_down[cols, :])
        sigma = jax.nn.sigmoid(gate)
        silu = gate * sigma
        act = (silu * up).astype(BF16)
        gate_grad = (act_grad * up * sigma * (1.0 + gate * (1.0 - sigma))).astype(BF16)
        up_grad = (act_grad * silu).astype(BF16)
        v.act[:, cols] = act
        v.gate_up[:, cols] = gate_grad
        v.gate_up[:, span(ff + tile * TILE, TILE, TILE)] = up_grad
        o_layer[...] += times(act, v.w_down[cols, :])
        v.two_grad[...] += back(gate_grad, v.w_gate[:, cols]) + back(up_grad, v.w_up[:, cols])

    loop(0, ff // TILE, feed)
    v.gain_rows[...] = jnp.zeros((16, width), F32)

    def norm_two_back(group):
        at = span(group * GROUP, GROUP, GROUP)
        x, grad, inv = v.mid[at, :], v.two_grad[at, :], v.inv_second[at, :1]
        term = grad * x * inv
        v.gain_rows[8:16, :] += term[:8] + term[8:]
        scaled = grad * ffn_gain[...]
        mean = jnp.mean(scaled * x, axis=-1, keepdims=True)
        value = cot[at, :].astype(F32) + inv * scaled - x * (inv * inv * inv * mean)
        v.mid_grad[at, :] = value
        v.mid_b[at, :] = value.astype(BF16)

    loop(0, rows // GROUP, norm_two_back)

    def out_back(step):
        chip = turned_chip(step)
        value = back(v.mid_b[...], v.w_out[span(chip * TILE, TILE, TILE), :]).astype(BF16)
        for core in range(2):
            v.out_pack[2 * chip + core] = value[:, core * LANES : (core + 1) * LANES]
            give_out.start(2 * chip + core)

    loop(1, chips + 1, out_back)
    for item in gifts_gu + [gift_act, gift_mid]:
        item.start()

    give_out.all_arrived()

    def prepare(block):
        at, both = span(block * TILE, TILE, TILE), span(block * 2 * TILE, 2 * TILE, 2 * TILE)
        grad = (stacked(v.out_grad[at, :].astype(F32)) * v.row[both, :]).astype(BF16)
        v.do2[both, :] = grad
        attended = v.o32[at, :]
        delta = jnp.sum(grad.astype(F32) * jnp.concatenate([attended, attended], axis=0), axis=1, keepdims=True)
        v.row[both, :] = jnp.broadcast_to(delta, (2 * TILE, LANES))
        v.dq[both, :] = jnp.zeros((2 * TILE, LANES), F32)

    loop(0, chips, prepare)
    give_qkv.all_left()

    def key_block(block):
        at = span(block * TILE, TILE, TILE)
        v.dk[...] = jnp.zeros((TILE, LANES), F32)
        v.dv[...] = jnp.zeros((TILE, LANES), F32)

        def query_block(other):
            both = span(other * 2 * TILE, 2 * TILE, 2 * TILE)
            prob = v.prob[both, at]
            grad = back(v.do2[both, :], v.qkv[2, at, :])
            score_grad = (prob.astype(F32) * (grad - v.row[both, :1])).astype(BF16)
            v.dk[...] += outer(score_grad, v.q2[both, :])
            v.dv[...] += outer(prob, v.do2[both, :])
            v.dq[both, :] += times(score_grad, v.qkv[1, at, :])

        loop(block, chips, query_block)
        dq = (unstacked(v.dq[span(block * 2 * TILE, 2 * TILE, 2 * TILE), :]) * scale).astype(BF16)
        dk, dv = v.dk[...].astype(BF16), v.dv[...].astype(BF16)
        for core in range(2):
            peer = 2 * block + core
            part = slice(core * rows, (core + 1) * rows)
            v.pack[peer, 0] = dq[part]
            v.pack[peer, 1] = dk[part]
            v.pack[peer, 2] = dv[part]
            give_grads.start(peer)

    loop(0, chips, key_block)

    chunk, down = width // n_blk, ff // n_blk
    sems = tuple(item.at[0] for item in (sem.csend, sem.crecv, sem.zsend, sem.zrecv))
    tail_sems = tuple(item.at[1] for item in (sem.csend, sem.crecv, sem.zsend, sem.zrecv))

    def stack_in(ref, size, columns, top):
        return lambda index: ref.at[span(top + index * size, size, 32), :columns]

    def square_in(ref):
        def place(index):
            return ref.at[
                span(lax.rem(index, 2) * down, down, 32), span(lax.div(index, 2) * width, width, width)
            ]

        return place

    part = v.w_gate.at[:, :wide]
    sum_gu = Sum(
        blk, n_blk, chunk, part,
        stack_in(v.w_up, chunk, wide, 0), stack_in(v.w_up, chunk, wide, chips * chunk), v.total, sems,
    )
    sum_down = Sum(
        blk, n_blk, down, v.w_down, square_in(v.w_up), square_in(v.w_gate), v.total_down, sems
    )
    sum_tail = Sum(
        blk, n_blk, chunk, v.w_out,
        stack_in(v.got_tail, chunk, width, 0), stack_in(v.got_tail, chunk, width, chips * chunk),
        v.total_tail, tail_sems,
    )
    early = [[gifts_two[0], gifts_gu[0]], [gifts_two[1], gifts_gu[1]], [gifts_two[2], gifts_gu[2], gift_att, gift_mid],
             [gift_cot, gift_act]]
    for owner in range(n_seq):

        @pl.when(seq == owner)
        def _(owner=owner):
            for item in early[owner]:
                item.arrived()

    @pl.when(seq < 3)
    def _():
        def one(step):
            chip = turned_chip(step)

            @pl.when(seq < 2)
            def _():
                outer_tiles(v.buf_a, v.buf_b, v.w_gate, v.turned, chip, split[0], 0)

            @pl.when(seq == 2)
            def _():
                spare = wide - split[2] * TILE - width
                if spare:
                    v.w_gate[span(chip * TILE, TILE, TILE), wide - spare : wide] = jnp.zeros((TILE, spare), BF16)
                outer_tiles(v.buf_a, v.buf_b, v.w_gate, v.turned, chip, split[2], 0)
                outer_tiles(
                    v.buf_att, v.buf_mid, v.w_gate, v.turned, chip, width // TILE, split[2] * TILE
                )

            sum_gu.swap(chip).start()

        loop(1, chips + 1, one)
        sum_gu.begin()

    @pl.when(seq == 3)
    def _():
        def one(index):
            at = span(index * TILE, TILE, TILE)
            v.turned[...] = v.buf_b[:, at].T
            v.w_down[at, :] = times(v.turned[...], v.buf_a[...]).astype(BF16)

        loop(0, ff // TILE, one)
        loop(1, chips + 1, lambda step: sum_down.swap(turned_chip(step)).start())
        sum_down.begin()

    give_grads.all_arrived()

    def rotate_back(index):
        cols = span(index * LANES, LANES, LANES)
        v.pre_grad[0, :, cols] = rotated_back(v.grads[0, :, cols].astype(F32)).astype(BF16)
        v.pre_grad[1, :, cols] = rotated_back(v.grads[1, :, cols].astype(F32)).astype(BF16)
        value = MIX * v.grads[2, :, cols].astype(F32)
        v.pre_grad[2, :, cols] = value.astype(BF16)
        o_first[:, cols] = value

    loop(0, width // LANES, rotate_back)
    for item in gifts_pre:
        item.start()

    def normed_back(tile):
        at = span(tile * TILE, TILE, TILE)
        o_tokens[:, at] = (
            back(v.pre_grad[0], v.w_query[at, :])
            + back(v.pre_grad[1], v.w_key[at, :])
            + back(v.pre_grad[2], v.w_value[at, :])
        )

    loop(0, width // TILE, normed_back)

    def norm_back(group):
        at = span(group * GROUP, GROUP, GROUP)
        x, grad, inv = tokens[at, :].astype(F32), o_tokens[at, :], v.inv_first[at, :1]
        term = grad * x * inv
        v.gain_rows[0:8, :] += term[:8] + term[8:]
        scaled = grad * attn_gain[...]
        mean = jnp.mean(scaled * x, axis=-1, keepdims=True)
        o_tokens[at, :] = v.mid_grad[at, :] + inv * scaled - x * (inv * inv * inv * mean)

    loop(0, rows // GROUP, norm_back)

    for peer in range(n_blk):
        v.gains[peer] = v.gain_rows[:, peer * LANES : (peer + 1) * LANES]

    def gain_copy(step):
        other = lax.rem(blk + step, n_blk)
        return remote(
            v.gains.at[other], v.gain_got.at[step - 1], sem.hsend.at[step - 1], sem.hrecv.at[step - 1],
            {"blk": other},
        )

    for step in range(1, n_blk):
        gain_copy(step).start()

    for owner in range(3):

        @pl.when(seq == owner)
        def _(owner=owner):
            gifts_normed[owner].arrived()
            gifts_pre[owner].arrived()

    @pl.when(seq < 3)
    def _():
        def one(step):
            chip = turned_chip(step)
            outer_tiles(v.buf_n, v.buf_t, v.w_out, v.turned, chip, width // TILE, 0)
            sum_tail.swap(chip).start()

        loop(1, chips + 1, one)
        sum_tail.begin()

    def spread(owner, kind, src, dst):
        return Spread(seq, n_seq, owner, kind, src, dst, sem.gsend, sem.grecv, sem.glocal)

    last = cuts[3] - cuts[2]
    spreads = [
        spread(0, 0, v.total.at[:, : cuts[1] - cuts[0]], o_gu.at[:, cuts[0] : cuts[1]]),
        spread(1, 1, v.total.at[:, : cuts[2] - cuts[1]], o_gu.at[:, cuts[1] : cuts[2]]),
        spread(2, 2, v.total.at[:, :last], o_gu.at[:, cuts[2] : cuts[3]]),
        spread(2, 3, v.total.at[:, last : last + width], o_out),
        spread(3, 4, v.total_down, o_down),
    ]
    tails = [
        spread(0, 5, v.total_tail, o_query),
        spread(1, 6, v.total_tail, o_key),
        spread(2, 7, v.total_tail, o_value),
    ]

    @pl.when(seq < 3)
    def _():
        sum_gu.end()

    @pl.when(seq == 3)
    def _():
        sum_down.end()

    for item in spreads:
        item.start()

    value = v.gains[blk]
    for step in range(1, n_blk):
        gain_copy(step).wait()
        value = value + v.gain_got[step - 1]
    v.gain_sum[seq] = value
    for step in range(1, n_seq):
        other = lax.rem(seq + step, n_seq)
        mine = v.gain_sum.at[seq]
        remote(mine, mine, sem.isend.at[step - 1], sem.irecv.at[seq], {"seq": other}).start()

    @pl.when(seq < 3)
    def _():
        sum_tail.end()

    for item in tails:
        item.start()

    for step in range(1, n_seq):
        other = lax.rem(seq + step, n_seq)
        theirs = v.gain_sum.at[other]
        remote(theirs, theirs, sem.isend.at[step - 1], sem.irecv.at[other], {"seq": other}).wait()
    value = v.gain_sum[0]
    for group in range(1, n_seq):
        value = value + v.gain_sum[group]
    o_gain[0:8, :] = jnp.broadcast_to(jnp.sum(value[:8], axis=0, keepdims=True), (8, LANES))
    o_gain[8:16, :] = jnp.broadcast_to(jnp.sum(value[8:], axis=0, keepdims=True), (8, LANES))

    for item in spreads + tails:
        item.finish()
    for item in (
        [gift_cot, gift_act, gift_att, gift_mid] + gifts_two + gifts_gu + gifts_normed + gifts_pre
    ):
        item.left()
    for item in (give_att, give_out, give_grads):
        item.all_left()


def tile_split(width, ff):
    tiles, more = 2 * ff // TILE, width // TILE
    each = -(-(tiles + more) // 3)
    return (each, each, tiles - 2 * each)


def fits(n_seq, n_blk, rows, width, ff):
    return (
        n_seq == 4
        and n_blk % 2 == 0
        and n_blk * LANES == width
        and rows == LANES
        and ff % TILE == 0
        and (ff // n_blk) % 32 == 0
        and 2 * (ff // n_blk) <= width
        and n_blk // 2 <= 4
    )


def local_fast(
    n_seq,
    n_blk,
    tokens,
    first_values,
    doc_lengths,
    attn_gain,
    query_weight,
    key_weight,
    value_weight,
    out_weight,
    ffn_gain,
    gate_weight,
    up_weight,
    down_weight,
    cotangent,
):
    rows, width = tokens.shape
    ff = gate_weight.shape[1]
    split = tile_split(width, ff)
    sizes = (rows, width, ff, n_seq, n_blk, split)
    half = HEAD_DIM // 2
    freq = THETA ** (-(jnp.arange(half).astype(jnp.float32) * 2.0 / HEAD_DIM))
    freq = jnp.tile(freq, LANES // half)[None, :]
    wide = max(split) * TILE
    chunk, down, chips = width // n_blk, ff // n_blk, n_blk // 2
    all_rows, group = n_seq * rows, n_blk * rows
    vmem = pl.BlockSpec(memory_space=pltpu.VMEM)
    hbm = pl.BlockSpec(memory_space=pl.ANY)
    smem = pl.BlockSpec(memory_space=pltpu.SMEM)
    shape = jax.ShapeDtypeStruct

    def half_type(*dims):
        return pltpu.VMEM(dims, BF16)

    def full_type(*dims):
        return pltpu.VMEM(dims, F32)

    scratch = dict(
        w_query=half_type(width, width), w_key=half_type(width, width), w_value=half_type(width, width),
        w_out=half_type(width, width), w_gate=half_type(width, ff), w_up=half_type(width, ff),
        w_down=half_type(ff, width),
        normed=half_type(rows, width), inv_first=full_type(rows, LANES), inv_second=full_type(rows, LANES),
        cos=full_type(rows, LANES), sin=full_type(rows, LANES),
        pack=half_type(n_blk, 3, rows, LANES), qkv=half_type(3, group, LANES),
        q2=half_type(2 * group, LANES), do2=half_type(2 * group, LANES), prob=half_type(2 * group, group),
        score=full_type(2 * TILE, group), top=full_type(2 * TILE, LANES), o2=full_type(2 * TILE, LANES),
        row=full_type(2 * group, LANES), o32=full_type(group, LANES), ob=half_type(group, LANES),
        dq=full_type(2 * group, LANES), dk=full_type(TILE, LANES), dv=full_type(TILE, LANES),
        att=half_type(rows, width), mid=full_type(rows, width), two=half_type(rows, width),
        act=half_type(rows, ff), gate_up=half_type(rows, 2 * ff), two_grad=full_type(rows, width),
        mid_grad=full_type(rows, width), mid_b=half_type(rows, width),
        out_pack=half_type(n_blk, rows, LANES), out_grad=half_type(group, LANES),
        grads=half_type(3, rows, width), pre_grad=half_type(3, rows, width),
        buf_a=half_type(all_rows, width), buf_b=half_type(all_rows, ff), buf_att=half_type(all_rows, width),
        buf_mid=half_type(all_rows, width), buf_n=half_type(all_rows, width), buf_t=half_type(all_rows, width),
        turned=half_type(TILE, all_rows),
        got_tail=half_type((2 * chips - 1) * chunk, width),
        total=half_type(chunk, wide), total_down=half_type(down, width), total_tail=half_type(chunk, width),
        gain_rows=full_type(16, width), gains=full_type(n_blk, 16, LANES), gain_got=full_type(n_blk - 1, 16, LANES),
        gain_sum=full_type(n_seq, 16, LANES),
    )
    dma = pltpu.SemaphoreType.DMA
    sems = dict(
        load=dma((7,)), asend=dma((4, n_blk)), arecv=dma((4, n_blk)), xsend=dma((6, n_seq)), xrecv=dma((6, n_seq)),
        csend=dma((2, chips)), crecv=dma((2, chips)), zsend=dma((2, chips - 1)), zrecv=dma((2, chips - 1)),
        gsend=dma((8, n_seq)), grecv=dma((8,)), glocal=dma((8,)),
        hsend=dma((n_blk - 1,)), hrecv=dma((n_blk - 1,)), isend=dma((n_seq - 1,)), irecv=dma((n_seq,)),
    )
    layer, grad_tokens, grad_first, out_gu, out_down, out_out, out_query, out_key, out_value, out_gain = pl.pallas_call(
        functools.partial(layer_kernel, sizes),
        out_shape=(
            shape((rows, width), F32),
            shape((rows, width), F32),
            shape((rows, width), F32),
            shape((chunk, 2 * ff), BF16),
            shape((down, width), BF16),
            shape((chunk, width), BF16),
            shape((chunk, width), BF16),
            shape((chunk, width), BF16),
            shape((chunk, width), BF16),
            shape((16, LANES), F32),
        ),
        in_specs=[vmem, vmem, vmem, smem, vmem, vmem, vmem] + [hbm] * 7,
        out_specs=(vmem, vmem, vmem) + (hbm,) * 6 + (vmem,),
        scratch_shapes=(scratch, sems),
        compiler_params=pltpu.CompilerParams(
            collective_id=0, has_side_effects=True, vmem_limit_bytes=63 * 1024 * 1024
        ),
        name="layer",
    )(
        freq, tokens, first_values, doc_lengths, attn_gain[None, :], ffn_gain[None, :], cotangent,
        query_weight, key_weight, value_weight, out_weight, gate_weight, up_weight, down_weight,
    )
    return (
        layer,
        grad_tokens,
        grad_first,
        out_gain[0],
        out_query.astype(F32),
        out_key.astype(F32),
        out_value.astype(F32),
        out_out.astype(F32),
        out_gain[8],
        out_gu[:, :ff].astype(F32),
        out_gu[:, ff:].astype(F32),
        out_down.astype(F32),
    )


def local(
    tokens,
    first_values,
    doc_lengths,
    attn_gain,
    query_weight,
    key_weight,
    value_weight,
    out_weight,
    ffn_gain,
    gate_weight,
    up_weight,
    down_weight,
    cotangent,
):
    rows, width = tokens.shape
    heads = width // HEAD_DIM
    scale = HEAD_DIM ** (-0.5)
    shape3 = (rows, heads, HEAD_DIM)
    my_start = lax.axis_index("blk") * rows
    my_index = my_start + jnp.arange(rows, dtype=jnp.int32)
    my_doc, my_pos = doc_layout(doc_lengths, my_index)
    cosine, sine = tables(my_pos)
    source = tokens.astype(jnp.float32)
    inv_first = lax.rsqrt(jnp.mean(source * source, axis=-1, keepdims=True) + EPS)
    normed = (source * inv_first * attn_gain).astype(jnp.bfloat16)
    query_pre = jnp.dot(normed, query_weight, preferred_element_type=jnp.float32)
    key_pre = jnp.dot(normed, key_weight, preferred_element_type=jnp.float32)
    value_pre = jnp.dot(normed, value_weight, preferred_element_type=jnp.float32)
    queries = rotate(query_pre.reshape(shape3), cosine, sine).astype(jnp.bfloat16)
    keys = rotate(key_pre.reshape(shape3), cosine, sine).astype(jnp.bfloat16).reshape(rows, width)
    mixed = (MIX * value_pre + MIX * first_values.astype(jnp.float32)).astype(jnp.bfloat16)
    keys_local = keys.reshape(shape3)
    mixed_local = mixed.reshape(shape3)

    def allowed_mask(query_index, query_doc, key_index, key_doc):
        return (query_doc[:, None] == key_doc[None, :]) & (
            key_index[None, :] <= query_index[:, None]
        )

    def forward_step(state, pieces, start):
        count = pieces[0].shape[0]
        keys_piece = pieces[0].reshape(count, heads, HEAD_DIM)
        values_piece = pieces[1].reshape(count, heads, HEAD_DIM)
        key_index = start + jnp.arange(count, dtype=jnp.int32)

        def forward_compute(state):
            high, total, accum = state
            key_doc, unused = doc_layout(doc_lengths, key_index)
            allowed = allowed_mask(my_index, my_doc, key_index, key_doc)[None]
            score = (
                jnp.einsum("qhd,khd->hqk", queries, keys_piece, preferred_element_type=jnp.float32)
                * scale
            )
            score = jnp.where(allowed, score, NEG)
            new_high = jnp.maximum(high, jnp.max(score, axis=-1))
            weight = jnp.where(allowed, jnp.exp(score - new_high[:, :, None]), 0.0)
            factor = jnp.exp(high - new_high)
            total = total * factor + jnp.sum(weight, axis=-1)
            accum = accum * factor.T[:, :, None] + jnp.einsum(
                "hqk,khd->qhd",
                weight.astype(jnp.bfloat16),
                values_piece,
                preferred_element_type=jnp.float32,
            )
            return (new_high, total, accum)

        return lax.cond(start <= my_index[-1], forward_compute, lambda kept: kept, state)

    def query_grad_step(grad_q, pieces, start):
        count = pieces[0].shape[0]
        keys_piece = pieces[0].reshape(count, heads, HEAD_DIM)
        values_piece = pieces[1].reshape(count, heads, HEAD_DIM)
        key_index = start + jnp.arange(count, dtype=jnp.int32)

        def query_compute(grad_q):
            key_doc, unused = doc_layout(doc_lengths, key_index)
            allowed = allowed_mask(my_index, my_doc, key_index, key_doc)[None]
            score = (
                jnp.einsum("qhd,khd->hqk", queries, keys_piece, preferred_element_type=jnp.float32)
                * scale
            )
            prob = jnp.where(allowed, jnp.exp(score - logsum[:, :, None]), 0.0)
            prob_grad = jnp.einsum(
                "qhd,khd->hqk", outgrad_local, values_piece, preferred_element_type=jnp.float32
            )
            score_grad = (prob * (prob_grad - delta[:, :, None])).astype(jnp.bfloat16)
            return (
                grad_q
                + jnp.einsum(
                    "hqk,khd->qhd", score_grad, keys_piece, preferred_element_type=jnp.float32
                )
                * scale
            )

        return lax.cond(start <= my_index[-1], query_compute, lambda kept: kept, grad_q)

    init = (
        jnp.full((heads, rows), NEG, jnp.float32),
        jnp.zeros((heads, rows), jnp.float32),
        jnp.zeros(shape3, jnp.float32),
    )
    state = by_blocks(
        forward_step,
        init,
        (
            lax.all_gather(keys, "blk", axis=0, tiled=True),
            lax.all_gather(mixed, "blk", axis=0, tiled=True),
        ),
        jnp.int32(0),
    )
    high, total, accum = state
    logsum = high + jnp.log(total)
    attended = accum / total.T[:, :, None]
    attended_b = attended.astype(jnp.bfloat16).reshape(rows, width)
    mid = source + jnp.dot(attended_b, out_weight, preferred_element_type=jnp.float32)
    inv_second = lax.rsqrt(jnp.mean(mid * mid, axis=-1, keepdims=True) + EPS)
    normed_two = (mid * inv_second * ffn_gain).astype(jnp.bfloat16)
    gate = jnp.dot(normed_two, gate_weight, preferred_element_type=jnp.float32)
    up = jnp.dot(normed_two, up_weight, preferred_element_type=jnp.float32)
    act = (jax.nn.silu(gate) * up).astype(jnp.bfloat16)
    layer_output = mid + jnp.dot(act, down_weight, preferred_element_type=jnp.float32)
    cot_float = cotangent.astype(jnp.float32)
    grad_down = outer(act, cotangent)
    act_grad = back(cotangent, down_weight)
    sigma = jax.nn.sigmoid(gate)
    gate_grad = (act_grad * up * sigma * (1.0 + gate * (1.0 - sigma))).astype(jnp.bfloat16)
    up_grad = (act_grad * gate * sigma).astype(jnp.bfloat16)
    grad_gate = outer(normed_two, gate_grad)
    grad_up = outer(normed_two, up_grad)
    normed_two_grad = back(gate_grad, gate_weight) + back(up_grad, up_weight)
    grad_ffn_gain = jnp.sum(normed_two_grad * mid * inv_second, axis=0)
    scaled_two = normed_two_grad * ffn_gain
    mid_grad = (
        cot_float
        + inv_second * scaled_two
        - mid * inv_second**3 * jnp.mean(scaled_two * mid, axis=-1, keepdims=True)
    )
    mid_grad_b = mid_grad.astype(jnp.bfloat16)
    grad_out_weight = outer(attended_b, mid_grad_b)
    attended_grad = back(mid_grad_b, out_weight).astype(jnp.bfloat16)
    outgrad_local = attended_grad.reshape(shape3)
    delta = jnp.sum(outgrad_local.astype(jnp.float32) * attended, axis=-1).T
    zeros3 = jnp.zeros(shape3, jnp.float32)
    grad_q = by_blocks(
        query_grad_step,
        zeros3,
        (
            lax.all_gather(keys, "blk", axis=0, tiled=True),
            lax.all_gather(mixed, "blk", axis=0, tiled=True),
        ),
        jnp.int32(0),
    )
    all_logsum, all_delta = (
        lax.all_gather(logsum.T, "blk", axis=0, tiled=True),
        lax.all_gather(delta.T, "blk", axis=0, tiled=True),
    )

    def key_grad_step(state, pieces, start):
        count = pieces[0].shape[0]
        query_piece = pieces[0].reshape(count, heads, HEAD_DIM)
        outgrad_piece = pieces[1].reshape(count, heads, HEAD_DIM)
        query_index = start + jnp.arange(count, dtype=jnp.int32)

        def key_compute(state):
            grad_k, grad_v = state
            logsum_piece = lax.dynamic_slice_in_dim(all_logsum, start, count, 0).T
            delta_piece = lax.dynamic_slice_in_dim(all_delta, start, count, 0).T
            query_doc, unused = doc_layout(doc_lengths, query_index)
            allowed = allowed_mask(query_index, query_doc, my_index, my_doc)[None]
            score = (
                jnp.einsum(
                    "qhd,khd->hqk", query_piece, keys_local, preferred_element_type=jnp.float32
                )
                * scale
            )
            prob = jnp.where(allowed, jnp.exp(score - logsum_piece[:, :, None]), 0.0)
            grad_v = grad_v + jnp.einsum(
                "hqk,qhd->khd",
                prob.astype(jnp.bfloat16),
                outgrad_piece,
                preferred_element_type=jnp.float32,
            )
            prob_grad = jnp.einsum(
                "qhd,khd->hqk", outgrad_piece, mixed_local, preferred_element_type=jnp.float32
            )
            score_grad = (prob * (prob_grad - delta_piece[:, :, None])).astype(jnp.bfloat16)
            grad_k = (
                grad_k
                + jnp.einsum(
                    "hqk,qhd->khd", score_grad, query_piece, preferred_element_type=jnp.float32
                )
                * scale
            )
            return (grad_k, grad_v)

        return lax.cond(query_index[-1] >= my_start, key_compute, lambda kept: kept, state)

    grad_k, grad_v = by_blocks(
        key_grad_step,
        (zeros3, zeros3),
        (
            lax.all_gather(queries.reshape(rows, width), "blk", axis=0, tiled=True),
            lax.all_gather(attended_grad, "blk", axis=0, tiled=True),
        ),
        jnp.int32(0),
    )
    queries_grad = grad_q.astype(jnp.bfloat16)
    keys_grad = grad_k.astype(jnp.bfloat16)
    mixed_grad = grad_v.astype(jnp.bfloat16).reshape(rows, width)
    q_pre_grad = (
        rotate(queries_grad.astype(jnp.float32), cosine, -sine)
        .astype(jnp.bfloat16)
        .reshape(rows, width)
    )
    k_pre_grad = (
        rotate(keys_grad.astype(jnp.float32), cosine, -sine)
        .astype(jnp.bfloat16)
        .reshape(rows, width)
    )
    grad_first = MIX * mixed_grad.astype(jnp.float32)
    value_grad = grad_first.astype(jnp.bfloat16)
    grad_query = outer(normed, q_pre_grad)
    grad_key = outer(normed, k_pre_grad)
    grad_value = outer(normed, value_grad)
    normed_grad = (
        back(q_pre_grad, query_weight)
        + back(k_pre_grad, key_weight)
        + back(value_grad, value_weight)
    )
    grad_attn_gain = jnp.sum(normed_grad * source * inv_first, axis=0)
    scaled_one = normed_grad * attn_gain
    grad_tokens = (
        mid_grad
        + inv_first * scaled_one
        - source * inv_first**3 * jnp.mean(scaled_one * source, axis=-1, keepdims=True)
    )
    summed = (
        lax.psum_scatter(grad_attn_gain, "blk", scatter_dimension=0, tiled=True),
        lax.psum_scatter(grad_query, "blk", scatter_dimension=0, tiled=True),
        lax.psum_scatter(grad_key, "blk", scatter_dimension=0, tiled=True),
        lax.psum_scatter(grad_value, "blk", scatter_dimension=0, tiled=True),
        lax.psum_scatter(grad_out_weight, "blk", scatter_dimension=0, tiled=True),
        lax.psum_scatter(grad_ffn_gain, "blk", scatter_dimension=0, tiled=True),
        lax.psum_scatter(grad_gate, "blk", scatter_dimension=0, tiled=True),
        lax.psum_scatter(grad_up, "blk", scatter_dimension=0, tiled=True),
        lax.psum_scatter(grad_down, "blk", scatter_dimension=0, tiled=True),
    )
    summed = (
        lax.psum(summed[0].astype(jnp.bfloat16), "seq").astype(jnp.float32),
        lax.psum(summed[1].astype(jnp.bfloat16), "seq").astype(jnp.float32),
        lax.psum(summed[2].astype(jnp.bfloat16), "seq").astype(jnp.float32),
        lax.psum(summed[3].astype(jnp.bfloat16), "seq").astype(jnp.float32),
        lax.psum(summed[4].astype(jnp.bfloat16), "seq").astype(jnp.float32),
        lax.psum(summed[5].astype(jnp.bfloat16), "seq").astype(jnp.float32),
        lax.psum(summed[6].astype(jnp.bfloat16), "seq").astype(jnp.float32),
        lax.psum(summed[7].astype(jnp.bfloat16), "seq").astype(jnp.float32),
        lax.psum(summed[8].astype(jnp.bfloat16), "seq").astype(jnp.float32),
    )
    return (
        layer_output,
        grad_tokens,
        grad_first,
        summed[0],
        summed[1],
        summed[2],
        summed[3],
        summed[4],
        summed[5],
        summed[6],
        summed[7],
        summed[8],
    )


def solution(mesh):
    n_seq, n_blk = mesh.shape["seq"], mesh.shape["blk"]

    def chosen(*args):
        rows, width = args[0].shape
        if fits(n_seq, n_blk, rows, width, args[9].shape[1]):
            return local_fast(n_seq, n_blk, *args)
        return local(*args)

    return jax.shard_map(
        chosen,
        mesh=mesh,
        in_specs=(
            P(("seq", "blk"), None),
            P(("seq", "blk"), None),
            P("seq", None),
            P(),
            P(),
            P(),
            P(),
            P(),
            P(),
            P(),
            P(),
            P(),
            P(("seq", "blk"), None),
        ),
        out_specs=(
            P(("seq", "blk"), None),
            P(("seq", "blk"), None),
            P(("seq", "blk"), None),
            P("blk"),
            P("blk", None),
            P("blk", None),
            P("blk", None),
            P("blk", None),
            P("blk"),
            P("blk", None),
            P("blk", None),
            P("blk", None),
        ),
        check_vma=False,
    )
```

```python
import functools
import math
import types

import jax
import jax.numpy as jnp
import numpy as np
from jax import lax
from jax.experimental import pallas as pl
from jax.experimental.pallas import tpu as pltpu
from jax.sharding import PartitionSpec as P

HEAD_DIM = 64


EPS = 1e-05
THETA = 10000.0
MIX = 0.5
NEG = -1e30


def doc_layout(lengths, index):
    ends = jnp.cumsum(lengths, axis=-1)
    past = (index[:, None] >= ends).astype(jnp.int32)
    return (jnp.sum(past, axis=1), index - jnp.sum(past * lengths, axis=1))


def tables(position):
    half = HEAD_DIM // 2
    freq = THETA ** (-(jnp.arange(half).astype(jnp.float32) * 2.0 / HEAD_DIM))
    angle = position.astype(jnp.float32)[:, None] * freq[None, :]
    return (jnp.cos(angle)[:, None, :], jnp.sin(angle)[:, None, :])


def rotate(values, cosine, sine):
    half = values.shape[-1] // 2
    first = values[..., :half]
    second = values[..., half:]
    return jnp.concatenate(
        [first * cosine - second * sine, second * cosine + first * sine], axis=-1
    )


def by_blocks(step, carry, pieces, start):
    rows = pieces[0].shape[0]
    size = math.gcd(rows, 1024)
    count = rows // size
    if count == 1:
        return step(carry, pieces, start)
    stacked = tuple((piece.reshape((count, size) + piece.shape[1:]) for piece in pieces))
    offsets = jnp.arange(count, dtype=jnp.int32) * size

    def turn(state, inputs):
        return (step(state, inputs[1], start + inputs[0]), None)

    result, unused = lax.scan(turn, carry, (offsets, stacked))
    return result


def outer(left, right):
    return lax.dot_general(
        left, right, (((0,), (0,)), ((), ())), preferred_element_type=jnp.float32
    )


def back(left, weight):
    return lax.dot_general(
        left, weight, (((1,), (1,)), ((), ())), preferred_element_type=jnp.float32
    )


TILE = 256
LANES = 128
GROUP = 16
MESH = pl.DeviceIdType.MESH
F32 = jnp.float32
BF16 = jnp.bfloat16


def remote(src, dst, send, recv, where):
    return pltpu.make_async_remote_copy(
        src_ref=src, dst_ref=dst, send_sem=send, recv_sem=recv, device_id=where, device_id_type=MESH
    )


def span(start, size, unit):
    return pl.ds(pl.multiple_of(start, unit), size)


def times(left, right):
    return jnp.dot(left, right, preferred_element_type=F32)


def iota(shape, dim):
    return lax.broadcasted_iota(jnp.int32, shape, dim)


def loop(low, high, body):
    def turn(index, unused):
        body(index)
        return unused

    lax.fori_loop(low, high, turn, 0)


class Trade:
    def __init__(self, blk, n_blk, phase, send, recv, source, place):
        self.blk, self.n_blk = blk, n_blk
        self.send, self.recv = send.at[phase], recv.at[phase]
        self.source, self.place = source, place

    def start(self, peer):
        src, dst = self.source(peer), self.place(self.blk)

        @pl.when(peer != self.blk)
        def _():
            remote(src, dst, self.send.at[peer], self.recv.at[self.blk], {"blk": peer}).start()

        @pl.when(peer == self.blk)
        def _():
            pltpu.make_async_copy(src, dst, self.recv.at[self.blk]).start()

    def arrived(self, peer):
        src, dst = self.source(peer), self.place(peer)

        @pl.when(peer != self.blk)
        def _():
            remote(src, dst, self.send.at[peer], self.recv.at[peer], {"blk": peer}).wait_recv()

        @pl.when(peer == self.blk)
        def _():
            pltpu.make_async_copy(src, dst, self.recv.at[peer]).wait()

    def all_arrived(self):
        loop(0, self.n_blk, self.arrived)

    def all_left(self):
        def left(peer):
            @pl.when(peer != self.blk)
            def _():
                remote(
                    self.source(peer), self.place(self.blk), self.send.at[peer], self.recv.at[self.blk], {"blk": peer}
                ).wait_send()

        loop(0, self.n_blk, left)


class Gift:
    def __init__(self, seq, n_seq, rows, owner, kind, src, dst, send, recv):
        self.seq, self.n_seq, self.rows, self.owner, self.kind = seq, n_seq, rows, owner, kind
        self.src, self.dst, self.send, self.recv = src, dst, send, recv

    def copy(self, other, send):
        dst = self.dst.at[span(other * self.rows, self.rows, self.rows)]
        return remote(self.src, dst, self.send.at[self.kind, send], self.recv.at[self.kind, other], {"seq": send})

    def own(self):
        dst = self.dst.at[pl.ds(self.owner * self.rows, self.rows)]
        return pltpu.make_async_copy(self.src, dst, self.recv.at[self.kind, self.owner])

    def start(self):
        @pl.when(self.seq != self.owner)
        def _():
            self.copy(self.seq, self.owner).start()

        @pl.when(self.seq == self.owner)
        def _():
            self.own().start()

    def arrived(self):
        for other in range(self.n_seq):
            if other == self.owner:
                self.own().wait()
            else:
                self.copy(other, other).wait_recv()

    def left(self):
        @pl.when(self.seq != self.owner)
        def _():
            self.copy(self.seq, self.owner).wait_send()


class Sum:
    def __init__(self, blk, size, part, cgot, rgot, zgot, total, sems):
        self.blk, self.size = blk, size
        self.core, self.chip = lax.rem(blk, 2), lax.div(blk, 2)
        side = lax.div(self.chip, 2)
        self.far = 2 * (1 - side)
        self.partner = self.chip + 1 - 2 * lax.rem(self.chip, 2)
        self.inner = lax.rem(self.chip, 2) != side
        self.far_inner = 2 - side
        self.part, self.cgot, self.rgot, self.zgot, self.total = part, cgot, rgot, zgot, total
        self.csend, self.crecv, self.rsend, self.rrecv, self.zsend, self.zrecv = sems

    def order(self, step):
        return jnp.where(step < 2, self.far + step, jnp.where(step == 2, self.partner, self.chip))

    def chunk(self, index):
        return self.part.at[span(index * self.size, self.size, 32)]

    def mine(self, chip):
        return self.chunk(2 * chip + self.core)

    def swap(self, chip):
        return remote(
            self.chunk(2 * chip + 1 - self.core),
            self.cgot(chip),
            self.csend.at[chip],
            self.crecv.at[chip],
            {"blk": 2 * self.chip + 1 - self.core},
        )

    def lend(self, index):
        return remote(
            self.mine(self.far + index),
            self.rgot(index),
            self.rsend.at[index],
            self.rrecv.at[index],
            {"blk": 2 * self.partner + self.core},
        )

    def send_far(self, index):
        return remote(
            self.mine(self.far + index),
            self.zgot(1),
            self.zsend.at[index],
            self.zrecv.at[1],
            {"blk": 2 * (self.far + index) + self.core},
        )

    def send_near(self):
        return remote(
            self.mine(self.partner),
            self.zgot(0),
            self.zsend.at[2],
            self.zrecv.at[0],
            {"blk": 2 * self.partner + self.core},
        )

    def add(self, mine, other):
        def group(index):
            at = span(index * 32, 32, 32)
            mine[at, :] = (mine[at, :].astype(F32) + other[at, :].astype(F32)).astype(BF16)

        loop(0, self.size // 32, group)

    def begin(self):
        for index in range(2):
            chip = self.far + index
            self.swap(chip).wait()
            self.add(self.mine(chip), self.cgot(chip))

            @pl.when(jnp.logical_not(self.inner))
            def _(index=index):
                self.lend(index).start()

        self.swap(self.partner).wait()
        self.add(self.mine(self.partner), self.cgot(self.partner))
        self.send_near().start()
        self.swap(self.chip).wait()

    def relay(self):
        @pl.when(self.inner)
        def _():
            for index in range(2):
                self.lend(index).wait_recv()
                self.add(self.mine(self.far + index), self.rgot(index))
                self.send_far(index).start()

    def end(self):
        self.send_near().wait_recv()
        self.send_far(0).wait_recv()
        mine, other = self.mine(self.chip), self.cgot(self.chip)

        def group(index):
            at = span(index * 32, 32, 32)
            value = mine[at, :].astype(F32) + other[at, :].astype(F32)
            value = value + self.zgot(0)[at, :].astype(F32) + self.zgot(1)[at, :].astype(F32)
            self.total[at, :] = value.astype(BF16)

        loop(0, self.size // 32, group)

    def left(self):
        self.send_near().wait_send()

        @pl.when(self.inner)
        def _():
            for index in range(2):
                self.send_far(index).wait_send()

        @pl.when(jnp.logical_not(self.inner))
        def _():
            for index in range(2):
                self.lend(index).wait_send()


class TileGift:
    def __init__(self, seq, n_seq, rows, src, dst, send, recv, owner_of):
        self.seq, self.n_seq, self.rows, self.src, self.dst = seq, n_seq, rows, src, dst
        self.send, self.recv, self.owner_of = send, recv, owner_of

    def place(self, other, slot):
        return self.dst.at[span(other * self.rows, self.rows, self.rows), span(slot * TILE, TILE, TILE)]

    def tile(self, index):
        return self.src.at[:, span(index * TILE, TILE, TILE)]

    def start(self, index):
        owner, slot = self.owner_of(index)
        src, dst, recv = self.tile(index), self.place(self.seq, slot), self.recv.at[slot, self.seq]

        @pl.when(owner != self.seq)
        def _():
            remote(src, dst, self.send.at[index], recv, {"seq": owner}).start()

        @pl.when(owner == self.seq)
        def _():
            pltpu.make_async_copy(src, dst, recv).start()

    def arrived(self, low, high):
        def one(slot):
            def other_one(other):
                dst, recv = self.place(other, slot), self.recv.at[slot, other]

                @pl.when(other != self.seq)
                def _():
                    remote(self.tile(0), dst, self.send.at[0], recv, {"seq": other}).wait_recv()

                @pl.when(other == self.seq)
                def _():
                    pltpu.make_async_copy(self.tile(0), dst, recv).wait()

            loop(0, self.n_seq, other_one)

        loop(low, high, one)

    def left(self, count):
        def one(index):
            owner, slot = self.owner_of(index)

            @pl.when(owner != self.seq)
            def _():
                remote(
                    self.tile(index), self.place(self.seq, slot), self.send.at[index], self.recv.at[slot, self.seq],
                    {"seq": owner},
                ).wait_send()

        loop(0, count, one)


class Spread:
    def __init__(self, seq, n_seq, owner, kind, src, dst, send, recv, local):
        self.seq, self.n_seq, self.owner, self.kind, self.src, self.dst = seq, n_seq, owner, kind, src, dst
        self.send, self.recv, self.local = send, recv, local

    def copy(self, other):
        return remote(self.src, self.dst, self.send.at[self.kind, other], self.recv.at[self.kind], {"seq": other})

    def own(self):
        return pltpu.make_async_copy(self.src, self.dst, self.local.at[self.kind])

    def start(self):
        @pl.when(self.seq == self.owner)
        def _():
            for other in range(self.n_seq):
                if other != self.owner:
                    self.copy(other).start()
            self.own().start()

    def finish(self):
        @pl.when(self.seq == self.owner)
        def _():
            for other in range(self.n_seq):
                if other != self.owner:
                    self.copy(other).wait_send()
            self.own().wait()

        @pl.when(self.seq != self.owner)
        def _():
            self.copy(self.owner).wait_recv()


def turn_over(src, dst):
    def one(index):
        at = span(index * TILE, TILE, TILE)
        dst[at, :] = src[:, at].T

    loop(0, src.shape[1] // TILE, one)


def outer_tiles(turned, rhs, part, chip, tiles, rhs_at, part_at):
    rows = span(chip * TILE, TILE, TILE)

    def tile(index):
        value = times(turned[rows, :], rhs[:, span(rhs_at + index * TILE, TILE, TILE)])
        part[rows, span(part_at + index * TILE, TILE, TILE)] = value.astype(BF16)

    loop(0, tiles, tile)


def layer_kernel(
    sizes,
    freq, tokens, first, lengths, attn_gain, ffn_gain, cot,
    h_query, h_key, h_value, h_out, h_gate, h_up, h_down,
    o_layer, o_tokens, o_first, o_gu, o_down, o_out, o_query, o_key, o_value, o_gain,
    v, sem,
):
    rows, width, ff, n_seq, n_blk, split = sizes
    v, sem = types.SimpleNamespace(**v), types.SimpleNamespace(**sem)
    docs = lengths.shape[1]
    chips = n_blk // 2
    scale = HEAD_DIM ** (-0.5)
    seq, blk = lax.axis_index("seq"), lax.axis_index("blk")
    chip_at = lax.div(blk, 2)

    def turned_chip(step):
        return lax.rem(chip_at + step, chips)

    barrier = pltpu.get_barrier_semaphore()
    for step in range(1, n_seq):
        pl.semaphore_signal(barrier, inc=1, device_id={"seq": lax.rem(seq + step, n_seq)}, device_id_type=MESH)
    for step in range(1, n_blk):
        pl.semaphore_signal(barrier, inc=1, device_id={"blk": lax.rem(blk + step, n_blk)}, device_id_type=MESH)

    def load(index, src, dst):
        copy = pltpu.make_async_copy(src, dst, sem.load.at[index])
        copy.start()
        return copy

    load_query = load(0, h_query, v.w_query)
    load_key = load(1, h_key, v.w_key)
    load_value = load(2, h_value, v.w_value)
    load_out = load(3, h_out, v.w_out)
    load_gate = load(4, h_gate, v.w_gate)
    load_up = load(5, h_up, v.w_up)
    load_down = load(6, h_down, v.w_down)

    def norm(group):
        at = span(group * GROUP, GROUP, GROUP)
        x = tokens[at, :].astype(F32)
        inv = lax.rsqrt(jnp.mean(x * x, axis=-1, keepdims=True) + EPS)
        v.normed[at, :] = (x * inv * attn_gain[...]).astype(BF16)
        v.inv_first[at, :] = jnp.broadcast_to(inv, (GROUP, LANES))

    loop(0, rows // GROUP, norm)

    def doc_start(index):
        start, end = jnp.zeros_like(index), jnp.int32(0)
        for doc in range(docs):
            end = end + lengths[0, doc]
            start = jnp.where(index >= end, end, start)
        return start

    my_index = blk * rows + iota((rows, LANES), 0)
    low_half = lax.rem(iota((rows, LANES), 1), HEAD_DIM) < HEAD_DIM // 2
    angle = (my_index - doc_start(my_index)).astype(F32) * freq[...]
    v.cos[...] = jnp.cos(angle)
    sine = jnp.sin(angle)
    v.sin[...] = jnp.where(low_half, -sine, sine)

    def halves_changed(u):
        half = HEAD_DIM // 2
        return jnp.where(low_half, pltpu.roll(u, LANES - half, 1), pltpu.roll(u, half, 1))

    def rotated(u):
        return u * v.cos[...] + halves_changed(u) * v.sin[...]

    def rotated_back(u):
        return u * v.cos[...] - halves_changed(u) * v.sin[...]

    cuts = [0]
    for tiles in split:
        cuts.append(cuts[-1] + tiles * TILE)
    wide = max(split) * TILE

    def gift(owner, kind, src, dst):
        return Gift(seq, n_seq, rows, owner, kind, src, dst, sem.xsend, sem.xrecv)

    gift_cot = gift(3, 0, cot, v.buf_a)
    gifts_two = [gift(owner, 0, v.two, v.buf_a) for owner in range(3)]
    each, hidden = split[0], ff // TILE
    gift_gu = TileGift(
        seq, n_seq, rows, v.gate_up, v.buf_b, sem.gusend, sem.gurecv,
        lambda index: (lax.div(index, each), lax.rem(index, each)),
    )
    gift_act = TileGift(seq, n_seq, rows, v.act, v.buf_b, sem.actsend, sem.actrecv, lambda index: (3, index))
    gift_att = gift(2, 2, v.att, v.buf_att)
    gift_mid = gift(2, 3, v.mid_b, v.buf_mid)
    gifts_normed = [gift(owner, 4, v.normed, v.buf_n) for owner in range(3)]
    gifts_pre = [gift(owner, 5, v.pre_grad.at[owner], v.buf_t) for owner in range(3)]

    def trade(phase, source, place):
        return Trade(blk, n_blk, phase, sem.asend, sem.arecv, source, place)

    def block_rows(ref):
        return lambda peer: ref.at[span(peer * rows, rows, rows)]

    def block_columns(ref):
        return lambda peer: ref.at[:, span(peer * LANES, LANES, LANES)]

    give_qkv = trade(0, lambda peer: v.pack.at[peer], lambda peer: v.qkv.at[:, span(peer * rows, rows, rows)])
    give_att = trade(1, block_rows(v.ob), block_columns(v.att))
    give_out = trade(2, lambda peer: v.out_pack.at[peer], block_rows(v.out_grad))
    give_grads = trade(
        3, lambda peer: v.pack.at[peer], lambda peer: v.grads.at[:, :, span(peer * LANES, LANES, LANES)]
    )

    pl.semaphore_wait(barrier, n_seq + n_blk - 2)
    gift_cot.start()
    for item in gifts_normed:
        item.start()

    for item in (load_query, load_key, load_value):
        item.wait()

    def project(step):
        chip = turned_chip(step)
        at = span(chip * TILE, TILE, TILE)
        left = v.normed[...]
        q, k, val = times(left, v.w_query[:, at]), times(left, v.w_key[:, at]), times(left, v.w_value[:, at])
        old = first[:, at].astype(F32)
        for core in range(2):
            peer = 2 * chip + core
            cols = slice(core * LANES, (core + 1) * LANES)
            v.pack[peer, 0] = (rotated(q[:, cols]) * scale).astype(BF16)
            v.pack[peer, 1] = rotated(k[:, cols]).astype(BF16)
            v.pack[peer, 2] = (MIX * val[:, cols] + MIX * old[:, cols]).astype(BF16)
            give_qkv.start(peer)

    loop(1, chips + 1, project)

    first_head = iota((TILE, LANES), 1) < HEAD_DIM

    def stacked(values):
        return jnp.concatenate([jnp.where(first_head, values, 0.0), jnp.where(first_head, 0.0, values)], axis=0)

    def unstacked(values):
        return jnp.where(first_head, values[:TILE], values[TILE:])

    def attend(block):
        for core in range(2):
            give_qkv.arrived(2 * block + core)
        at, both = span(block * TILE, TILE, TILE), span(block * 2 * TILE, 2 * TILE, 2 * TILE)
        v.q2[both, :] = stacked(v.qkv[0, at, :].astype(F32)).astype(BF16)
        index = block * TILE + lax.rem(iota((2 * TILE, 1), 0), TILE)
        start = doc_start(index)
        v.top[...] = jnp.full((2 * TILE, LANES), NEG, F32)

        def scores(tile):
            cols = span(tile * TILE, TILE, TILE)
            score = back(v.q2[both, :], v.qkv[1, cols, :])
            key = tile * TILE + iota((2 * TILE, TILE), 1)
            score = jnp.where((key <= index) & (key >= start), score, NEG)
            v.score[:, cols] = score
            v.top[...] = jnp.maximum(v.top[...], jnp.maximum(score[:, :LANES], score[:, LANES:]))

        loop(0, block + 1, scores)
        top = jnp.max(v.top[...], axis=1, keepdims=True)
        v.top[...] = jnp.zeros((2 * TILE, LANES), F32)
        v.o2[...] = jnp.zeros((2 * TILE, LANES), F32)

        def weights(tile):
            cols = span(tile * TILE, TILE, TILE)
            weight = jnp.exp(v.score[:, cols] - top)
            v.top[...] += weight[:, :LANES] + weight[:, LANES:]
            weight = weight.astype(BF16)
            v.prob[both, cols] = weight
            v.o2[...] += times(weight, v.qkv[2, cols, :])

        loop(0, block + 1, weights)
        inv = 1.0 / jnp.sum(v.top[...], axis=1, keepdims=True)
        v.row[both, :] = jnp.broadcast_to(inv, (2 * TILE, LANES))
        attended = unstacked(v.o2[...] * inv)
        v.o32[at, :] = attended
        v.ob[at, :] = attended.astype(BF16)
        for core in range(2):
            give_att.start(2 * block + core)

    loop(0, chips, attend)
    give_att.all_arrived()
    gift_att.start()

    load_out.wait()

    def middle(tile):
        cols = span(tile * TILE, TILE, TILE)
        value = tokens[:, cols].astype(F32) + times(v.att[...], v.w_out[:, cols])
        v.mid[:, cols] = value
        o_layer[:, cols] = value

    loop(0, width // TILE, middle)

    def norm_two(group):
        at = span(group * GROUP, GROUP, GROUP)
        x = v.mid[at, :]
        inv = lax.rsqrt(jnp.mean(x * x, axis=-1, keepdims=True) + EPS)
        v.two[at, :] = (x * inv * ffn_gain[...]).astype(BF16)
        v.inv_second[at, :] = jnp.broadcast_to(inv, (GROUP, LANES))

    loop(0, rows // GROUP, norm_two)
    for item in gifts_two:
        item.start()

    for item in (load_gate, load_up, load_down):
        item.wait()
    v.two_grad[...] = jnp.zeros((rows, width), F32)

    def feed(step):
        tile = lax.rem(split[0] + step, hidden)
        cols = span(tile * TILE, TILE, TILE)
        gate = times(v.two[...], v.w_gate[:, cols])
        up = times(v.two[...], v.w_up[:, cols])
        act_grad = back(cot[...], v.w_down[cols, :])
        sigma = jax.nn.sigmoid(gate)
        silu = gate * sigma
        act = (silu * up).astype(BF16)
        gate_grad = (act_grad * up * sigma * (1.0 + gate * (1.0 - sigma))).astype(BF16)
        up_grad = (act_grad * silu).astype(BF16)
        v.act[:, cols] = act
        v.gate_up[:, cols] = gate_grad
        v.gate_up[:, span(ff + tile * TILE, TILE, TILE)] = up_grad
        gift_gu.start(tile)
        gift_gu.start(hidden + tile)
        gift_act.start(tile)
        o_layer[...] += times(act, v.w_down[cols, :])
        v.two_grad[...] += back(gate_grad, v.w_gate[:, cols]) + back(up_grad, v.w_up[:, cols])

    loop(0, hidden, feed)
    for step in range(1, n_blk):
        pl.semaphore_signal(sem.ready, inc=1, device_id={"blk": lax.rem(blk + step, n_blk)}, device_id_type=MESH)
    v.gain_rows[...] = jnp.zeros((16, width), F32)

    def norm_two_back(group):
        at = span(group * GROUP, GROUP, GROUP)
        x, grad, inv = v.mid[at, :], v.two_grad[at, :], v.inv_second[at, :1]
        term = grad * x * inv
        v.gain_rows[8:16, :] += term[:8] + term[8:]
        scaled = grad * ffn_gain[...]
        mean = jnp.mean(scaled * x, axis=-1, keepdims=True)
        value = cot[at, :].astype(F32) + inv * scaled - x * (inv * inv * inv * mean)
        v.mid_grad[at, :] = value
        v.mid_b[at, :] = value.astype(BF16)

    loop(0, rows // GROUP, norm_two_back)
    gift_mid.start()

    def out_back(step):
        chip = turned_chip(step)
        value = back(v.mid_b[...], v.w_out[span(chip * TILE, TILE, TILE), :]).astype(BF16)
        for core in range(2):
            v.out_pack[2 * chip + core] = value[:, core * LANES : (core + 1) * LANES]
            give_out.start(2 * chip + core)

    loop(1, chips + 1, out_back)

    pl.semaphore_wait(sem.ready, n_blk - 1)
    chunk, down = width // n_blk, ff // n_blk

    def sems_of(index):
        return tuple(
            item.at[index] for item in (sem.csend, sem.crecv, sem.rsend, sem.rrecv, sem.zsend, sem.zrecv)
        )

    def stack_in(ref, top, cols):
        return lambda index: ref.at[span(top + index * chunk, chunk, 32), cols]

    def square_in(ref, more):
        def place(index):
            index = index + more
            return ref.at[
                span(lax.rem(index, 2) * down, down, 32), span(lax.div(index, 2) * width, width, width)
            ]

        return place

    def piece(index, low, high):
        cols = slice(low, high)
        return Sum(
            blk, chunk, v.w_gate.at[:, cols], stack_in(v.w_up, 0, cols), stack_in(v.w_up, chips * chunk, cols),
            stack_in(v.w_up, (chips + 2) * chunk, cols), v.total.at[:, cols], sems_of(index),
        )

    third = -(-each // 3)
    edges = [0, third, 2 * third, each]
    thirds = [piece(index, edges[index] * TILE, edges[index + 1] * TILE) for index in range(3)]
    last = split[2] * TILE
    halves = [piece(0, 0, last), piece(1, last, last + width)]
    sum_down = Sum(
        blk, down, v.w_down, square_in(v.w_up, 0), square_in(v.w_gate, 0), square_in(v.w_gate, 2), v.total_down,
        sems_of(0),
    )
    sum_tail = Sum(
        blk, chunk, v.w_out, stack_in(v.got_tail, 0, slice(None)), stack_in(v.got_tail, chips * chunk, slice(None)),
        stack_in(v.got_tail, (chips + 2) * chunk, slice(None)), v.total_tail, sems_of(3),
    )
    first_two, third_one, fourth = seq < 2, seq == 2, seq == 3

    def spread(owner, kind, src, dst):
        return Spread(seq, n_seq, owner, kind, src, dst, sem.gsend, sem.grecv, sem.glocal)

    spreads = [
        [
            spread(
                owner,
                3 * owner + index,
                v.total.at[:, edges[index] * TILE : edges[index + 1] * TILE],
                o_gu.at[:, cuts[owner] + edges[index] * TILE : cuts[owner] + edges[index + 1] * TILE],
            )
            for index in range(3)
        ]
        for owner in range(2)
    ] + [
        [
            spread(2, 6, v.total.at[:, :last], o_gu.at[:, cuts[2] : cuts[3]]),
            spread(2, 7, v.total.at[:, last : last + width], o_out),
        ],
        [spread(3, 8, v.total_down, o_down)],
    ]
    tails = [
        spread(0, 9, v.total_tail, o_query),
        spread(1, 10, v.total_tail, o_key),
        spread(2, 11, v.total_tail, o_value),
    ]

    def products(item, turned, rhs, tiles, rhs_at, part_at):
        def one(step):
            chip = item.order(step)
            outer_tiles(turned, rhs, v.w_gate, chip, tiles, rhs_at, part_at)
            item.swap(chip).start()

        loop(0, chips, one)
        item.begin()

    def gate_up_piece(index):
        gift_gu.arrived(edges[index], edges[index + 1])
        at = edges[index] * TILE
        products(thirds[index], v.turned, v.buf_b, edges[index + 1] - edges[index], at, at)

    def down_products():
        gift_act.arrived(0, hidden)

        def one(index):
            at = span(index * TILE, TILE, TILE)
            v.turned[:TILE, :] = v.buf_b[:, at].T
            v.w_down[at, :] = times(v.turned[:TILE, :], v.buf_a[...]).astype(BF16)

        loop(0, hidden, one)
        loop(0, chips, lambda step: sum_down.swap(sum_down.order(step)).start())
        sum_down.begin()

    for owner in range(n_seq):

        @pl.when(seq == owner)
        def _(owner=owner):
            (gifts_two + [gift_cot])[owner].arrived()

    @pl.when(first_two)
    def _():
        turn_over(v.buf_a, v.turned)
        gate_up_piece(0)

    give_out.all_arrived()

    def prepare(block):
        at, both = span(block * TILE, TILE, TILE), span(block * 2 * TILE, 2 * TILE, 2 * TILE)
        grad = (stacked(v.out_grad[at, :].astype(F32)) * v.row[both, :]).astype(BF16)
        v.do2[both, :] = grad
        attended = v.o32[at, :]
        delta = jnp.sum(grad.astype(F32) * jnp.concatenate([attended, attended], axis=0), axis=1, keepdims=True)
        v.row[both, :] = jnp.broadcast_to(delta, (2 * TILE, LANES))
        v.dq[both, :] = jnp.zeros((2 * TILE, LANES), F32)

    loop(0, chips, prepare)
    give_qkv.all_left()

    def key_block(block):
        at = span(block * TILE, TILE, TILE)
        v.dk[...] = jnp.zeros((TILE, LANES), F32)
        v.dv[...] = jnp.zeros((TILE, LANES), F32)

        def query_block(other):
            both = span(other * 2 * TILE, 2 * TILE, 2 * TILE)
            prob = v.prob[both, at]
            grad = back(v.do2[both, :], v.qkv[2, at, :])
            score_grad = (prob.astype(F32) * (grad - v.row[both, :1])).astype(BF16)
            v.dk[...] += outer(score_grad, v.q2[both, :])
            v.dv[...] += outer(prob, v.do2[both, :])
            v.dq[both, :] += times(score_grad, v.qkv[1, at, :])

        loop(block, chips, query_block)
        dq = (unstacked(v.dq[span(block * 2 * TILE, 2 * TILE, 2 * TILE), :]) * scale).astype(BF16)
        dk, dv = v.dk[...].astype(BF16), v.dv[...].astype(BF16)
        for core in range(2):
            peer = 2 * block + core
            part = slice(core * rows, (core + 1) * rows)
            v.pack[peer, 0] = dq[part]
            v.pack[peer, 1] = dk[part]
            v.pack[peer, 2] = dv[part]
            give_grads.start(peer)

    loop(0, chips, key_block)

    @pl.when(first_two)
    def _():
        thirds[0].relay()
        gate_up_piece(1)
        gate_up_piece(2)
        thirds[1].relay()

    @pl.when(third_one)
    def _():
        turn_over(v.buf_a, v.turned)
        gift_gu.arrived(0, split[2])
        products(halves[0], v.turned, v.buf_b, split[2], 0, 0)
        gift_att.arrived()
        gift_mid.arrived()
        turn_over(v.buf_att, v.turned)
        products(halves[1], v.turned, v.buf_mid, width // TILE, 0, last)
        halves[0].relay()

    @pl.when(fourth)
    def _():
        down_products()
        sum_down.relay()

    give_grads.all_arrived()

    def rotate_back(index):
        cols = span(index * LANES, LANES, LANES)
        v.pre_grad[0, :, cols] = rotated_back(v.grads[0, :, cols].astype(F32)).astype(BF16)
        v.pre_grad[1, :, cols] = rotated_back(v.grads[1, :, cols].astype(F32)).astype(BF16)
        value = MIX * v.grads[2, :, cols].astype(F32)
        v.pre_grad[2, :, cols] = value.astype(BF16)
        o_first[:, cols] = value

    loop(0, width // LANES, rotate_back)
    for item in gifts_pre:
        item.start()

    def normed_back(tile):
        at = span(tile * TILE, TILE, TILE)
        o_tokens[:, at] = (
            back(v.pre_grad[0], v.w_query[at, :])
            + back(v.pre_grad[1], v.w_key[at, :])
            + back(v.pre_grad[2], v.w_value[at, :])
        )

    loop(0, width // TILE, normed_back)

    def norm_back(group):
        at = span(group * GROUP, GROUP, GROUP)
        x, grad, inv = tokens[at, :].astype(F32), o_tokens[at, :], v.inv_first[at, :1]
        term = grad * x * inv
        v.gain_rows[0:8, :] += term[:8] + term[8:]
        scaled = grad * attn_gain[...]
        mean = jnp.mean(scaled * x, axis=-1, keepdims=True)
        o_tokens[at, :] = v.mid_grad[at, :] + inv * scaled - x * (inv * inv * inv * mean)

    loop(0, rows // GROUP, norm_back)

    for peer in range(n_blk):
        v.gains[peer] = v.gain_rows[:, peer * LANES : (peer + 1) * LANES]

    def gain_copy(step):
        other = lax.rem(blk + step, n_blk)
        return remote(
            v.gains.at[other], v.gain_got.at[step - 1], sem.hsend.at[step - 1], sem.hrecv.at[step - 1],
            {"blk": other},
        )

    for step in range(1, n_blk):
        gain_copy(step).start()

    @pl.when(first_two)
    def _():
        thirds[2].relay()
        thirds[0].end()

    for owner in range(2):
        spreads[owner][0].start()

    @pl.when(first_two)
    def _():
        thirds[1].end()

    for owner in range(2):
        spreads[owner][1].start()

    @pl.when(third_one)
    def _():
        halves[1].relay()
        halves[0].end()

    spreads[2][0].start()

    for owner in range(3):

        @pl.when(seq == owner)
        def _(owner=owner):
            gifts_normed[owner].arrived()
            gifts_pre[owner].arrived()

    @pl.when(seq < 3)
    def _():
        turn_over(v.buf_n, v.turned)

        def one(step):
            chip = sum_tail.order(step)
            outer_tiles(v.turned, v.buf_t, v.w_out, chip, width // TILE, 0, 0)
            sum_tail.swap(chip).start()

        loop(0, chips, one)
        sum_tail.begin()
        sum_tail.relay()

    @pl.when(first_two)
    def _():
        thirds[2].end()

    for owner in range(2):
        spreads[owner][2].start()

    @pl.when(third_one)
    def _():
        halves[1].end()

    spreads[2][1].start()

    @pl.when(fourth)
    def _():
        sum_down.end()

    spreads[3][0].start()

    value = v.gains[blk]
    for step in range(1, n_blk):
        gain_copy(step).wait()
        value = value + v.gain_got[step - 1]
    v.gain_sum[seq] = value
    for step in range(1, n_seq):
        other = lax.rem(seq + step, n_seq)
        mine = v.gain_sum.at[seq]
        remote(mine, mine, sem.isend.at[step - 1], sem.irecv.at[seq], {"seq": other}).start()

    @pl.when(seq < 3)
    def _():
        sum_tail.end()

    for item in tails:
        item.start()

    for step in range(1, n_seq):
        other = lax.rem(seq + step, n_seq)
        theirs = v.gain_sum.at[other]
        remote(theirs, theirs, sem.isend.at[step - 1], sem.irecv.at[other], {"seq": other}).wait()
    value = v.gain_sum[0]
    for group in range(1, n_seq):
        value = value + v.gain_sum[group]
    o_gain[0:8, :] = jnp.broadcast_to(jnp.sum(value[:8], axis=0, keepdims=True), (8, LANES))
    o_gain[8:16, :] = jnp.broadcast_to(jnp.sum(value[8:], axis=0, keepdims=True), (8, LANES))

    for item in sum(spreads, []) + tails:
        item.finish()
    for item in [gift_cot, gift_att, gift_mid] + gifts_two + gifts_normed + gifts_pre:
        item.left()
    gift_gu.left(2 * hidden)
    gift_act.left(hidden)
    for item in (give_att, give_out, give_grads):
        item.all_left()

    @pl.when(first_two)
    def _():
        for item in thirds:
            item.left()

    @pl.when(third_one)
    def _():
        for item in halves:
            item.left()

    @pl.when(fourth)
    def _():
        sum_down.left()

    @pl.when(seq < 3)
    def _():
        sum_tail.left()


def finish_kernel(
    layer, tokens, first, gu, down, out, query, key, value, gain,
    o_layer, o_tokens, o_first, o_gain, o_gain_two, o_query, o_key, o_value, o_out, o_gate, o_up, o_down,
    kept, small, large, sem_kept_in, sem_kept_out, sem_in, sem_out,
):
    kept_in = [
        pltpu.make_async_copy(src, kept[index], sem_kept_in.at[index])
        for index, src in enumerate((layer, tokens, first))
    ]
    kept_out = [
        pltpu.make_async_copy(kept[index], dst, sem_kept_out.at[index])
        for index, dst in enumerate((o_layer, o_tokens, o_first))
    ]
    ff = o_gate.shape[1]
    sources = [gu.at[:, :ff], gu.at[:, ff:], down, query, key, value, out]
    targets = [o_gate, o_up, o_down, o_query, o_key, o_value, o_out]
    loads = [pltpu.make_async_copy(src, small[index], sem_in.at[index]) for index, src in enumerate(sources)]
    stores = [pltpu.make_async_copy(large[index], dst, sem_out.at[index]) for index, dst in enumerate(targets)]
    for item in kept_in + loads:
        item.start()
    for coming, going in zip(kept_in, kept_out):
        coming.wait()
        going.start()
    for index in range(len(sources)):
        loads[index].wait()

        def group(step, index=index):
            at = span(step * GROUP, GROUP, GROUP)
            large[index][at, :] = small[index][at, :].astype(F32)

        loop(0, targets[index].shape[0] // GROUP, group)
        stores[index].start()
    o_gain[...] = gain[0:1, :]
    o_gain_two[...] = gain[8:9, :]
    for item in stores + kept_out:
        item.wait()


def finish(layer, tokens, first, gu, down, out, query, key, value, gain):
    hbm, vmem = pl.BlockSpec(memory_space=pl.ANY), pl.BlockSpec(memory_space=pltpu.VMEM)
    shape = jax.ShapeDtypeStruct
    ff = gu.shape[1] // 2
    dims = [(gu.shape[0], ff), (gu.shape[0], ff), down.shape, query.shape, key.shape, value.shape, out.shape]
    dma = pltpu.SemaphoreType.DMA
    results = pl.pallas_call(
        finish_kernel,
        out_shape=tuple(
            shape(each, F32)
            for each in (
                layer.shape, tokens.shape, first.shape, (1, LANES), (1, LANES), dims[3], dims[4], dims[5], dims[6], dims[0], dims[1], dims[2]
            )
        ),
        in_specs=[hbm] * 9 + [vmem],
        out_specs=(hbm,) * 3 + (vmem,) * 2 + (hbm,) * 7,
        scratch_shapes=(
            [pltpu.VMEM(each.shape, F32) for each in (layer, tokens, first)],
            [pltpu.VMEM(each, BF16) for each in dims],
            [pltpu.VMEM(each, F32) for each in dims],
            dma((3,)), dma((3,)), dma((7,)), dma((7,)),
        ),
        compiler_params=pltpu.CompilerParams(vmem_limit_bytes=63 * 1024 * 1024),
        name="finish",
    )(layer, tokens, first, gu, down, out, query, key, value, gain)
    return results[:3] + (results[3][0],) + results[5:9] + (results[4][0],) + results[9:]


def tile_split(width, ff):
    tiles, more = 2 * ff // TILE, width // TILE
    each = -(-(tiles + more) // 3)
    return (each, each, tiles - 2 * each)


def fits(n_seq, n_blk, rows, width, ff):
    return (
        n_seq == 4
        and n_blk % 2 == 0
        and n_blk * LANES == width
        and rows == LANES
        and ff % TILE == 0
        and (ff // n_blk) % 32 == 0
        and 2 * (ff // n_blk) <= width
        and n_blk == 8
    )


def local_fast(
    n_seq,
    n_blk,
    tokens,
    first_values,
    doc_lengths,
    attn_gain,
    query_weight,
    key_weight,
    value_weight,
    out_weight,
    ffn_gain,
    gate_weight,
    up_weight,
    down_weight,
    cotangent,
):
    rows, width = tokens.shape
    ff = gate_weight.shape[1]
    split = tile_split(width, ff)
    sizes = (rows, width, ff, n_seq, n_blk, split)
    half = HEAD_DIM // 2
    freq = THETA ** (-(np.arange(half) * 2.0 / HEAD_DIM))
    freq = np.tile(freq, LANES // half)[None, :].astype(np.float32)
    wide = max(split) * TILE
    chunk, down, chips = width // n_blk, ff // n_blk, n_blk // 2
    all_rows, group = n_seq * rows, n_blk * rows
    vmem = pl.BlockSpec(memory_space=pltpu.VMEM)
    hbm = pl.BlockSpec(memory_space=pl.ANY)
    smem = pl.BlockSpec(memory_space=pltpu.SMEM)
    shape = jax.ShapeDtypeStruct

    def half_type(*dims):
        return pltpu.VMEM(dims, BF16)

    def full_type(*dims):
        return pltpu.VMEM(dims, F32)

    scratch = dict(
        w_query=half_type(width, width), w_key=half_type(width, width), w_value=half_type(width, width),
        w_out=half_type(width, width), w_gate=half_type(width, ff), w_up=half_type(width, ff),
        w_down=half_type(ff, width),
        normed=half_type(rows, width), inv_first=full_type(rows, LANES), inv_second=full_type(rows, LANES),
        cos=full_type(rows, LANES), sin=full_type(rows, LANES),
        pack=half_type(n_blk, 3, rows, LANES), qkv=half_type(3, group, LANES),
        q2=half_type(2 * group, LANES), do2=half_type(2 * group, LANES), prob=half_type(2 * group, group),
        score=full_type(2 * TILE, group), top=full_type(2 * TILE, LANES), o2=full_type(2 * TILE, LANES),
        row=full_type(2 * group, LANES), o32=full_type(group, LANES), ob=half_type(group, LANES),
        dq=full_type(2 * group, LANES), dk=full_type(TILE, LANES), dv=full_type(TILE, LANES),
        att=half_type(rows, width), mid=full_type(rows, width), two=half_type(rows, width),
        act=half_type(rows, ff), gate_up=half_type(rows, 2 * ff), two_grad=full_type(rows, width),
        mid_grad=full_type(rows, width), mid_b=half_type(rows, width),
        out_pack=half_type(n_blk, rows, LANES), out_grad=half_type(group, LANES),
        grads=half_type(3, rows, width), pre_grad=half_type(3, rows, width),
        buf_a=half_type(all_rows, width), buf_b=half_type(all_rows, ff), buf_att=half_type(all_rows, width),
        buf_mid=half_type(all_rows, width), buf_n=half_type(all_rows, width), buf_t=half_type(all_rows, width),
        turned=half_type(width, all_rows),
        got_tail=half_type(2 * chips * chunk, width),
        total=half_type(chunk, wide), total_down=half_type(down, width), total_tail=half_type(chunk, width),
        gain_rows=full_type(16, width), gains=full_type(n_blk, 16, LANES), gain_got=full_type(n_blk - 1, 16, LANES),
        gain_sum=full_type(n_seq, 16, LANES),
    )
    dma = pltpu.SemaphoreType.DMA
    sems = dict(
        load=dma((7,)), asend=dma((4, n_blk)), arecv=dma((4, n_blk)), xsend=dma((6, n_seq)), xrecv=dma((6, n_seq)),
        gusend=dma((2 * ff // TILE,)), gurecv=dma((split[0], n_seq)), actsend=dma((ff // TILE,)),
        actrecv=dma((ff // TILE, n_seq)), ready=pltpu.SemaphoreType.REGULAR,
        csend=dma((4, chips)), crecv=dma((4, chips)), rsend=dma((4, 2)), rrecv=dma((4, 2)), zsend=dma((4, 3)),
        zrecv=dma((4, 2)), gsend=dma((12, n_seq)), grecv=dma((12,)), glocal=dma((12,)),
        hsend=dma((n_blk - 1,)), hrecv=dma((n_blk - 1,)), isend=dma((n_seq - 1,)), irecv=dma((n_seq,)),
    )
    layer, grad_tokens, grad_first, out_gu, out_down, out_out, out_query, out_key, out_value, out_gain = pl.pallas_call(
        functools.partial(layer_kernel, sizes),
        out_shape=(
            shape((rows, width), F32),
            shape((rows, width), F32),
            shape((rows, width), F32),
            shape((chunk, 2 * ff), BF16),
            shape((down, width), BF16),
            shape((chunk, width), BF16),
            shape((chunk, width), BF16),
            shape((chunk, width), BF16),
            shape((chunk, width), BF16),
            shape((16, LANES), F32),
        ),
        in_specs=[vmem, vmem, vmem, smem, vmem, vmem, vmem] + [hbm] * 7,
        out_specs=(vmem, vmem, vmem) + (hbm,) * 6 + (vmem,),
        scratch_shapes=(scratch, sems),
        compiler_params=pltpu.CompilerParams(
            collective_id=0, has_side_effects=True, vmem_limit_bytes=63 * 1024 * 1024
        ),
        name="layer",
    )(
        freq, tokens, first_values, doc_lengths, attn_gain[None, :], ffn_gain[None, :], cotangent,
        query_weight, key_weight, value_weight, out_weight, gate_weight, up_weight, down_weight,
    )
    return finish(layer, grad_tokens, grad_first, out_gu, out_down, out_out, out_query, out_key, out_value, out_gain)


def local(
    tokens,
    first_values,
    doc_lengths,
    attn_gain,
    query_weight,
    key_weight,
    value_weight,
    out_weight,
    ffn_gain,
    gate_weight,
    up_weight,
    down_weight,
    cotangent,
):
    rows, width = tokens.shape
    heads = width // HEAD_DIM
    scale = HEAD_DIM ** (-0.5)
    shape3 = (rows, heads, HEAD_DIM)
    my_start = lax.axis_index("blk") * rows
    my_index = my_start + jnp.arange(rows, dtype=jnp.int32)
    my_doc, my_pos = doc_layout(doc_lengths, my_index)
    cosine, sine = tables(my_pos)
    source = tokens.astype(jnp.float32)
    inv_first = lax.rsqrt(jnp.mean(source * source, axis=-1, keepdims=True) + EPS)
    normed = (source * inv_first * attn_gain).astype(jnp.bfloat16)
    query_pre = jnp.dot(normed, query_weight, preferred_element_type=jnp.float32)
    key_pre = jnp.dot(normed, key_weight, preferred_element_type=jnp.float32)
    value_pre = jnp.dot(normed, value_weight, preferred_element_type=jnp.float32)
    queries = rotate(query_pre.reshape(shape3), cosine, sine).astype(jnp.bfloat16)
    keys = rotate(key_pre.reshape(shape3), cosine, sine).astype(jnp.bfloat16).reshape(rows, width)
    mixed = (MIX * value_pre + MIX * first_values.astype(jnp.float32)).astype(jnp.bfloat16)
    keys_local = keys.reshape(shape3)
    mixed_local = mixed.reshape(shape3)

    def allowed_mask(query_index, query_doc, key_index, key_doc):
        return (query_doc[:, None] == key_doc[None, :]) & (
            key_index[None, :] <= query_index[:, None]
        )

    def forward_step(state, pieces, start):
        count = pieces[0].shape[0]
        keys_piece = pieces[0].reshape(count, heads, HEAD_DIM)
        values_piece = pieces[1].reshape(count, heads, HEAD_DIM)
        key_index = start + jnp.arange(count, dtype=jnp.int32)

        def forward_compute(state):
            high, total, accum = state
            key_doc, unused = doc_layout(doc_lengths, key_index)
            allowed = allowed_mask(my_index, my_doc, key_index, key_doc)[None]
            score = (
                jnp.einsum("qhd,khd->hqk", queries, keys_piece, preferred_element_type=jnp.float32)
                * scale
            )
            score = jnp.where(allowed, score, NEG)
            new_high = jnp.maximum(high, jnp.max(score, axis=-1))
            weight = jnp.where(allowed, jnp.exp(score - new_high[:, :, None]), 0.0)
            factor = jnp.exp(high - new_high)
            total = total * factor + jnp.sum(weight, axis=-1)
            accum = accum * factor.T[:, :, None] + jnp.einsum(
                "hqk,khd->qhd",
                weight.astype(jnp.bfloat16),
                values_piece,
                preferred_element_type=jnp.float32,
            )
            return (new_high, total, accum)

        return lax.cond(start <= my_index[-1], forward_compute, lambda kept: kept, state)

    def query_grad_step(grad_q, pieces, start):
        count = pieces[0].shape[0]
        keys_piece = pieces[0].reshape(count, heads, HEAD_DIM)
        values_piece = pieces[1].reshape(count, heads, HEAD_DIM)
        key_index = start + jnp.arange(count, dtype=jnp.int32)

        def query_compute(grad_q):
            key_doc, unused = doc_layout(doc_lengths, key_index)
            allowed = allowed_mask(my_index, my_doc, key_index, key_doc)[None]
            score = (
                jnp.einsum("qhd,khd->hqk", queries, keys_piece, preferred_element_type=jnp.float32)
                * scale
            )
            prob = jnp.where(allowed, jnp.exp(score - logsum[:, :, None]), 0.0)
            prob_grad = jnp.einsum(
                "qhd,khd->hqk", outgrad_local, values_piece, preferred_element_type=jnp.float32
            )
            score_grad = (prob * (prob_grad - delta[:, :, None])).astype(jnp.bfloat16)
            return (
                grad_q
                + jnp.einsum(
                    "hqk,khd->qhd", score_grad, keys_piece, preferred_element_type=jnp.float32
                )
                * scale
            )

        return lax.cond(start <= my_index[-1], query_compute, lambda kept: kept, grad_q)

    init = (
        jnp.full((heads, rows), NEG, jnp.float32),
        jnp.zeros((heads, rows), jnp.float32),
        jnp.zeros(shape3, jnp.float32),
    )
    state = by_blocks(
        forward_step,
        init,
        (
            lax.all_gather(keys, "blk", axis=0, tiled=True),
            lax.all_gather(mixed, "blk", axis=0, tiled=True),
        ),
        jnp.int32(0),
    )
    high, total, accum = state
    logsum = high + jnp.log(total)
    attended = accum / total.T[:, :, None]
    attended_b = attended.astype(jnp.bfloat16).reshape(rows, width)
    mid = source + jnp.dot(attended_b, out_weight, preferred_element_type=jnp.float32)
    inv_second = lax.rsqrt(jnp.mean(mid * mid, axis=-1, keepdims=True) + EPS)
    normed_two = (mid * inv_second * ffn_gain).astype(jnp.bfloat16)
    gate = jnp.dot(normed_two, gate_weight, preferred_element_type=jnp.float32)
    up = jnp.dot(normed_two, up_weight, preferred_element_type=jnp.float32)
    act = (jax.nn.silu(gate) * up).astype(jnp.bfloat16)
    layer_output = mid + jnp.dot(act, down_weight, preferred_element_type=jnp.float32)
    cot_float = cotangent.astype(jnp.float32)
    grad_down = outer(act, cotangent)
    act_grad = back(cotangent, down_weight)
    sigma = jax.nn.sigmoid(gate)
    gate_grad = (act_grad * up * sigma * (1.0 + gate * (1.0 - sigma))).astype(jnp.bfloat16)
    up_grad = (act_grad * gate * sigma).astype(jnp.bfloat16)
    grad_gate = outer(normed_two, gate_grad)
    grad_up = outer(normed_two, up_grad)
    normed_two_grad = back(gate_grad, gate_weight) + back(up_grad, up_weight)
    grad_ffn_gain = jnp.sum(normed_two_grad * mid * inv_second, axis=0)
    scaled_two = normed_two_grad * ffn_gain
    mid_grad = (
        cot_float
        + inv_second * scaled_two
        - mid * inv_second**3 * jnp.mean(scaled_two * mid, axis=-1, keepdims=True)
    )
    mid_grad_b = mid_grad.astype(jnp.bfloat16)
    grad_out_weight = outer(attended_b, mid_grad_b)
    attended_grad = back(mid_grad_b, out_weight).astype(jnp.bfloat16)
    outgrad_local = attended_grad.reshape(shape3)
    delta = jnp.sum(outgrad_local.astype(jnp.float32) * attended, axis=-1).T
    zeros3 = jnp.zeros(shape3, jnp.float32)
    grad_q = by_blocks(
        query_grad_step,
        zeros3,
        (
            lax.all_gather(keys, "blk", axis=0, tiled=True),
            lax.all_gather(mixed, "blk", axis=0, tiled=True),
        ),
        jnp.int32(0),
    )
    all_logsum, all_delta = (
        lax.all_gather(logsum.T, "blk", axis=0, tiled=True),
        lax.all_gather(delta.T, "blk", axis=0, tiled=True),
    )

    def key_grad_step(state, pieces, start):
        count = pieces[0].shape[0]
        query_piece = pieces[0].reshape(count, heads, HEAD_DIM)
        outgrad_piece = pieces[1].reshape(count, heads, HEAD_DIM)
        query_index = start + jnp.arange(count, dtype=jnp.int32)

        def key_compute(state):
            grad_k, grad_v = state
            logsum_piece = lax.dynamic_slice_in_dim(all_logsum, start, count, 0).T
            delta_piece = lax.dynamic_slice_in_dim(all_delta, start, count, 0).T
            query_doc, unused = doc_layout(doc_lengths, query_index)
            allowed = allowed_mask(query_index, query_doc, my_index, my_doc)[None]
            score = (
                jnp.einsum(
                    "qhd,khd->hqk", query_piece, keys_local, preferred_element_type=jnp.float32
                )
                * scale
            )
            prob = jnp.where(allowed, jnp.exp(score - logsum_piece[:, :, None]), 0.0)
            grad_v = grad_v + jnp.einsum(
                "hqk,qhd->khd",
                prob.astype(jnp.bfloat16),
                outgrad_piece,
                preferred_element_type=jnp.float32,
            )
            prob_grad = jnp.einsum(
                "qhd,khd->hqk", outgrad_piece, mixed_local, preferred_element_type=jnp.float32
            )
            score_grad = (prob * (prob_grad - delta_piece[:, :, None])).astype(jnp.bfloat16)
            grad_k = (
                grad_k
                + jnp.einsum(
                    "hqk,qhd->khd", score_grad, query_piece, preferred_element_type=jnp.float32
                )
                * scale
            )
            return (grad_k, grad_v)

        return lax.cond(query_index[-1] >= my_start, key_compute, lambda kept: kept, state)

    grad_k, grad_v = by_blocks(
        key_grad_step,
        (zeros3, zeros3),
        (
            lax.all_gather(queries.reshape(rows, width), "blk", axis=0, tiled=True),
            lax.all_gather(attended_grad, "blk", axis=0, tiled=True),
        ),
        jnp.int32(0),
    )
    queries_grad = grad_q.astype(jnp.bfloat16)
    keys_grad = grad_k.astype(jnp.bfloat16)
    mixed_grad = grad_v.astype(jnp.bfloat16).reshape(rows, width)
    q_pre_grad = (
        rotate(queries_grad.astype(jnp.float32), cosine, -sine)
        .astype(jnp.bfloat16)
        .reshape(rows, width)
    )
    k_pre_grad = (
        rotate(keys_grad.astype(jnp.float32), cosine, -sine)
        .astype(jnp.bfloat16)
        .reshape(rows, width)
    )
    grad_first = MIX * mixed_grad.astype(jnp.float32)
    value_grad = grad_first.astype(jnp.bfloat16)
    grad_query = outer(normed, q_pre_grad)
    grad_key = outer(normed, k_pre_grad)
    grad_value = outer(normed, value_grad)
    normed_grad = (
        back(q_pre_grad, query_weight)
        + back(k_pre_grad, key_weight)
        + back(value_grad, value_weight)
    )
    grad_attn_gain = jnp.sum(normed_grad * source * inv_first, axis=0)
    scaled_one = normed_grad * attn_gain
    grad_tokens = (
        mid_grad
        + inv_first * scaled_one
        - source * inv_first**3 * jnp.mean(scaled_one * source, axis=-1, keepdims=True)
    )
    summed = (
        lax.psum_scatter(grad_attn_gain, "blk", scatter_dimension=0, tiled=True),
        lax.psum_scatter(grad_query, "blk", scatter_dimension=0, tiled=True),
        lax.psum_scatter(grad_key, "blk", scatter_dimension=0, tiled=True),
        lax.psum_scatter(grad_value, "blk", scatter_dimension=0, tiled=True),
        lax.psum_scatter(grad_out_weight, "blk", scatter_dimension=0, tiled=True),
        lax.psum_scatter(grad_ffn_gain, "blk", scatter_dimension=0, tiled=True),
        lax.psum_scatter(grad_gate, "blk", scatter_dimension=0, tiled=True),
        lax.psum_scatter(grad_up, "blk", scatter_dimension=0, tiled=True),
        lax.psum_scatter(grad_down, "blk", scatter_dimension=0, tiled=True),
    )
    summed = (
        lax.psum(summed[0].astype(jnp.bfloat16), "seq").astype(jnp.float32),
        lax.psum(summed[1].astype(jnp.bfloat16), "seq").astype(jnp.float32),
        lax.psum(summed[2].astype(jnp.bfloat16), "seq").astype(jnp.float32),
        lax.psum(summed[3].astype(jnp.bfloat16), "seq").astype(jnp.float32),
        lax.psum(summed[4].astype(jnp.bfloat16), "seq").astype(jnp.float32),
        lax.psum(summed[5].astype(jnp.bfloat16), "seq").astype(jnp.float32),
        lax.psum(summed[6].astype(jnp.bfloat16), "seq").astype(jnp.float32),
        lax.psum(summed[7].astype(jnp.bfloat16), "seq").astype(jnp.float32),
        lax.psum(summed[8].astype(jnp.bfloat16), "seq").astype(jnp.float32),
    )
    return (
        layer_output,
        grad_tokens,
        grad_first,
        summed[0],
        summed[1],
        summed[2],
        summed[3],
        summed[4],
        summed[5],
        summed[6],
        summed[7],
        summed[8],
    )


def solution(mesh):
    n_seq, n_blk = mesh.shape["seq"], mesh.shape["blk"]

    def chosen(*args):
        rows, width = args[0].shape
        if fits(n_seq, n_blk, rows, width, args[9].shape[1]):
            return local_fast(n_seq, n_blk, *args)
        return local(*args)

    return jax.shard_map(
        chosen,
        mesh=mesh,
        in_specs=(
            P(("seq", "blk"), None),
            P(("seq", "blk"), None),
            P("seq", None),
            P(),
            P(),
            P(),
            P(),
            P(),
            P(),
            P(),
            P(),
            P(),
            P(("seq", "blk"), None),
        ),
        out_specs=(
            P(("seq", "blk"), None),
            P(("seq", "blk"), None),
            P(("seq", "blk"), None),
            P("blk"),
            P("blk", None),
            P("blk", None),
            P("blk", None),
            P("blk", None),
            P("blk"),
            P("blk", None),
            P("blk", None),
            P("blk", None),
        ),
        check_vma=False,
    )
```

```python
import functools
import math
import types

import jax
import jax.numpy as jnp
import numpy as np
from jax import lax
from jax.experimental import pallas as pl
from jax.experimental.pallas import tpu as pltpu
from jax.sharding import PartitionSpec as P

HEAD_DIM = 64


EPS = 1e-05
THETA = 10000.0
MIX = 0.5
NEG = -1e30


def doc_layout(lengths, index):
    ends = jnp.cumsum(lengths, axis=-1)
    past = (index[:, None] >= ends).astype(jnp.int32)
    return (jnp.sum(past, axis=1), index - jnp.sum(past * lengths, axis=1))


def tables(position):
    half = HEAD_DIM // 2
    freq = THETA ** (-(jnp.arange(half).astype(jnp.float32) * 2.0 / HEAD_DIM))
    angle = position.astype(jnp.float32)[:, None] * freq[None, :]
    return (jnp.cos(angle)[:, None, :], jnp.sin(angle)[:, None, :])


def rotate(values, cosine, sine):
    half = values.shape[-1] // 2
    first = values[..., :half]
    second = values[..., half:]
    return jnp.concatenate(
        [first * cosine - second * sine, second * cosine + first * sine], axis=-1
    )


def by_blocks(step, carry, pieces, start):
    rows = pieces[0].shape[0]
    size = math.gcd(rows, 1024)
    count = rows // size
    if count == 1:
        return step(carry, pieces, start)
    stacked = tuple((piece.reshape((count, size) + piece.shape[1:]) for piece in pieces))
    offsets = jnp.arange(count, dtype=jnp.int32) * size

    def turn(state, inputs):
        return (step(state, inputs[1], start + inputs[0]), None)

    result, unused = lax.scan(turn, carry, (offsets, stacked))
    return result


def outer(left, right):
    return lax.dot_general(
        left, right, (((0,), (0,)), ((), ())), preferred_element_type=jnp.float32
    )


def back(left, weight):
    return lax.dot_general(
        left, weight, (((1,), (1,)), ((), ())), preferred_element_type=jnp.float32
    )


TILE = 256
LANES = 128
GROUP = 16
MESH = pl.DeviceIdType.MESH
F32 = jnp.float32
BF16 = jnp.bfloat16


def remote(src, dst, send, recv, where):
    return pltpu.make_async_remote_copy(
        src_ref=src, dst_ref=dst, send_sem=send, recv_sem=recv, device_id=where, device_id_type=MESH
    )


def span(start, size, unit):
    return pl.ds(pl.multiple_of(start, unit), size)


def times(left, right):
    return jnp.dot(left, right, preferred_element_type=F32)


def iota(shape, dim):
    return lax.broadcasted_iota(jnp.int32, shape, dim)


def loop(low, high, body):
    def turn(index, unused):
        body(index)
        return unused

    lax.fori_loop(low, high, turn, 0)


class Trade:
    def __init__(self, blk, n_blk, phase, send, recv, source, place):
        self.blk, self.n_blk = blk, n_blk
        self.send, self.recv = send.at[phase], recv.at[phase]
        self.source, self.place = source, place

    def start(self, peer):
        src, dst = self.source(peer), self.place(self.blk)

        @pl.when(peer != self.blk)
        def _():
            remote(src, dst, self.send.at[peer], self.recv.at[self.blk], {"blk": peer}).start()

        @pl.when(peer == self.blk)
        def _():
            pltpu.make_async_copy(src, dst, self.recv.at[self.blk]).start()

    def arrived(self, peer):
        src, dst = self.source(peer), self.place(peer)

        @pl.when(peer != self.blk)
        def _():
            remote(src, dst, self.send.at[peer], self.recv.at[peer], {"blk": peer}).wait_recv()

        @pl.when(peer == self.blk)
        def _():
            pltpu.make_async_copy(src, dst, self.recv.at[peer]).wait()

    def all_arrived(self):
        loop(0, self.n_blk, self.arrived)

    def all_left(self):
        def left(peer):
            @pl.when(peer != self.blk)
            def _():
                remote(
                    self.source(peer), self.place(self.blk), self.send.at[peer], self.recv.at[self.blk], {"blk": peer}
                ).wait_send()

        loop(0, self.n_blk, left)


class Gift:
    def __init__(self, seq, n_seq, rows, owner, kind, src, dst, send, recv):
        self.seq, self.n_seq, self.rows, self.owner, self.kind = seq, n_seq, rows, owner, kind
        self.src, self.dst, self.send, self.recv = src, dst, send, recv

    def copy(self, other, send):
        dst = self.dst.at[span(other * self.rows, self.rows, self.rows)]
        return remote(self.src, dst, self.send.at[self.kind, send], self.recv.at[self.kind, other], {"seq": send})

    def own(self):
        dst = self.dst.at[pl.ds(self.owner * self.rows, self.rows)]
        return pltpu.make_async_copy(self.src, dst, self.recv.at[self.kind, self.owner])

    def start(self):
        @pl.when(self.seq != self.owner)
        def _():
            self.copy(self.seq, self.owner).start()

        @pl.when(self.seq == self.owner)
        def _():
            self.own().start()

    def arrived(self):
        for other in range(self.n_seq):
            if other == self.owner:
                self.own().wait()
            else:
                self.copy(other, other).wait_recv()

    def left(self):
        @pl.when(self.seq != self.owner)
        def _():
            self.copy(self.seq, self.owner).wait_send()


class Sum:
    def __init__(self, blk, size, part, cgot, rgot, zgot, total, sems):
        self.blk, self.size = blk, size
        self.core, self.chip = lax.rem(blk, 2), lax.div(blk, 2)
        side = lax.div(self.chip, 2)
        self.far = 2 * (1 - side)
        self.partner = self.chip + 1 - 2 * lax.rem(self.chip, 2)
        self.inner = lax.rem(self.chip, 2) != side
        self.far_inner = 2 - side
        self.part, self.cgot, self.rgot, self.zgot, self.total = part, cgot, rgot, zgot, total
        self.csend, self.crecv, self.rsend, self.rrecv, self.zsend, self.zrecv = sems

    def order(self, step):
        return jnp.where(step < 2, self.far + step, jnp.where(step == 2, self.partner, self.chip))

    def chunk(self, index):
        return self.part.at[span(index * self.size, self.size, 32)]

    def mine(self, chip):
        return self.chunk(2 * chip + self.core)

    def swap(self, chip):
        return remote(
            self.chunk(2 * chip + 1 - self.core),
            self.cgot(chip),
            self.csend.at[chip],
            self.crecv.at[chip],
            {"blk": 2 * self.chip + 1 - self.core},
        )

    def lend(self, index):
        return remote(
            self.mine(self.far + index),
            self.rgot(index),
            self.rsend.at[index],
            self.rrecv.at[index],
            {"blk": 2 * self.partner + self.core},
        )

    def send_far(self, index):
        return remote(
            self.mine(self.far + index),
            self.zgot(1),
            self.zsend.at[index],
            self.zrecv.at[1],
            {"blk": 2 * (self.far + index) + self.core},
        )

    def send_near(self):
        return remote(
            self.mine(self.partner),
            self.zgot(0),
            self.zsend.at[2],
            self.zrecv.at[0],
            {"blk": 2 * self.partner + self.core},
        )

    def add(self, mine, other):
        def group(index):
            at = span(index * 32, 32, 32)
            mine[at, :] = (mine[at, :].astype(F32) + other[at, :].astype(F32)).astype(BF16)

        loop(0, self.size // 32, group)

    def begin(self):
        for index in range(2):
            chip = self.far + index
            self.swap(chip).wait()
            self.add(self.mine(chip), self.cgot(chip))

            @pl.when(jnp.logical_not(self.inner))
            def _(index=index):
                self.lend(index).start()

        self.swap(self.partner).wait()
        self.add(self.mine(self.partner), self.cgot(self.partner))
        self.send_near().start()
        self.swap(self.chip).wait()

    def relay(self):
        @pl.when(self.inner)
        def _():
            for index in range(2):
                self.lend(index).wait_recv()
                self.add(self.mine(self.far + index), self.rgot(index))
                self.send_far(index).start()

    def end(self):
        self.send_near().wait_recv()
        self.send_far(0).wait_recv()
        mine, other = self.mine(self.chip), self.cgot(self.chip)

        def group(index):
            at = span(index * 32, 32, 32)
            value = mine[at, :].astype(F32) + other[at, :].astype(F32)
            value = value + self.zgot(0)[at, :].astype(F32) + self.zgot(1)[at, :].astype(F32)
            self.total[at, :] = value.astype(BF16)

        loop(0, self.size // 32, group)

    def left(self):
        self.send_near().wait_send()

        @pl.when(self.inner)
        def _():
            for index in range(2):
                self.send_far(index).wait_send()

        @pl.when(jnp.logical_not(self.inner))
        def _():
            for index in range(2):
                self.lend(index).wait_send()


class TileGift:
    def __init__(self, seq, n_seq, rows, src, dst, send, recv, owner_of):
        self.seq, self.n_seq, self.rows, self.src, self.dst = seq, n_seq, rows, src, dst
        self.send, self.recv, self.owner_of = send, recv, owner_of

    def place(self, other, slot):
        return self.dst.at[span(other * self.rows, self.rows, self.rows), span(slot * TILE, TILE, TILE)]

    def tile(self, index):
        return self.src.at[:, span(index * TILE, TILE, TILE)]

    def start(self, index):
        owner, slot = self.owner_of(index)
        src, dst, recv = self.tile(index), self.place(self.seq, slot), self.recv.at[slot, self.seq]

        @pl.when(owner != self.seq)
        def _():
            remote(src, dst, self.send.at[index], recv, {"seq": owner}).start()

        @pl.when(owner == self.seq)
        def _():
            pltpu.make_async_copy(src, dst, recv).start()

    def arrived(self, low, high):
        def one(slot):
            def other_one(other):
                dst, recv = self.place(other, slot), self.recv.at[slot, other]

                @pl.when(other != self.seq)
                def _():
                    remote(self.tile(0), dst, self.send.at[0], recv, {"seq": other}).wait_recv()

                @pl.when(other == self.seq)
                def _():
                    pltpu.make_async_copy(self.tile(0), dst, recv).wait()

            loop(0, self.n_seq, other_one)

        loop(low, high, one)

    def left(self, count):
        def one(index):
            owner, slot = self.owner_of(index)

            @pl.when(owner != self.seq)
            def _():
                remote(
                    self.tile(index), self.place(self.seq, slot), self.send.at[index], self.recv.at[slot, self.seq],
                    {"seq": owner},
                ).wait_send()

        loop(0, count, one)


class Spread:
    def __init__(self, seq, n_seq, owner, kind, src, dst, send, recv, local):
        self.seq, self.n_seq, self.owner, self.kind, self.src, self.dst = seq, n_seq, owner, kind, src, dst
        self.send, self.recv, self.local = send, recv, local

    def copy(self, other):
        return remote(self.src, self.dst, self.send.at[self.kind, other], self.recv.at[self.kind], {"seq": other})

    def own(self):
        return pltpu.make_async_copy(self.src, self.dst, self.local.at[self.kind])

    def start(self):
        @pl.when(self.seq == self.owner)
        def _():
            for other in range(self.n_seq):
                if other != self.owner:
                    self.copy(other).start()
            self.own().start()

    def finish(self):
        @pl.when(self.seq == self.owner)
        def _():
            for other in range(self.n_seq):
                if other != self.owner:
                    self.copy(other).wait_send()
            self.own().wait()

        @pl.when(self.seq != self.owner)
        def _():
            self.copy(self.owner).wait_recv()


def turn_over(src, dst):
    def one(index):
        at = span(index * TILE, TILE, TILE)
        dst[at, :] = src[:, at].T

    loop(0, src.shape[1] // TILE, one)


def outer_tiles(turned, rhs, part, chip, tiles, rhs_at, part_at):
    rows = span(chip * TILE, TILE, TILE)

    def tile(index):
        value = times(turned[rows, :], rhs[:, span(rhs_at + index * TILE, TILE, TILE)])
        part[rows, span(part_at + index * TILE, TILE, TILE)] = value.astype(BF16)

    loop(0, tiles, tile)


def layer_kernel(
    sizes,
    freq, tokens, first, lengths, attn_gain, ffn_gain, cot,
    h_query, h_key, h_value, h_out, h_gate, h_up, h_down,
    o_layer, o_tokens, o_first, o_gu, o_down, o_out, o_query, o_key, o_value, o_gain,
    v, sem,
):
    rows, width, ff, n_seq, n_blk, split = sizes
    v, sem = types.SimpleNamespace(**v), types.SimpleNamespace(**sem)
    docs = lengths.shape[1]
    chips = n_blk // 2
    scale = HEAD_DIM ** (-0.5)
    seq, blk = lax.axis_index("seq"), lax.axis_index("blk")
    chip_at = lax.div(blk, 2)

    def turned_chip(step):
        return lax.rem(chip_at + step, chips)

    barrier = pltpu.get_barrier_semaphore()
    for step in range(1, n_seq):
        pl.semaphore_signal(barrier, inc=1, device_id={"seq": lax.rem(seq + step, n_seq)}, device_id_type=MESH)
    for step in range(1, n_blk):
        pl.semaphore_signal(barrier, inc=1, device_id={"blk": lax.rem(blk + step, n_blk)}, device_id_type=MESH)

    def load(index, src, dst):
        copy = pltpu.make_async_copy(src, dst, sem.load.at[index])
        copy.start()
        return copy

    load_query = load(0, h_query, v.w_query)
    load_key = load(1, h_key, v.w_key)
    load_value = load(2, h_value, v.w_value)
    load_out = load(3, h_out, v.w_out)
    load_gate = load(4, h_gate, v.w_gate)
    load_up = load(5, h_up, v.w_up)
    load_down = load(6, h_down, v.w_down)

    def norm(group):
        at = span(group * GROUP, GROUP, GROUP)
        x = tokens[at, :].astype(F32)
        inv = lax.rsqrt(jnp.mean(x * x, axis=-1, keepdims=True) + EPS)
        v.normed[at, :] = (x * inv * attn_gain[...]).astype(BF16)
        v.inv_first[at, :] = jnp.broadcast_to(inv, (GROUP, LANES))

    loop(0, rows // GROUP, norm)

    def doc_start(index):
        start, end = jnp.zeros_like(index), jnp.int32(0)
        for doc in range(docs):
            end = end + lengths[0, doc]
            start = jnp.where(index >= end, end, start)
        return start

    half = HEAD_DIM // 2

    def low_half(count):
        return lax.rem(iota((count, LANES), 1), HEAD_DIM) < half

    def set_tables(start, count, cosine_ref, sine_ref):
        index = start + iota((count, LANES), 0)
        angle = (index - doc_start(index)).astype(F32) * freq[...]
        cosine_ref[...] = jnp.cos(angle)
        sine = jnp.sin(angle)
        sine_ref[...] = jnp.where(low_half(count), -sine, sine)

    def halves_changed(u):
        return jnp.where(low_half(u.shape[0]), pltpu.roll(u, LANES - half, 1), pltpu.roll(u, half, 1))

    set_tables(blk * rows, rows, v.cos, v.sin)

    def rotated(u):
        return u * v.cos[...] + halves_changed(u) * v.sin[...]

    cuts = [0]
    for tiles in split:
        cuts.append(cuts[-1] + tiles * TILE)
    wide = max(split) * TILE

    def gift(owner, kind, src, dst):
        return Gift(seq, n_seq, rows, owner, kind, src, dst, sem.xsend, sem.xrecv)

    gift_cot = gift(3, 0, cot, v.buf_a)
    gifts_two = [gift(owner, 0, v.two, v.buf_a) for owner in range(3)]
    each, hidden = split[0], ff // TILE
    gift_gu = TileGift(
        seq, n_seq, rows, v.gate_up, v.buf_b, sem.gusend, sem.gurecv,
        lambda index: (lax.div(index, each), lax.rem(index, each)),
    )
    gift_act = TileGift(seq, n_seq, rows, v.act, v.buf_b, sem.actsend, sem.actrecv, lambda index: (3, index))
    gift_att = gift(2, 2, v.att, v.buf_att)
    gift_mid = gift(2, 3, v.mid_b, v.buf_mid)
    def trade(phase, source, place):
        return Trade(blk, n_blk, phase, sem.asend, sem.arecv, source, place)

    def block_rows(ref):
        return lambda peer: ref.at[span(peer * rows, rows, rows)]

    def block_columns(ref):
        return lambda peer: ref.at[:, span(peer * LANES, LANES, LANES)]

    give_qkv = trade(0, lambda peer: v.pack.at[peer], lambda peer: v.qkv.at[:, span(peer * rows, rows, rows)])
    give_att = trade(1, block_rows(v.ob), block_columns(v.att))
    give_out = trade(2, lambda peer: v.out_pack.at[peer], block_rows(v.out_grad))
    give_grads = trade(
        3, lambda peer: v.pack.at[peer], lambda peer: v.grads.at[:, :, span(peer * LANES, LANES, LANES)]
    )

    give_tail = trade(4, lambda peer: v.tail_sum.at[peer], lambda peer: v.tail_got.at[peer])
    core = lax.rem(blk, 2)
    mate = blk + 1 - 2 * core

    def block_of(step):
        return 2 * turned_chip(step) + core

    def rows_of(block):
        return v.normed_all.at[span(block * rows, rows, rows)]

    def normed_out(step):
        return remote(
            v.normed, rows_of(blk), sem.nsend.at[step - 1], sem.nrecv.at[step - 1], {"blk": block_of(step)}
        )

    def normed_over(step):
        there = rows_of(block_of(step))
        return remote(there, there, sem.fsend.at[step], sem.frecv.at[step], {"blk": mate})

    def mates_normed(step):
        there = rows_of(2 * turned_chip(step) + 1 - core)
        return remote(there, there, sem.fsend.at[step], sem.frecv.at[step], {"blk": mate})

    pl.semaphore_wait(barrier, n_seq + n_blk - 2)
    gift_cot.start()
    own_normed = pltpu.make_async_copy(v.normed, rows_of(blk), sem.nlocal.at[0])
    own_normed.start()

    for item in (load_query, load_key, load_value):
        item.wait()

    def project(step):
        chip = turned_chip(step)
        at = span(chip * TILE, TILE, TILE)
        left = v.normed[...]
        q, k, val = times(left, v.w_query[:, at]), times(left, v.w_key[:, at]), times(left, v.w_value[:, at])
        old = first[:, at].astype(F32)
        for core in range(2):
            peer = 2 * chip + core
            cols = slice(core * LANES, (core + 1) * LANES)
            v.pack[peer, 0] = (rotated(q[:, cols]) * scale).astype(BF16)
            v.pack[peer, 1] = rotated(k[:, cols]).astype(BF16)
            v.pack[peer, 2] = (MIX * val[:, cols] + MIX * old[:, cols]).astype(BF16)
            give_qkv.start(peer)

    loop(1, chips + 1, project)

    first_head = iota((TILE, LANES), 1) < HEAD_DIM

    def stacked(values):
        return jnp.concatenate([jnp.where(first_head, values, 0.0), jnp.where(first_head, 0.0, values)], axis=0)

    def unstacked(values):
        return jnp.where(first_head, values[:TILE], values[TILE:])

    def attend(block):
        for core in range(2):
            give_qkv.arrived(2 * block + core)
        at, both = span(block * TILE, TILE, TILE), span(block * 2 * TILE, 2 * TILE, 2 * TILE)
        v.q2[both, :] = stacked(v.qkv[0, at, :].astype(F32)).astype(BF16)
        index = block * TILE + lax.rem(iota((2 * TILE, 1), 0), TILE)
        start = doc_start(index)
        v.top[...] = jnp.full((2 * TILE, LANES), NEG, F32)

        def scores(tile):
            cols = span(tile * TILE, TILE, TILE)
            score = back(v.q2[both, :], v.qkv[1, cols, :])
            key = tile * TILE + iota((2 * TILE, TILE), 1)
            score = jnp.where((key <= index) & (key >= start), score, NEG)
            v.score[:, cols] = score
            v.top[...] = jnp.maximum(v.top[...], jnp.maximum(score[:, :LANES], score[:, LANES:]))

        loop(0, block + 1, scores)
        top = jnp.max(v.top[...], axis=1, keepdims=True)
        v.top[...] = jnp.zeros((2 * TILE, LANES), F32)
        v.o2[...] = jnp.zeros((2 * TILE, LANES), F32)

        def weights(tile):
            cols = span(tile * TILE, TILE, TILE)
            weight = jnp.exp(v.score[:, cols] - top)
            v.top[...] += weight[:, :LANES] + weight[:, LANES:]
            weight = weight.astype(BF16)
            v.prob[both, cols] = weight
            v.o2[...] += times(weight, v.qkv[2, cols, :])

        loop(0, block + 1, weights)
        inv = 1.0 / jnp.sum(v.top[...], axis=1, keepdims=True)
        v.row[both, :] = jnp.broadcast_to(inv, (2 * TILE, LANES))
        attended = unstacked(v.o2[...] * inv)
        v.o32[at, :] = attended
        v.ob[at, :] = attended.astype(BF16)
        for core in range(2):
            give_att.start(2 * block + core)

    loop(0, chips, attend)
    loop(
        0,
        chips,
        lambda block: set_tables(
            block * TILE,
            TILE,
            v.score.at[:TILE, span(block * TILE, LANES, LANES)],
            v.score.at[:TILE, span(block * TILE + LANES, LANES, LANES)],
        ),
    )
    give_att.all_arrived()
    gift_att.start()
    for step in range(1, chips):
        normed_out(step).start()

    load_out.wait()

    def middle(tile):
        cols = span(tile * TILE, TILE, TILE)
        value = tokens[:, cols].astype(F32) + times(v.att[...], v.w_out[:, cols])
        v.mid[:, cols] = value
        o_layer[:, cols] = value

    loop(0, width // TILE, middle)

    def norm_two(group):
        at = span(group * GROUP, GROUP, GROUP)
        x = v.mid[at, :]
        inv = lax.rsqrt(jnp.mean(x * x, axis=-1, keepdims=True) + EPS)
        v.two[at, :] = (x * inv * ffn_gain[...]).astype(BF16)
        v.inv_second[at, :] = jnp.broadcast_to(inv, (GROUP, LANES))

    loop(0, rows // GROUP, norm_two)
    for item in gifts_two:
        item.start()

    for item in (load_gate, load_up, load_down):
        item.wait()
    v.two_grad[...] = jnp.zeros((rows, width), F32)

    def feed(step):
        tile = lax.rem(split[0] + step, hidden)
        cols = span(tile * TILE, TILE, TILE)
        gate = times(v.two[...], v.w_gate[:, cols])
        up = times(v.two[...], v.w_up[:, cols])
        act_grad = back(cot[...], v.w_down[cols, :])
        sigma = jax.nn.sigmoid(gate)
        silu = gate * sigma
        act = (silu * up).astype(BF16)
        gate_grad = (act_grad * up * sigma * (1.0 + gate * (1.0 - sigma))).astype(BF16)
        up_grad = (act_grad * silu).astype(BF16)
        v.act[:, cols] = act
        v.gate_up[:, cols] = gate_grad
        v.gate_up[:, span(ff + tile * TILE, TILE, TILE)] = up_grad
        gift_gu.start(tile)
        gift_gu.start(hidden + tile)
        gift_act.start(tile)
        o_layer[...] += times(act, v.w_down[cols, :])
        v.two_grad[...] += back(gate_grad, v.w_gate[:, cols]) + back(up_grad, v.w_up[:, cols])

    loop(0, hidden, feed)
    for step in range(1, n_blk):
        pl.semaphore_signal(sem.ready, inc=1, device_id={"blk": lax.rem(blk + step, n_blk)}, device_id_type=MESH)
    v.gain_rows[...] = jnp.zeros((16, width), F32)

    def norm_two_back(group):
        at = span(group * GROUP, GROUP, GROUP)
        x, grad, inv = v.mid[at, :], v.two_grad[at, :], v.inv_second[at, :1]
        term = grad * x * inv
        v.gain_rows[8:16, :] += term[:8] + term[8:]
        scaled = grad * ffn_gain[...]
        mean = jnp.mean(scaled * x, axis=-1, keepdims=True)
        value = cot[at, :].astype(F32) + inv * scaled - x * (inv * inv * inv * mean)
        v.mid_grad[at, :] = value
        v.mid_b[at, :] = value.astype(BF16)

    loop(0, rows // GROUP, norm_two_back)
    gift_mid.start()

    def out_back(step):
        chip = turned_chip(step)
        value = back(v.mid_b[...], v.w_out[span(chip * TILE, TILE, TILE), :]).astype(BF16)
        for core in range(2):
            v.out_pack[2 * chip + core] = value[:, core * LANES : (core + 1) * LANES]
            give_out.start(2 * chip + core)

    loop(1, chips + 1, out_back)
    own_normed.wait()
    normed_over(0).start()
    for step in range(1, chips):
        normed_out(chips - step).wait_recv()
        normed_over(step).start()

    pl.semaphore_wait(sem.ready, n_blk - 1)
    chunk, down = width // n_blk, ff // n_blk

    def sems_of(index):
        return tuple(
            item.at[index] for item in (sem.csend, sem.crecv, sem.rsend, sem.rrecv, sem.zsend, sem.zrecv)
        )

    def stack_in(ref, top, cols):
        return lambda index: ref.at[span(top + index * chunk, chunk, 32), cols]

    def square_in(ref, more, low):
        def place(index):
            index = index + more
            return ref.at[
                span(lax.rem(index, 2) * down, down, 32), span(lax.div(index, 2) * width + low, TILE, TILE)
            ]

        return place

    def piece(index, low, high):
        cols = slice(low, high)
        return Sum(
            blk, chunk, v.w_gate.at[:, cols], stack_in(v.w_up, 0, cols), stack_in(v.w_up, chips * chunk, cols),
            stack_in(v.w_up, (chips + 2) * chunk, cols), v.total.at[:, cols], sems_of(index),
        )

    third = -(-each // 3)
    edges = [0, third, 2 * third, each]
    thirds = [piece(index, edges[index] * TILE, edges[index + 1] * TILE) for index in range(3)]
    last = split[2] * TILE
    halves = [piece(0, 0, last), piece(1, last, last + width)]
    quarters = [
        Sum(
            blk, down, v.w_down.at[:, low : low + TILE], square_in(v.w_up, 0, low), square_in(v.w_gate, 0, low),
            square_in(v.w_gate, 2, low), v.total_down.at[:, low : low + TILE], sems_of(low // TILE),
        )
        for low in range(0, width, TILE)
    ]

    first_two, third_one, fourth = seq < 2, seq == 2, seq == 3

    def spread(owner, kind, src, dst):
        return Spread(seq, n_seq, owner, kind, src, dst, sem.gsend, sem.grecv, sem.glocal)

    spreads = [
        [
            spread(
                owner,
                3 * owner + index,
                v.total.at[:, edges[index] * TILE : edges[index + 1] * TILE],
                o_gu.at[:, cuts[owner] + edges[index] * TILE : cuts[owner] + edges[index + 1] * TILE],
            )
            for index in range(3)
        ]
        for owner in range(2)
    ] + [
        [
            spread(2, 6, v.total.at[:, :last], o_gu.at[:, cuts[2] : cuts[3]]),
            spread(2, 7, v.total.at[:, last : last + width], o_out),
        ],
        [
            spread(3, 8 + index, v.total_down.at[:, low : low + TILE], o_down.at[:, low : low + TILE])
            for index, low in enumerate(range(0, width, TILE))
        ],
    ]
    def products(item, turned, rhs, tiles, rhs_at, part_at):
        def one(step):
            chip = item.order(step)
            outer_tiles(turned, rhs, v.w_gate, chip, tiles, rhs_at, part_at)
            item.swap(chip).start()

        loop(0, chips, one)
        item.begin()

    def gate_up_piece(index):
        gift_gu.arrived(edges[index], edges[index + 1])
        at = edges[index] * TILE
        products(thirds[index], v.turned, v.buf_b, edges[index + 1] - edges[index], at, at)

    def down_products():
        def one(step):
            index = lax.rem(split[0] + step, hidden)
            gift_act.arrived(index, index + 1)
            at = span(index * TILE, TILE, TILE)
            v.turned[:TILE, :] = v.buf_b[:, at].T
            v.w_down[at, :] = times(v.turned[:TILE, :], v.buf_a[...]).astype(BF16)

        loop(0, hidden, one)
        for item in quarters:
            loop(0, chips, lambda step, item=item: item.swap(item.order(step)).start())
        for item in quarters:
            item.begin()

    for owner in range(n_seq):

        @pl.when(seq == owner)
        def _(owner=owner):
            (gifts_two + [gift_cot])[owner].arrived()

    @pl.when(first_two)
    def _():
        turn_over(v.buf_a, v.turned)
        gate_up_piece(0)

    give_out.all_arrived()

    def prepare(block):
        at, both = span(block * TILE, TILE, TILE), span(block * 2 * TILE, 2 * TILE, 2 * TILE)
        grad = (stacked(v.out_grad[at, :].astype(F32)) * v.row[both, :]).astype(BF16)
        v.do2[both, :] = grad
        attended = v.o32[at, :]
        delta = jnp.sum(grad.astype(F32) * jnp.concatenate([attended, attended], axis=0), axis=1, keepdims=True)
        v.row[both, :] = jnp.broadcast_to(delta, (2 * TILE, LANES))
        v.dq[both, :] = jnp.zeros((2 * TILE, LANES), F32)

    loop(0, chips, prepare)
    give_qkv.all_left()

    def key_block(block):
        at = span(block * TILE, TILE, TILE)
        v.dk[...] = jnp.zeros((TILE, LANES), F32)
        v.dv[...] = jnp.zeros((TILE, LANES), F32)

        def query_block(other):
            both = span(other * 2 * TILE, 2 * TILE, 2 * TILE)
            prob = v.prob[both, at]
            grad = back(v.do2[both, :], v.qkv[2, at, :])
            score_grad = (prob.astype(F32) * (grad - v.row[both, :1])).astype(BF16)
            v.dk[...] += outer(score_grad, v.q2[both, :])
            v.dv[...] += outer(prob, v.do2[both, :])
            v.dq[both, :] += times(score_grad, v.qkv[1, at, :])

        loop(block, chips, query_block)
        cosine = v.score[:TILE, span(block * TILE, LANES, LANES)]
        sine = v.score[:TILE, span(block * TILE + LANES, LANES, LANES)]

        def rotated_back(u):
            u = u.astype(BF16).astype(F32)
            return (u * cosine - halves_changed(u) * sine).astype(BF16)

        dq = rotated_back(unstacked(v.dq[span(block * 2 * TILE, 2 * TILE, 2 * TILE), :]) * scale)
        dk = rotated_back(v.dk[...])
        dv = (MIX * v.dv[...].astype(BF16).astype(F32)).astype(BF16)
        for index, value in enumerate((dq, dk, dv)):
            v.heads_grad[at, index * LANES : (index + 1) * LANES] = value
            for half_at in range(2):
                v.pack[2 * block + half_at, index] = value[half_at * rows : (half_at + 1) * rows]
        for half_at in range(2):
            give_grads.start(2 * block + half_at)

    loop(0, chips, key_block)

    for step in range(chips):
        mates_normed(step).wait_recv()

    def project_back(index):
        value = outer(v.normed_all[:, span(index * TILE, TILE, TILE)], v.heads_grad[...]).astype(BF16)
        v.tail_part[2 * index] = value[:LANES]
        v.tail_part[2 * index + 1] = value[LANES:]

    loop(0, width // TILE, project_back)
    quarter = LANES // n_seq

    def tail_share(step):
        other = lax.rem(seq + step, n_seq)
        return remote(
            v.tail_part.at[:, span(other * quarter, quarter, quarter)],
            v.tail_shares.at[step - 1],
            sem.qsend.at[step - 1],
            sem.qrecv.at[step - 1],
            {"seq": other},
        )

    for step in range(1, n_seq):
        tail_share(step).start()

    def when(which, *steps):
        @pl.when(which)
        def _():
            for step in steps:
                step()

    def ended(item, goes):
        def step():
            item.end()
            for other in goes:
                other.start()

        return step

    def third_products():
        turn_over(v.buf_a, v.turned)
        gift_gu.arrived(0, split[2])
        products(halves[0], v.turned, v.buf_b, split[2], 0, 0)
        gift_att.arrived()
        gift_mid.arrived()
        turn_over(v.buf_att, v.turned)
        products(halves[1], v.turned, v.buf_mid, width // TILE, 0, last)

    when(first_two, lambda: gate_up_piece(1), thirds[0].relay, lambda: gate_up_piece(2))
    when(third_one, third_products)
    when(fourth, down_products)

    def tail_add(index):
        value = v.tail_part[index, span(seq * quarter, quarter, quarter), :].astype(F32)
        for step in range(1, n_seq):
            value = value + v.tail_shares[step - 1, index].astype(F32)
        v.tail_sum[index] = value.astype(BF16)
        give_tail.start(index)

    for step in range(1, n_seq):
        tail_share(step).wait()
    loop(0, n_blk, tail_add)

    give_grads.all_arrived()

    def gone(index, *owners):
        return [spreads[owner][index] for owner in owners]

    when(first_two, thirds[1].relay, ended(thirds[0], []))
    for item in gone(0, 0, 1):
        item.start()
    when(fourth, quarters[0].relay)

    def normed_back(tile):
        at = span(tile * TILE, TILE, TILE)
        o_tokens[:, at] = (
            back(v.grads[0], v.w_query[at, :])
            + back(v.grads[1], v.w_key[at, :])
            + back(v.grads[2], v.w_value[at, :])
        )

    loop(0, width // TILE, normed_back)
    o_first[...] = v.grads[2].astype(F32)
    when(fourth, ended(quarters[0], gone(0, 3)), quarters[1].relay)

    def norm_back(group):
        at = span(group * GROUP, GROUP, GROUP)
        x, grad, inv = tokens[at, :].astype(F32), o_tokens[at, :], v.inv_first[at, :1]
        term = grad * x * inv
        v.gain_rows[0:8, :] += term[:8] + term[8:]
        scaled = grad * attn_gain[...]
        mean = jnp.mean(scaled * x, axis=-1, keepdims=True)
        o_tokens[at, :] = v.mid_grad[at, :] + inv * scaled - x * (inv * inv * inv * mean)

    loop(0, rows // GROUP, norm_back)

    for peer in range(n_blk):
        v.gains[peer] = v.gain_rows[:, peer * LANES : (peer + 1) * LANES]

    def gain_copy(step):
        other = lax.rem(blk + step, n_blk)
        return remote(
            v.gains.at[other], v.gain_got.at[step - 1], sem.hsend.at[step - 1], sem.hrecv.at[step - 1],
            {"blk": other},
        )

    for step in range(1, n_blk):
        gain_copy(step).start()

    when(
        first_two,
        ended(thirds[1], gone(1, 0, 1)),
        thirds[2].relay,
        ended(thirds[2], gone(2, 0, 1)),
    )
    when(
        third_one,
        halves[0].relay,
        ended(halves[0], gone(0, 2)),
        halves[1].relay,
        ended(halves[1], gone(1, 2)),
    )
    when(
        fourth,
        ended(quarters[1], gone(1, 3)),
        quarters[2].relay,
        ended(quarters[2], gone(2, 3)),
        quarters[3].relay,
        ended(quarters[3], gone(3, 3)),
    )
    give_tail.all_arrived()
    for index in range(3):
        for peer in range(n_blk):
            v.tail_done[index, :, peer * LANES : (peer + 1) * LANES] = v.tail_got[
                peer, :, index * LANES : (index + 1) * LANES
            ]

    def tail_spread(index, step, owner):
        at = span(owner * quarter, quarter, quarter)
        return remote(
            v.tail_done.at[index],
            (o_query, o_key, o_value)[index].at[at],
            sem.tsend.at[index, step - 1],
            sem.trecv.at[index, owner],
            {"seq": lax.rem(seq + step, n_seq)},
        )

    def tail_own(index):
        at = span(seq * quarter, quarter, quarter)
        return pltpu.make_async_copy(
            v.tail_done.at[index], (o_query, o_key, o_value)[index].at[at], sem.trecv.at[index, seq]
        )

    for index in range(3):
        tail_own(index).start()
        for step in range(1, n_seq):
            tail_spread(index, step, seq).start()

    value = v.gains[blk]
    for step in range(1, n_blk):
        gain_copy(step).wait()
        value = value + v.gain_got[step - 1]
    v.gain_sum[seq] = value
    for step in range(1, n_seq):
        other = lax.rem(seq + step, n_seq)
        mine = v.gain_sum.at[seq]
        remote(mine, mine, sem.isend.at[step - 1], sem.irecv.at[seq], {"seq": other}).start()

    for step in range(1, n_seq):
        other = lax.rem(seq + step, n_seq)
        theirs = v.gain_sum.at[other]
        remote(theirs, theirs, sem.isend.at[step - 1], sem.irecv.at[other], {"seq": other}).wait()
    value = v.gain_sum[0]
    for group in range(1, n_seq):
        value = value + v.gain_sum[group]
    o_gain[0:8, :] = jnp.broadcast_to(jnp.sum(value[:8], axis=0, keepdims=True), (8, LANES))
    o_gain[8:16, :] = jnp.broadcast_to(jnp.sum(value[8:], axis=0, keepdims=True), (8, LANES))

    for index in range(3):
        tail_own(index).wait()
        for step in range(1, n_seq):
            tail_spread(index, step, seq).wait_send()
            tail_spread(index, step, lax.rem(seq + step, n_seq)).wait_recv()
    for item in sum(spreads, []):
        item.finish()
    for item in [gift_cot, gift_att, gift_mid] + gifts_two:
        item.left()
    gift_gu.left(2 * hidden)
    gift_act.left(hidden)
    for item in (give_att, give_out, give_grads, give_tail):
        item.all_left()
    for step in range(chips):
        normed_over(step).wait_send()
        if step:
            normed_out(step).wait_send()

    @pl.when(first_two)
    def _():
        for item in thirds:
            item.left()

    @pl.when(third_one)
    def _():
        for item in halves:
            item.left()

    @pl.when(fourth)
    def _():
        for item in quarters:
            item.left()


def finish_kernel(
    layer, tokens, first, gu, down, out, query, key, value, gain,
    o_layer, o_tokens, o_first, o_gain, o_gain_two, o_query, o_key, o_value, o_out, o_gate, o_up, o_down,
    kept, small, large, sem_kept_in, sem_kept_out, sem_in, sem_out,
):
    kept_in = [
        pltpu.make_async_copy(src, kept[index], sem_kept_in.at[index])
        for index, src in enumerate((layer, tokens, first))
    ]
    kept_out = [
        pltpu.make_async_copy(kept[index], dst, sem_kept_out.at[index])
        for index, dst in enumerate((o_layer, o_tokens, o_first))
    ]
    ff = o_gate.shape[1]
    sources = [gu.at[:, :ff], gu.at[:, ff:], down, query, key, value, out]
    targets = [o_gate, o_up, o_down, o_query, o_key, o_value, o_out]
    loads = [pltpu.make_async_copy(src, small[index], sem_in.at[index]) for index, src in enumerate(sources)]
    stores = [pltpu.make_async_copy(large[index], dst, sem_out.at[index]) for index, dst in enumerate(targets)]
    for item in kept_in + loads:
        item.start()
    for coming, going in zip(kept_in, kept_out):
        coming.wait()
        going.start()
    for index in range(len(sources)):
        loads[index].wait()

        def group(step, index=index):
            at = span(step * GROUP, GROUP, GROUP)
            large[index][at, :] = small[index][at, :].astype(F32)

        loop(0, targets[index].shape[0] // GROUP, group)
        stores[index].start()
    o_gain[...] = gain[0:1, :]
    o_gain_two[...] = gain[8:9, :]
    for item in stores + kept_out:
        item.wait()


def finish(layer, tokens, first, gu, down, out, query, key, value, gain):
    hbm, vmem = pl.BlockSpec(memory_space=pl.ANY), pl.BlockSpec(memory_space=pltpu.VMEM)
    shape = jax.ShapeDtypeStruct
    ff = gu.shape[1] // 2
    dims = [(gu.shape[0], ff), (gu.shape[0], ff), down.shape, query.shape, key.shape, value.shape, out.shape]
    dma = pltpu.SemaphoreType.DMA
    results = pl.pallas_call(
        finish_kernel,
        out_shape=tuple(
            shape(each, F32)
            for each in (
                layer.shape, tokens.shape, first.shape, (1, LANES), (1, LANES), dims[3], dims[4], dims[5], dims[6], dims[0], dims[1], dims[2]
            )
        ),
        in_specs=[hbm] * 9 + [vmem],
        out_specs=(hbm,) * 3 + (vmem,) * 2 + (hbm,) * 7,
        scratch_shapes=(
            [pltpu.VMEM(each.shape, F32) for each in (layer, tokens, first)],
            [pltpu.VMEM(each, BF16) for each in dims],
            [pltpu.VMEM(each, F32) for each in dims],
            dma((3,)), dma((3,)), dma((7,)), dma((7,)),
        ),
        compiler_params=pltpu.CompilerParams(vmem_limit_bytes=63 * 1024 * 1024),
        name="finish",
    )(layer, tokens, first, gu, down, out, query, key, value, gain)
    return results[:3] + (results[3][0],) + results[5:9] + (results[4][0],) + results[9:]


def tile_split(width, ff):
    tiles, more = 2 * ff // TILE, width // TILE
    each = -(-(tiles + more) // 3)
    return (each, each, tiles - 2 * each)


def fits(n_seq, n_blk, rows, width, ff):
    return (
        n_seq == 4
        and n_blk % 2 == 0
        and n_blk * LANES == width
        and rows == LANES
        and ff % TILE == 0
        and (ff // n_blk) % 32 == 0
        and 2 * (ff // n_blk) <= width
        and n_blk == 8
        and width == n_seq * TILE
    )


def local_fast(
    n_seq,
    n_blk,
    tokens,
    first_values,
    doc_lengths,
    attn_gain,
    query_weight,
    key_weight,
    value_weight,
    out_weight,
    ffn_gain,
    gate_weight,
    up_weight,
    down_weight,
    cotangent,
):
    rows, width = tokens.shape
    ff = gate_weight.shape[1]
    split = tile_split(width, ff)
    sizes = (rows, width, ff, n_seq, n_blk, split)
    half = HEAD_DIM // 2
    freq = THETA ** (-(np.arange(half) * 2.0 / HEAD_DIM))
    freq = np.tile(freq, LANES // half)[None, :].astype(np.float32)
    wide = max(split) * TILE
    chunk, down, chips = width // n_blk, ff // n_blk, n_blk // 2
    all_rows, group = n_seq * rows, n_blk * rows
    vmem = pl.BlockSpec(memory_space=pltpu.VMEM)
    hbm = pl.BlockSpec(memory_space=pl.ANY)
    smem = pl.BlockSpec(memory_space=pltpu.SMEM)
    shape = jax.ShapeDtypeStruct

    def half_type(*dims):
        return pltpu.VMEM(dims, BF16)

    def full_type(*dims):
        return pltpu.VMEM(dims, F32)

    scratch = dict(
        w_query=half_type(width, width), w_key=half_type(width, width), w_value=half_type(width, width),
        w_out=half_type(width, width), w_gate=half_type(width, ff), w_up=half_type(width, ff),
        w_down=half_type(ff, width),
        normed=half_type(rows, width), inv_first=full_type(rows, LANES), inv_second=full_type(rows, LANES),
        cos=full_type(rows, LANES), sin=full_type(rows, LANES),
        pack=half_type(n_blk, 3, rows, LANES), qkv=half_type(3, group, LANES),
        q2=half_type(2 * group, LANES), do2=half_type(2 * group, LANES), prob=half_type(2 * group, group),
        score=full_type(2 * TILE, group), top=full_type(2 * TILE, LANES), o2=full_type(2 * TILE, LANES),
        row=full_type(2 * group, LANES), o32=full_type(group, LANES), ob=half_type(group, LANES),
        dq=full_type(2 * group, LANES), dk=full_type(TILE, LANES), dv=full_type(TILE, LANES),
        att=half_type(rows, width), mid=full_type(rows, width), two=half_type(rows, width),
        act=half_type(rows, ff), gate_up=half_type(rows, 2 * ff), two_grad=full_type(rows, width),
        mid_grad=full_type(rows, width), mid_b=half_type(rows, width),
        out_pack=half_type(n_blk, rows, LANES), out_grad=half_type(group, LANES),
        grads=half_type(3, rows, width),
        buf_a=half_type(all_rows, width), buf_b=half_type(all_rows, ff), buf_att=half_type(all_rows, width),
        buf_mid=half_type(all_rows, width), normed_all=half_type(group, width), heads_grad=half_type(group, 3 * LANES),
        tail_part=half_type(n_blk, chunk, 3 * LANES), tail_shares=half_type(n_seq - 1, n_blk, chunk // n_seq, 3 * LANES),
        tail_sum=half_type(n_blk, chunk // n_seq, 3 * LANES), tail_got=half_type(n_blk, chunk // n_seq, 3 * LANES),
        tail_done=half_type(3, chunk // n_seq, width),
        turned=half_type(width, all_rows),
        total=half_type(chunk, wide), total_down=half_type(down, width),
        gain_rows=full_type(16, width), gains=full_type(n_blk, 16, LANES), gain_got=full_type(n_blk - 1, 16, LANES),
        gain_sum=full_type(n_seq, 16, LANES),
    )
    dma = pltpu.SemaphoreType.DMA
    sems = dict(
        load=dma((7,)), asend=dma((5, n_blk)), arecv=dma((5, n_blk)), xsend=dma((4, n_seq)), xrecv=dma((4, n_seq)),
        gusend=dma((2 * ff // TILE,)), gurecv=dma((split[0], n_seq)), actsend=dma((ff // TILE,)),
        actrecv=dma((ff // TILE, n_seq)), ready=pltpu.SemaphoreType.REGULAR,
        csend=dma((4, chips)), crecv=dma((4, chips)), rsend=dma((4, 2)), rrecv=dma((4, 2)), zsend=dma((4, 3)),
        zrecv=dma((4, 2)), gsend=dma((12, n_seq)), grecv=dma((12,)), glocal=dma((12,)),
        nsend=dma((chips - 1,)), nrecv=dma((chips - 1,)), fsend=dma((chips,)), frecv=dma((chips,)), nlocal=dma((1,)),
        qsend=dma((n_seq - 1,)), qrecv=dma((n_seq - 1,)), tsend=dma((3, n_seq - 1)), trecv=dma((3, n_seq)),
        hsend=dma((n_blk - 1,)), hrecv=dma((n_blk - 1,)), isend=dma((n_seq - 1,)), irecv=dma((n_seq,)),
    )
    layer, grad_tokens, grad_first, out_gu, out_down, out_out, out_query, out_key, out_value, out_gain = pl.pallas_call(
        functools.partial(layer_kernel, sizes),
        out_shape=(
            shape((rows, width), F32),
            shape((rows, width), F32),
            shape((rows, width), F32),
            shape((chunk, 2 * ff), BF16),
            shape((down, width), BF16),
            shape((chunk, width), BF16),
            shape((chunk, width), BF16),
            shape((chunk, width), BF16),
            shape((chunk, width), BF16),
            shape((16, LANES), F32),
        ),
        in_specs=[vmem, vmem, vmem, smem, vmem, vmem, vmem] + [hbm] * 7,
        out_specs=(vmem, vmem, vmem) + (hbm,) * 6 + (vmem,),
        scratch_shapes=(scratch, sems),
        compiler_params=pltpu.CompilerParams(
            collective_id=0, has_side_effects=True, vmem_limit_bytes=63 * 1024 * 1024
        ),
        name="layer",
    )(
        freq, tokens, first_values, doc_lengths, attn_gain[None, :], ffn_gain[None, :], cotangent,
        query_weight, key_weight, value_weight, out_weight, gate_weight, up_weight, down_weight,
    )
    return finish(layer, grad_tokens, grad_first, out_gu, out_down, out_out, out_query, out_key, out_value, out_gain)


def local(
    tokens,
    first_values,
    doc_lengths,
    attn_gain,
    query_weight,
    key_weight,
    value_weight,
    out_weight,
    ffn_gain,
    gate_weight,
    up_weight,
    down_weight,
    cotangent,
):
    rows, width = tokens.shape
    heads = width // HEAD_DIM
    scale = HEAD_DIM ** (-0.5)
    shape3 = (rows, heads, HEAD_DIM)
    my_start = lax.axis_index("blk") * rows
    my_index = my_start + jnp.arange(rows, dtype=jnp.int32)
    my_doc, my_pos = doc_layout(doc_lengths, my_index)
    cosine, sine = tables(my_pos)
    source = tokens.astype(jnp.float32)
    inv_first = lax.rsqrt(jnp.mean(source * source, axis=-1, keepdims=True) + EPS)
    normed = (source * inv_first * attn_gain).astype(jnp.bfloat16)
    query_pre = jnp.dot(normed, query_weight, preferred_element_type=jnp.float32)
    key_pre = jnp.dot(normed, key_weight, preferred_element_type=jnp.float32)
    value_pre = jnp.dot(normed, value_weight, preferred_element_type=jnp.float32)
    queries = rotate(query_pre.reshape(shape3), cosine, sine).astype(jnp.bfloat16)
    keys = rotate(key_pre.reshape(shape3), cosine, sine).astype(jnp.bfloat16).reshape(rows, width)
    mixed = (MIX * value_pre + MIX * first_values.astype(jnp.float32)).astype(jnp.bfloat16)
    keys_local = keys.reshape(shape3)
    mixed_local = mixed.reshape(shape3)

    def allowed_mask(query_index, query_doc, key_index, key_doc):
        return (query_doc[:, None] == key_doc[None, :]) & (
            key_index[None, :] <= query_index[:, None]
        )

    def forward_step(state, pieces, start):
        count = pieces[0].shape[0]
        keys_piece = pieces[0].reshape(count, heads, HEAD_DIM)
        values_piece = pieces[1].reshape(count, heads, HEAD_DIM)
        key_index = start + jnp.arange(count, dtype=jnp.int32)

        def forward_compute(state):
            high, total, accum = state
            key_doc, unused = doc_layout(doc_lengths, key_index)
            allowed = allowed_mask(my_index, my_doc, key_index, key_doc)[None]
            score = (
                jnp.einsum("qhd,khd->hqk", queries, keys_piece, preferred_element_type=jnp.float32)
                * scale
            )
            score = jnp.where(allowed, score, NEG)
            new_high = jnp.maximum(high, jnp.max(score, axis=-1))
            weight = jnp.where(allowed, jnp.exp(score - new_high[:, :, None]), 0.0)
            factor = jnp.exp(high - new_high)
            total = total * factor + jnp.sum(weight, axis=-1)
            accum = accum * factor.T[:, :, None] + jnp.einsum(
                "hqk,khd->qhd",
                weight.astype(jnp.bfloat16),
                values_piece,
                preferred_element_type=jnp.float32,
            )
            return (new_high, total, accum)

        return lax.cond(start <= my_index[-1], forward_compute, lambda kept: kept, state)

    def query_grad_step(grad_q, pieces, start):
        count = pieces[0].shape[0]
        keys_piece = pieces[0].reshape(count, heads, HEAD_DIM)
        values_piece = pieces[1].reshape(count, heads, HEAD_DIM)
        key_index = start + jnp.arange(count, dtype=jnp.int32)

        def query_compute(grad_q):
            key_doc, unused = doc_layout(doc_lengths, key_index)
            allowed = allowed_mask(my_index, my_doc, key_index, key_doc)[None]
            score = (
                jnp.einsum("qhd,khd->hqk", queries, keys_piece, preferred_element_type=jnp.float32)
                * scale
            )
            prob = jnp.where(allowed, jnp.exp(score - logsum[:, :, None]), 0.0)
            prob_grad = jnp.einsum(
                "qhd,khd->hqk", outgrad_local, values_piece, preferred_element_type=jnp.float32
            )
            score_grad = (prob * (prob_grad - delta[:, :, None])).astype(jnp.bfloat16)
            return (
                grad_q
                + jnp.einsum(
                    "hqk,khd->qhd", score_grad, keys_piece, preferred_element_type=jnp.float32
                )
                * scale
            )

        return lax.cond(start <= my_index[-1], query_compute, lambda kept: kept, grad_q)

    init = (
        jnp.full((heads, rows), NEG, jnp.float32),
        jnp.zeros((heads, rows), jnp.float32),
        jnp.zeros(shape3, jnp.float32),
    )
    state = by_blocks(
        forward_step,
        init,
        (
            lax.all_gather(keys, "blk", axis=0, tiled=True),
            lax.all_gather(mixed, "blk", axis=0, tiled=True),
        ),
        jnp.int32(0),
    )
    high, total, accum = state
    logsum = high + jnp.log(total)
    attended = accum / total.T[:, :, None]
    attended_b = attended.astype(jnp.bfloat16).reshape(rows, width)
    mid = source + jnp.dot(attended_b, out_weight, preferred_element_type=jnp.float32)
    inv_second = lax.rsqrt(jnp.mean(mid * mid, axis=-1, keepdims=True) + EPS)
    normed_two = (mid * inv_second * ffn_gain).astype(jnp.bfloat16)
    gate = jnp.dot(normed_two, gate_weight, preferred_element_type=jnp.float32)
    up = jnp.dot(normed_two, up_weight, preferred_element_type=jnp.float32)
    act = (jax.nn.silu(gate) * up).astype(jnp.bfloat16)
    layer_output = mid + jnp.dot(act, down_weight, preferred_element_type=jnp.float32)
    cot_float = cotangent.astype(jnp.float32)
    grad_down = outer(act, cotangent)
    act_grad = back(cotangent, down_weight)
    sigma = jax.nn.sigmoid(gate)
    gate_grad = (act_grad * up * sigma * (1.0 + gate * (1.0 - sigma))).astype(jnp.bfloat16)
    up_grad = (act_grad * gate * sigma).astype(jnp.bfloat16)
    grad_gate = outer(normed_two, gate_grad)
    grad_up = outer(normed_two, up_grad)
    normed_two_grad = back(gate_grad, gate_weight) + back(up_grad, up_weight)
    grad_ffn_gain = jnp.sum(normed_two_grad * mid * inv_second, axis=0)
    scaled_two = normed_two_grad * ffn_gain
    mid_grad = (
        cot_float
        + inv_second * scaled_two
        - mid * inv_second**3 * jnp.mean(scaled_two * mid, axis=-1, keepdims=True)
    )
    mid_grad_b = mid_grad.astype(jnp.bfloat16)
    grad_out_weight = outer(attended_b, mid_grad_b)
    attended_grad = back(mid_grad_b, out_weight).astype(jnp.bfloat16)
    outgrad_local = attended_grad.reshape(shape3)
    delta = jnp.sum(outgrad_local.astype(jnp.float32) * attended, axis=-1).T
    zeros3 = jnp.zeros(shape3, jnp.float32)
    grad_q = by_blocks(
        query_grad_step,
        zeros3,
        (
            lax.all_gather(keys, "blk", axis=0, tiled=True),
            lax.all_gather(mixed, "blk", axis=0, tiled=True),
        ),
        jnp.int32(0),
    )
    all_logsum, all_delta = (
        lax.all_gather(logsum.T, "blk", axis=0, tiled=True),
        lax.all_gather(delta.T, "blk", axis=0, tiled=True),
    )

    def key_grad_step(state, pieces, start):
        count = pieces[0].shape[0]
        query_piece = pieces[0].reshape(count, heads, HEAD_DIM)
        outgrad_piece = pieces[1].reshape(count, heads, HEAD_DIM)
        query_index = start + jnp.arange(count, dtype=jnp.int32)

        def key_compute(state):
            grad_k, grad_v = state
            logsum_piece = lax.dynamic_slice_in_dim(all_logsum, start, count, 0).T
            delta_piece = lax.dynamic_slice_in_dim(all_delta, start, count, 0).T
            query_doc, unused = doc_layout(doc_lengths, query_index)
            allowed = allowed_mask(query_index, query_doc, my_index, my_doc)[None]
            score = (
                jnp.einsum(
                    "qhd,khd->hqk", query_piece, keys_local, preferred_element_type=jnp.float32
                )
                * scale
            )
            prob = jnp.where(allowed, jnp.exp(score - logsum_piece[:, :, None]), 0.0)
            grad_v = grad_v + jnp.einsum(
                "hqk,qhd->khd",
                prob.astype(jnp.bfloat16),
                outgrad_piece,
                preferred_element_type=jnp.float32,
            )
            prob_grad = jnp.einsum(
                "qhd,khd->hqk", outgrad_piece, mixed_local, preferred_element_type=jnp.float32
            )
            score_grad = (prob * (prob_grad - delta_piece[:, :, None])).astype(jnp.bfloat16)
            grad_k = (
                grad_k
                + jnp.einsum(
                    "hqk,qhd->khd", score_grad, query_piece, preferred_element_type=jnp.float32
                )
                * scale
            )
            return (grad_k, grad_v)

        return lax.cond(query_index[-1] >= my_start, key_compute, lambda kept: kept, state)

    grad_k, grad_v = by_blocks(
        key_grad_step,
        (zeros3, zeros3),
        (
            lax.all_gather(queries.reshape(rows, width), "blk", axis=0, tiled=True),
            lax.all_gather(attended_grad, "blk", axis=0, tiled=True),
        ),
        jnp.int32(0),
    )
    queries_grad = grad_q.astype(jnp.bfloat16)
    keys_grad = grad_k.astype(jnp.bfloat16)
    mixed_grad = grad_v.astype(jnp.bfloat16).reshape(rows, width)
    q_pre_grad = (
        rotate(queries_grad.astype(jnp.float32), cosine, -sine)
        .astype(jnp.bfloat16)
        .reshape(rows, width)
    )
    k_pre_grad = (
        rotate(keys_grad.astype(jnp.float32), cosine, -sine)
        .astype(jnp.bfloat16)
        .reshape(rows, width)
    )
    grad_first = MIX * mixed_grad.astype(jnp.float32)
    value_grad = grad_first.astype(jnp.bfloat16)
    grad_query = outer(normed, q_pre_grad)
    grad_key = outer(normed, k_pre_grad)
    grad_value = outer(normed, value_grad)
    normed_grad = (
        back(q_pre_grad, query_weight)
        + back(k_pre_grad, key_weight)
        + back(value_grad, value_weight)
    )
    grad_attn_gain = jnp.sum(normed_grad * source * inv_first, axis=0)
    scaled_one = normed_grad * attn_gain
    grad_tokens = (
        mid_grad
        + inv_first * scaled_one
        - source * inv_first**3 * jnp.mean(scaled_one * source, axis=-1, keepdims=True)
    )
    summed = (
        lax.psum_scatter(grad_attn_gain, "blk", scatter_dimension=0, tiled=True),
        lax.psum_scatter(grad_query, "blk", scatter_dimension=0, tiled=True),
        lax.psum_scatter(grad_key, "blk", scatter_dimension=0, tiled=True),
        lax.psum_scatter(grad_value, "blk", scatter_dimension=0, tiled=True),
        lax.psum_scatter(grad_out_weight, "blk", scatter_dimension=0, tiled=True),
        lax.psum_scatter(grad_ffn_gain, "blk", scatter_dimension=0, tiled=True),
        lax.psum_scatter(grad_gate, "blk", scatter_dimension=0, tiled=True),
        lax.psum_scatter(grad_up, "blk", scatter_dimension=0, tiled=True),
        lax.psum_scatter(grad_down, "blk", scatter_dimension=0, tiled=True),
    )
    summed = (
        lax.psum(summed[0].astype(jnp.bfloat16), "seq").astype(jnp.float32),
        lax.psum(summed[1].astype(jnp.bfloat16), "seq").astype(jnp.float32),
        lax.psum(summed[2].astype(jnp.bfloat16), "seq").astype(jnp.float32),
        lax.psum(summed[3].astype(jnp.bfloat16), "seq").astype(jnp.float32),
        lax.psum(summed[4].astype(jnp.bfloat16), "seq").astype(jnp.float32),
        lax.psum(summed[5].astype(jnp.bfloat16), "seq").astype(jnp.float32),
        lax.psum(summed[6].astype(jnp.bfloat16), "seq").astype(jnp.float32),
        lax.psum(summed[7].astype(jnp.bfloat16), "seq").astype(jnp.float32),
        lax.psum(summed[8].astype(jnp.bfloat16), "seq").astype(jnp.float32),
    )
    return (
        layer_output,
        grad_tokens,
        grad_first,
        summed[0],
        summed[1],
        summed[2],
        summed[3],
        summed[4],
        summed[5],
        summed[6],
        summed[7],
        summed[8],
    )


def solution(mesh):
    n_seq, n_blk = mesh.shape["seq"], mesh.shape["blk"]

    def chosen(*args):
        rows, width = args[0].shape
        if fits(n_seq, n_blk, rows, width, args[9].shape[1]):
            return local_fast(n_seq, n_blk, *args)
        return local(*args)

    return jax.shard_map(
        chosen,
        mesh=mesh,
        in_specs=(
            P(("seq", "blk"), None),
            P(("seq", "blk"), None),
            P("seq", None),
            P(),
            P(),
            P(),
            P(),
            P(),
            P(),
            P(),
            P(),
            P(),
            P(("seq", "blk"), None),
        ),
        out_specs=(
            P(("seq", "blk"), None),
            P(("seq", "blk"), None),
            P(("seq", "blk"), None),
            P("blk"),
            P("blk", None),
            P("blk", None),
            P("blk", None),
            P("blk", None),
            P("blk"),
            P("blk", None),
            P("blk", None),
            P("blk", None),
        ),
        check_vma=False,
    )
```

```python
import functools
import math
import types

import jax
import jax.numpy as jnp
import numpy as np
from jax import lax
from jax.experimental import pallas as pl
from jax.experimental.pallas import tpu as pltpu
from jax.sharding import PartitionSpec as P

HEAD_DIM = 64


EPS = 1e-05
THETA = 10000.0
MIX = 0.5
NEG = -1e30


def doc_layout(lengths, index):
    ends = jnp.cumsum(lengths, axis=-1)
    past = (index[:, None] >= ends).astype(jnp.int32)
    return (jnp.sum(past, axis=1), index - jnp.sum(past * lengths, axis=1))


def tables(position):
    half = HEAD_DIM // 2
    freq = THETA ** (-(jnp.arange(half).astype(jnp.float32) * 2.0 / HEAD_DIM))
    angle = position.astype(jnp.float32)[:, None] * freq[None, :]
    return (jnp.cos(angle)[:, None, :], jnp.sin(angle)[:, None, :])


def rotate(values, cosine, sine):
    half = values.shape[-1] // 2
    first = values[..., :half]
    second = values[..., half:]
    return jnp.concatenate(
        [first * cosine - second * sine, second * cosine + first * sine], axis=-1
    )


def by_blocks(step, carry, pieces, start):
    rows = pieces[0].shape[0]
    size = math.gcd(rows, 1024)
    count = rows // size
    if count == 1:
        return step(carry, pieces, start)
    stacked = tuple((piece.reshape((count, size) + piece.shape[1:]) for piece in pieces))
    offsets = jnp.arange(count, dtype=jnp.int32) * size

    def turn(state, inputs):
        return (step(state, inputs[1], start + inputs[0]), None)

    result, unused = lax.scan(turn, carry, (offsets, stacked))
    return result


def outer(left, right):
    return lax.dot_general(
        left, right, (((0,), (0,)), ((), ())), preferred_element_type=jnp.float32
    )


def back(left, weight):
    return lax.dot_general(
        left, weight, (((1,), (1,)), ((), ())), preferred_element_type=jnp.float32
    )


TILE = 256
LANES = 128
GROUP = 16
MESH = pl.DeviceIdType.MESH
F32 = jnp.float32
BF16 = jnp.bfloat16


def remote(src, dst, send, recv, where):
    return pltpu.make_async_remote_copy(
        src_ref=src, dst_ref=dst, send_sem=send, recv_sem=recv, device_id=where, device_id_type=MESH
    )


def span(start, size, unit):
    return pl.ds(pl.multiple_of(start, unit), size)


def times(left, right):
    return jnp.dot(left, right, preferred_element_type=F32)


def iota(shape, dim):
    return lax.broadcasted_iota(jnp.int32, shape, dim)


def loop(low, high, body):
    def turn(index, unused):
        body(index)
        return unused

    lax.fori_loop(low, high, turn, 0)


class Trade:
    def __init__(self, blk, n_blk, phase, send, recv, source, place):
        self.blk, self.n_blk = blk, n_blk
        self.send, self.recv = send.at[phase], recv.at[phase]
        self.source, self.place = source, place

    def start(self, peer):
        src, dst = self.source(peer), self.place(self.blk)

        @pl.when(peer != self.blk)
        def _():
            remote(src, dst, self.send.at[peer], self.recv.at[self.blk], {"blk": peer}).start()

        @pl.when(peer == self.blk)
        def _():
            pltpu.make_async_copy(src, dst, self.recv.at[self.blk]).start()

    def arrived(self, peer):
        src, dst = self.source(peer), self.place(peer)

        @pl.when(peer != self.blk)
        def _():
            remote(src, dst, self.send.at[peer], self.recv.at[peer], {"blk": peer}).wait_recv()

        @pl.when(peer == self.blk)
        def _():
            pltpu.make_async_copy(src, dst, self.recv.at[peer]).wait()

    def all_arrived(self):
        loop(0, self.n_blk, self.arrived)

    def all_left(self):
        def left(peer):
            @pl.when(peer != self.blk)
            def _():
                remote(
                    self.source(peer), self.place(self.blk), self.send.at[peer], self.recv.at[self.blk], {"blk": peer}
                ).wait_send()

        loop(0, self.n_blk, left)


class Gift:
    def __init__(self, seq, n_seq, rows, owner, kind, src, dst, send, recv):
        self.seq, self.n_seq, self.rows, self.owner, self.kind = seq, n_seq, rows, owner, kind
        self.src, self.dst, self.send, self.recv = src, dst, send, recv

    def copy(self, other, send):
        dst = self.dst.at[span(other * self.rows, self.rows, self.rows)]
        return remote(self.src, dst, self.send.at[self.kind, send], self.recv.at[self.kind, other], {"seq": send})

    def own(self):
        dst = self.dst.at[pl.ds(self.owner * self.rows, self.rows)]
        return pltpu.make_async_copy(self.src, dst, self.recv.at[self.kind, self.owner])

    def start(self):
        @pl.when(self.seq != self.owner)
        def _():
            self.copy(self.seq, self.owner).start()

        @pl.when(self.seq == self.owner)
        def _():
            self.own().start()

    def arrived(self):
        for other in range(self.n_seq):
            if other == self.owner:
                self.own().wait()
            else:
                self.copy(other, other).wait_recv()

    def left(self):
        @pl.when(self.seq != self.owner)
        def _():
            self.copy(self.seq, self.owner).wait_send()


class Sum:
    def __init__(self, blk, size, part, cgot, rgot, zgot, total, sems):
        self.blk, self.size = blk, size
        self.core, self.chip = lax.rem(blk, 2), lax.div(blk, 2)
        side = lax.div(self.chip, 2)
        self.far = 2 * (1 - side)
        self.partner = self.chip + 1 - 2 * lax.rem(self.chip, 2)
        self.inner = lax.rem(self.chip, 2) != side
        self.far_inner = 2 - side
        self.part, self.cgot, self.rgot, self.zgot, self.total = part, cgot, rgot, zgot, total
        self.csend, self.crecv, self.rsend, self.rrecv, self.zsend, self.zrecv = sems

    def order(self, step):
        return jnp.where(step < 2, self.far + step, jnp.where(step == 2, self.partner, self.chip))

    def chunk(self, index):
        return self.part.at[span(index * self.size, self.size, 32)]

    def mine(self, chip):
        return self.chunk(2 * chip + self.core)

    def swap(self, chip):
        return remote(
            self.chunk(2 * chip + 1 - self.core),
            self.cgot(chip),
            self.csend.at[chip],
            self.crecv.at[chip],
            {"blk": 2 * self.chip + 1 - self.core},
        )

    def lend(self, index):
        return remote(
            self.mine(self.far + index),
            self.rgot(index),
            self.rsend.at[index],
            self.rrecv.at[index],
            {"blk": 2 * self.partner + self.core},
        )

    def send_far(self, index):
        return remote(
            self.mine(self.far + index),
            self.zgot(1),
            self.zsend.at[index],
            self.zrecv.at[1],
            {"blk": 2 * (self.far + index) + self.core},
        )

    def send_near(self):
        return remote(
            self.mine(self.partner),
            self.zgot(0),
            self.zsend.at[2],
            self.zrecv.at[0],
            {"blk": 2 * self.partner + self.core},
        )

    def add(self, mine, other):
        def group(index):
            at = span(index * 32, 32, 32)
            mine[at, :] = (mine[at, :].astype(F32) + other[at, :].astype(F32)).astype(BF16)

        loop(0, self.size // 32, group)

    def begin(self):
        for index in range(2):
            chip = self.far + index
            self.swap(chip).wait()
            self.add(self.mine(chip), self.cgot(chip))

            @pl.when(jnp.logical_not(self.inner))
            def _(index=index):
                self.lend(index).start()

        self.swap(self.partner).wait()
        self.add(self.mine(self.partner), self.cgot(self.partner))
        self.send_near().start()
        self.swap(self.chip).wait()

    def relay(self):
        @pl.when(self.inner)
        def _():
            for index in range(2):
                self.lend(index).wait_recv()
                self.add(self.mine(self.far + index), self.rgot(index))
                self.send_far(index).start()

    def end(self):
        self.send_near().wait_recv()
        self.send_far(0).wait_recv()
        mine, other = self.mine(self.chip), self.cgot(self.chip)

        def group(index):
            at = span(index * 32, 32, 32)
            value = mine[at, :].astype(F32) + other[at, :].astype(F32)
            value = value + self.zgot(0)[at, :].astype(F32) + self.zgot(1)[at, :].astype(F32)
            self.total[at, :] = value.astype(BF16)

        loop(0, self.size // 32, group)

    def left(self):
        self.send_near().wait_send()

        @pl.when(self.inner)
        def _():
            for index in range(2):
                self.send_far(index).wait_send()

        @pl.when(jnp.logical_not(self.inner))
        def _():
            for index in range(2):
                self.lend(index).wait_send()


class TileGift:
    def __init__(self, seq, n_seq, rows, src, dst, send, recv, owner_of):
        self.seq, self.n_seq, self.rows, self.src, self.dst = seq, n_seq, rows, src, dst
        self.send, self.recv, self.owner_of = send, recv, owner_of

    def place(self, other, slot):
        return self.dst.at[span(other * self.rows, self.rows, self.rows), span(slot * TILE, TILE, TILE)]

    def tile(self, index):
        return self.src.at[:, span(index * TILE, TILE, TILE)]

    def start(self, index):
        owner, slot = self.owner_of(index)
        src, dst, recv = self.tile(index), self.place(self.seq, slot), self.recv.at[slot, self.seq]

        @pl.when(owner != self.seq)
        def _():
            remote(src, dst, self.send.at[index], recv, {"seq": owner}).start()

        @pl.when(owner == self.seq)
        def _():
            pltpu.make_async_copy(src, dst, recv).start()

    def arrived(self, low, high):
        def one(slot):
            def other_one(other):
                dst, recv = self.place(other, slot), self.recv.at[slot, other]

                @pl.when(other != self.seq)
                def _():
                    remote(self.tile(0), dst, self.send.at[0], recv, {"seq": other}).wait_recv()

                @pl.when(other == self.seq)
                def _():
                    pltpu.make_async_copy(self.tile(0), dst, recv).wait()

            loop(0, self.n_seq, other_one)

        loop(low, high, one)

    def left(self, count):
        def one(index):
            owner, slot = self.owner_of(index)

            @pl.when(owner != self.seq)
            def _():
                remote(
                    self.tile(index), self.place(self.seq, slot), self.send.at[index], self.recv.at[slot, self.seq],
                    {"seq": owner},
                ).wait_send()

        loop(0, count, one)


class Spread:
    def __init__(self, seq, owner, kind, src, dst, send, recv, local, on_send, on_recv):
        self.seq, self.owner, self.kind, self.src, self.dst = seq, owner, kind, src, dst
        self.send, self.recv, self.local, self.on_send, self.on_recv = send, recv, local, on_send, on_recv
        self.half = src.shape[0] // 2

    def copy(self, bit):
        return remote(
            self.src, self.dst, self.send.at[self.kind, bit], self.recv.at[self.kind], {"seq": self.owner ^ (bit + 1)}
        )

    def onward(self, bit):
        part = self.dst.at[bit * self.half : (bit + 1) * self.half]
        return remote(
            part, part, self.on_send.at[self.kind, bit], self.on_recv.at[self.kind, bit], {"seq": self.owner ^ 3}
        )

    def own(self):
        return pltpu.make_async_copy(self.src, self.dst, self.local.at[self.kind])

    def start(self):
        @pl.when(self.seq == self.owner)
        def _():
            for bit in range(2):
                self.copy(bit).start()
            self.own().start()

    def pass_on(self):
        for bit in range(2):

            @pl.when(self.seq == self.owner ^ (bit + 1))
            def _(bit=bit):
                self.copy(bit).wait_recv()
                self.onward(bit).start()

    def finish(self):
        @pl.when(self.seq == self.owner)
        def _():
            for bit in range(2):
                self.copy(bit).wait_send()
            self.own().wait()

        for bit in range(2):

            @pl.when(self.seq == self.owner ^ (bit + 1))
            def _(bit=bit):
                self.onward(bit).wait_send()

        @pl.when(self.seq == self.owner ^ 3)
        def _():
            for bit in range(2):
                self.onward(bit).wait_recv()


def turn_over(src, dst):
    def one(index):
        at = span(index * TILE, TILE, TILE)
        dst[at, :] = src[:, at].T

    loop(0, src.shape[1] // TILE, one)


def outer_tiles(turned, rhs, part, chip, tiles, rhs_at, part_at):
    rows = span(chip * TILE, TILE, TILE)

    def tile(index):
        value = times(turned[rows, :], rhs[:, span(rhs_at + index * TILE, TILE, TILE)])
        part[rows, span(part_at + index * TILE, TILE, TILE)] = value.astype(BF16)

    loop(0, tiles, tile)


def layer_kernel(
    sizes,
    freq, tokens, first, lengths, attn_gain, ffn_gain, cot,
    h_query, h_key, h_value, h_out, h_gate, h_up, h_down,
    o_layer, o_tokens, o_first, o_gu, o_down, o_out, o_query, o_key, o_value, o_gain,
    v, sem,
):
    rows, width, ff, n_seq, n_blk, split = sizes
    v, sem = types.SimpleNamespace(**v), types.SimpleNamespace(**sem)
    docs = lengths.shape[1]
    chips = n_blk // 2
    scale = HEAD_DIM ** (-0.5)
    seq, blk = lax.axis_index("seq"), lax.axis_index("blk")
    chip_at = lax.div(blk, 2)

    def turned_chip(step):
        return lax.rem(chip_at + step, chips)

    barrier = pltpu.get_barrier_semaphore()
    for step in range(1, n_seq):
        pl.semaphore_signal(barrier, inc=1, device_id={"seq": lax.rem(seq + step, n_seq)}, device_id_type=MESH)
    for step in range(1, n_blk):
        pl.semaphore_signal(barrier, inc=1, device_id={"blk": lax.rem(blk + step, n_blk)}, device_id_type=MESH)

    def load(index, src, dst):
        copy = pltpu.make_async_copy(src, dst, sem.load.at[index])
        copy.start()
        return copy

    load_query = load(0, h_query, v.w_query)
    load_key = load(1, h_key, v.w_key)
    load_value = load(2, h_value, v.w_value)
    load_out = load(3, h_out, v.w_out)
    load_gate = load(4, h_gate, v.w_gate)
    load_up = load(5, h_up, v.w_up)
    load_down = load(6, h_down, v.w_down)

    def norm(group):
        at = span(group * GROUP, GROUP, GROUP)
        x = tokens[at, :].astype(F32)
        inv = lax.rsqrt(jnp.mean(x * x, axis=-1, keepdims=True) + EPS)
        v.normed[at, :] = (x * inv * attn_gain[...]).astype(BF16)
        v.inv_first[at, :] = jnp.broadcast_to(inv, (GROUP, LANES))

    loop(0, rows // GROUP, norm)

    def doc_start(index):
        start, end = jnp.zeros_like(index), jnp.int32(0)
        for doc in range(docs):
            end = end + lengths[0, doc]
            start = jnp.where(index >= end, end, start)
        return start

    half = HEAD_DIM // 2

    def low_half(count):
        return lax.rem(iota((count, LANES), 1), HEAD_DIM) < half

    def set_tables(start, count, cosine_ref, sine_ref):
        index = start + iota((count, LANES), 0)
        angle = (index - doc_start(index)).astype(F32) * freq[...]
        cosine_ref[...] = jnp.cos(angle)
        sine = jnp.sin(angle)
        sine_ref[...] = jnp.where(low_half(count), -sine, sine)

    def halves_changed(u):
        return jnp.where(low_half(u.shape[0]), pltpu.roll(u, LANES - half, 1), pltpu.roll(u, half, 1))

    set_tables(blk * rows, rows, v.cos, v.sin)

    def rotated(u):
        return u * v.cos[...] + halves_changed(u) * v.sin[...]

    cuts = [0]
    for tiles in split:
        cuts.append(cuts[-1] + tiles * TILE)
    wide = max(split) * TILE

    def gift(owner, kind, src, dst):
        return Gift(seq, n_seq, rows, owner, kind, src, dst, sem.xsend, sem.xrecv)

    gift_cot = gift(3, 0, cot, v.buf_a)
    gifts_two = [gift(owner, 0, v.two, v.buf_a) for owner in range(3)]
    each, hidden = split[0], ff // TILE
    gift_gu = TileGift(
        seq, n_seq, rows, v.gate_up, v.buf_b, sem.gusend, sem.gurecv,
        lambda index: (lax.div(index, each), lax.rem(index, each)),
    )
    gift_act = TileGift(seq, n_seq, rows, v.act, v.buf_b, sem.actsend, sem.actrecv, lambda index: (3, index))
    gift_att = gift(2, 2, v.att, v.buf_att)
    gift_mid = gift(2, 3, v.mid_b, v.buf_mid)
    def trade(phase, source, place):
        return Trade(blk, n_blk, phase, sem.asend, sem.arecv, source, place)

    def block_rows(ref):
        return lambda peer: ref.at[span(peer * rows, rows, rows)]

    def block_columns(ref):
        return lambda peer: ref.at[:, span(peer * LANES, LANES, LANES)]

    give_qkv = trade(0, lambda peer: v.pack.at[peer], lambda peer: v.qkv.at[:, span(peer * rows, rows, rows)])
    give_att = trade(1, block_rows(v.ob), block_columns(v.att))
    give_out = trade(2, lambda peer: v.out_pack.at[peer], block_rows(v.out_grad))
    give_grads = trade(
        3, lambda peer: v.pack.at[peer], lambda peer: v.grads.at[:, :, span(peer * LANES, LANES, LANES)]
    )

    give_tail = trade(4, lambda peer: v.tail_sum.at[peer], lambda peer: v.tail_got.at[peer])
    core = lax.rem(blk, 2)
    mate = blk + 1 - 2 * core

    def block_of(step):
        return 2 * turned_chip(step) + core

    def rows_of(block):
        return v.normed_all.at[span(block * rows, rows, rows)]

    def normed_out(step):
        return remote(
            v.normed, rows_of(blk), sem.nsend.at[step - 1], sem.nrecv.at[step - 1], {"blk": block_of(step)}
        )

    def normed_over(step):
        there = rows_of(block_of(step))
        return remote(there, there, sem.fsend.at[step], sem.frecv.at[step], {"blk": mate})

    def mates_normed(step):
        there = rows_of(2 * turned_chip(step) + 1 - core)
        return remote(there, there, sem.fsend.at[step], sem.frecv.at[step], {"blk": mate})

    pl.semaphore_wait(barrier, n_seq + n_blk - 2)
    gift_cot.start()
    own_normed = pltpu.make_async_copy(v.normed, rows_of(blk), sem.nlocal.at[0])
    own_normed.start()

    for item in (load_query, load_key, load_value):
        item.wait()

    def project(step):
        chip = turned_chip(step)
        at = span(chip * TILE, TILE, TILE)
        left = v.normed[...]
        q, k, val = times(left, v.w_query[:, at]), times(left, v.w_key[:, at]), times(left, v.w_value[:, at])
        old = first[:, at].astype(F32)
        for core in range(2):
            peer = 2 * chip + core
            cols = slice(core * LANES, (core + 1) * LANES)
            v.pack[peer, 0] = (rotated(q[:, cols]) * scale).astype(BF16)
            v.pack[peer, 1] = rotated(k[:, cols]).astype(BF16)
            v.pack[peer, 2] = (MIX * val[:, cols] + MIX * old[:, cols]).astype(BF16)
            give_qkv.start(peer)

    loop(1, chips + 1, project)

    first_head = iota((TILE, LANES), 1) < HEAD_DIM

    def stacked(values):
        return jnp.concatenate([jnp.where(first_head, values, 0.0), jnp.where(first_head, 0.0, values)], axis=0)

    def unstacked(values):
        return jnp.where(first_head, values[:TILE], values[TILE:])

    def attend(block):
        for core in range(2):
            give_qkv.arrived(2 * block + core)
        at, both = span(block * TILE, TILE, TILE), span(block * 2 * TILE, 2 * TILE, 2 * TILE)
        queries = stacked(v.qkv[0, at, :].astype(F32)).astype(BF16)
        v.q2[both, :] = queries
        v.q2_turned[:, both] = queries.T
        index = block * TILE + lax.rem(iota((2 * TILE, 1), 0), TILE)
        start = doc_start(index)
        v.top[...] = jnp.full((2 * TILE, LANES), NEG, F32)

        def scores(tile):
            cols = span(tile * TILE, TILE, TILE)
            score = back(v.q2[both, :], v.qkv[1, cols, :])
            key = tile * TILE + iota((2 * TILE, TILE), 1)
            score = jnp.where((key <= index) & (key >= start), score, NEG)
            v.score[:, cols] = score
            v.top[...] = jnp.maximum(v.top[...], jnp.maximum(score[:, :LANES], score[:, LANES:]))

        loop(0, block + 1, scores)
        top = jnp.max(v.top[...], axis=1, keepdims=True)
        v.top[...] = jnp.zeros((2 * TILE, LANES), F32)
        v.o2[...] = jnp.zeros((2 * TILE, LANES), F32)

        def weights(tile):
            cols = span(tile * TILE, TILE, TILE)
            weight = jnp.exp(v.score[:, cols] - top)
            v.top[...] += weight[:, :LANES] + weight[:, LANES:]
            weight = weight.astype(BF16)
            v.prob[both, cols] = weight
            v.o2[...] += times(weight, v.qkv[2, cols, :])

        loop(0, block + 1, weights)
        inv = 1.0 / jnp.sum(v.top[...], axis=1, keepdims=True)
        v.row[both, :] = jnp.broadcast_to(inv, (2 * TILE, LANES))
        attended = unstacked(v.o2[...] * inv)
        v.o32[at, :] = attended
        v.ob[at, :] = attended.astype(BF16)
        for core in range(2):
            give_att.start(2 * block + core)

    loop(0, chips, attend)
    loop(
        0,
        chips,
        lambda block: set_tables(
            block * TILE,
            TILE,
            v.score.at[:TILE, span(block * TILE, LANES, LANES)],
            v.score.at[:TILE, span(block * TILE + LANES, LANES, LANES)],
        ),
    )
    give_att.all_arrived()
    gift_att.start()
    normed_out(1).start()
    normed_out(3).start()

    load_out.wait()

    def middle(tile):
        cols = span(tile * TILE, TILE, TILE)
        value = tokens[:, cols].astype(F32) + times(v.att[...], v.w_out[:, cols])
        v.mid[:, cols] = value

    loop(0, width // TILE, middle)

    def norm_two(group):
        at = span(group * GROUP, GROUP, GROUP)
        x = v.mid[at, :]
        inv = lax.rsqrt(jnp.mean(x * x, axis=-1, keepdims=True) + EPS)
        v.two[at, :] = (x * inv * ffn_gain[...]).astype(BF16)
        v.inv_second[at, :] = jnp.broadcast_to(inv, (GROUP, LANES))

    loop(0, rows // GROUP, norm_two)
    for item in gifts_two:
        item.start()

    for item in (load_gate, load_up, load_down):
        item.wait()
    v.two_grad[...] = jnp.zeros((rows, width), F32)

    def feed(step):
        tile = lax.rem(split[0] + step, hidden)
        cols = span(tile * TILE, TILE, TILE)
        gate = times(v.two[...], v.w_gate[:, cols])
        up = times(v.two[...], v.w_up[:, cols])
        act_grad = back(cot[...], v.w_down[cols, :])
        sigma = jax.nn.sigmoid(gate)
        silu = gate * sigma
        act = (silu * up).astype(BF16)
        gate_grad = (act_grad * up * sigma * (1.0 + gate * (1.0 - sigma))).astype(BF16)
        up_grad = (act_grad * silu).astype(BF16)
        v.act[:, cols] = act
        v.gate_up[:, cols] = gate_grad
        v.gate_up[:, span(ff + tile * TILE, TILE, TILE)] = up_grad
        gift_gu.start(tile)
        gift_gu.start(hidden + tile)
        gift_act.start(tile)
        v.two_grad[...] += back(gate_grad, v.w_gate[:, cols]) + back(up_grad, v.w_up[:, cols])

    loop(0, hidden, feed)
    v.gain_rows[...] = jnp.zeros((16, width), F32)

    def norm_two_back(group):
        at = span(group * GROUP, GROUP, GROUP)
        x, grad, inv = v.mid[at, :], v.two_grad[at, :], v.inv_second[at, :1]
        term = grad * x * inv
        v.gain_rows[8:16, :] += term[:8] + term[8:]
        scaled = grad * ffn_gain[...]
        mean = jnp.mean(scaled * x, axis=-1, keepdims=True)
        value = cot[at, :].astype(F32) + inv * scaled - x * (inv * inv * inv * mean)
        v.mid_grad[at, :] = value
        v.mid_b[at, :] = value.astype(BF16)

    loop(0, rows // GROUP, norm_two_back)
    gift_mid.start()

    def out_back(step):
        chip = turned_chip(step)
        value = back(v.mid_b[...], v.w_out[span(chip * TILE, TILE, TILE), :]).astype(BF16)
        for core in range(2):
            v.out_pack[2 * chip + core] = value[:, core * LANES : (core + 1) * LANES]
            give_out.start(2 * chip + core)

    loop(1, chips + 1, out_back)
    normed_out(2).start()

    def layer_out(tile):
        cols = span(tile * TILE, TILE, TILE)
        o_layer[:, cols] = v.mid[:, cols] + times(v.act[...], v.w_down[:, cols])

    loop(0, width // TILE, layer_out)
    own_normed.wait()
    normed_over(0).start()
    for step in (1, 3):
        normed_out(chips - step).wait_recv()
        normed_over(step).start()

    chunk, down = width // n_blk, ff // n_blk

    def sems_of(index):
        return tuple(
            item.at[index] for item in (sem.csend, sem.crecv, sem.rsend, sem.rrecv, sem.zsend, sem.zrecv)
        )

    def stack_in(ref, top, cols):
        return lambda index: ref.at[span(top + index * chunk, chunk, 32), cols]

    def square_in(ref, more, low, high):
        def place(index):
            index = index + more
            return ref.at[
                span(lax.rem(index, 2) * down, down, 32), span(lax.div(index, 2) * width + low, high - low, LANES)
            ]

        return place

    def piece(index, low, high):
        cols = slice(low, high)
        return Sum(
            blk, chunk, v.w_gate.at[:, cols], stack_in(v.w_up, 0, cols), stack_in(v.w_up, chips * chunk, cols),
            stack_in(v.w_up, (chips + 2) * chunk, cols), v.total.at[:, cols], sems_of(index),
        )

    edges = [0, each // 3, 7 * each // 9, each]
    thirds = [piece(index, edges[index] * TILE, edges[index + 1] * TILE) for index in range(3)]
    last = split[2] * TILE
    halves = [piece(0, 0, last), piece(1, last, last + width)]
    bounds = [0, width // 4, width // 2, 3 * width // 4, 7 * width // 8, width]
    fifths = [
        Sum(
            blk, down, v.w_down.at[:, low:high], square_in(v.w_up, 0, low, high), square_in(v.w_gate, 0, low, high),
            square_in(v.w_gate, 2, low, high), v.total_down.at[:, low:high], sems_of(index),
        )
        for index, (low, high) in enumerate(zip(bounds[:-1], bounds[1:]))
    ]
    first_two, third_one, fourth = seq < 2, seq == 2, seq == 3

    def spread(owner, kind, src, dst):
        return Spread(
            seq, owner, kind, src, dst, sem.gsend, sem.grecv, sem.glocal, sem.onsend, sem.onrecv
        )

    spreads = [
        [
            spread(
                owner,
                3 * owner + index,
                v.total.at[:, edges[index] * TILE : edges[index + 1] * TILE],
                o_gu.at[:, cuts[owner] + edges[index] * TILE : cuts[owner] + edges[index + 1] * TILE],
            )
            for index in range(3)
        ]
        for owner in range(2)
    ] + [
        [
            spread(2, 6, v.total.at[:, :last], o_gu.at[:, cuts[2] : cuts[3]]),
            spread(2, 7, v.total.at[:, last : last + width], o_out),
        ],
        [
            spread(3, 8 + index, v.total_down.at[:, low:high], o_down.at[:, low:high])
            for index, (low, high) in enumerate(zip(bounds[:-1], bounds[1:]))
        ],
    ]
    def products(item, turned, rhs, tiles, rhs_at, part_at):
        def one(step):
            chip = item.order(step)
            outer_tiles(turned, rhs, v.w_gate, chip, tiles, rhs_at, part_at)

        loop(0, chips, one)

    def swaps(item):
        loop(0, chips, lambda step: item.swap(item.order(step)).start())

    def gate_up_piece(index):
        gift_gu.arrived(edges[index], edges[index + 1])
        at = edges[index] * TILE
        products(thirds[index], v.turned, v.buf_b, edges[index + 1] - edges[index], at, at)

    def down_products(low, high):
        def one(step):
            index = lax.rem(split[0] + step, hidden)
            gift_act.arrived(index, index + 1)
            at = span(index * TILE, TILE, TILE)
            v.turned[:TILE, :] = v.buf_b[:, at].T
            v.w_down[at, :] = times(v.turned[:TILE, :], v.buf_a[...]).astype(BF16)

        loop(low, high, one)

    def down_swaps():
        for item in fifths:
            swaps(item)

    for owner in range(n_seq):

        @pl.when(seq == owner)
        def _(owner=owner):
            (gifts_two + [gift_cot])[owner].arrived()

    @pl.when(first_two)
    def _():
        turn_over(v.buf_a, v.turned)

    @pl.when(third_one)
    def _():
        turn_over(v.buf_a, v.turned)

    @pl.when(fourth)
    def _():
        down_products(0, hidden // 2)

    give_out.all_arrived()


    def prepare(block):
        at, both = span(block * TILE, TILE, TILE), span(block * 2 * TILE, 2 * TILE, 2 * TILE)
        grad = (stacked(v.out_grad[at, :].astype(F32)) * v.row[both, :]).astype(BF16)
        v.do2[both, :] = grad
        v.do2_turned[:, both] = grad.T
        attended = v.o32[at, :]
        delta = jnp.sum(grad.astype(F32) * jnp.concatenate([attended, attended], axis=0), axis=1, keepdims=True)
        v.row[both, :] = jnp.broadcast_to(delta, (2 * TILE, LANES))
        v.dq[both, :] = jnp.zeros((2 * TILE, LANES), F32)

    loop(0, chips, prepare)
    give_qkv.all_left()

    def key_block(block):
        at = span(block * TILE, TILE, TILE)
        v.dk[...] = jnp.zeros((LANES, TILE), F32)
        v.dv[...] = jnp.zeros((LANES, TILE), F32)

        def query_block(other):
            both = span(other * 2 * TILE, 2 * TILE, 2 * TILE)
            prob = v.prob[both, at]
            grad = back(v.do2[both, :], v.qkv[2, at, :])
            score_grad = (prob.astype(F32) * (grad - v.row[both, :1])).astype(BF16)
            v.dk[...] += times(v.q2_turned[:, both], score_grad)
            v.dv[...] += times(v.do2_turned[:, both], prob)
            v.dq[both, :] += times(score_grad, v.qkv[1, at, :])

        loop(block, chips, query_block)
        cosine = v.score[:TILE, span(block * TILE, LANES, LANES)]
        sine = v.score[:TILE, span(block * TILE + LANES, LANES, LANES)]

        def rotated_back(u):
            u = u.astype(BF16).astype(F32)
            return (u * cosine - halves_changed(u) * sine).astype(BF16)

        dq = rotated_back(unstacked(v.dq[span(block * 2 * TILE, 2 * TILE, 2 * TILE), :]) * scale)
        dk = rotated_back(v.dk[...].T)
        dv = (MIX * v.dv[...].T.astype(BF16).astype(F32)).astype(BF16)
        for index, value in enumerate((dq, dk, dv)):
            v.heads_grad[at, index * LANES : (index + 1) * LANES] = value
            for half_at in range(2):
                v.pack[2 * block + half_at, index] = value[half_at * rows : (half_at + 1) * rows]
        for half_at in range(2):
            give_grads.start(2 * block + half_at)

    loop(0, chips, key_block)

    def when(which, *steps):
        @pl.when(which)
        def _():
            for step in steps:
                step()

    def ended(item, goes):
        def step():
            item.end()
            for other in goes:
                other.start()

        return step

    def first_half():
        gift_gu.arrived(0, split[2])
        products(halves[0], v.turned, v.buf_b, split[2], 0, 0)
        swaps(halves[0])
        halves[0].begin()

    def second_half():
        gift_att.arrived()
        gift_mid.arrived()
        turn_over(v.buf_att, v.turned)
        products(halves[1], v.turned, v.buf_mid, width // TILE, 0, last)
        swaps(halves[1])

    def gate_up_gone(index):
        gate_up_piece(index)
        swaps(thirds[index])

    when(first_two, lambda: gate_up_gone(0), thirds[0].begin)
    when(third_one, first_half)
    when(fourth, lambda: down_products(hidden // 2, hidden), down_swaps, fifths[0].begin)

    normed_out(2).wait_recv()
    normed_over(2).start()
    for step in range(chips):
        mates_normed(step).wait_recv()

    def project_back(index):
        value = outer(v.normed_all[:, span(index * TILE, TILE, TILE)], v.heads_grad[...]).astype(BF16)
        v.tail_part[2 * index] = value[:LANES]
        v.tail_part[2 * index + 1] = value[LANES:]

    loop(0, width // TILE, project_back)
    quarter = LANES // n_seq

    def tail_share(step):
        other = lax.rem(seq + step, n_seq)
        return remote(
            v.tail_part.at[:, span(other * quarter, quarter, quarter)],
            v.tail_shares.at[step - 1],
            sem.qsend.at[step - 1],
            sem.qrecv.at[step - 1],
            {"seq": other},
        )

    for step in range(1, n_seq):
        tail_share(step).start()

    when(first_two, lambda: gate_up_gone(1), thirds[1].begin, thirds[0].relay, lambda: gate_up_gone(2))
    when(third_one, second_half)

    def tail_add(index):
        value = v.tail_part[index, span(seq * quarter, quarter, quarter), :].astype(F32)
        for step in range(1, n_seq):
            value = value + v.tail_shares[step - 1, index].astype(F32)
        v.tail_sum[index] = value.astype(BF16)
        give_tail.start(index)

    for step in range(1, n_seq):
        tail_share(step).wait()
    loop(0, n_blk, tail_add)
    when(first_two, thirds[2].begin)
    when(third_one, halves[1].begin)
    when(fourth, fifths[1].begin)

    give_grads.all_arrived()

    def gone(index, *owners):
        return [spreads[owner][index] for owner in owners]

    when(first_two, thirds[1].relay, ended(thirds[0], []))
    for item in gone(0, 0, 1):
        item.start()
    when(fourth, fifths[0].relay, fifths[2].begin)

    def normed_back(tile):
        at = span(tile * TILE, TILE, TILE)
        o_tokens[:, at] = (
            back(v.grads[0], v.w_query[at, :])
            + back(v.grads[1], v.w_key[at, :])
            + back(v.grads[2], v.w_value[at, :])
        )

    loop(0, width // TILE, normed_back)
    o_first[...] = v.grads[2].astype(F32)

    def norm_back(group):
        at = span(group * GROUP, GROUP, GROUP)
        x, grad, inv = tokens[at, :].astype(F32), o_tokens[at, :], v.inv_first[at, :1]
        term = grad * x * inv
        v.gain_rows[0:8, :] += term[:8] + term[8:]
        scaled = grad * attn_gain[...]
        mean = jnp.mean(scaled * x, axis=-1, keepdims=True)
        o_tokens[at, :] = v.mid_grad[at, :] + inv * scaled - x * (inv * inv * inv * mean)

    loop(0, rows // GROUP, norm_back)

    for peer in range(n_blk):
        v.gains[peer] = v.gain_rows[:, peer * LANES : (peer + 1) * LANES]

    def gain_copy(step):
        other = lax.rem(blk + step, n_blk)
        return remote(
            v.gains.at[other], v.gain_got.at[step - 1], sem.hsend.at[step - 1], sem.hrecv.at[step - 1],
            {"blk": other},
        )

    for step in range(1, n_blk):
        gain_copy(step).start()
    when(fourth, ended(fifths[0], gone(0, 3)), fifths[1].relay, fifths[3].begin, fifths[4].begin)

    when(first_two, ended(thirds[1], gone(1, 0, 1)))
    when(third_one, halves[0].relay, ended(halves[0], gone(0, 2)))
    when(fourth, ended(fifths[1], gone(1, 3)))

    give_tail.all_arrived()
    for index in range(3):
        for peer in range(n_blk):
            v.tail_done[index, :, peer * LANES : (peer + 1) * LANES] = v.tail_got[
                peer, :, index * LANES : (index + 1) * LANES
            ]

    def tail_spread(index, step, owner):
        at = span(owner * quarter, quarter, quarter)
        return remote(
            v.tail_done.at[index],
            (o_query, o_key, o_value)[index].at[at],
            sem.tsend.at[index, step - 1],
            sem.trecv.at[index, owner],
            {"seq": lax.rem(seq + step, n_seq)},
        )

    def tail_own(index):
        at = span(seq * quarter, quarter, quarter)
        return pltpu.make_async_copy(
            v.tail_done.at[index], (o_query, o_key, o_value)[index].at[at], sem.trecv.at[index, seq]
        )

    for index in range(3):
        tail_own(index).start()
        for step in range(1, n_seq):
            tail_spread(index, step, seq).start()

    def pass_on(*items):
        for item in items:
            item.pass_on()

    pass_on(*gone(0, 0, 1, 3))
    when(first_two, thirds[2].relay, ended(thirds[2], gone(2, 0, 1)))
    when(third_one, halves[1].relay, ended(halves[1], gone(1, 2)))
    when(
        fourth,
        fifths[2].relay,
        ended(fifths[2], gone(2, 3)),
        fifths[3].relay,
        ended(fifths[3], gone(3, 3)),
    )
    pass_on(*gone(0, 2), *gone(1, 3, 0, 1))
    value = v.gains[blk]
    for step in range(1, n_blk):
        gain_copy(step).wait()
        value = value + v.gain_got[step - 1]
    v.gain_sum[seq] = value
    for step in range(1, n_seq):
        other = lax.rem(seq + step, n_seq)
        mine = v.gain_sum.at[seq]
        remote(mine, mine, sem.isend.at[step - 1], sem.irecv.at[seq], {"seq": other}).start()

    when(fourth, fifths[4].relay, ended(fifths[4], gone(4, 3)))
    pass_on(*gone(1, 2), *gone(2, 3, 0, 1), *gone(3, 3), *gone(4, 3))

    for step in range(1, n_seq):
        other = lax.rem(seq + step, n_seq)
        theirs = v.gain_sum.at[other]
        remote(theirs, theirs, sem.isend.at[step - 1], sem.irecv.at[other], {"seq": other}).wait()
    value = v.gain_sum[0]
    for group in range(1, n_seq):
        value = value + v.gain_sum[group]
    o_gain[0:8, :] = jnp.broadcast_to(jnp.sum(value[:8], axis=0, keepdims=True), (8, LANES))
    o_gain[8:16, :] = jnp.broadcast_to(jnp.sum(value[8:], axis=0, keepdims=True), (8, LANES))

    for index in range(3):
        tail_own(index).wait()
        for step in range(1, n_seq):
            tail_spread(index, step, seq).wait_send()
            tail_spread(index, step, lax.rem(seq + step, n_seq)).wait_recv()
    for item in sum(spreads, []):
        item.finish()
    for item in [gift_cot, gift_att, gift_mid] + gifts_two:
        item.left()
    gift_gu.left(2 * hidden)
    gift_act.left(hidden)
    for item in (give_att, give_out, give_grads, give_tail):
        item.all_left()
    for step in range(chips):
        normed_over(step).wait_send()
        if step:
            normed_out(step).wait_send()

    @pl.when(first_two)
    def _():
        for item in thirds:
            item.left()

    @pl.when(third_one)
    def _():
        for item in halves:
            item.left()

    @pl.when(fourth)
    def _():
        for item in fifths:
            item.left()


def finish_kernel(
    layer, tokens, first, gu, down, out, query, key, value, gain,
    o_layer, o_tokens, o_first, o_gain, o_gain_two, o_query, o_key, o_value, o_out, o_gate, o_up, o_down,
    kept, small, large, sem_kept_in, sem_kept_out, sem_in, sem_out,
):
    kept_in = [
        pltpu.make_async_copy(src, kept[index], sem_kept_in.at[index])
        for index, src in enumerate((layer, tokens, first))
    ]
    kept_out = [
        pltpu.make_async_copy(kept[index], dst, sem_kept_out.at[index])
        for index, dst in enumerate((o_layer, o_tokens, o_first))
    ]
    ff = o_gate.shape[1]
    sources = [gu.at[:, :ff], gu.at[:, ff:], down, query, key, value, out]
    targets = [o_gate, o_up, o_down, o_query, o_key, o_value, o_out]
    loads = [pltpu.make_async_copy(src, small[index], sem_in.at[index]) for index, src in enumerate(sources)]
    stores = [pltpu.make_async_copy(large[index], dst, sem_out.at[index]) for index, dst in enumerate(targets)]
    for item in kept_in + loads:
        item.start()
    for coming, going in zip(kept_in, kept_out):
        coming.wait()
        going.start()
    for index in range(len(sources)):
        loads[index].wait()

        def group(step, index=index):
            at = span(step * GROUP, GROUP, GROUP)
            large[index][at, :] = small[index][at, :].astype(F32)

        loop(0, targets[index].shape[0] // GROUP, group)
        stores[index].start()
    o_gain[...] = gain[0:1, :]
    o_gain_two[...] = gain[8:9, :]
    for item in stores + kept_out:
        item.wait()


def finish(layer, tokens, first, gu, down, out, query, key, value, gain):
    hbm, vmem = pl.BlockSpec(memory_space=pl.ANY), pl.BlockSpec(memory_space=pltpu.VMEM)
    shape = jax.ShapeDtypeStruct
    ff = gu.shape[1] // 2
    dims = [(gu.shape[0], ff), (gu.shape[0], ff), down.shape, query.shape, key.shape, value.shape, out.shape]
    dma = pltpu.SemaphoreType.DMA
    results = pl.pallas_call(
        finish_kernel,
        out_shape=tuple(
            shape(each, F32)
            for each in (
                layer.shape, tokens.shape, first.shape, (1, LANES), (1, LANES), dims[3], dims[4], dims[5], dims[6], dims[0], dims[1], dims[2]
            )
        ),
        in_specs=[hbm] * 9 + [vmem],
        out_specs=(hbm,) * 3 + (vmem,) * 2 + (hbm,) * 7,
        scratch_shapes=(
            [pltpu.VMEM(each.shape, F32) for each in (layer, tokens, first)],
            [pltpu.VMEM(each, BF16) for each in dims],
            [pltpu.VMEM(each, F32) for each in dims],
            dma((3,)), dma((3,)), dma((7,)), dma((7,)),
        ),
        compiler_params=pltpu.CompilerParams(vmem_limit_bytes=63 * 1024 * 1024),
        name="finish",
    )(layer, tokens, first, gu, down, out, query, key, value, gain)
    return results[:3] + (results[3][0],) + results[5:9] + (results[4][0],) + results[9:]


def tile_split(width, ff):
    tiles, more = 2 * ff // TILE, width // TILE
    each = -(-(tiles + more) // 3)
    return (each, each, tiles - 2 * each)


def fits(n_seq, n_blk, rows, width, ff):
    return (
        n_seq == 4
        and n_blk % 2 == 0
        and n_blk * LANES == width
        and rows == LANES
        and ff % TILE == 0
        and (ff // n_blk) % 32 == 0
        and 2 * (ff // n_blk) <= width
        and n_blk == 8
        and width == n_seq * TILE
    )


def local_fast(
    n_seq,
    n_blk,
    tokens,
    first_values,
    doc_lengths,
    attn_gain,
    query_weight,
    key_weight,
    value_weight,
    out_weight,
    ffn_gain,
    gate_weight,
    up_weight,
    down_weight,
    cotangent,
):
    rows, width = tokens.shape
    ff = gate_weight.shape[1]
    split = tile_split(width, ff)
    sizes = (rows, width, ff, n_seq, n_blk, split)
    half = HEAD_DIM // 2
    freq = THETA ** (-(np.arange(half) * 2.0 / HEAD_DIM))
    freq = np.tile(freq, LANES // half)[None, :].astype(np.float32)
    wide = max(split) * TILE
    chunk, down, chips = width // n_blk, ff // n_blk, n_blk // 2
    all_rows, group = n_seq * rows, n_blk * rows
    vmem = pl.BlockSpec(memory_space=pltpu.VMEM)
    hbm = pl.BlockSpec(memory_space=pl.ANY)
    smem = pl.BlockSpec(memory_space=pltpu.SMEM)
    shape = jax.ShapeDtypeStruct

    def half_type(*dims):
        return pltpu.VMEM(dims, BF16)

    def full_type(*dims):
        return pltpu.VMEM(dims, F32)

    scratch = dict(
        w_query=half_type(width, width), w_key=half_type(width, width), w_value=half_type(width, width),
        w_out=half_type(width, width), w_gate=half_type(width, ff), w_up=half_type(width, ff),
        w_down=half_type(ff, width),
        normed=half_type(rows, width), inv_first=full_type(rows, LANES), inv_second=full_type(rows, LANES),
        cos=full_type(rows, LANES), sin=full_type(rows, LANES),
        pack=half_type(n_blk, 3, rows, LANES), qkv=half_type(3, group, LANES),
        q2=half_type(2 * group, LANES), do2=half_type(2 * group, LANES), prob=half_type(2 * group, group),
        score=full_type(2 * TILE, group), top=full_type(2 * TILE, LANES), o2=full_type(2 * TILE, LANES),
        row=full_type(2 * group, LANES), o32=full_type(group, LANES), ob=half_type(group, LANES),
        dq=full_type(2 * group, LANES), dk=full_type(LANES, TILE), dv=full_type(LANES, TILE),
        q2_turned=half_type(LANES, 2 * group), do2_turned=half_type(LANES, 2 * group),
        att=half_type(rows, width), mid=full_type(rows, width), two=half_type(rows, width),
        act=half_type(rows, ff), gate_up=half_type(rows, 2 * ff), two_grad=full_type(rows, width),
        mid_grad=full_type(rows, width), mid_b=half_type(rows, width),
        out_pack=half_type(n_blk, rows, LANES), out_grad=half_type(group, LANES),
        grads=half_type(3, rows, width),
        buf_a=half_type(all_rows, width), buf_b=half_type(all_rows, ff), buf_att=half_type(all_rows, width),
        buf_mid=half_type(all_rows, width), normed_all=half_type(group, width), heads_grad=half_type(group, 3 * LANES),
        tail_part=half_type(n_blk, chunk, 3 * LANES), tail_shares=half_type(n_seq - 1, n_blk, chunk // n_seq, 3 * LANES),
        tail_sum=half_type(n_blk, chunk // n_seq, 3 * LANES), tail_got=half_type(n_blk, chunk // n_seq, 3 * LANES),
        tail_done=half_type(3, chunk // n_seq, width),
        turned=half_type(width, all_rows),
        total=half_type(chunk, wide), total_down=half_type(down, width),
        gain_rows=full_type(16, width), gains=full_type(n_blk, 16, LANES), gain_got=full_type(n_blk - 1, 16, LANES),
        gain_sum=full_type(n_seq, 16, LANES),
    )
    dma = pltpu.SemaphoreType.DMA
    sems = dict(
        load=dma((7,)), asend=dma((5, n_blk)), arecv=dma((5, n_blk)), xsend=dma((4, n_seq)), xrecv=dma((4, n_seq)),
        gusend=dma((2 * ff // TILE,)), gurecv=dma((split[0], n_seq)), actsend=dma((ff // TILE,)),
        actrecv=dma((ff // TILE, n_seq)),
        csend=dma((5, chips)), crecv=dma((5, chips)), rsend=dma((5, 2)), rrecv=dma((5, 2)), zsend=dma((5, 3)),
        zrecv=dma((5, 2)), gsend=dma((13, 2)), grecv=dma((13,)), glocal=dma((13,)), onsend=dma((13, 2)), onrecv=dma((13, 2)),
        nsend=dma((chips - 1,)), nrecv=dma((chips - 1,)), fsend=dma((chips,)), frecv=dma((chips,)), nlocal=dma((1,)),
        qsend=dma((n_seq - 1,)), qrecv=dma((n_seq - 1,)), tsend=dma((3, n_seq - 1)), trecv=dma((3, n_seq)),
        hsend=dma((n_blk - 1,)), hrecv=dma((n_blk - 1,)), isend=dma((n_seq - 1,)), irecv=dma((n_seq,)),
    )
    layer, grad_tokens, grad_first, out_gu, out_down, out_out, out_query, out_key, out_value, out_gain = pl.pallas_call(
        functools.partial(layer_kernel, sizes),
        out_shape=(
            shape((rows, width), F32),
            shape((rows, width), F32),
            shape((rows, width), F32),
            shape((chunk, 2 * ff), BF16),
            shape((down, width), BF16),
            shape((chunk, width), BF16),
            shape((chunk, width), BF16),
            shape((chunk, width), BF16),
            shape((chunk, width), BF16),
            shape((16, LANES), F32),
        ),
        in_specs=[vmem, vmem, vmem, smem, vmem, vmem, vmem] + [hbm] * 7,
        out_specs=(vmem, vmem, vmem) + (hbm,) * 6 + (vmem,),
        scratch_shapes=(scratch, sems),
        compiler_params=pltpu.CompilerParams(
            collective_id=0, has_side_effects=True, vmem_limit_bytes=63 * 1024 * 1024
        ),
        name="layer",
    )(
        freq, tokens, first_values, doc_lengths, attn_gain[None, :], ffn_gain[None, :], cotangent,
        query_weight, key_weight, value_weight, out_weight, gate_weight, up_weight, down_weight,
    )
    return finish(layer, grad_tokens, grad_first, out_gu, out_down, out_out, out_query, out_key, out_value, out_gain)


def local(
    tokens,
    first_values,
    doc_lengths,
    attn_gain,
    query_weight,
    key_weight,
    value_weight,
    out_weight,
    ffn_gain,
    gate_weight,
    up_weight,
    down_weight,
    cotangent,
):
    rows, width = tokens.shape
    heads = width // HEAD_DIM
    scale = HEAD_DIM ** (-0.5)
    shape3 = (rows, heads, HEAD_DIM)
    my_start = lax.axis_index("blk") * rows
    my_index = my_start + jnp.arange(rows, dtype=jnp.int32)
    my_doc, my_pos = doc_layout(doc_lengths, my_index)
    cosine, sine = tables(my_pos)
    source = tokens.astype(jnp.float32)
    inv_first = lax.rsqrt(jnp.mean(source * source, axis=-1, keepdims=True) + EPS)
    normed = (source * inv_first * attn_gain).astype(jnp.bfloat16)
    query_pre = jnp.dot(normed, query_weight, preferred_element_type=jnp.float32)
    key_pre = jnp.dot(normed, key_weight, preferred_element_type=jnp.float32)
    value_pre = jnp.dot(normed, value_weight, preferred_element_type=jnp.float32)
    queries = rotate(query_pre.reshape(shape3), cosine, sine).astype(jnp.bfloat16)
    keys = rotate(key_pre.reshape(shape3), cosine, sine).astype(jnp.bfloat16).reshape(rows, width)
    mixed = (MIX * value_pre + MIX * first_values.astype(jnp.float32)).astype(jnp.bfloat16)
    keys_local = keys.reshape(shape3)
    mixed_local = mixed.reshape(shape3)

    def allowed_mask(query_index, query_doc, key_index, key_doc):
        return (query_doc[:, None] == key_doc[None, :]) & (
            key_index[None, :] <= query_index[:, None]
        )

    def forward_step(state, pieces, start):
        count = pieces[0].shape[0]
        keys_piece = pieces[0].reshape(count, heads, HEAD_DIM)
        values_piece = pieces[1].reshape(count, heads, HEAD_DIM)
        key_index = start + jnp.arange(count, dtype=jnp.int32)

        def forward_compute(state):
            high, total, accum = state
            key_doc, unused = doc_layout(doc_lengths, key_index)
            allowed = allowed_mask(my_index, my_doc, key_index, key_doc)[None]
            score = (
                jnp.einsum("qhd,khd->hqk", queries, keys_piece, preferred_element_type=jnp.float32)
                * scale
            )
            score = jnp.where(allowed, score, NEG)
            new_high = jnp.maximum(high, jnp.max(score, axis=-1))
            weight = jnp.where(allowed, jnp.exp(score - new_high[:, :, None]), 0.0)
            factor = jnp.exp(high - new_high)
            total = total * factor + jnp.sum(weight, axis=-1)
            accum = accum * factor.T[:, :, None] + jnp.einsum(
                "hqk,khd->qhd",
                weight.astype(jnp.bfloat16),
                values_piece,
                preferred_element_type=jnp.float32,
            )
            return (new_high, total, accum)

        return lax.cond(start <= my_index[-1], forward_compute, lambda kept: kept, state)

    def query_grad_step(grad_q, pieces, start):
        count = pieces[0].shape[0]
        keys_piece = pieces[0].reshape(count, heads, HEAD_DIM)
        values_piece = pieces[1].reshape(count, heads, HEAD_DIM)
        key_index = start + jnp.arange(count, dtype=jnp.int32)

        def query_compute(grad_q):
            key_doc, unused = doc_layout(doc_lengths, key_index)
            allowed = allowed_mask(my_index, my_doc, key_index, key_doc)[None]
            score = (
                jnp.einsum("qhd,khd->hqk", queries, keys_piece, preferred_element_type=jnp.float32)
                * scale
            )
            prob = jnp.where(allowed, jnp.exp(score - logsum[:, :, None]), 0.0)
            prob_grad = jnp.einsum(
                "qhd,khd->hqk", outgrad_local, values_piece, preferred_element_type=jnp.float32
            )
            score_grad = (prob * (prob_grad - delta[:, :, None])).astype(jnp.bfloat16)
            return (
                grad_q
                + jnp.einsum(
                    "hqk,khd->qhd", score_grad, keys_piece, preferred_element_type=jnp.float32
                )
                * scale
            )

        return lax.cond(start <= my_index[-1], query_compute, lambda kept: kept, grad_q)

    init = (
        jnp.full((heads, rows), NEG, jnp.float32),
        jnp.zeros((heads, rows), jnp.float32),
        jnp.zeros(shape3, jnp.float32),
    )
    state = by_blocks(
        forward_step,
        init,
        (
            lax.all_gather(keys, "blk", axis=0, tiled=True),
            lax.all_gather(mixed, "blk", axis=0, tiled=True),
        ),
        jnp.int32(0),
    )
    high, total, accum = state
    logsum = high + jnp.log(total)
    attended = accum / total.T[:, :, None]
    attended_b = attended.astype(jnp.bfloat16).reshape(rows, width)
    mid = source + jnp.dot(attended_b, out_weight, preferred_element_type=jnp.float32)
    inv_second = lax.rsqrt(jnp.mean(mid * mid, axis=-1, keepdims=True) + EPS)
    normed_two = (mid * inv_second * ffn_gain).astype(jnp.bfloat16)
    gate = jnp.dot(normed_two, gate_weight, preferred_element_type=jnp.float32)
    up = jnp.dot(normed_two, up_weight, preferred_element_type=jnp.float32)
    act = (jax.nn.silu(gate) * up).astype(jnp.bfloat16)
    layer_output = mid + jnp.dot(act, down_weight, preferred_element_type=jnp.float32)
    cot_float = cotangent.astype(jnp.float32)
    grad_down = outer(act, cotangent)
    act_grad = back(cotangent, down_weight)
    sigma = jax.nn.sigmoid(gate)
    gate_grad = (act_grad * up * sigma * (1.0 + gate * (1.0 - sigma))).astype(jnp.bfloat16)
    up_grad = (act_grad * gate * sigma).astype(jnp.bfloat16)
    grad_gate = outer(normed_two, gate_grad)
    grad_up = outer(normed_two, up_grad)
    normed_two_grad = back(gate_grad, gate_weight) + back(up_grad, up_weight)
    grad_ffn_gain = jnp.sum(normed_two_grad * mid * inv_second, axis=0)
    scaled_two = normed_two_grad * ffn_gain
    mid_grad = (
        cot_float
        + inv_second * scaled_two
        - mid * inv_second**3 * jnp.mean(scaled_two * mid, axis=-1, keepdims=True)
    )
    mid_grad_b = mid_grad.astype(jnp.bfloat16)
    grad_out_weight = outer(attended_b, mid_grad_b)
    attended_grad = back(mid_grad_b, out_weight).astype(jnp.bfloat16)
    outgrad_local = attended_grad.reshape(shape3)
    delta = jnp.sum(outgrad_local.astype(jnp.float32) * attended, axis=-1).T
    zeros3 = jnp.zeros(shape3, jnp.float32)
    grad_q = by_blocks(
        query_grad_step,
        zeros3,
        (
            lax.all_gather(keys, "blk", axis=0, tiled=True),
            lax.all_gather(mixed, "blk", axis=0, tiled=True),
        ),
        jnp.int32(0),
    )
    all_logsum, all_delta = (
        lax.all_gather(logsum.T, "blk", axis=0, tiled=True),
        lax.all_gather(delta.T, "blk", axis=0, tiled=True),
    )

    def key_grad_step(state, pieces, start):
        count = pieces[0].shape[0]
        query_piece = pieces[0].reshape(count, heads, HEAD_DIM)
        outgrad_piece = pieces[1].reshape(count, heads, HEAD_DIM)
        query_index = start + jnp.arange(count, dtype=jnp.int32)

        def key_compute(state):
            grad_k, grad_v = state
            logsum_piece = lax.dynamic_slice_in_dim(all_logsum, start, count, 0).T
            delta_piece = lax.dynamic_slice_in_dim(all_delta, start, count, 0).T
            query_doc, unused = doc_layout(doc_lengths, query_index)
            allowed = allowed_mask(query_index, query_doc, my_index, my_doc)[None]
            score = (
                jnp.einsum(
                    "qhd,khd->hqk", query_piece, keys_local, preferred_element_type=jnp.float32
                )
                * scale
            )
            prob = jnp.where(allowed, jnp.exp(score - logsum_piece[:, :, None]), 0.0)
            grad_v = grad_v + jnp.einsum(
                "hqk,qhd->khd",
                prob.astype(jnp.bfloat16),
                outgrad_piece,
                preferred_element_type=jnp.float32,
            )
            prob_grad = jnp.einsum(
                "qhd,khd->hqk", outgrad_piece, mixed_local, preferred_element_type=jnp.float32
            )
            score_grad = (prob * (prob_grad - delta_piece[:, :, None])).astype(jnp.bfloat16)
            grad_k = (
                grad_k
                + jnp.einsum(
                    "hqk,qhd->khd", score_grad, query_piece, preferred_element_type=jnp.float32
                )
                * scale
            )
            return (grad_k, grad_v)

        return lax.cond(query_index[-1] >= my_start, key_compute, lambda kept: kept, state)

    grad_k, grad_v = by_blocks(
        key_grad_step,
        (zeros3, zeros3),
        (
            lax.all_gather(queries.reshape(rows, width), "blk", axis=0, tiled=True),
            lax.all_gather(attended_grad, "blk", axis=0, tiled=True),
        ),
        jnp.int32(0),
    )
    queries_grad = grad_q.astype(jnp.bfloat16)
    keys_grad = grad_k.astype(jnp.bfloat16)
    mixed_grad = grad_v.astype(jnp.bfloat16).reshape(rows, width)
    q_pre_grad = (
        rotate(queries_grad.astype(jnp.float32), cosine, -sine)
        .astype(jnp.bfloat16)
        .reshape(rows, width)
    )
    k_pre_grad = (
        rotate(keys_grad.astype(jnp.float32), cosine, -sine)
        .astype(jnp.bfloat16)
        .reshape(rows, width)
    )
    grad_first = MIX * mixed_grad.astype(jnp.float32)
    value_grad = grad_first.astype(jnp.bfloat16)
    grad_query = outer(normed, q_pre_grad)
    grad_key = outer(normed, k_pre_grad)
    grad_value = outer(normed, value_grad)
    normed_grad = (
        back(q_pre_grad, query_weight)
        + back(k_pre_grad, key_weight)
        + back(value_grad, value_weight)
    )
    grad_attn_gain = jnp.sum(normed_grad * source * inv_first, axis=0)
    scaled_one = normed_grad * attn_gain
    grad_tokens = (
        mid_grad
        + inv_first * scaled_one
        - source * inv_first**3 * jnp.mean(scaled_one * source, axis=-1, keepdims=True)
    )
    summed = (
        lax.psum_scatter(grad_attn_gain, "blk", scatter_dimension=0, tiled=True),
        lax.psum_scatter(grad_query, "blk", scatter_dimension=0, tiled=True),
        lax.psum_scatter(grad_key, "blk", scatter_dimension=0, tiled=True),
        lax.psum_scatter(grad_value, "blk", scatter_dimension=0, tiled=True),
        lax.psum_scatter(grad_out_weight, "blk", scatter_dimension=0, tiled=True),
        lax.psum_scatter(grad_ffn_gain, "blk", scatter_dimension=0, tiled=True),
        lax.psum_scatter(grad_gate, "blk", scatter_dimension=0, tiled=True),
        lax.psum_scatter(grad_up, "blk", scatter_dimension=0, tiled=True),
        lax.psum_scatter(grad_down, "blk", scatter_dimension=0, tiled=True),
    )
    summed = (
        lax.psum(summed[0].astype(jnp.bfloat16), "seq").astype(jnp.float32),
        lax.psum(summed[1].astype(jnp.bfloat16), "seq").astype(jnp.float32),
        lax.psum(summed[2].astype(jnp.bfloat16), "seq").astype(jnp.float32),
        lax.psum(summed[3].astype(jnp.bfloat16), "seq").astype(jnp.float32),
        lax.psum(summed[4].astype(jnp.bfloat16), "seq").astype(jnp.float32),
        lax.psum(summed[5].astype(jnp.bfloat16), "seq").astype(jnp.float32),
        lax.psum(summed[6].astype(jnp.bfloat16), "seq").astype(jnp.float32),
        lax.psum(summed[7].astype(jnp.bfloat16), "seq").astype(jnp.float32),
        lax.psum(summed[8].astype(jnp.bfloat16), "seq").astype(jnp.float32),
    )
    return (
        layer_output,
        grad_tokens,
        grad_first,
        summed[0],
        summed[1],
        summed[2],
        summed[3],
        summed[4],
        summed[5],
        summed[6],
        summed[7],
        summed[8],
    )


def solution(mesh):
    n_seq, n_blk = mesh.shape["seq"], mesh.shape["blk"]

    def chosen(*args):
        rows, width = args[0].shape
        if fits(n_seq, n_blk, rows, width, args[9].shape[1]):
            return local_fast(n_seq, n_blk, *args)
        return local(*args)

    return jax.shard_map(
        chosen,
        mesh=mesh,
        in_specs=(
            P(("seq", "blk"), None),
            P(("seq", "blk"), None),
            P("seq", None),
            P(),
            P(),
            P(),
            P(),
            P(),
            P(),
            P(),
            P(),
            P(),
            P(("seq", "blk"), None),
        ),
        out_specs=(
            P(("seq", "blk"), None),
            P(("seq", "blk"), None),
            P(("seq", "blk"), None),
            P("blk"),
            P("blk", None),
            P("blk", None),
            P("blk", None),
            P("blk", None),
            P("blk"),
            P("blk", None),
            P("blk", None),
            P("blk", None),
        ),
        check_vma=False,
    )
```

```python
import functools
import math
import types

import jax
import jax.numpy as jnp
import numpy as np
from jax import lax
from jax.experimental import pallas as pl
from jax.experimental.pallas import tpu as pltpu
from jax.sharding import PartitionSpec as P

HEAD_DIM = 64


EPS = 1e-05
THETA = 10000.0
MIX = 0.5
NEG = -1e30


def doc_layout(lengths, index):
    ends = jnp.cumsum(lengths, axis=-1)
    past = (index[:, None] >= ends).astype(jnp.int32)
    return (jnp.sum(past, axis=1), index - jnp.sum(past * lengths, axis=1))


def tables(position):
    half = HEAD_DIM // 2
    freq = THETA ** (-(jnp.arange(half).astype(jnp.float32) * 2.0 / HEAD_DIM))
    angle = position.astype(jnp.float32)[:, None] * freq[None, :]
    return (jnp.cos(angle)[:, None, :], jnp.sin(angle)[:, None, :])


def rotate(values, cosine, sine):
    half = values.shape[-1] // 2
    first = values[..., :half]
    second = values[..., half:]
    return jnp.concatenate(
        [first * cosine - second * sine, second * cosine + first * sine], axis=-1
    )


def by_blocks(step, carry, pieces, start):
    rows = pieces[0].shape[0]
    size = math.gcd(rows, 1024)
    count = rows // size
    if count == 1:
        return step(carry, pieces, start)
    stacked = tuple((piece.reshape((count, size) + piece.shape[1:]) for piece in pieces))
    offsets = jnp.arange(count, dtype=jnp.int32) * size

    def turn(state, inputs):
        return (step(state, inputs[1], start + inputs[0]), None)

    result, unused = lax.scan(turn, carry, (offsets, stacked))
    return result


def outer(left, right):
    return lax.dot_general(
        left, right, (((0,), (0,)), ((), ())), preferred_element_type=jnp.float32
    )


def back(left, weight):
    return lax.dot_general(
        left, weight, (((1,), (1,)), ((), ())), preferred_element_type=jnp.float32
    )


TILE = 256
LANES = 128
GROUP = 16
MESH = pl.DeviceIdType.MESH
F32 = jnp.float32
BF16 = jnp.bfloat16


def remote(src, dst, send, recv, where):
    return pltpu.make_async_remote_copy(
        src_ref=src, dst_ref=dst, send_sem=send, recv_sem=recv, device_id=where, device_id_type=MESH
    )


def span(start, size, unit):
    return pl.ds(pl.multiple_of(start, unit), size)


def times(left, right):
    return jnp.dot(left, right, preferred_element_type=F32)


def iota(shape, dim):
    return lax.broadcasted_iota(jnp.int32, shape, dim)


def loop(low, high, body):
    def turn(index, unused):
        body(index)
        return unused

    lax.fori_loop(low, high, turn, 0)


class Trade:
    def __init__(self, blk, n_blk, phase, send, recv, source, place):
        self.blk, self.n_blk = blk, n_blk
        self.send, self.recv = send.at[phase], recv.at[phase]
        self.source, self.place = source, place

    def start(self, peer):
        src, dst = self.source(peer), self.place(self.blk)

        @pl.when(peer != self.blk)
        def _():
            remote(src, dst, self.send.at[peer], self.recv.at[self.blk], {"blk": peer}).start()

        @pl.when(peer == self.blk)
        def _():
            pltpu.make_async_copy(src, dst, self.recv.at[self.blk]).start()

    def arrived(self, peer):
        src, dst = self.source(peer), self.place(peer)

        @pl.when(peer != self.blk)
        def _():
            remote(src, dst, self.send.at[peer], self.recv.at[peer], {"blk": peer}).wait_recv()

        @pl.when(peer == self.blk)
        def _():
            pltpu.make_async_copy(src, dst, self.recv.at[peer]).wait()

    def all_arrived(self):
        loop(0, self.n_blk, self.arrived)

    def all_left(self):
        def left(peer):
            @pl.when(peer != self.blk)
            def _():
                remote(
                    self.source(peer), self.place(self.blk), self.send.at[peer], self.recv.at[self.blk], {"blk": peer}
                ).wait_send()

        loop(0, self.n_blk, left)


class Gift:
    def __init__(self, seq, n_seq, rows, owner, kind, src, dst, send, recv):
        self.seq, self.n_seq, self.rows, self.owner, self.kind = seq, n_seq, rows, owner, kind
        self.src, self.dst, self.send, self.recv = src, dst, send, recv

    def copy(self, other, send):
        dst = self.dst.at[span(other * self.rows, self.rows, self.rows)]
        return remote(self.src, dst, self.send.at[self.kind, send], self.recv.at[self.kind, other], {"seq": send})

    def own(self):
        dst = self.dst.at[pl.ds(self.owner * self.rows, self.rows)]
        return pltpu.make_async_copy(self.src, dst, self.recv.at[self.kind, self.owner])

    def start(self):
        @pl.when(self.seq != self.owner)
        def _():
            self.copy(self.seq, self.owner).start()

        @pl.when(self.seq == self.owner)
        def _():
            self.own().start()

    def arrived(self):
        for other in range(self.n_seq):
            if other == self.owner:
                self.own().wait()
            else:
                self.copy(other, other).wait_recv()

    def left(self):
        @pl.when(self.seq != self.owner)
        def _():
            self.copy(self.seq, self.owner).wait_send()


class Sum:
    def __init__(self, blk, size, part, cgot, rgot, zgot, total, sems):
        self.blk, self.size = blk, size
        self.core, self.chip = lax.rem(blk, 2), lax.div(blk, 2)
        side = lax.div(self.chip, 2)
        self.far = 2 * (1 - side)
        self.partner = self.chip + 1 - 2 * lax.rem(self.chip, 2)
        self.inner = lax.rem(self.chip, 2) != side
        self.far_inner = 2 - side
        self.part, self.cgot, self.rgot, self.zgot, self.total = part, cgot, rgot, zgot, total
        self.csend, self.crecv, self.rsend, self.rrecv, self.zsend, self.zrecv = sems

    def order(self, step):
        return jnp.where(step < 2, self.far + step, jnp.where(step == 2, self.partner, self.chip))

    def chunk(self, index):
        return self.part.at[span(index * self.size, self.size, 32)]

    def mine(self, chip):
        return self.chunk(2 * chip + self.core)

    def swap(self, chip):
        return remote(
            self.chunk(2 * chip + 1 - self.core),
            self.cgot(chip),
            self.csend.at[chip],
            self.crecv.at[chip],
            {"blk": 2 * self.chip + 1 - self.core},
        )

    def lend(self, index):
        return remote(
            self.mine(self.far + index),
            self.rgot(index),
            self.rsend.at[index],
            self.rrecv.at[index],
            {"blk": 2 * self.partner + self.core},
        )

    def send_far(self, index):
        return remote(
            self.mine(self.far + index),
            self.zgot(1),
            self.zsend.at[index],
            self.zrecv.at[1],
            {"blk": 2 * (self.far + index) + self.core},
        )

    def send_near(self):
        return remote(
            self.mine(self.partner),
            self.zgot(0),
            self.zsend.at[2],
            self.zrecv.at[0],
            {"blk": 2 * self.partner + self.core},
        )

    def add(self, mine, other):
        def group(index):
            at = span(index * 32, 32, 32)
            mine[at, :] = (mine[at, :].astype(F32) + other[at, :].astype(F32)).astype(BF16)

        loop(0, self.size // 32, group)

    def begin(self):
        for index in range(2):
            chip = self.far + index
            self.swap(chip).wait()
            self.add(self.mine(chip), self.cgot(chip))

            @pl.when(jnp.logical_not(self.inner))
            def _(index=index):
                self.lend(index).start()

        self.swap(self.partner).wait()
        self.add(self.mine(self.partner), self.cgot(self.partner))
        self.send_near().start()
        self.swap(self.chip).wait()

    def relay(self):
        @pl.when(self.inner)
        def _():
            for index in range(2):
                self.lend(index).wait_recv()
                self.add(self.mine(self.far + index), self.rgot(index))
                self.send_far(index).start()

    def end(self):
        self.send_near().wait_recv()
        self.send_far(0).wait_recv()
        mine, other = self.mine(self.chip), self.cgot(self.chip)

        def group(index):
            at = span(index * 32, 32, 32)
            value = mine[at, :].astype(F32) + other[at, :].astype(F32)
            value = value + self.zgot(0)[at, :].astype(F32) + self.zgot(1)[at, :].astype(F32)
            self.total[at, :] = value.astype(BF16)

        loop(0, self.size // 32, group)

    def left(self):
        self.send_near().wait_send()

        @pl.when(self.inner)
        def _():
            for index in range(2):
                self.send_far(index).wait_send()

        @pl.when(jnp.logical_not(self.inner))
        def _():
            for index in range(2):
                self.lend(index).wait_send()


class TileGift:
    def __init__(self, seq, n_seq, rows, src, dst, send, recv, owner_of):
        self.seq, self.n_seq, self.rows, self.src, self.dst = seq, n_seq, rows, src, dst
        self.send, self.recv, self.owner_of = send, recv, owner_of

    def place(self, other, slot):
        return self.dst.at[span(other * self.rows, self.rows, self.rows), span(slot * TILE, TILE, TILE)]

    def tile(self, index):
        return self.src.at[:, span(index * TILE, TILE, TILE)]

    def start(self, index):
        owner, slot = self.owner_of(index)
        src, dst, recv = self.tile(index), self.place(self.seq, slot), self.recv.at[slot, self.seq]

        @pl.when(owner != self.seq)
        def _():
            remote(src, dst, self.send.at[index], recv, {"seq": owner}).start()

        @pl.when(owner == self.seq)
        def _():
            pltpu.make_async_copy(src, dst, recv).start()

    def arrived(self, low, high):
        def one(slot):
            def other_one(other):
                dst, recv = self.place(other, slot), self.recv.at[slot, other]

                @pl.when(other != self.seq)
                def _():
                    remote(self.tile(0), dst, self.send.at[0], recv, {"seq": other}).wait_recv()

                @pl.when(other == self.seq)
                def _():
                    pltpu.make_async_copy(self.tile(0), dst, recv).wait()

            loop(0, self.n_seq, other_one)

        loop(low, high, one)

    def left(self, count):
        def one(index):
            owner, slot = self.owner_of(index)

            @pl.when(owner != self.seq)
            def _():
                remote(
                    self.tile(index), self.place(self.seq, slot), self.send.at[index], self.recv.at[slot, self.seq],
                    {"seq": owner},
                ).wait_send()

        loop(0, count, one)


class Spread:
    def __init__(self, seq, owner, kind, src, dst, send, recv, local, on_send, on_recv):
        self.seq, self.owner, self.kind, self.src, self.dst = seq, owner, kind, src, dst
        self.send, self.recv, self.local, self.on_send, self.on_recv = send, recv, local, on_send, on_recv
        self.half = src.shape[0] // 2

    def copy(self, bit):
        return remote(
            self.src, self.dst, self.send.at[self.kind, bit], self.recv.at[self.kind], {"seq": self.owner ^ (bit + 1)}
        )

    def onward(self, bit):
        part = self.dst.at[bit * self.half : (bit + 1) * self.half]
        return remote(
            part, part, self.on_send.at[self.kind, bit], self.on_recv.at[self.kind, bit], {"seq": self.owner ^ 3}
        )

    def own(self):
        return pltpu.make_async_copy(self.src, self.dst, self.local.at[self.kind])

    def start(self):
        @pl.when(self.seq == self.owner)
        def _():
            for bit in range(2):
                self.copy(bit).start()
            self.own().start()

    def pass_on(self):
        for bit in range(2):

            @pl.when(self.seq == self.owner ^ (bit + 1))
            def _(bit=bit):
                self.copy(bit).wait_recv()
                self.onward(bit).start()

    def finish(self):
        @pl.when(self.seq == self.owner)
        def _():
            for bit in range(2):
                self.copy(bit).wait_send()
            self.own().wait()

        for bit in range(2):

            @pl.when(self.seq == self.owner ^ (bit + 1))
            def _(bit=bit):
                self.onward(bit).wait_send()

        @pl.when(self.seq == self.owner ^ 3)
        def _():
            for bit in range(2):
                self.onward(bit).wait_recv()


def turn_over(src, dst):
    def one(index):
        at = span(index * TILE, TILE, TILE)
        dst[at, :] = src[:, at].T

    loop(0, src.shape[1] // TILE, one)


def outer_tiles(turned, rhs, part, chip, tiles, rhs_at, part_at):
    rows = span(chip * TILE, TILE, TILE)

    def tile(index):
        value = times(turned[rows, :], rhs[:, span(rhs_at + index * TILE, TILE, TILE)])
        part[rows, span(part_at + index * TILE, TILE, TILE)] = value.astype(BF16)

    loop(0, tiles, tile)


def layer_kernel(
    sizes,
    freq, tokens, first, lengths, attn_gain, ffn_gain, cot,
    h_query, h_key, h_value, h_out, h_gate, h_up, h_down,
    o_layer, o_tokens, o_first, o_gu, o_down, o_out, o_query, o_key, o_value, o_gain,
    v, sem,
):
    rows, width, ff, n_seq, n_blk, split = sizes
    v, sem = types.SimpleNamespace(**v), types.SimpleNamespace(**sem)
    docs = lengths.shape[1]
    chips = n_blk // 2
    scale = HEAD_DIM ** (-0.5)
    seq, blk = lax.axis_index("seq"), lax.axis_index("blk")
    chip_at = lax.div(blk, 2)

    def turned_chip(step):
        return lax.rem(chip_at + step, chips)

    barrier = pltpu.get_barrier_semaphore()
    for step in range(1, n_seq):
        pl.semaphore_signal(barrier, inc=1, device_id={"seq": lax.rem(seq + step, n_seq)}, device_id_type=MESH)
    for step in range(1, n_blk):
        pl.semaphore_signal(barrier, inc=1, device_id={"blk": lax.rem(blk + step, n_blk)}, device_id_type=MESH)

    def load(index, src, dst):
        copy = pltpu.make_async_copy(src, dst, sem.load.at[index])
        copy.start()
        return copy

    load_query = load(0, h_query, v.w_query)
    load_key = load(1, h_key, v.w_key)
    load_value = load(2, h_value, v.w_value)
    load_out = load(3, h_out, v.w_out)
    load_gate = load(4, h_gate, v.w_gate)
    load_up = load(5, h_up, v.w_up)
    load_down = load(6, h_down, v.w_down)

    def norm(group):
        at = span(group * GROUP, GROUP, GROUP)
        x = tokens[at, :].astype(F32)
        inv = lax.rsqrt(jnp.mean(x * x, axis=-1, keepdims=True) + EPS)
        v.normed[at, :] = (x * inv * attn_gain[...]).astype(BF16)
        v.inv_first[at, :] = jnp.broadcast_to(inv, (GROUP, LANES))

    loop(0, rows // GROUP, norm)

    def doc_start(index):
        start, end = jnp.zeros_like(index), jnp.int32(0)
        for doc in range(docs):
            end = end + lengths[0, doc]
            start = jnp.where(index >= end, end, start)
        return start

    half = HEAD_DIM // 2

    def low_half(count):
        return lax.rem(iota((count, LANES), 1), HEAD_DIM) < half

    def set_tables(start, count, cosine_ref, sine_ref):
        index = start + iota((count, LANES), 0)
        angle = (index - doc_start(index)).astype(F32) * freq[...]
        cosine_ref[...] = jnp.cos(angle)
        sine = jnp.sin(angle)
        sine_ref[...] = jnp.where(low_half(count), -sine, sine)

    def halves_changed(u):
        return jnp.where(low_half(u.shape[0]), pltpu.roll(u, LANES - half, 1), pltpu.roll(u, half, 1))

    set_tables(blk * rows, rows, v.cos, v.sin)

    def rotated(u):
        return u * v.cos[...] + halves_changed(u) * v.sin[...]

    cuts = [0]
    for tiles in split:
        cuts.append(cuts[-1] + tiles * TILE)
    wide = max(split) * TILE

    def gift(owner, kind, src, dst):
        return Gift(seq, n_seq, rows, owner, kind, src, dst, sem.xsend, sem.xrecv)

    gift_cot = gift(3, 0, cot, v.buf_a)
    gifts_two = [gift(owner, 0, v.two, v.buf_a) for owner in range(3)]
    each, hidden = split[0], ff // TILE
    gift_gu = TileGift(
        seq, n_seq, rows, v.gate_up, v.buf_b, sem.gusend, sem.gurecv,
        lambda index: (lax.div(index, each), lax.rem(index, each)),
    )
    gift_act = TileGift(seq, n_seq, rows, v.act, v.buf_b, sem.actsend, sem.actrecv, lambda index: (3, index))
    gift_att = gift(2, 2, v.att, v.buf_att)
    gift_mid = gift(2, 3, v.mid_b, v.buf_mid)
    def trade(phase, source, place):
        return Trade(blk, n_blk, phase, sem.asend, sem.arecv, source, place)

    def block_rows(ref):
        return lambda peer: ref.at[span(peer * rows, rows, rows)]

    def block_columns(ref):
        return lambda peer: ref.at[:, span(peer * LANES, LANES, LANES)]

    give_qkv = trade(0, lambda peer: v.pack.at[peer], lambda peer: v.qkv.at[:, span(peer * rows, rows, rows)])
    give_att = trade(1, block_rows(v.ob), block_columns(v.att))
    give_out = trade(2, lambda peer: v.out_pack.at[peer], block_rows(v.out_grad))
    give_grads = trade(
        3, lambda peer: v.pack.at[peer], lambda peer: v.grads.at[:, :, span(peer * LANES, LANES, LANES)]
    )

    give_tail = trade(4, lambda peer: v.tail_sum.at[peer], lambda peer: v.tail_got.at[peer])
    core = lax.rem(blk, 2)
    mate = blk + 1 - 2 * core

    def block_of(step):
        return 2 * turned_chip(step) + core

    def rows_of(block):
        return v.normed_all.at[span(block * rows, rows, rows)]

    def normed_out(step):
        return remote(
            v.normed, rows_of(blk), sem.nsend.at[step - 1], sem.nrecv.at[step - 1], {"blk": block_of(step)}
        )

    def normed_over(step):
        there = rows_of(block_of(step))
        return remote(there, there, sem.fsend.at[step], sem.frecv.at[step], {"blk": mate})

    def mates_normed(step):
        there = rows_of(2 * turned_chip(step) + 1 - core)
        return remote(there, there, sem.fsend.at[step], sem.frecv.at[step], {"blk": mate})

    pl.semaphore_wait(barrier, n_seq + n_blk - 2)
    gift_cot.start()
    own_normed = pltpu.make_async_copy(v.normed, rows_of(blk), sem.nlocal.at[0])
    own_normed.start()

    for item in (load_query, load_key, load_value):
        item.wait()

    def project(step):
        chip = turned_chip(step)
        at = span(chip * TILE, TILE, TILE)
        left = v.normed[...]
        q, k, val = times(left, v.w_query[:, at]), times(left, v.w_key[:, at]), times(left, v.w_value[:, at])
        old = first[:, at].astype(F32)
        for core in range(2):
            peer = 2 * chip + core
            cols = slice(core * LANES, (core + 1) * LANES)
            v.pack[peer, 0] = (rotated(q[:, cols]) * scale).astype(BF16)
            v.pack[peer, 1] = rotated(k[:, cols]).astype(BF16)
            v.pack[peer, 2] = (MIX * val[:, cols] + MIX * old[:, cols]).astype(BF16)
            give_qkv.start(peer)

    loop(1, chips + 1, project)

    load_down.wait()

    def act_back(tile):
        cols = span(tile * TILE, TILE, TILE)
        v.act_grad[:, cols] = back(cot[...], v.w_down[cols, :])

    loop(0, ff // TILE, act_back)

    first_head = iota((TILE, LANES), 1) < HEAD_DIM

    def stacked(values):
        return jnp.concatenate([jnp.where(first_head, values, 0.0), jnp.where(first_head, 0.0, values)], axis=0)

    def unstacked(values):
        return jnp.where(first_head, values[:TILE], values[TILE:])

    def attend(block):
        for core in range(2):
            give_qkv.arrived(2 * block + core)
        at, both = span(block * TILE, TILE, TILE), span(block * 2 * TILE, 2 * TILE, 2 * TILE)
        queries = stacked(v.qkv[0, at, :].astype(F32)).astype(BF16)
        v.q2[both, :] = queries
        v.q2_turned[:, both] = queries.T
        index = block * TILE + lax.rem(iota((2 * TILE, 1), 0), TILE)
        start = doc_start(index)
        v.top[...] = jnp.full((2 * TILE, LANES), NEG, F32)

        def scores(tile):
            cols = span(tile * TILE, TILE, TILE)
            score = back(v.q2[both, :], v.qkv[1, cols, :])
            key = tile * TILE + iota((2 * TILE, TILE), 1)
            score = jnp.where((key <= index) & (key >= start), score, NEG)
            v.score[:, cols] = score
            v.top[...] = jnp.maximum(v.top[...], jnp.maximum(score[:, :LANES], score[:, LANES:]))

        loop(0, block + 1, scores)
        top = jnp.max(v.top[...], axis=1, keepdims=True)
        v.top[...] = jnp.zeros((2 * TILE, LANES), F32)
        v.o2[...] = jnp.zeros((2 * TILE, LANES), F32)

        def weights(tile):
            cols = span(tile * TILE, TILE, TILE)
            weight = jnp.exp(v.score[:, cols] - top)
            v.top[...] += weight[:, :LANES] + weight[:, LANES:]
            weight = weight.astype(BF16)
            v.prob[both, cols] = weight
            v.o2[...] += times(weight, v.qkv[2, cols, :])

        loop(0, block + 1, weights)
        inv = 1.0 / jnp.sum(v.top[...], axis=1, keepdims=True)
        v.row[both, :] = jnp.broadcast_to(inv, (2 * TILE, LANES))
        attended = unstacked(v.o2[...] * inv)
        v.o32[at, :] = attended
        v.ob[at, :] = attended.astype(BF16)
        for core in range(2):
            give_att.start(2 * block + core)

    loop(0, chips, attend)
    loop(
        0,
        chips,
        lambda block: set_tables(
            block * TILE,
            TILE,
            v.score.at[:TILE, span(block * TILE, LANES, LANES)],
            v.score.at[:TILE, span(block * TILE + LANES, LANES, LANES)],
        ),
    )
    give_att.all_arrived()
    gift_att.start()
    normed_out(1).start()
    normed_out(3).start()

    load_out.wait()

    def middle(tile):
        cols = span(tile * TILE, TILE, TILE)
        value = tokens[:, cols].astype(F32) + times(v.att[...], v.w_out[:, cols])
        v.mid[:, cols] = value

    loop(0, width // TILE, middle)

    def norm_two(group):
        at = span(group * GROUP, GROUP, GROUP)
        x = v.mid[at, :]
        inv = lax.rsqrt(jnp.mean(x * x, axis=-1, keepdims=True) + EPS)
        v.two[at, :] = (x * inv * ffn_gain[...]).astype(BF16)
        v.inv_second[at, :] = jnp.broadcast_to(inv, (GROUP, LANES))

    loop(0, rows // GROUP, norm_two)
    for item in gifts_two:
        item.start()

    for item in (load_gate, load_up):
        item.wait()
    v.two_grad[...] = jnp.zeros((rows, width), F32)

    def feed(step):
        tile = lax.rem(split[0] + step, hidden)
        cols = span(tile * TILE, TILE, TILE)
        gate = times(v.two[...], v.w_gate[:, cols])
        up = times(v.two[...], v.w_up[:, cols])
        act_grad = v.act_grad[:, cols]
        sigma = jax.nn.sigmoid(gate)
        silu = gate * sigma
        act = (silu * up).astype(BF16)
        gate_grad = (act_grad * up * sigma * (1.0 + gate * (1.0 - sigma))).astype(BF16)
        up_grad = (act_grad * silu).astype(BF16)
        v.act[:, cols] = act
        v.gate_up[:, cols] = gate_grad
        v.gate_up[:, span(ff + tile * TILE, TILE, TILE)] = up_grad
        gift_gu.start(tile)
        gift_gu.start(hidden + tile)
        gift_act.start(tile)
        v.two_grad[...] += back(gate_grad, v.w_gate[:, cols]) + back(up_grad, v.w_up[:, cols])

    loop(0, hidden, feed)
    v.gain_rows[...] = jnp.zeros((16, width), F32)

    def norm_two_back(group):
        at = span(group * GROUP, GROUP, GROUP)
        x, grad, inv = v.mid[at, :], v.two_grad[at, :], v.inv_second[at, :1]
        term = grad * x * inv
        v.gain_rows[8:16, :] += term[:8] + term[8:]
        scaled = grad * ffn_gain[...]
        mean = jnp.mean(scaled * x, axis=-1, keepdims=True)
        value = cot[at, :].astype(F32) + inv * scaled - x * (inv * inv * inv * mean)
        v.mid_grad[at, :] = value
        v.mid_b[at, :] = value.astype(BF16)

    loop(0, rows // GROUP, norm_two_back)
    gift_mid.start()

    def out_back(step):
        chip = turned_chip(step)
        value = back(v.mid_b[...], v.w_out[span(chip * TILE, TILE, TILE), :]).astype(BF16)
        for core in range(2):
            v.out_pack[2 * chip + core] = value[:, core * LANES : (core + 1) * LANES]
            give_out.start(2 * chip + core)

    loop(1, chips + 1, out_back)

    def layer_out(tile):
        cols = span(tile * TILE, TILE, TILE)
        o_layer[:, cols] = v.mid[:, cols] + times(v.act[...], v.w_down[:, cols])

    loop(0, width // TILE, layer_out)
    own_normed.wait()
    normed_over(0).start()
    for step in (1, 3):
        normed_out(chips - step).wait_recv()
        normed_over(step).start()

    chunk, down = width // n_blk, ff // n_blk

    def sems_of(index):
        return tuple(
            item.at[index] for item in (sem.csend, sem.crecv, sem.rsend, sem.rrecv, sem.zsend, sem.zrecv)
        )

    def stack_in(ref, top, cols):
        return lambda index: ref.at[span(top + index * chunk, chunk, 32), cols]

    def square_in(ref, more, low, high):
        def place(index):
            index = index + more
            return ref.at[
                span(lax.rem(index, 2) * down, down, 32), span(lax.div(index, 2) * width + low, high - low, LANES)
            ]

        return place

    def piece(index, low, high):
        cols = slice(low, high)
        return Sum(
            blk, chunk, v.w_gate.at[:, cols], stack_in(v.w_up, 0, cols), stack_in(v.w_up, chips * chunk, cols),
            stack_in(v.w_up, (chips + 2) * chunk, cols), v.total.at[:, cols], sems_of(index),
        )

    edges = [0, each // 3, 7 * each // 9, each]
    thirds = [piece(index, edges[index] * TILE, edges[index + 1] * TILE) for index in range(3)]
    last = split[2] * TILE
    halves = [piece(0, 0, last), piece(1, last, last + width)]
    bounds = [0, width // 4, width // 2, 3 * width // 4, 7 * width // 8, width]
    fifths = [
        Sum(
            blk, down, v.w_down.at[:, low:high], square_in(v.w_up, 0, low, high), square_in(v.w_gate, 0, low, high),
            square_in(v.w_gate, 2, low, high), v.total_down.at[:, low:high], sems_of(index),
        )
        for index, (low, high) in enumerate(zip(bounds[:-1], bounds[1:]))
    ]
    first_two, third_one, fourth = seq < 2, seq == 2, seq == 3

    def spread(owner, kind, src, dst):
        return Spread(
            seq, owner, kind, src, dst, sem.gsend, sem.grecv, sem.glocal, sem.onsend, sem.onrecv
        )

    spreads = [
        [
            spread(
                owner,
                3 * owner + index,
                v.total.at[:, edges[index] * TILE : edges[index + 1] * TILE],
                o_gu.at[:, cuts[owner] + edges[index] * TILE : cuts[owner] + edges[index + 1] * TILE],
            )
            for index in range(3)
        ]
        for owner in range(2)
    ] + [
        [
            spread(2, 6, v.total.at[:, :last], o_gu.at[:, cuts[2] : cuts[3]]),
            spread(2, 7, v.total.at[:, last : last + width], o_out),
        ],
        [
            spread(3, 8 + index, v.total_down.at[:, low:high], o_down.at[:, low:high])
            for index, (low, high) in enumerate(zip(bounds[:-1], bounds[1:]))
        ],
    ]
    def products(item, turned, rhs, tiles, rhs_at, part_at):
        def one(step):
            chip = item.order(step)
            outer_tiles(turned, rhs, v.w_gate, chip, tiles, rhs_at, part_at)

        loop(0, chips, one)

    def swaps(item):
        loop(0, chips, lambda step: item.swap(item.order(step)).start())

    def gate_up_piece(index):
        gift_gu.arrived(edges[index], edges[index + 1])
        at = edges[index] * TILE
        products(thirds[index], v.turned, v.buf_b, edges[index + 1] - edges[index], at, at)

    def down_products(low, high):
        def one(step):
            index = lax.rem(split[0] + step, hidden)
            gift_act.arrived(index, index + 1)
            at = span(index * TILE, TILE, TILE)
            v.turned[:TILE, :] = v.buf_b[:, at].T
            v.w_down[at, :] = times(v.turned[:TILE, :], v.buf_a[...]).astype(BF16)

        loop(low, high, one)

    def down_swaps():
        for item in fifths:
            swaps(item)

    for owner in range(2):

        @pl.when(seq == owner)
        def _(owner=owner):
            gifts_two[owner].arrived()
            turn_over(v.buf_a, v.turned)

    @pl.when(fourth)
    def _():
        gift_cot.arrived()
        down_products(0, hidden // 4)

    give_out.all_arrived()
    normed_out(2).start()


    def prepare(block):
        at, both = span(block * TILE, TILE, TILE), span(block * 2 * TILE, 2 * TILE, 2 * TILE)
        grad = (stacked(v.out_grad[at, :].astype(F32)) * v.row[both, :]).astype(BF16)
        v.do2[both, :] = grad
        v.do2_turned[:, both] = grad.T
        attended = v.o32[at, :]
        delta = jnp.sum(grad.astype(F32) * jnp.concatenate([attended, attended], axis=0), axis=1, keepdims=True)
        v.row[both, :] = jnp.broadcast_to(delta, (2 * TILE, LANES))
        v.dq[both, :] = jnp.zeros((2 * TILE, LANES), F32)

    loop(0, chips, prepare)
    give_qkv.all_left()

    def key_block(block):
        at = span(block * TILE, TILE, TILE)
        v.dk[...] = jnp.zeros((LANES, TILE), F32)
        v.dv[...] = jnp.zeros((LANES, TILE), F32)

        def query_block(other):
            both = span(other * 2 * TILE, 2 * TILE, 2 * TILE)
            prob = v.prob[both, at]
            grad = back(v.do2[both, :], v.qkv[2, at, :])
            score_grad = (prob.astype(F32) * (grad - v.row[both, :1])).astype(BF16)
            v.dk[...] += times(v.q2_turned[:, both], score_grad)
            v.dv[...] += times(v.do2_turned[:, both], prob)
            v.dq[both, :] += times(score_grad, v.qkv[1, at, :])

        loop(block, chips, query_block)
        cosine = v.score[:TILE, span(block * TILE, LANES, LANES)]
        sine = v.score[:TILE, span(block * TILE + LANES, LANES, LANES)]

        def rotated_back(u):
            u = u.astype(BF16).astype(F32)
            return (u * cosine - halves_changed(u) * sine).astype(BF16)

        dq = rotated_back(unstacked(v.dq[span(block * 2 * TILE, 2 * TILE, 2 * TILE), :]) * scale)
        dk = rotated_back(v.dk[...].T)
        dv = (MIX * v.dv[...].T.astype(BF16).astype(F32)).astype(BF16)
        for index, value in enumerate((dq, dk, dv)):
            v.heads_grad[at, index * LANES : (index + 1) * LANES] = value
            for half_at in range(2):
                v.pack[2 * block + half_at, index] = value[half_at * rows : (half_at + 1) * rows]
        for half_at in range(2):
            give_grads.start(2 * block + half_at)

    loop(0, chips, key_block)

    def when(which, *steps):
        @pl.when(which)
        def _():
            for step in steps:
                step()

    def ended(item, goes):
        def step():
            item.end()
            for other in goes:
                other.start()

        return step

    def first_half():
        gifts_two[2].arrived()
        turn_over(v.buf_a, v.turned)
        gift_gu.arrived(0, split[2])
        products(halves[0], v.turned, v.buf_b, split[2], 0, 0)
        swaps(halves[0])
        halves[0].begin()

    def second_half():
        gift_att.arrived()
        gift_mid.arrived()
        turn_over(v.buf_att, v.turned)
        products(halves[1], v.turned, v.buf_mid, width // TILE, 0, last)
        swaps(halves[1])

    def gate_up_gone(index):
        gate_up_piece(index)
        swaps(thirds[index])

    when(first_two, lambda: gate_up_gone(0), thirds[0].begin, lambda: gate_up_gone(1), thirds[1].begin)
    when(third_one, first_half)
    when(fourth, lambda: down_products(hidden // 4, hidden), down_swaps, fifths[0].begin, fifths[1].begin)

    normed_out(2).wait_recv()
    normed_over(2).start()
    for step in range(chips):
        mates_normed(step).wait_recv()

    def project_back(index):
        value = outer(v.normed_all[:, span(index * TILE, TILE, TILE)], v.heads_grad[...]).astype(BF16)
        v.tail_part[2 * index] = value[:LANES]
        v.tail_part[2 * index + 1] = value[LANES:]

    loop(0, width // TILE, project_back)
    quarter = LANES // n_seq

    def tail_share(step):
        other = lax.rem(seq + step, n_seq)
        return remote(
            v.tail_part.at[:, span(other * quarter, quarter, quarter)],
            v.tail_shares.at[step - 1],
            sem.qsend.at[step - 1],
            sem.qrecv.at[step - 1],
            {"seq": other},
        )

    for step in range(1, n_seq):
        tail_share(step).start()

    when(first_two, thirds[0].relay, lambda: gate_up_gone(2))
    when(third_one, second_half)

    def tail_add(index):
        value = v.tail_part[index, span(seq * quarter, quarter, quarter), :].astype(F32)
        for step in range(1, n_seq):
            value = value + v.tail_shares[step - 1, index].astype(F32)
        v.tail_sum[index] = value.astype(BF16)
        give_tail.start(index)

    for step in range(1, n_seq):
        tail_share(step).wait()
    loop(0, n_blk, tail_add)
    when(first_two, thirds[2].begin)
    when(third_one, halves[1].begin)

    give_grads.all_arrived()

    def gone(index, *owners):
        return [spreads[owner][index] for owner in owners]

    when(first_two, thirds[1].relay, ended(thirds[0], []))
    for item in gone(0, 0, 1):
        item.start()
    when(fourth, fifths[0].relay, fifths[2].begin)

    def normed_back(tile):
        at = span(tile * TILE, TILE, TILE)
        o_tokens[:, at] = (
            back(v.grads[0], v.w_query[at, :])
            + back(v.grads[1], v.w_key[at, :])
            + back(v.grads[2], v.w_value[at, :])
        )

    loop(0, width // TILE, normed_back)
    o_first[...] = v.grads[2].astype(F32)

    def norm_back(group):
        at = span(group * GROUP, GROUP, GROUP)
        x, grad, inv = tokens[at, :].astype(F32), o_tokens[at, :], v.inv_first[at, :1]
        term = grad * x * inv
        v.gain_rows[0:8, :] += term[:8] + term[8:]
        scaled = grad * attn_gain[...]
        mean = jnp.mean(scaled * x, axis=-1, keepdims=True)
        o_tokens[at, :] = v.mid_grad[at, :] + inv * scaled - x * (inv * inv * inv * mean)

    loop(0, rows // GROUP, norm_back)

    for peer in range(n_blk):
        v.gains[peer] = v.gain_rows[:, peer * LANES : (peer + 1) * LANES]

    def gain_copy(step):
        other = lax.rem(blk + step, n_blk)
        return remote(
            v.gains.at[other], v.gain_got.at[step - 1], sem.hsend.at[step - 1], sem.hrecv.at[step - 1],
            {"blk": other},
        )

    for step in range(1, n_blk):
        gain_copy(step).start()
    when(fourth, ended(fifths[0], gone(0, 3)), fifths[1].relay, fifths[3].begin, fifths[4].begin)

    when(first_two, ended(thirds[1], gone(1, 0, 1)))
    when(third_one, halves[0].relay, ended(halves[0], gone(0, 2)))
    when(fourth, ended(fifths[1], gone(1, 3)))

    give_tail.all_arrived()
    for index in range(3):
        for peer in range(n_blk):
            v.tail_done[index, :, peer * LANES : (peer + 1) * LANES] = v.tail_got[
                peer, :, index * LANES : (index + 1) * LANES
            ]

    def tail_spread(index, step, owner):
        at = span(owner * quarter, quarter, quarter)
        return remote(
            v.tail_done.at[index],
            (o_query, o_key, o_value)[index].at[at],
            sem.tsend.at[index, step - 1],
            sem.trecv.at[index, owner],
            {"seq": lax.rem(seq + step, n_seq)},
        )

    def tail_own(index):
        at = span(seq * quarter, quarter, quarter)
        return pltpu.make_async_copy(
            v.tail_done.at[index], (o_query, o_key, o_value)[index].at[at], sem.trecv.at[index, seq]
        )

    for index in range(3):
        tail_own(index).start()
        for step in range(1, n_seq):
            tail_spread(index, step, seq).start()

    def pass_on(*items):
        for item in items:
            item.pass_on()

    pass_on(*gone(0, 0, 1, 3))
    when(first_two, thirds[2].relay, ended(thirds[2], gone(2, 0, 1)))
    when(third_one, halves[1].relay, ended(halves[1], gone(1, 2)))
    when(fourth, fifths[2].relay, fifths[3].relay, ended(fifths[2], gone(2, 3)))
    when(fourth, fifths[4].relay, ended(fifths[3], gone(3, 3)), ended(fifths[4], gone(4, 3)))
    pass_on(*gone(0, 2), *gone(1, 3, 0, 1))
    value = v.gains[blk]
    for step in range(1, n_blk):
        gain_copy(step).wait()
        value = value + v.gain_got[step - 1]
    v.gain_sum[seq] = value
    for step in range(1, n_seq):
        other = lax.rem(seq + step, n_seq)
        mine = v.gain_sum.at[seq]
        remote(mine, mine, sem.isend.at[step - 1], sem.irecv.at[seq], {"seq": other}).start()

    pass_on(*gone(1, 2), *gone(2, 3, 0, 1), *gone(3, 3), *gone(4, 3))

    for step in range(1, n_seq):
        other = lax.rem(seq + step, n_seq)
        theirs = v.gain_sum.at[other]
        remote(theirs, theirs, sem.isend.at[step - 1], sem.irecv.at[other], {"seq": other}).wait()
    value = v.gain_sum[0]
    for group in range(1, n_seq):
        value = value + v.gain_sum[group]
    o_gain[0:8, :] = jnp.broadcast_to(jnp.sum(value[:8], axis=0, keepdims=True), (8, LANES))
    o_gain[8:16, :] = jnp.broadcast_to(jnp.sum(value[8:], axis=0, keepdims=True), (8, LANES))

    for index in range(3):
        tail_own(index).wait()
        for step in range(1, n_seq):
            tail_spread(index, step, seq).wait_send()
            tail_spread(index, step, lax.rem(seq + step, n_seq)).wait_recv()
    for item in sum(spreads, []):
        item.finish()
    for item in [gift_cot, gift_att, gift_mid] + gifts_two:
        item.left()
    gift_gu.left(2 * hidden)
    gift_act.left(hidden)
    for item in (give_att, give_out, give_grads, give_tail):
        item.all_left()
    for step in range(chips):
        normed_over(step).wait_send()
        if step:
            normed_out(step).wait_send()

    @pl.when(first_two)
    def _():
        for item in thirds:
            item.left()

    @pl.when(third_one)
    def _():
        for item in halves:
            item.left()

    @pl.when(fourth)
    def _():
        for item in fifths:
            item.left()


def finish_kernel(
    layer, tokens, first, gu, down, out, query, key, value, gain,
    o_layer, o_tokens, o_first, o_gain, o_gain_two, o_query, o_key, o_value, o_out, o_gate, o_up, o_down,
    kept, small, large, sem_kept_in, sem_kept_out, sem_in, sem_out,
):
    kept_in = [
        pltpu.make_async_copy(src, kept[index], sem_kept_in.at[index])
        for index, src in enumerate((layer, tokens, first))
    ]
    kept_out = [
        pltpu.make_async_copy(kept[index], dst, sem_kept_out.at[index])
        for index, dst in enumerate((o_layer, o_tokens, o_first))
    ]
    ff = o_gate.shape[1]
    sources = [query, key, value, out, down, gu.at[:, :ff], gu.at[:, ff:]]
    targets = [o_query, o_key, o_value, o_out, o_down, o_gate, o_up]
    loads = [pltpu.make_async_copy(src, small[index], sem_in.at[index]) for index, src in enumerate(sources)]
    stores = [pltpu.make_async_copy(large[index], dst, sem_out.at[index]) for index, dst in enumerate(targets)]
    for item in loads + kept_in:
        item.start()
    for index in range(len(sources)):
        loads[index].wait()

        def group(step, index=index):
            at = span(step * GROUP, GROUP, GROUP)
            large[index][at, :] = small[index][at, :].astype(F32)

        loop(0, targets[index].shape[0] // GROUP, group)
        stores[index].start()
    for coming, going in zip(kept_in, kept_out):
        coming.wait()
        going.start()
    o_gain[...] = gain[0:1, :]
    o_gain_two[...] = gain[8:9, :]
    for item in stores + kept_out:
        item.wait()


def finish(layer, tokens, first, gu, down, out, query, key, value, gain):
    hbm, vmem = pl.BlockSpec(memory_space=pl.ANY), pl.BlockSpec(memory_space=pltpu.VMEM)
    shape = jax.ShapeDtypeStruct
    ff = gu.shape[1] // 2
    dims = [query.shape, key.shape, value.shape, out.shape, down.shape, (gu.shape[0], ff), (gu.shape[0], ff)]
    dma = pltpu.SemaphoreType.DMA
    results = pl.pallas_call(
        finish_kernel,
        out_shape=tuple(
            shape(each, F32)
            for each in (
                layer.shape, tokens.shape, first.shape, (1, LANES), (1, LANES), dims[0], dims[1], dims[2], dims[3], dims[5], dims[6], dims[4]
            )
        ),
        in_specs=[hbm] * 9 + [vmem],
        out_specs=(hbm,) * 3 + (vmem,) * 2 + (hbm,) * 7,
        scratch_shapes=(
            [pltpu.VMEM(each.shape, F32) for each in (layer, tokens, first)],
            [pltpu.VMEM(each, BF16) for each in dims],
            [pltpu.VMEM(each, F32) for each in dims],
            dma((3,)), dma((3,)), dma((7,)), dma((7,)),
        ),
        compiler_params=pltpu.CompilerParams(vmem_limit_bytes=63 * 1024 * 1024),
        name="finish",
    )(layer, tokens, first, gu, down, out, query, key, value, gain)
    return results[:3] + (results[3][0],) + results[5:9] + (results[4][0],) + results[9:]


def tile_split(width, ff):
    tiles, more = 2 * ff // TILE, width // TILE
    each = -(-(tiles + more) // 3)
    return (each, each, tiles - 2 * each)


def fits(n_seq, n_blk, rows, width, ff):
    return (
        n_seq == 4
        and n_blk % 2 == 0
        and n_blk * LANES == width
        and rows == LANES
        and ff % TILE == 0
        and (ff // n_blk) % 32 == 0
        and 2 * (ff // n_blk) <= width
        and n_blk == 8
        and width == n_seq * TILE
    )


def local_fast(
    n_seq,
    n_blk,
    tokens,
    first_values,
    doc_lengths,
    attn_gain,
    query_weight,
    key_weight,
    value_weight,
    out_weight,
    ffn_gain,
    gate_weight,
    up_weight,
    down_weight,
    cotangent,
):
    rows, width = tokens.shape
    ff = gate_weight.shape[1]
    split = tile_split(width, ff)
    sizes = (rows, width, ff, n_seq, n_blk, split)
    half = HEAD_DIM // 2
    freq = THETA ** (-(np.arange(half) * 2.0 / HEAD_DIM))
    freq = np.tile(freq, LANES // half)[None, :].astype(np.float32)
    wide = max(split) * TILE
    chunk, down, chips = width // n_blk, ff // n_blk, n_blk // 2
    all_rows, group = n_seq * rows, n_blk * rows
    vmem = pl.BlockSpec(memory_space=pltpu.VMEM)
    hbm = pl.BlockSpec(memory_space=pl.ANY)
    smem = pl.BlockSpec(memory_space=pltpu.SMEM)
    shape = jax.ShapeDtypeStruct

    def half_type(*dims):
        return pltpu.VMEM(dims, BF16)

    def full_type(*dims):
        return pltpu.VMEM(dims, F32)

    scratch = dict(
        w_query=half_type(width, width), w_key=half_type(width, width), w_value=half_type(width, width),
        w_out=half_type(width, width), w_gate=half_type(width, ff), w_up=half_type(width, ff),
        w_down=half_type(ff, width),
        normed=half_type(rows, width), inv_first=full_type(rows, LANES), inv_second=full_type(rows, LANES),
        cos=full_type(rows, LANES), sin=full_type(rows, LANES),
        pack=half_type(n_blk, 3, rows, LANES), qkv=half_type(3, group, LANES),
        q2=half_type(2 * group, LANES), do2=half_type(2 * group, LANES), prob=half_type(2 * group, group),
        score=full_type(2 * TILE, group), top=full_type(2 * TILE, LANES), o2=full_type(2 * TILE, LANES),
        row=full_type(2 * group, LANES), o32=full_type(group, LANES), ob=half_type(group, LANES),
        dq=full_type(2 * group, LANES), dk=full_type(LANES, TILE), dv=full_type(LANES, TILE),
        q2_turned=half_type(LANES, 2 * group), do2_turned=half_type(LANES, 2 * group),
        att=half_type(rows, width), mid=full_type(rows, width), two=half_type(rows, width),
        act=half_type(rows, ff), act_grad=full_type(rows, ff), gate_up=half_type(rows, 2 * ff), two_grad=full_type(rows, width),
        mid_grad=full_type(rows, width), mid_b=half_type(rows, width),
        out_pack=half_type(n_blk, rows, LANES), out_grad=half_type(group, LANES),
        grads=half_type(3, rows, width),
        buf_a=half_type(all_rows, width), buf_b=half_type(all_rows, ff), buf_att=half_type(all_rows, width),
        buf_mid=half_type(all_rows, width), normed_all=half_type(group, width), heads_grad=half_type(group, 3 * LANES),
        tail_part=half_type(n_blk, chunk, 3 * LANES), tail_shares=half_type(n_seq - 1, n_blk, chunk // n_seq, 3 * LANES),
        tail_sum=half_type(n_blk, chunk // n_seq, 3 * LANES), tail_got=half_type(n_blk, chunk // n_seq, 3 * LANES),
        tail_done=half_type(3, chunk // n_seq, width),
        turned=half_type(width, all_rows),
        total=half_type(chunk, wide), total_down=half_type(down, width),
        gain_rows=full_type(16, width), gains=full_type(n_blk, 16, LANES), gain_got=full_type(n_blk - 1, 16, LANES),
        gain_sum=full_type(n_seq, 16, LANES),
    )
    dma = pltpu.SemaphoreType.DMA
    sems = dict(
        load=dma((7,)), asend=dma((5, n_blk)), arecv=dma((5, n_blk)), xsend=dma((4, n_seq)), xrecv=dma((4, n_seq)),
        gusend=dma((2 * ff // TILE,)), gurecv=dma((split[0], n_seq)), actsend=dma((ff // TILE,)),
        actrecv=dma((ff // TILE, n_seq)),
        csend=dma((5, chips)), crecv=dma((5, chips)), rsend=dma((5, 2)), rrecv=dma((5, 2)), zsend=dma((5, 3)),
        zrecv=dma((5, 2)), gsend=dma((13, 2)), grecv=dma((13,)), glocal=dma((13,)), onsend=dma((13, 2)), onrecv=dma((13, 2)),
        nsend=dma((chips - 1,)), nrecv=dma((chips - 1,)), fsend=dma((chips,)), frecv=dma((chips,)), nlocal=dma((1,)),
        qsend=dma((n_seq - 1,)), qrecv=dma((n_seq - 1,)), tsend=dma((3, n_seq - 1)), trecv=dma((3, n_seq)),
        hsend=dma((n_blk - 1,)), hrecv=dma((n_blk - 1,)), isend=dma((n_seq - 1,)), irecv=dma((n_seq,)),
    )
    layer, grad_tokens, grad_first, out_gu, out_down, out_out, out_query, out_key, out_value, out_gain = pl.pallas_call(
        functools.partial(layer_kernel, sizes),
        out_shape=(
            shape((rows, width), F32),
            shape((rows, width), F32),
            shape((rows, width), F32),
            shape((chunk, 2 * ff), BF16),
            shape((down, width), BF16),
            shape((chunk, width), BF16),
            shape((chunk, width), BF16),
            shape((chunk, width), BF16),
            shape((chunk, width), BF16),
            shape((16, LANES), F32),
        ),
        in_specs=[vmem, vmem, vmem, smem, vmem, vmem, vmem] + [hbm] * 7,
        out_specs=(vmem, vmem, vmem) + (hbm,) * 6 + (vmem,),
        scratch_shapes=(scratch, sems),
        compiler_params=pltpu.CompilerParams(
            collective_id=0, has_side_effects=True, vmem_limit_bytes=63 * 1024 * 1024
        ),
        name="layer",
    )(
        freq, tokens, first_values, doc_lengths, attn_gain[None, :], ffn_gain[None, :], cotangent,
        query_weight, key_weight, value_weight, out_weight, gate_weight, up_weight, down_weight,
    )
    return finish(layer, grad_tokens, grad_first, out_gu, out_down, out_out, out_query, out_key, out_value, out_gain)


def local(
    tokens,
    first_values,
    doc_lengths,
    attn_gain,
    query_weight,
    key_weight,
    value_weight,
    out_weight,
    ffn_gain,
    gate_weight,
    up_weight,
    down_weight,
    cotangent,
):
    rows, width = tokens.shape
    heads = width // HEAD_DIM
    scale = HEAD_DIM ** (-0.5)
    shape3 = (rows, heads, HEAD_DIM)
    my_start = lax.axis_index("blk") * rows
    my_index = my_start + jnp.arange(rows, dtype=jnp.int32)
    my_doc, my_pos = doc_layout(doc_lengths, my_index)
    cosine, sine = tables(my_pos)
    source = tokens.astype(jnp.float32)
    inv_first = lax.rsqrt(jnp.mean(source * source, axis=-1, keepdims=True) + EPS)
    normed = (source * inv_first * attn_gain).astype(jnp.bfloat16)
    query_pre = jnp.dot(normed, query_weight, preferred_element_type=jnp.float32)
    key_pre = jnp.dot(normed, key_weight, preferred_element_type=jnp.float32)
    value_pre = jnp.dot(normed, value_weight, preferred_element_type=jnp.float32)
    queries = rotate(query_pre.reshape(shape3), cosine, sine).astype(jnp.bfloat16)
    keys = rotate(key_pre.reshape(shape3), cosine, sine).astype(jnp.bfloat16).reshape(rows, width)
    mixed = (MIX * value_pre + MIX * first_values.astype(jnp.float32)).astype(jnp.bfloat16)
    keys_local = keys.reshape(shape3)
    mixed_local = mixed.reshape(shape3)

    def allowed_mask(query_index, query_doc, key_index, key_doc):
        return (query_doc[:, None] == key_doc[None, :]) & (
            key_index[None, :] <= query_index[:, None]
        )

    def forward_step(state, pieces, start):
        count = pieces[0].shape[0]
        keys_piece = pieces[0].reshape(count, heads, HEAD_DIM)
        values_piece = pieces[1].reshape(count, heads, HEAD_DIM)
        key_index = start + jnp.arange(count, dtype=jnp.int32)

        def forward_compute(state):
            high, total, accum = state
            key_doc, unused = doc_layout(doc_lengths, key_index)
            allowed = allowed_mask(my_index, my_doc, key_index, key_doc)[None]
            score = (
                jnp.einsum("qhd,khd->hqk", queries, keys_piece, preferred_element_type=jnp.float32)
                * scale
            )
            score = jnp.where(allowed, score, NEG)
            new_high = jnp.maximum(high, jnp.max(score, axis=-1))
            weight = jnp.where(allowed, jnp.exp(score - new_high[:, :, None]), 0.0)
            factor = jnp.exp(high - new_high)
            total = total * factor + jnp.sum(weight, axis=-1)
            accum = accum * factor.T[:, :, None] + jnp.einsum(
                "hqk,khd->qhd",
                weight.astype(jnp.bfloat16),
                values_piece,
                preferred_element_type=jnp.float32,
            )
            return (new_high, total, accum)

        return lax.cond(start <= my_index[-1], forward_compute, lambda kept: kept, state)

    def query_grad_step(grad_q, pieces, start):
        count = pieces[0].shape[0]
        keys_piece = pieces[0].reshape(count, heads, HEAD_DIM)
        values_piece = pieces[1].reshape(count, heads, HEAD_DIM)
        key_index = start + jnp.arange(count, dtype=jnp.int32)

        def query_compute(grad_q):
            key_doc, unused = doc_layout(doc_lengths, key_index)
            allowed = allowed_mask(my_index, my_doc, key_index, key_doc)[None]
            score = (
                jnp.einsum("qhd,khd->hqk", queries, keys_piece, preferred_element_type=jnp.float32)
                * scale
            )
            prob = jnp.where(allowed, jnp.exp(score - logsum[:, :, None]), 0.0)
            prob_grad = jnp.einsum(
                "qhd,khd->hqk", outgrad_local, values_piece, preferred_element_type=jnp.float32
            )
            score_grad = (prob * (prob_grad - delta[:, :, None])).astype(jnp.bfloat16)
            return (
                grad_q
                + jnp.einsum(
                    "hqk,khd->qhd", score_grad, keys_piece, preferred_element_type=jnp.float32
                )
                * scale
            )

        return lax.cond(start <= my_index[-1], query_compute, lambda kept: kept, grad_q)

    init = (
        jnp.full((heads, rows), NEG, jnp.float32),
        jnp.zeros((heads, rows), jnp.float32),
        jnp.zeros(shape3, jnp.float32),
    )
    state = by_blocks(
        forward_step,
        init,
        (
            lax.all_gather(keys, "blk", axis=0, tiled=True),
            lax.all_gather(mixed, "blk", axis=0, tiled=True),
        ),
        jnp.int32(0),
    )
    high, total, accum = state
    logsum = high + jnp.log(total)
    attended = accum / total.T[:, :, None]
    attended_b = attended.astype(jnp.bfloat16).reshape(rows, width)
    mid = source + jnp.dot(attended_b, out_weight, preferred_element_type=jnp.float32)
    inv_second = lax.rsqrt(jnp.mean(mid * mid, axis=-1, keepdims=True) + EPS)
    normed_two = (mid * inv_second * ffn_gain).astype(jnp.bfloat16)
    gate = jnp.dot(normed_two, gate_weight, preferred_element_type=jnp.float32)
    up = jnp.dot(normed_two, up_weight, preferred_element_type=jnp.float32)
    act = (jax.nn.silu(gate) * up).astype(jnp.bfloat16)
    layer_output = mid + jnp.dot(act, down_weight, preferred_element_type=jnp.float32)
    cot_float = cotangent.astype(jnp.float32)
    grad_down = outer(act, cotangent)
    act_grad = back(cotangent, down_weight)
    sigma = jax.nn.sigmoid(gate)
    gate_grad = (act_grad * up * sigma * (1.0 + gate * (1.0 - sigma))).astype(jnp.bfloat16)
    up_grad = (act_grad * gate * sigma).astype(jnp.bfloat16)
    grad_gate = outer(normed_two, gate_grad)
    grad_up = outer(normed_two, up_grad)
    normed_two_grad = back(gate_grad, gate_weight) + back(up_grad, up_weight)
    grad_ffn_gain = jnp.sum(normed_two_grad * mid * inv_second, axis=0)
    scaled_two = normed_two_grad * ffn_gain
    mid_grad = (
        cot_float
        + inv_second * scaled_two
        - mid * inv_second**3 * jnp.mean(scaled_two * mid, axis=-1, keepdims=True)
    )
    mid_grad_b = mid_grad.astype(jnp.bfloat16)
    grad_out_weight = outer(attended_b, mid_grad_b)
    attended_grad = back(mid_grad_b, out_weight).astype(jnp.bfloat16)
    outgrad_local = attended_grad.reshape(shape3)
    delta = jnp.sum(outgrad_local.astype(jnp.float32) * attended, axis=-1).T
    zeros3 = jnp.zeros(shape3, jnp.float32)
    grad_q = by_blocks(
        query_grad_step,
        zeros3,
        (
            lax.all_gather(keys, "blk", axis=0, tiled=True),
            lax.all_gather(mixed, "blk", axis=0, tiled=True),
        ),
        jnp.int32(0),
    )
    all_logsum, all_delta = (
        lax.all_gather(logsum.T, "blk", axis=0, tiled=True),
        lax.all_gather(delta.T, "blk", axis=0, tiled=True),
    )

    def key_grad_step(state, pieces, start):
        count = pieces[0].shape[0]
        query_piece = pieces[0].reshape(count, heads, HEAD_DIM)
        outgrad_piece = pieces[1].reshape(count, heads, HEAD_DIM)
        query_index = start + jnp.arange(count, dtype=jnp.int32)

        def key_compute(state):
            grad_k, grad_v = state
            logsum_piece = lax.dynamic_slice_in_dim(all_logsum, start, count, 0).T
            delta_piece = lax.dynamic_slice_in_dim(all_delta, start, count, 0).T
            query_doc, unused = doc_layout(doc_lengths, query_index)
            allowed = allowed_mask(query_index, query_doc, my_index, my_doc)[None]
            score = (
                jnp.einsum(
                    "qhd,khd->hqk", query_piece, keys_local, preferred_element_type=jnp.float32
                )
                * scale
            )
            prob = jnp.where(allowed, jnp.exp(score - logsum_piece[:, :, None]), 0.0)
            grad_v = grad_v + jnp.einsum(
                "hqk,qhd->khd",
                prob.astype(jnp.bfloat16),
                outgrad_piece,
                preferred_element_type=jnp.float32,
            )
            prob_grad = jnp.einsum(
                "qhd,khd->hqk", outgrad_piece, mixed_local, preferred_element_type=jnp.float32
            )
            score_grad = (prob * (prob_grad - delta_piece[:, :, None])).astype(jnp.bfloat16)
            grad_k = (
                grad_k
                + jnp.einsum(
                    "hqk,qhd->khd", score_grad, query_piece, preferred_element_type=jnp.float32
                )
                * scale
            )
            return (grad_k, grad_v)

        return lax.cond(query_index[-1] >= my_start, key_compute, lambda kept: kept, state)

    grad_k, grad_v = by_blocks(
        key_grad_step,
        (zeros3, zeros3),
        (
            lax.all_gather(queries.reshape(rows, width), "blk", axis=0, tiled=True),
            lax.all_gather(attended_grad, "blk", axis=0, tiled=True),
        ),
        jnp.int32(0),
    )
    queries_grad = grad_q.astype(jnp.bfloat16)
    keys_grad = grad_k.astype(jnp.bfloat16)
    mixed_grad = grad_v.astype(jnp.bfloat16).reshape(rows, width)
    q_pre_grad = (
        rotate(queries_grad.astype(jnp.float32), cosine, -sine)
        .astype(jnp.bfloat16)
        .reshape(rows, width)
    )
    k_pre_grad = (
        rotate(keys_grad.astype(jnp.float32), cosine, -sine)
        .astype(jnp.bfloat16)
        .reshape(rows, width)
    )
    grad_first = MIX * mixed_grad.astype(jnp.float32)
    value_grad = grad_first.astype(jnp.bfloat16)
    grad_query = outer(normed, q_pre_grad)
    grad_key = outer(normed, k_pre_grad)
    grad_value = outer(normed, value_grad)
    normed_grad = (
        back(q_pre_grad, query_weight)
        + back(k_pre_grad, key_weight)
        + back(value_grad, value_weight)
    )
    grad_attn_gain = jnp.sum(normed_grad * source * inv_first, axis=0)
    scaled_one = normed_grad * attn_gain
    grad_tokens = (
        mid_grad
        + inv_first * scaled_one
        - source * inv_first**3 * jnp.mean(scaled_one * source, axis=-1, keepdims=True)
    )
    summed = (
        lax.psum_scatter(grad_attn_gain, "blk", scatter_dimension=0, tiled=True),
        lax.psum_scatter(grad_query, "blk", scatter_dimension=0, tiled=True),
        lax.psum_scatter(grad_key, "blk", scatter_dimension=0, tiled=True),
        lax.psum_scatter(grad_value, "blk", scatter_dimension=0, tiled=True),
        lax.psum_scatter(grad_out_weight, "blk", scatter_dimension=0, tiled=True),
        lax.psum_scatter(grad_ffn_gain, "blk", scatter_dimension=0, tiled=True),
        lax.psum_scatter(grad_gate, "blk", scatter_dimension=0, tiled=True),
        lax.psum_scatter(grad_up, "blk", scatter_dimension=0, tiled=True),
        lax.psum_scatter(grad_down, "blk", scatter_dimension=0, tiled=True),
    )
    summed = (
        lax.psum(summed[0].astype(jnp.bfloat16), "seq").astype(jnp.float32),
        lax.psum(summed[1].astype(jnp.bfloat16), "seq").astype(jnp.float32),
        lax.psum(summed[2].astype(jnp.bfloat16), "seq").astype(jnp.float32),
        lax.psum(summed[3].astype(jnp.bfloat16), "seq").astype(jnp.float32),
        lax.psum(summed[4].astype(jnp.bfloat16), "seq").astype(jnp.float32),
        lax.psum(summed[5].astype(jnp.bfloat16), "seq").astype(jnp.float32),
        lax.psum(summed[6].astype(jnp.bfloat16), "seq").astype(jnp.float32),
        lax.psum(summed[7].astype(jnp.bfloat16), "seq").astype(jnp.float32),
        lax.psum(summed[8].astype(jnp.bfloat16), "seq").astype(jnp.float32),
    )
    return (
        layer_output,
        grad_tokens,
        grad_first,
        summed[0],
        summed[1],
        summed[2],
        summed[3],
        summed[4],
        summed[5],
        summed[6],
        summed[7],
        summed[8],
    )


def solution(mesh):
    n_seq, n_blk = mesh.shape["seq"], mesh.shape["blk"]

    def chosen(*args):
        rows, width = args[0].shape
        if fits(n_seq, n_blk, rows, width, args[9].shape[1]):
            return local_fast(n_seq, n_blk, *args)
        return local(*args)

    return jax.shard_map(
        chosen,
        mesh=mesh,
        in_specs=(
            P(("seq", "blk"), None),
            P(("seq", "blk"), None),
            P("seq", None),
            P(),
            P(),
            P(),
            P(),
            P(),
            P(),
            P(),
            P(),
            P(),
            P(("seq", "blk"), None),
        ),
        out_specs=(
            P(("seq", "blk"), None),
            P(("seq", "blk"), None),
            P(("seq", "blk"), None),
            P("blk"),
            P("blk", None),
            P("blk", None),
            P("blk", None),
            P("blk", None),
            P("blk"),
            P("blk", None),
            P("blk", None),
            P("blk", None),
        ),
        check_vma=False,
    )
```

```python
import functools
import math
import types

import jax
import jax.numpy as jnp
import numpy as np
from jax import lax
from jax.experimental import pallas as pl
from jax.experimental.pallas import tpu as pltpu
from jax.sharding import PartitionSpec as P

HEAD_DIM = 64


EPS = 1e-05
THETA = 10000.0
MIX = 0.5
NEG = -1e30


def doc_layout(lengths, index):
    ends = jnp.cumsum(lengths, axis=-1)
    past = (index[:, None] >= ends).astype(jnp.int32)
    return (jnp.sum(past, axis=1), index - jnp.sum(past * lengths, axis=1))


def tables(position):
    half = HEAD_DIM // 2
    freq = THETA ** (-(jnp.arange(half).astype(jnp.float32) * 2.0 / HEAD_DIM))
    angle = position.astype(jnp.float32)[:, None] * freq[None, :]
    return (jnp.cos(angle)[:, None, :], jnp.sin(angle)[:, None, :])


def rotate(values, cosine, sine):
    half = values.shape[-1] // 2
    first = values[..., :half]
    second = values[..., half:]
    return jnp.concatenate(
        [first * cosine - second * sine, second * cosine + first * sine], axis=-1
    )


def by_blocks(step, carry, pieces, start):
    rows = pieces[0].shape[0]
    size = math.gcd(rows, 1024)
    count = rows // size
    if count == 1:
        return step(carry, pieces, start)
    stacked = tuple((piece.reshape((count, size) + piece.shape[1:]) for piece in pieces))
    offsets = jnp.arange(count, dtype=jnp.int32) * size

    def turn(state, inputs):
        return (step(state, inputs[1], start + inputs[0]), None)

    result, unused = lax.scan(turn, carry, (offsets, stacked))
    return result


def outer(left, right):
    return lax.dot_general(
        left, right, (((0,), (0,)), ((), ())), preferred_element_type=jnp.float32
    )


def back(left, weight):
    return lax.dot_general(
        left, weight, (((1,), (1,)), ((), ())), preferred_element_type=jnp.float32
    )


TILE = 256
LANES = 128
GROUP = 16
MESH = pl.DeviceIdType.MESH
F32 = jnp.float32
BF16 = jnp.bfloat16


def remote(src, dst, send, recv, where):
    return pltpu.make_async_remote_copy(
        src_ref=src, dst_ref=dst, send_sem=send, recv_sem=recv, device_id=where, device_id_type=MESH
    )


def span(start, size, unit):
    return pl.ds(pl.multiple_of(start, unit), size)


def times(left, right):
    return jnp.dot(left, right, preferred_element_type=F32)


def iota(shape, dim):
    return lax.broadcasted_iota(jnp.int32, shape, dim)


def loop(low, high, body):
    def turn(index, unused):
        body(index)
        return unused

    lax.fori_loop(low, high, turn, 0)


class Trade:
    def __init__(self, blk, n_blk, phase, send, recv, source, place):
        self.blk, self.n_blk = blk, n_blk
        self.send, self.recv = send.at[phase], recv.at[phase]
        self.source, self.place = source, place

    def start(self, peer):
        src, dst = self.source(peer), self.place(self.blk)

        @pl.when(peer != self.blk)
        def _():
            remote(src, dst, self.send.at[peer], self.recv.at[self.blk], {"blk": peer}).start()

        @pl.when(peer == self.blk)
        def _():
            pltpu.make_async_copy(src, dst, self.recv.at[self.blk]).start()

    def arrived(self, peer):
        src, dst = self.source(peer), self.place(peer)

        @pl.when(peer != self.blk)
        def _():
            remote(src, dst, self.send.at[peer], self.recv.at[peer], {"blk": peer}).wait_recv()

        @pl.when(peer == self.blk)
        def _():
            pltpu.make_async_copy(src, dst, self.recv.at[peer]).wait()

    def all_arrived(self):
        loop(0, self.n_blk, self.arrived)

    def all_left(self):
        def left(peer):
            @pl.when(peer != self.blk)
            def _():
                remote(
                    self.source(peer), self.place(self.blk), self.send.at[peer], self.recv.at[self.blk], {"blk": peer}
                ).wait_send()

        loop(0, self.n_blk, left)


class Gift:
    def __init__(self, seq, n_seq, rows, owner, kind, src, dst, send, recv):
        self.seq, self.n_seq, self.rows, self.owner, self.kind = seq, n_seq, rows, owner, kind
        self.src, self.dst, self.send, self.recv = src, dst, send, recv

    def copy(self, other, send):
        dst = self.dst.at[span(other * self.rows, self.rows, self.rows)]
        return remote(self.src, dst, self.send.at[self.kind, send], self.recv.at[self.kind, other], {"seq": send})

    def own(self):
        dst = self.dst.at[pl.ds(self.owner * self.rows, self.rows)]
        return pltpu.make_async_copy(self.src, dst, self.recv.at[self.kind, self.owner])

    def start(self):
        @pl.when(self.seq != self.owner)
        def _():
            self.copy(self.seq, self.owner).start()

        @pl.when(self.seq == self.owner)
        def _():
            self.own().start()

    def arrived(self):
        for other in range(self.n_seq):
            if other == self.owner:
                self.own().wait()
            else:
                self.copy(other, other).wait_recv()

    def left(self):
        @pl.when(self.seq != self.owner)
        def _():
            self.copy(self.seq, self.owner).wait_send()


class Sum:
    def __init__(self, blk, size, part, cgot, rgot, zgot, total, sems):
        self.blk, self.size = blk, size
        self.core, self.chip = lax.rem(blk, 2), lax.div(blk, 2)
        side = lax.div(self.chip, 2)
        self.far = 2 * (1 - side)
        self.partner = self.chip + 1 - 2 * lax.rem(self.chip, 2)
        self.inner = lax.rem(self.chip, 2) != side
        self.far_inner = 2 - side
        self.part, self.cgot, self.rgot, self.zgot, self.total = part, cgot, rgot, zgot, total
        self.csend, self.crecv, self.rsend, self.rrecv, self.zsend, self.zrecv = sems

    def order(self, step):
        return jnp.where(step < 2, self.far + step, jnp.where(step == 2, self.partner, self.chip))

    def chunk(self, index):
        return self.part.at[span(index * self.size, self.size, 32)]

    def mine(self, chip):
        return self.chunk(2 * chip + self.core)

    def swap(self, chip):
        return remote(
            self.chunk(2 * chip + 1 - self.core),
            self.cgot(chip),
            self.csend.at[chip],
            self.crecv.at[chip],
            {"blk": 2 * self.chip + 1 - self.core},
        )

    def lend(self, index):
        return remote(
            self.mine(self.far + index),
            self.rgot(index),
            self.rsend.at[index],
            self.rrecv.at[index],
            {"blk": 2 * self.partner + self.core},
        )

    def send_far(self, index):
        return remote(
            self.mine(self.far + index),
            self.zgot(1),
            self.zsend.at[index],
            self.zrecv.at[1],
            {"blk": 2 * (self.far + index) + self.core},
        )

    def send_near(self):
        return remote(
            self.mine(self.partner),
            self.zgot(0),
            self.zsend.at[2],
            self.zrecv.at[0],
            {"blk": 2 * self.partner + self.core},
        )

    def add(self, mine, other):
        def group(index):
            at = span(index * 32, 32, 32)
            mine[at, :] = (mine[at, :].astype(F32) + other[at, :].astype(F32)).astype(BF16)

        loop(0, self.size // 32, group)

    def begin(self):
        for index in range(2):
            chip = self.far + index
            self.swap(chip).wait()
            self.add(self.mine(chip), self.cgot(chip))

            @pl.when(jnp.logical_not(self.inner))
            def _(index=index):
                self.lend(index).start()

        self.swap(self.partner).wait()
        self.add(self.mine(self.partner), self.cgot(self.partner))
        self.send_near().start()
        self.swap(self.chip).wait()

    def relay(self):
        @pl.when(self.inner)
        def _():
            for index in range(2):
                self.lend(index).wait_recv()
                self.add(self.mine(self.far + index), self.rgot(index))
                self.send_far(index).start()

    def end(self):
        self.send_near().wait_recv()
        self.send_far(0).wait_recv()
        mine, other = self.mine(self.chip), self.cgot(self.chip)

        def group(index):
            at = span(index * 32, 32, 32)
            value = mine[at, :].astype(F32) + other[at, :].astype(F32)
            value = value + self.zgot(0)[at, :].astype(F32) + self.zgot(1)[at, :].astype(F32)
            self.total[at, :] = value.astype(BF16)

        loop(0, self.size // 32, group)

    def left(self):
        self.send_near().wait_send()

        @pl.when(self.inner)
        def _():
            for index in range(2):
                self.send_far(index).wait_send()

        @pl.when(jnp.logical_not(self.inner))
        def _():
            for index in range(2):
                self.lend(index).wait_send()


class TileGift:
    def __init__(self, seq, n_seq, rows, src, dst, send, recv, owner_of):
        self.seq, self.n_seq, self.rows, self.src, self.dst = seq, n_seq, rows, src, dst
        self.send, self.recv, self.owner_of = send, recv, owner_of

    def place(self, other, slot):
        return self.dst.at[span(other * self.rows, self.rows, self.rows), span(slot * TILE, TILE, TILE)]

    def tile(self, index):
        return self.src.at[:, span(index * TILE, TILE, TILE)]

    def start(self, index):
        owner, slot = self.owner_of(index)
        src, dst, recv = self.tile(index), self.place(self.seq, slot), self.recv.at[slot, self.seq]

        @pl.when(owner != self.seq)
        def _():
            remote(src, dst, self.send.at[index], recv, {"seq": owner}).start()

        @pl.when(owner == self.seq)
        def _():
            pltpu.make_async_copy(src, dst, recv).start()

    def arrived(self, low, high):
        def one(slot):
            def other_one(other):
                dst, recv = self.place(other, slot), self.recv.at[slot, other]

                @pl.when(other != self.seq)
                def _():
                    remote(self.tile(0), dst, self.send.at[0], recv, {"seq": other}).wait_recv()

                @pl.when(other == self.seq)
                def _():
                    pltpu.make_async_copy(self.tile(0), dst, recv).wait()

            loop(0, self.n_seq, other_one)

        loop(low, high, one)

    def left(self, count):
        def one(index):
            owner, slot = self.owner_of(index)

            @pl.when(owner != self.seq)
            def _():
                remote(
                    self.tile(index), self.place(self.seq, slot), self.send.at[index], self.recv.at[slot, self.seq],
                    {"seq": owner},
                ).wait_send()

        loop(0, count, one)


class Spread:
    def __init__(self, seq, owner, kind, src, dst, send, recv, local, on_send, on_recv):
        self.seq, self.owner, self.kind, self.src, self.dst = seq, owner, kind, src, dst
        self.send, self.recv, self.local, self.on_send, self.on_recv = send, recv, local, on_send, on_recv
        self.half = src.shape[0] // 2

    def copy(self, bit):
        return remote(
            self.src, self.dst, self.send.at[self.kind, bit], self.recv.at[self.kind], {"seq": self.owner ^ (bit + 1)}
        )

    def onward(self, bit):
        part = self.dst.at[bit * self.half : (bit + 1) * self.half]
        return remote(
            part, part, self.on_send.at[self.kind, bit], self.on_recv.at[self.kind, bit], {"seq": self.owner ^ 3}
        )

    def own(self):
        return pltpu.make_async_copy(self.src, self.dst, self.local.at[self.kind])

    def start(self):
        @pl.when(self.seq == self.owner)
        def _():
            for bit in range(2):
                self.copy(bit).start()
            self.own().start()

    def pass_on(self):
        for bit in range(2):

            @pl.when(self.seq == self.owner ^ (bit + 1))
            def _(bit=bit):
                self.copy(bit).wait_recv()
                self.onward(bit).start()

    def finish(self):
        @pl.when(self.seq == self.owner)
        def _():
            for bit in range(2):
                self.copy(bit).wait_send()
            self.own().wait()

        for bit in range(2):

            @pl.when(self.seq == self.owner ^ (bit + 1))
            def _(bit=bit):
                self.onward(bit).wait_send()

        @pl.when(self.seq == self.owner ^ 3)
        def _():
            for bit in range(2):
                self.onward(bit).wait_recv()


def turn_over(src, dst):
    def one(index):
        at = span(index * TILE, TILE, TILE)
        dst[at, :] = src[:, at].T

    loop(0, src.shape[1] // TILE, one)


def outer_tiles(turned, rhs, part, chip, tiles, rhs_at, part_at):
    rows = span(chip * TILE, TILE, TILE)

    def tile(index):
        value = times(turned[rows, :], rhs[:, span(rhs_at + index * TILE, TILE, TILE)])
        part[rows, span(part_at + index * TILE, TILE, TILE)] = value.astype(BF16)

    loop(0, tiles, tile)


def layer_kernel(
    sizes,
    freq, tokens, first, lengths, attn_gain, ffn_gain, cot,
    h_query, h_key, h_value, h_out, h_gate, h_up, h_down,
    o_layer, o_tokens, o_first, o_gu, o_down, o_out, o_query, o_key, o_value, o_gain,
    v, sem,
):
    rows, width, ff, n_seq, n_blk, split = sizes
    v, sem = types.SimpleNamespace(**v), types.SimpleNamespace(**sem)
    docs = lengths.shape[1]
    chips = n_blk // 2
    scale = HEAD_DIM ** (-0.5)
    seq, blk = lax.axis_index("seq"), lax.axis_index("blk")
    chip_at = lax.div(blk, 2)

    def turned_chip(step):
        return lax.rem(chip_at + step, chips)

    barrier = pltpu.get_barrier_semaphore()
    for step in range(1, n_seq):
        pl.semaphore_signal(barrier, inc=1, device_id={"seq": lax.rem(seq + step, n_seq)}, device_id_type=MESH)
    for step in range(1, n_blk):
        pl.semaphore_signal(barrier, inc=1, device_id={"blk": lax.rem(blk + step, n_blk)}, device_id_type=MESH)

    def load(index, src, dst):
        copy = pltpu.make_async_copy(src, dst, sem.load.at[index])
        copy.start()
        return copy

    load_query = load(0, h_query, v.w_query)
    load_key = load(1, h_key, v.w_key)
    load_value = load(2, h_value, v.w_value)
    load_out = load(3, h_out, v.w_out)
    load_gate = load(4, h_gate, v.w_gate)
    load_up = load(5, h_up, v.w_up)
    load_down = load(6, h_down, v.w_down)

    def norm(group):
        at = span(group * GROUP, GROUP, GROUP)
        x = tokens[at, :].astype(F32)
        inv = lax.rsqrt(jnp.mean(x * x, axis=-1, keepdims=True) + EPS)
        v.normed[at, :] = (x * inv * attn_gain[...]).astype(BF16)
        v.inv_first[at, :] = jnp.broadcast_to(inv, (GROUP, LANES))

    loop(0, rows // GROUP, norm)

    def doc_start(index):
        start, end = jnp.zeros_like(index), jnp.int32(0)
        for doc in range(docs):
            end = end + lengths[0, doc]
            start = jnp.where(index >= end, end, start)
        return start

    half = HEAD_DIM // 2

    def low_half(count):
        return lax.rem(iota((count, LANES), 1), HEAD_DIM) < half

    def set_tables(start, count, cosine_ref, sine_ref):
        index = start + iota((count, LANES), 0)
        angle = (index - doc_start(index)).astype(F32) * freq[...]
        cosine_ref[...] = jnp.cos(angle)
        sine = jnp.sin(angle)
        sine_ref[...] = jnp.where(low_half(count), -sine, sine)

    def halves_changed(u):
        return jnp.where(low_half(u.shape[0]), pltpu.roll(u, LANES - half, 1), pltpu.roll(u, half, 1))

    set_tables(blk * rows, rows, v.cos, v.sin)

    def rotated(u):
        return u * v.cos[...] + halves_changed(u) * v.sin[...]

    cuts = [0]
    for tiles in split:
        cuts.append(cuts[-1] + tiles * TILE)
    wide = max(split) * TILE

    def gift(owner, kind, src, dst):
        return Gift(seq, n_seq, rows, owner, kind, src, dst, sem.xsend, sem.xrecv)

    gift_cot = gift(3, 0, cot, v.buf_a)
    gifts_two = [gift(owner, 0, v.two, v.buf_a) for owner in range(3)]
    each, hidden = split[0], ff // TILE
    gift_gu = TileGift(
        seq, n_seq, rows, v.gate_up, v.buf_b, sem.gusend, sem.gurecv,
        lambda index: (lax.div(index, each), lax.rem(index, each)),
    )
    gift_act = TileGift(seq, n_seq, rows, v.act, v.buf_b, sem.actsend, sem.actrecv, lambda index: (3, index))
    gift_att = gift(2, 2, v.att, v.buf_att)
    gift_mid = gift(2, 3, v.mid_b, v.buf_mid)
    def trade(phase, source, place):
        return Trade(blk, n_blk, phase, sem.asend, sem.arecv, source, place)

    def block_rows(ref):
        return lambda peer: ref.at[span(peer * rows, rows, rows)]

    def block_columns(ref):
        return lambda peer: ref.at[:, span(peer * LANES, LANES, LANES)]

    give_qkv = trade(0, lambda peer: v.pack.at[peer], lambda peer: v.qkv.at[:, span(peer * rows, rows, rows)])
    give_att = trade(1, block_rows(v.ob), block_columns(v.att))
    give_out = trade(2, lambda peer: v.out_pack.at[peer], block_rows(v.out_grad))
    give_grads = trade(
        3, lambda peer: v.pack.at[peer], lambda peer: v.grads.at[:, :, span(peer * LANES, LANES, LANES)]
    )

    give_tail = trade(4, lambda peer: v.tail_sum.at[peer], lambda peer: v.tail_got.at[peer])
    core = lax.rem(blk, 2)
    mate = blk + 1 - 2 * core

    def block_of(step):
        return 2 * turned_chip(step) + core

    def rows_of(block):
        return v.normed_all.at[span(block * rows, rows, rows)]

    def normed_out(step):
        return remote(
            v.normed, rows_of(blk), sem.nsend.at[step - 1], sem.nrecv.at[step - 1], {"blk": block_of(step)}
        )

    def normed_over(step):
        there = rows_of(block_of(step))
        return remote(there, there, sem.fsend.at[step], sem.frecv.at[step], {"blk": mate})

    def mates_normed(step):
        there = rows_of(2 * turned_chip(step) + 1 - core)
        return remote(there, there, sem.fsend.at[step], sem.frecv.at[step], {"blk": mate})

    pl.semaphore_wait(barrier, n_seq + n_blk - 2)
    gift_cot.start()
    own_normed = pltpu.make_async_copy(v.normed, rows_of(blk), sem.nlocal.at[0])
    own_normed.start()

    for item in (load_query, load_key, load_value):
        item.wait()

    def project(step):
        chip = turned_chip(step)
        at = span(chip * TILE, TILE, TILE)
        left = v.normed[...]
        q, k, val = times(left, v.w_query[:, at]), times(left, v.w_key[:, at]), times(left, v.w_value[:, at])
        old = first[:, at].astype(F32)
        for core in range(2):
            peer = 2 * chip + core
            cols = slice(core * LANES, (core + 1) * LANES)
            v.pack[peer, 0] = (rotated(q[:, cols]) * scale).astype(BF16)
            v.pack[peer, 1] = rotated(k[:, cols]).astype(BF16)
            v.pack[peer, 2] = (MIX * val[:, cols] + MIX * old[:, cols]).astype(BF16)
            give_qkv.start(peer)

    loop(1, chips + 1, project)

    load_down.wait()

    def act_back(tile):
        cols = span(tile * TILE, TILE, TILE)
        v.act_grad[:, cols] = back(cot[...], v.w_down[cols, :])

    loop(0, ff // TILE, act_back)

    first_head = iota((TILE, LANES), 1) < HEAD_DIM

    def stacked(values):
        return jnp.concatenate([jnp.where(first_head, values, 0.0), jnp.where(first_head, 0.0, values)], axis=0)

    def unstacked(values):
        return jnp.where(first_head, values[:TILE], values[TILE:])

    def attend(block):
        for core in range(2):
            give_qkv.arrived(2 * block + core)
        at, both = span(block * TILE, TILE, TILE), span(block * 2 * TILE, 2 * TILE, 2 * TILE)
        queries = stacked(v.qkv[0, at, :].astype(F32)).astype(BF16)
        v.q2[both, :] = queries
        v.q2_turned[:, both] = queries.T
        index = block * TILE + lax.rem(iota((2 * TILE, 1), 0), TILE)
        start = doc_start(index)
        v.top[...] = jnp.full((2 * TILE, LANES), NEG, F32)

        def scores(tile):
            cols = span(tile * TILE, TILE, TILE)
            score = back(v.q2[both, :], v.qkv[1, cols, :])
            key = tile * TILE + iota((2 * TILE, TILE), 1)
            score = jnp.where((key <= index) & (key >= start), score, NEG)
            v.score[:, cols] = score
            v.top[...] = jnp.maximum(v.top[...], jnp.maximum(score[:, :LANES], score[:, LANES:]))

        loop(0, block + 1, scores)
        top = jnp.max(v.top[...], axis=1, keepdims=True)
        v.top[...] = jnp.zeros((2 * TILE, LANES), F32)
        v.o2[...] = jnp.zeros((2 * TILE, LANES), F32)

        def weights(tile):
            cols = span(tile * TILE, TILE, TILE)
            weight = jnp.exp(v.score[:, cols] - top)
            v.top[...] += weight[:, :LANES] + weight[:, LANES:]
            weight = weight.astype(BF16)
            v.prob[both, cols] = weight
            v.o2[...] += times(weight, v.qkv[2, cols, :])

        loop(0, block + 1, weights)
        inv = 1.0 / jnp.sum(v.top[...], axis=1, keepdims=True)
        v.row[both, :] = jnp.broadcast_to(inv, (2 * TILE, LANES))
        attended = unstacked(v.o2[...] * inv)
        v.o32[at, :] = attended
        v.ob[at, :] = attended.astype(BF16)
        for core in range(2):
            give_att.start(2 * block + core)

    loop(0, chips, attend)
    loop(
        0,
        chips,
        lambda block: set_tables(
            block * TILE,
            TILE,
            v.score.at[:TILE, span(block * TILE, LANES, LANES)],
            v.score.at[:TILE, span(block * TILE + LANES, LANES, LANES)],
        ),
    )
    give_att.all_arrived()
    gift_att.start()
    normed_out(1).start()
    normed_out(3).start()

    load_out.wait()

    def middle(tile):
        cols = span(tile * TILE, TILE, TILE)
        value = tokens[:, cols].astype(F32) + times(v.att[...], v.w_out[:, cols])
        v.mid[:, cols] = value

    loop(0, width // TILE, middle)

    def norm_two(group):
        at = span(group * GROUP, GROUP, GROUP)
        x = v.mid[at, :]
        inv = lax.rsqrt(jnp.mean(x * x, axis=-1, keepdims=True) + EPS)
        v.two[at, :] = (x * inv * ffn_gain[...]).astype(BF16)
        v.inv_second[at, :] = jnp.broadcast_to(inv, (GROUP, LANES))

    loop(0, rows // GROUP, norm_two)
    for item in gifts_two:
        item.start()

    for item in (load_gate, load_up):
        item.wait()
    v.two_grad[...] = jnp.zeros((rows, width), F32)

    def feed(step):
        tile = lax.rem(split[0] + step, hidden)
        cols = span(tile * TILE, TILE, TILE)
        gate = times(v.two[...], v.w_gate[:, cols])
        up = times(v.two[...], v.w_up[:, cols])
        act_grad = v.act_grad[:, cols]
        sigma = jax.nn.sigmoid(gate)
        silu = gate * sigma
        act = (silu * up).astype(BF16)
        gate_grad = (act_grad * up * sigma * (1.0 + gate * (1.0 - sigma))).astype(BF16)
        up_grad = (act_grad * silu).astype(BF16)
        v.act[:, cols] = act
        v.gate_up[:, cols] = gate_grad
        v.gate_up[:, span(ff + tile * TILE, TILE, TILE)] = up_grad
        gift_gu.start(tile)
        gift_gu.start(hidden + tile)
        gift_act.start(tile)
        v.two_grad[...] += back(gate_grad, v.w_gate[:, cols]) + back(up_grad, v.w_up[:, cols])

    loop(0, hidden, feed)
    v.gain_rows[...] = jnp.zeros((16, width), F32)

    def norm_two_back(group):
        at = span(group * GROUP, GROUP, GROUP)
        x, grad, inv = v.mid[at, :], v.two_grad[at, :], v.inv_second[at, :1]
        term = grad * x * inv
        v.gain_rows[8:16, :] += term[:8] + term[8:]
        scaled = grad * ffn_gain[...]
        mean = jnp.mean(scaled * x, axis=-1, keepdims=True)
        value = cot[at, :].astype(F32) + inv * scaled - x * (inv * inv * inv * mean)
        v.mid_grad[at, :] = value
        v.mid_b[at, :] = value.astype(BF16)

    loop(0, rows // GROUP, norm_two_back)
    gift_mid.start()

    def out_back(step):
        chip = turned_chip(step)
        value = back(v.mid_b[...], v.w_out[span(chip * TILE, TILE, TILE), :]).astype(BF16)
        for core in range(2):
            v.out_pack[2 * chip + core] = value[:, core * LANES : (core + 1) * LANES]
            give_out.start(2 * chip + core)

    loop(1, chips + 1, out_back)

    def layer_out(tile):
        cols = span(tile * TILE, TILE, TILE)
        o_layer[:, cols] = v.mid[:, cols] + times(v.act[...], v.w_down[:, cols])

    loop(0, width // TILE, layer_out)
    own_normed.wait()
    normed_over(0).start()
    for step in (1, 3):
        normed_out(chips - step).wait_recv()
        normed_over(step).start()

    chunk, down = width // n_blk, ff // n_blk

    def sems_of(index):
        return tuple(
            item.at[index] for item in (sem.csend, sem.crecv, sem.rsend, sem.rrecv, sem.zsend, sem.zrecv)
        )

    def stack_in(ref, top, cols):
        return lambda index: ref.at[span(top + index * chunk, chunk, 32), cols]

    def square_in(ref, more, low, high):
        def place(index):
            index = index + more
            return ref.at[
                span(lax.rem(index, 2) * down, down, 32), span(lax.div(index, 2) * width + low, high - low, LANES)
            ]

        return place

    def piece(index, low, high):
        cols = slice(low, high)
        return Sum(
            blk, chunk, v.w_gate.at[:, cols], stack_in(v.w_up, 0, cols), stack_in(v.w_up, chips * chunk, cols),
            stack_in(v.w_up, (chips + 2) * chunk, cols), v.total.at[:, cols], sems_of(index),
        )

    edges = [0, each // 3, 2 * each // 3, each]
    thirds = [piece(index, edges[index] * TILE, edges[index + 1] * TILE) for index in range(3)]
    last = split[2] * TILE
    halves = [piece(0, 0, last), piece(1, last, last + width)]
    bounds = [0, width // 4, width // 2, 3 * width // 4, 7 * width // 8, width]
    fifths = [
        Sum(
            blk, down, v.w_down.at[:, low:high], square_in(v.w_up, 0, low, high), square_in(v.w_gate, 0, low, high),
            square_in(v.w_gate, 2, low, high), v.total_down.at[:, low:high], sems_of(index),
        )
        for index, (low, high) in enumerate(zip(bounds[:-1], bounds[1:]))
    ]
    first_two, third_one, fourth = seq < 2, seq == 2, seq == 3

    def spread(owner, kind, src, dst):
        return Spread(
            seq, owner, kind, src, dst, sem.gsend, sem.grecv, sem.glocal, sem.onsend, sem.onrecv
        )

    spreads = [
        [
            spread(
                owner,
                3 * owner + index,
                v.total.at[:, edges[index] * TILE : edges[index + 1] * TILE],
                o_gu.at[:, cuts[owner] + edges[index] * TILE : cuts[owner] + edges[index + 1] * TILE],
            )
            for index in range(3)
        ]
        for owner in range(2)
    ] + [
        [
            spread(2, 6, v.total.at[:, :last], o_gu.at[:, cuts[2] : cuts[3]]),
            spread(2, 7, v.total.at[:, last : last + width], o_out),
        ],
        [
            spread(3, 8 + index, v.total_down.at[:, low:high], o_down.at[:, low:high])
            for index, (low, high) in enumerate(zip(bounds[:-1], bounds[1:]))
        ],
    ]
    def products(item, turned, rhs, tiles, rhs_at, part_at):
        def one(step):
            chip = item.order(step)
            outer_tiles(turned, rhs, v.w_gate, chip, tiles, rhs_at, part_at)

        loop(0, chips, one)

    def swaps(item):
        loop(0, chips, lambda step: item.swap(item.order(step)).start())

    def gate_up_piece(index):
        gift_gu.arrived(edges[index], edges[index + 1])
        at = edges[index] * TILE
        products(thirds[index], v.turned, v.buf_b, edges[index + 1] - edges[index], at, at)

    def down_products(low, high):
        def one(step):
            index = lax.rem(split[0] + step, hidden)
            gift_act.arrived(index, index + 1)
            at = span(index * TILE, TILE, TILE)
            v.turned[:TILE, :] = v.buf_b[:, at].T
            v.w_down[at, :] = times(v.turned[:TILE, :], v.buf_a[...]).astype(BF16)

        loop(low, high, one)

    def down_swaps():
        for item in fifths:
            swaps(item)

    for owner in range(2):

        @pl.when(seq == owner)
        def _(owner=owner):
            gifts_two[owner].arrived()
            turn_over(v.buf_a, v.turned)

    @pl.when(fourth)
    def _():
        gift_cot.arrived()
        down_products(0, hidden // 4)

    give_out.all_arrived()
    normed_out(2).start()


    def prepare(block):
        at, both = span(block * TILE, TILE, TILE), span(block * 2 * TILE, 2 * TILE, 2 * TILE)
        grad = (stacked(v.out_grad[at, :].astype(F32)) * v.row[both, :]).astype(BF16)
        v.do2[both, :] = grad
        v.do2_turned[:, both] = grad.T
        attended = v.o32[at, :]
        delta = jnp.sum(grad.astype(F32) * jnp.concatenate([attended, attended], axis=0), axis=1, keepdims=True)
        v.row[both, :] = jnp.broadcast_to(delta, (2 * TILE, LANES))
        v.dq[both, :] = jnp.zeros((2 * TILE, LANES), F32)

    loop(0, chips, prepare)
    give_qkv.all_left()

    def key_block(block):
        at = span(block * TILE, TILE, TILE)
        v.dk[...] = jnp.zeros((LANES, TILE), F32)
        v.dv[...] = jnp.zeros((LANES, TILE), F32)

        def query_block(other):
            both = span(other * 2 * TILE, 2 * TILE, 2 * TILE)
            prob = v.prob[both, at]
            grad = back(v.do2[both, :], v.qkv[2, at, :])
            score_grad = (prob.astype(F32) * (grad - v.row[both, :1])).astype(BF16)
            v.dk[...] += times(v.q2_turned[:, both], score_grad)
            v.dv[...] += times(v.do2_turned[:, both], prob)
            v.dq[both, :] += times(score_grad, v.qkv[1, at, :])

        loop(block, chips, query_block)
        cosine = v.score[:TILE, span(block * TILE, LANES, LANES)]
        sine = v.score[:TILE, span(block * TILE + LANES, LANES, LANES)]

        def rotated_back(u):
            u = u.astype(BF16).astype(F32)
            return (u * cosine - halves_changed(u) * sine).astype(BF16)

        dq = rotated_back(unstacked(v.dq[span(block * 2 * TILE, 2 * TILE, 2 * TILE), :]) * scale)
        dk = rotated_back(v.dk[...].T)
        dv = (MIX * v.dv[...].T.astype(BF16).astype(F32)).astype(BF16)
        for index, value in enumerate((dq, dk, dv)):
            v.heads_grad[at, index * LANES : (index + 1) * LANES] = value
            for half_at in range(2):
                v.pack[2 * block + half_at, index] = value[half_at * rows : (half_at + 1) * rows]
        for half_at in range(2):
            give_grads.start(2 * block + half_at)

    loop(0, chips, key_block)

    def when(which, *steps):
        @pl.when(which)
        def _():
            for step in steps:
                step()

    def ended(item, goes):
        def step():
            item.end()
            for other in goes:
                other.start()

        return step

    def first_half():
        gifts_two[2].arrived()
        turn_over(v.buf_a, v.turned)
        gift_gu.arrived(0, split[2])
        products(halves[0], v.turned, v.buf_b, split[2], 0, 0)
        swaps(halves[0])
        halves[0].begin()

    def second_half():
        gift_att.arrived()
        gift_mid.arrived()
        turn_over(v.buf_att, v.turned)
        products(halves[1], v.turned, v.buf_mid, width // TILE, 0, last)
        swaps(halves[1])

    def gate_up_gone(index):
        gate_up_piece(index)
        swaps(thirds[index])

    when(first_two, lambda: gate_up_gone(0), thirds[0].begin, lambda: gate_up_gone(1), thirds[1].begin)
    when(third_one, first_half)
    when(fourth, lambda: down_products(hidden // 4, hidden), down_swaps, fifths[0].begin, fifths[1].begin)

    normed_out(2).wait_recv()
    normed_over(2).start()
    for step in range(chips):
        mates_normed(step).wait_recv()

    def project_back(index):
        value = outer(v.normed_all[:, span(index * TILE, TILE, TILE)], v.heads_grad[...]).astype(BF16)
        v.tail_part[2 * index] = value[:LANES]
        v.tail_part[2 * index + 1] = value[LANES:]

    loop(0, width // TILE, project_back)
    quarter = LANES // n_seq

    def tail_share(step):
        other = lax.rem(seq + step, n_seq)
        return remote(
            v.tail_part.at[:, span(other * quarter, quarter, quarter)],
            v.tail_shares.at[step - 1],
            sem.qsend.at[step - 1],
            sem.qrecv.at[step - 1],
            {"seq": other},
        )

    for step in range(1, n_seq):
        tail_share(step).start()

    when(first_two, thirds[0].relay, lambda: gate_up_gone(2))
    when(third_one, second_half)

    def tail_add(index):
        value = v.tail_part[index, span(seq * quarter, quarter, quarter), :].astype(F32)
        for step in range(1, n_seq):
            value = value + v.tail_shares[step - 1, index].astype(F32)
        v.tail_sum[index] = value.astype(BF16)
        give_tail.start(index)

    for step in range(1, n_seq):
        tail_share(step).wait()
    loop(0, n_blk, tail_add)
    when(first_two, thirds[2].begin)
    when(third_one, halves[1].begin)

    give_grads.all_arrived()

    def gone(index, *owners):
        return [spreads[owner][index] for owner in owners]

    when(first_two, thirds[1].relay, ended(thirds[0], []))
    for item in gone(0, 0, 1):
        item.start()
    when(fourth, fifths[0].relay, fifths[2].begin)

    def normed_back(tile):
        at = span(tile * TILE, TILE, TILE)
        o_tokens[:, at] = (
            back(v.grads[0], v.w_query[at, :])
            + back(v.grads[1], v.w_key[at, :])
            + back(v.grads[2], v.w_value[at, :])
        )

    loop(0, width // TILE, normed_back)
    o_first[...] = v.grads[2].astype(F32)

    def norm_back(group):
        at = span(group * GROUP, GROUP, GROUP)
        x, grad, inv = tokens[at, :].astype(F32), o_tokens[at, :], v.inv_first[at, :1]
        term = grad * x * inv
        v.gain_rows[0:8, :] += term[:8] + term[8:]
        scaled = grad * attn_gain[...]
        mean = jnp.mean(scaled * x, axis=-1, keepdims=True)
        o_tokens[at, :] = v.mid_grad[at, :] + inv * scaled - x * (inv * inv * inv * mean)

    loop(0, rows // GROUP, norm_back)

    for peer in range(n_blk):
        v.gains[peer] = v.gain_rows[:, peer * LANES : (peer + 1) * LANES]

    def gain_copy(step):
        other = lax.rem(blk + step, n_blk)
        return remote(
            v.gains.at[other], v.gain_got.at[step - 1], sem.hsend.at[step - 1], sem.hrecv.at[step - 1],
            {"blk": other},
        )

    for step in range(1, n_blk):
        gain_copy(step).start()
    when(fourth, ended(fifths[0], gone(0, 3)), fifths[1].relay, fifths[3].begin, fifths[4].begin)

    when(first_two, ended(thirds[1], gone(1, 0, 1)))
    when(third_one, halves[0].relay, ended(halves[0], gone(0, 2)))
    when(fourth, ended(fifths[1], gone(1, 3)))

    give_tail.all_arrived()
    for index in range(3):
        for peer in range(n_blk):
            v.tail_done[index, :, peer * LANES : (peer + 1) * LANES] = v.tail_got[
                peer, :, index * LANES : (index + 1) * LANES
            ]

    def tail_spread(index, step, owner):
        at = span(owner * quarter, quarter, quarter)
        return remote(
            v.tail_done.at[index],
            (o_query, o_key, o_value)[index].at[at],
            sem.tsend.at[index, step - 1],
            sem.trecv.at[index, owner],
            {"seq": lax.rem(seq + step, n_seq)},
        )

    def tail_own(index):
        at = span(seq * quarter, quarter, quarter)
        return pltpu.make_async_copy(
            v.tail_done.at[index], (o_query, o_key, o_value)[index].at[at], sem.trecv.at[index, seq]
        )

    for index in range(3):
        tail_own(index).start()
        for step in range(1, n_seq):
            tail_spread(index, step, seq).start()

    def pass_on(*items):
        for item in items:
            item.pass_on()

    pass_on(*gone(0, 0, 1, 3))
    when(first_two, thirds[2].relay, ended(thirds[2], gone(2, 0, 1)))
    when(third_one, halves[1].relay, ended(halves[1], gone(1, 2)))
    when(fourth, fifths[2].relay, fifths[3].relay, ended(fifths[2], gone(2, 3)))
    value = v.gains[blk]
    for step in range(1, n_blk):
        gain_copy(step).wait()
        value = value + v.gain_got[step - 1]
    v.gain_sum[seq] = value
    for step in range(1, n_seq):
        other = lax.rem(seq + step, n_seq)
        mine = v.gain_sum.at[seq]
        remote(mine, mine, sem.isend.at[step - 1], sem.irecv.at[seq], {"seq": other}).start()

    when(fourth, fifths[4].relay, ended(fifths[3], gone(3, 3)), ended(fifths[4], gone(4, 3)))
    pass_on(*gone(0, 2), *gone(1, 3, 0, 1))
    pass_on(*gone(2, 0, 1, 3), *gone(1, 2), *gone(3, 3), *gone(4, 3))

    for step in range(1, n_seq):
        other = lax.rem(seq + step, n_seq)
        theirs = v.gain_sum.at[other]
        remote(theirs, theirs, sem.isend.at[step - 1], sem.irecv.at[other], {"seq": other}).wait()
    value = v.gain_sum[0]
    for group in range(1, n_seq):
        value = value + v.gain_sum[group]
    o_gain[0:8, :] = jnp.broadcast_to(jnp.sum(value[:8], axis=0, keepdims=True), (8, LANES))
    o_gain[8:16, :] = jnp.broadcast_to(jnp.sum(value[8:], axis=0, keepdims=True), (8, LANES))

    for index in range(3):
        tail_own(index).wait()
        for step in range(1, n_seq):
            tail_spread(index, step, seq).wait_send()
            tail_spread(index, step, lax.rem(seq + step, n_seq)).wait_recv()
    for item in sum(spreads, []):
        item.finish()
    for item in [gift_cot, gift_att, gift_mid] + gifts_two:
        item.left()
    gift_gu.left(2 * hidden)
    gift_act.left(hidden)
    for item in (give_att, give_out, give_grads, give_tail):
        item.all_left()
    for step in range(chips):
        normed_over(step).wait_send()
        if step:
            normed_out(step).wait_send()

    @pl.when(first_two)
    def _():
        for item in thirds:
            item.left()

    @pl.when(third_one)
    def _():
        for item in halves:
            item.left()

    @pl.when(fourth)
    def _():
        for item in fifths:
            item.left()


def finish_kernel(
    layer, tokens, first, gu, down, out, query, key, value, gain,
    o_layer, o_tokens, o_first, o_gain, o_gain_two, o_query, o_key, o_value, o_out, o_gate, o_up, o_down,
    kept, small, large, sem_kept_in, sem_kept_out, sem_in, sem_out,
):
    kept_in = [
        pltpu.make_async_copy(src, kept[index], sem_kept_in.at[index])
        for index, src in enumerate((layer, tokens, first))
    ]
    kept_out = [
        pltpu.make_async_copy(kept[index], dst, sem_kept_out.at[index])
        for index, dst in enumerate((o_layer, o_tokens, o_first))
    ]
    ff = o_gate.shape[1]
    sources = [query, key, value, out, down, gu.at[:, :ff], gu.at[:, ff:]]
    targets = [o_query, o_key, o_value, o_out, o_down, o_gate, o_up]
    loads = [pltpu.make_async_copy(src, small[index], sem_in.at[index]) for index, src in enumerate(sources)]
    stores = [pltpu.make_async_copy(large[index], dst, sem_out.at[index]) for index, dst in enumerate(targets)]
    for item in loads + kept_in:
        item.start()
    for index in range(len(sources)):
        loads[index].wait()

        def group(step, index=index):
            at = span(step * GROUP, GROUP, GROUP)
            large[index][at, :] = small[index][at, :].astype(F32)

        loop(0, targets[index].shape[0] // GROUP, group)
        stores[index].start()
    for coming, going in zip(kept_in, kept_out):
        coming.wait()
        going.start()
    o_gain[...] = gain[0:1, :]
    o_gain_two[...] = gain[8:9, :]
    for item in stores + kept_out:
        item.wait()


def finish(layer, tokens, first, gu, down, out, query, key, value, gain):
    hbm, vmem = pl.BlockSpec(memory_space=pl.ANY), pl.BlockSpec(memory_space=pltpu.VMEM)
    shape = jax.ShapeDtypeStruct
    ff = gu.shape[1] // 2
    dims = [query.shape, key.shape, value.shape, out.shape, down.shape, (gu.shape[0], ff), (gu.shape[0], ff)]
    dma = pltpu.SemaphoreType.DMA
    results = pl.pallas_call(
        finish_kernel,
        out_shape=tuple(
            shape(each, F32)
            for each in (
                layer.shape, tokens.shape, first.shape, (1, LANES), (1, LANES), dims[0], dims[1], dims[2], dims[3], dims[5], dims[6], dims[4]
            )
        ),
        in_specs=[hbm] * 9 + [vmem],
        out_specs=(hbm,) * 3 + (vmem,) * 2 + (hbm,) * 7,
        scratch_shapes=(
            [pltpu.VMEM(each.shape, F32) for each in (layer, tokens, first)],
            [pltpu.VMEM(each, BF16) for each in dims],
            [pltpu.VMEM(each, F32) for each in dims],
            dma((3,)), dma((3,)), dma((7,)), dma((7,)),
        ),
        compiler_params=pltpu.CompilerParams(vmem_limit_bytes=63 * 1024 * 1024),
        name="finish",
    )(layer, tokens, first, gu, down, out, query, key, value, gain)
    return results[:3] + (results[3][0],) + results[5:9] + (results[4][0],) + results[9:]


def tile_split(width, ff):
    tiles, more = 2 * ff // TILE, width // TILE
    each = -(-(tiles + more) // 3)
    return (each, each, tiles - 2 * each)


def fits(n_seq, n_blk, rows, width, ff):
    return (
        n_seq == 4
        and n_blk % 2 == 0
        and n_blk * LANES == width
        and rows == LANES
        and ff % TILE == 0
        and (ff // n_blk) % 32 == 0
        and 2 * (ff // n_blk) <= width
        and n_blk == 8
        and width == n_seq * TILE
    )


def local_fast(
    n_seq,
    n_blk,
    tokens,
    first_values,
    doc_lengths,
    attn_gain,
    query_weight,
    key_weight,
    value_weight,
    out_weight,
    ffn_gain,
    gate_weight,
    up_weight,
    down_weight,
    cotangent,
):
    rows, width = tokens.shape
    ff = gate_weight.shape[1]
    split = tile_split(width, ff)
    sizes = (rows, width, ff, n_seq, n_blk, split)
    half = HEAD_DIM // 2
    freq = THETA ** (-(np.arange(half) * 2.0 / HEAD_DIM))
    freq = np.tile(freq, LANES // half)[None, :].astype(np.float32)
    wide = max(split) * TILE
    chunk, down, chips = width // n_blk, ff // n_blk, n_blk // 2
    all_rows, group = n_seq * rows, n_blk * rows
    vmem = pl.BlockSpec(memory_space=pltpu.VMEM)
    hbm = pl.BlockSpec(memory_space=pl.ANY)
    smem = pl.BlockSpec(memory_space=pltpu.SMEM)
    shape = jax.ShapeDtypeStruct

    def half_type(*dims):
        return pltpu.VMEM(dims, BF16)

    def full_type(*dims):
        return pltpu.VMEM(dims, F32)

    scratch = dict(
        w_query=half_type(width, width), w_key=half_type(width, width), w_value=half_type(width, width),
        w_out=half_type(width, width), w_gate=half_type(width, ff), w_up=half_type(width, ff),
        w_down=half_type(ff, width),
        normed=half_type(rows, width), inv_first=full_type(rows, LANES), inv_second=full_type(rows, LANES),
        cos=full_type(rows, LANES), sin=full_type(rows, LANES),
        pack=half_type(n_blk, 3, rows, LANES), qkv=half_type(3, group, LANES),
        q2=half_type(2 * group, LANES), do2=half_type(2 * group, LANES), prob=half_type(2 * group, group),
        score=full_type(2 * TILE, group), top=full_type(2 * TILE, LANES), o2=full_type(2 * TILE, LANES),
        row=full_type(2 * group, LANES), o32=full_type(group, LANES), ob=half_type(group, LANES),
        dq=full_type(2 * group, LANES), dk=full_type(LANES, TILE), dv=full_type(LANES, TILE),
        q2_turned=half_type(LANES, 2 * group), do2_turned=half_type(LANES, 2 * group),
        att=half_type(rows, width), mid=full_type(rows, width), two=half_type(rows, width),
        act=half_type(rows, ff), act_grad=full_type(rows, ff), gate_up=half_type(rows, 2 * ff), two_grad=full_type(rows, width),
        mid_grad=full_type(rows, width), mid_b=half_type(rows, width),
        out_pack=half_type(n_blk, rows, LANES), out_grad=half_type(group, LANES),
        grads=half_type(3, rows, width),
        buf_a=half_type(all_rows, width), buf_b=half_type(all_rows, ff), buf_att=half_type(all_rows, width),
        buf_mid=half_type(all_rows, width), normed_all=half_type(group, width), heads_grad=half_type(group, 3 * LANES),
        tail_part=half_type(n_blk, chunk, 3 * LANES), tail_shares=half_type(n_seq - 1, n_blk, chunk // n_seq, 3 * LANES),
        tail_sum=half_type(n_blk, chunk // n_seq, 3 * LANES), tail_got=half_type(n_blk, chunk // n_seq, 3 * LANES),
        tail_done=half_type(3, chunk // n_seq, width),
        turned=half_type(width, all_rows),
        total=half_type(chunk, wide), total_down=half_type(down, width),
        gain_rows=full_type(16, width), gains=full_type(n_blk, 16, LANES), gain_got=full_type(n_blk - 1, 16, LANES),
        gain_sum=full_type(n_seq, 16, LANES),
    )
    dma = pltpu.SemaphoreType.DMA
    sems = dict(
        load=dma((7,)), asend=dma((5, n_blk)), arecv=dma((5, n_blk)), xsend=dma((4, n_seq)), xrecv=dma((4, n_seq)),
        gusend=dma((2 * ff // TILE,)), gurecv=dma((split[0], n_seq)), actsend=dma((ff // TILE,)),
        actrecv=dma((ff // TILE, n_seq)),
        csend=dma((5, chips)), crecv=dma((5, chips)), rsend=dma((5, 2)), rrecv=dma((5, 2)), zsend=dma((5, 3)),
        zrecv=dma((5, 2)), gsend=dma((13, 2)), grecv=dma((13,)), glocal=dma((13,)), onsend=dma((13, 2)), onrecv=dma((13, 2)),
        nsend=dma((chips - 1,)), nrecv=dma((chips - 1,)), fsend=dma((chips,)), frecv=dma((chips,)), nlocal=dma((1,)),
        qsend=dma((n_seq - 1,)), qrecv=dma((n_seq - 1,)), tsend=dma((3, n_seq - 1)), trecv=dma((3, n_seq)),
        hsend=dma((n_blk - 1,)), hrecv=dma((n_blk - 1,)), isend=dma((n_seq - 1,)), irecv=dma((n_seq,)),
    )
    layer, grad_tokens, grad_first, out_gu, out_down, out_out, out_query, out_key, out_value, out_gain = pl.pallas_call(
        functools.partial(layer_kernel, sizes),
        out_shape=(
            shape((rows, width), F32),
            shape((rows, width), F32),
            shape((rows, width), F32),
            shape((chunk, 2 * ff), BF16),
            shape((down, width), BF16),
            shape((chunk, width), BF16),
            shape((chunk, width), BF16),
            shape((chunk, width), BF16),
            shape((chunk, width), BF16),
            shape((16, LANES), F32),
        ),
        in_specs=[vmem, vmem, vmem, smem, vmem, vmem, vmem] + [hbm] * 7,
        out_specs=(vmem, vmem, vmem) + (hbm,) * 6 + (vmem,),
        scratch_shapes=(scratch, sems),
        compiler_params=pltpu.CompilerParams(
            collective_id=0, has_side_effects=True, vmem_limit_bytes=63 * 1024 * 1024
        ),
        name="layer",
    )(
        freq, tokens, first_values, doc_lengths, attn_gain[None, :], ffn_gain[None, :], cotangent,
        query_weight, key_weight, value_weight, out_weight, gate_weight, up_weight, down_weight,
    )
    return finish(layer, grad_tokens, grad_first, out_gu, out_down, out_out, out_query, out_key, out_value, out_gain)


def local(
    tokens,
    first_values,
    doc_lengths,
    attn_gain,
    query_weight,
    key_weight,
    value_weight,
    out_weight,
    ffn_gain,
    gate_weight,
    up_weight,
    down_weight,
    cotangent,
):
    rows, width = tokens.shape
    heads = width // HEAD_DIM
    scale = HEAD_DIM ** (-0.5)
    shape3 = (rows, heads, HEAD_DIM)
    my_start = lax.axis_index("blk") * rows
    my_index = my_start + jnp.arange(rows, dtype=jnp.int32)
    my_doc, my_pos = doc_layout(doc_lengths, my_index)
    cosine, sine = tables(my_pos)
    source = tokens.astype(jnp.float32)
    inv_first = lax.rsqrt(jnp.mean(source * source, axis=-1, keepdims=True) + EPS)
    normed = (source * inv_first * attn_gain).astype(jnp.bfloat16)
    query_pre = jnp.dot(normed, query_weight, preferred_element_type=jnp.float32)
    key_pre = jnp.dot(normed, key_weight, preferred_element_type=jnp.float32)
    value_pre = jnp.dot(normed, value_weight, preferred_element_type=jnp.float32)
    queries = rotate(query_pre.reshape(shape3), cosine, sine).astype(jnp.bfloat16)
    keys = rotate(key_pre.reshape(shape3), cosine, sine).astype(jnp.bfloat16).reshape(rows, width)
    mixed = (MIX * value_pre + MIX * first_values.astype(jnp.float32)).astype(jnp.bfloat16)
    keys_local = keys.reshape(shape3)
    mixed_local = mixed.reshape(shape3)

    def allowed_mask(query_index, query_doc, key_index, key_doc):
        return (query_doc[:, None] == key_doc[None, :]) & (
            key_index[None, :] <= query_index[:, None]
        )

    def forward_step(state, pieces, start):
        count = pieces[0].shape[0]
        keys_piece = pieces[0].reshape(count, heads, HEAD_DIM)
        values_piece = pieces[1].reshape(count, heads, HEAD_DIM)
        key_index = start + jnp.arange(count, dtype=jnp.int32)

        def forward_compute(state):
            high, total, accum = state
            key_doc, unused = doc_layout(doc_lengths, key_index)
            allowed = allowed_mask(my_index, my_doc, key_index, key_doc)[None]
            score = (
                jnp.einsum("qhd,khd->hqk", queries, keys_piece, preferred_element_type=jnp.float32)
                * scale
            )
            score = jnp.where(allowed, score, NEG)
            new_high = jnp.maximum(high, jnp.max(score, axis=-1))
            weight = jnp.where(allowed, jnp.exp(score - new_high[:, :, None]), 0.0)
            factor = jnp.exp(high - new_high)
            total = total * factor + jnp.sum(weight, axis=-1)
            accum = accum * factor.T[:, :, None] + jnp.einsum(
                "hqk,khd->qhd",
                weight.astype(jnp.bfloat16),
                values_piece,
                preferred_element_type=jnp.float32,
            )
            return (new_high, total, accum)

        return lax.cond(start <= my_index[-1], forward_compute, lambda kept: kept, state)

    def query_grad_step(grad_q, pieces, start):
        count = pieces[0].shape[0]
        keys_piece = pieces[0].reshape(count, heads, HEAD_DIM)
        values_piece = pieces[1].reshape(count, heads, HEAD_DIM)
        key_index = start + jnp.arange(count, dtype=jnp.int32)

        def query_compute(grad_q):
            key_doc, unused = doc_layout(doc_lengths, key_index)
            allowed = allowed_mask(my_index, my_doc, key_index, key_doc)[None]
            score = (
                jnp.einsum("qhd,khd->hqk", queries, keys_piece, preferred_element_type=jnp.float32)
                * scale
            )
            prob = jnp.where(allowed, jnp.exp(score - logsum[:, :, None]), 0.0)
            prob_grad = jnp.einsum(
                "qhd,khd->hqk", outgrad_local, values_piece, preferred_element_type=jnp.float32
            )
            score_grad = (prob * (prob_grad - delta[:, :, None])).astype(jnp.bfloat16)
            return (
                grad_q
                + jnp.einsum(
                    "hqk,khd->qhd", score_grad, keys_piece, preferred_element_type=jnp.float32
                )
                * scale
            )

        return lax.cond(start <= my_index[-1], query_compute, lambda kept: kept, grad_q)

    init = (
        jnp.full((heads, rows), NEG, jnp.float32),
        jnp.zeros((heads, rows), jnp.float32),
        jnp.zeros(shape3, jnp.float32),
    )
    state = by_blocks(
        forward_step,
        init,
        (
            lax.all_gather(keys, "blk", axis=0, tiled=True),
            lax.all_gather(mixed, "blk", axis=0, tiled=True),
        ),
        jnp.int32(0),
    )
    high, total, accum = state
    logsum = high + jnp.log(total)
    attended = accum / total.T[:, :, None]
    attended_b = attended.astype(jnp.bfloat16).reshape(rows, width)
    mid = source + jnp.dot(attended_b, out_weight, preferred_element_type=jnp.float32)
    inv_second = lax.rsqrt(jnp.mean(mid * mid, axis=-1, keepdims=True) + EPS)
    normed_two = (mid * inv_second * ffn_gain).astype(jnp.bfloat16)
    gate = jnp.dot(normed_two, gate_weight, preferred_element_type=jnp.float32)
    up = jnp.dot(normed_two, up_weight, preferred_element_type=jnp.float32)
    act = (jax.nn.silu(gate) * up).astype(jnp.bfloat16)
    layer_output = mid + jnp.dot(act, down_weight, preferred_element_type=jnp.float32)
    cot_float = cotangent.astype(jnp.float32)
    grad_down = outer(act, cotangent)
    act_grad = back(cotangent, down_weight)
    sigma = jax.nn.sigmoid(gate)
    gate_grad = (act_grad * up * sigma * (1.0 + gate * (1.0 - sigma))).astype(jnp.bfloat16)
    up_grad = (act_grad * gate * sigma).astype(jnp.bfloat16)
    grad_gate = outer(normed_two, gate_grad)
    grad_up = outer(normed_two, up_grad)
    normed_two_grad = back(gate_grad, gate_weight) + back(up_grad, up_weight)
    grad_ffn_gain = jnp.sum(normed_two_grad * mid * inv_second, axis=0)
    scaled_two = normed_two_grad * ffn_gain
    mid_grad = (
        cot_float
        + inv_second * scaled_two
        - mid * inv_second**3 * jnp.mean(scaled_two * mid, axis=-1, keepdims=True)
    )
    mid_grad_b = mid_grad.astype(jnp.bfloat16)
    grad_out_weight = outer(attended_b, mid_grad_b)
    attended_grad = back(mid_grad_b, out_weight).astype(jnp.bfloat16)
    outgrad_local = attended_grad.reshape(shape3)
    delta = jnp.sum(outgrad_local.astype(jnp.float32) * attended, axis=-1).T
    zeros3 = jnp.zeros(shape3, jnp.float32)
    grad_q = by_blocks(
        query_grad_step,
        zeros3,
        (
            lax.all_gather(keys, "blk", axis=0, tiled=True),
            lax.all_gather(mixed, "blk", axis=0, tiled=True),
        ),
        jnp.int32(0),
    )
    all_logsum, all_delta = (
        lax.all_gather(logsum.T, "blk", axis=0, tiled=True),
        lax.all_gather(delta.T, "blk", axis=0, tiled=True),
    )

    def key_grad_step(state, pieces, start):
        count = pieces[0].shape[0]
        query_piece = pieces[0].reshape(count, heads, HEAD_DIM)
        outgrad_piece = pieces[1].reshape(count, heads, HEAD_DIM)
        query_index = start + jnp.arange(count, dtype=jnp.int32)

        def key_compute(state):
            grad_k, grad_v = state
            logsum_piece = lax.dynamic_slice_in_dim(all_logsum, start, count, 0).T
            delta_piece = lax.dynamic_slice_in_dim(all_delta, start, count, 0).T
            query_doc, unused = doc_layout(doc_lengths, query_index)
            allowed = allowed_mask(query_index, query_doc, my_index, my_doc)[None]
            score = (
                jnp.einsum(
                    "qhd,khd->hqk", query_piece, keys_local, preferred_element_type=jnp.float32
                )
                * scale
            )
            prob = jnp.where(allowed, jnp.exp(score - logsum_piece[:, :, None]), 0.0)
            grad_v = grad_v + jnp.einsum(
                "hqk,qhd->khd",
                prob.astype(jnp.bfloat16),
                outgrad_piece,
                preferred_element_type=jnp.float32,
            )
            prob_grad = jnp.einsum(
                "qhd,khd->hqk", outgrad_piece, mixed_local, preferred_element_type=jnp.float32
            )
            score_grad = (prob * (prob_grad - delta_piece[:, :, None])).astype(jnp.bfloat16)
            grad_k = (
                grad_k
                + jnp.einsum(
                    "hqk,qhd->khd", score_grad, query_piece, preferred_element_type=jnp.float32
                )
                * scale
            )
            return (grad_k, grad_v)

        return lax.cond(query_index[-1] >= my_start, key_compute, lambda kept: kept, state)

    grad_k, grad_v = by_blocks(
        key_grad_step,
        (zeros3, zeros3),
        (
            lax.all_gather(queries.reshape(rows, width), "blk", axis=0, tiled=True),
            lax.all_gather(attended_grad, "blk", axis=0, tiled=True),
        ),
        jnp.int32(0),
    )
    queries_grad = grad_q.astype(jnp.bfloat16)
    keys_grad = grad_k.astype(jnp.bfloat16)
    mixed_grad = grad_v.astype(jnp.bfloat16).reshape(rows, width)
    q_pre_grad = (
        rotate(queries_grad.astype(jnp.float32), cosine, -sine)
        .astype(jnp.bfloat16)
        .reshape(rows, width)
    )
    k_pre_grad = (
        rotate(keys_grad.astype(jnp.float32), cosine, -sine)
        .astype(jnp.bfloat16)
        .reshape(rows, width)
    )
    grad_first = MIX * mixed_grad.astype(jnp.float32)
    value_grad = grad_first.astype(jnp.bfloat16)
    grad_query = outer(normed, q_pre_grad)
    grad_key = outer(normed, k_pre_grad)
    grad_value = outer(normed, value_grad)
    normed_grad = (
        back(q_pre_grad, query_weight)
        + back(k_pre_grad, key_weight)
        + back(value_grad, value_weight)
    )
    grad_attn_gain = jnp.sum(normed_grad * source * inv_first, axis=0)
    scaled_one = normed_grad * attn_gain
    grad_tokens = (
        mid_grad
        + inv_first * scaled_one
        - source * inv_first**3 * jnp.mean(scaled_one * source, axis=-1, keepdims=True)
    )
    summed = (
        lax.psum_scatter(grad_attn_gain, "blk", scatter_dimension=0, tiled=True),
        lax.psum_scatter(grad_query, "blk", scatter_dimension=0, tiled=True),
        lax.psum_scatter(grad_key, "blk", scatter_dimension=0, tiled=True),
        lax.psum_scatter(grad_value, "blk", scatter_dimension=0, tiled=True),
        lax.psum_scatter(grad_out_weight, "blk", scatter_dimension=0, tiled=True),
        lax.psum_scatter(grad_ffn_gain, "blk", scatter_dimension=0, tiled=True),
        lax.psum_scatter(grad_gate, "blk", scatter_dimension=0, tiled=True),
        lax.psum_scatter(grad_up, "blk", scatter_dimension=0, tiled=True),
        lax.psum_scatter(grad_down, "blk", scatter_dimension=0, tiled=True),
    )
    summed = (
        lax.psum(summed[0].astype(jnp.bfloat16), "seq").astype(jnp.float32),
        lax.psum(summed[1].astype(jnp.bfloat16), "seq").astype(jnp.float32),
        lax.psum(summed[2].astype(jnp.bfloat16), "seq").astype(jnp.float32),
        lax.psum(summed[3].astype(jnp.bfloat16), "seq").astype(jnp.float32),
        lax.psum(summed[4].astype(jnp.bfloat16), "seq").astype(jnp.float32),
        lax.psum(summed[5].astype(jnp.bfloat16), "seq").astype(jnp.float32),
        lax.psum(summed[6].astype(jnp.bfloat16), "seq").astype(jnp.float32),
        lax.psum(summed[7].astype(jnp.bfloat16), "seq").astype(jnp.float32),
        lax.psum(summed[8].astype(jnp.bfloat16), "seq").astype(jnp.float32),
    )
    return (
        layer_output,
        grad_tokens,
        grad_first,
        summed[0],
        summed[1],
        summed[2],
        summed[3],
        summed[4],
        summed[5],
        summed[6],
        summed[7],
        summed[8],
    )


def solution(mesh):
    n_seq, n_blk = mesh.shape["seq"], mesh.shape["blk"]

    def chosen(*args):
        rows, width = args[0].shape
        if fits(n_seq, n_blk, rows, width, args[9].shape[1]):
            return local_fast(n_seq, n_blk, *args)
        return local(*args)

    return jax.shard_map(
        chosen,
        mesh=mesh,
        in_specs=(
            P(("seq", "blk"), None),
            P(("seq", "blk"), None),
            P("seq", None),
            P(),
            P(),
            P(),
            P(),
            P(),
            P(),
            P(),
            P(),
            P(),
            P(("seq", "blk"), None),
        ),
        out_specs=(
            P(("seq", "blk"), None),
            P(("seq", "blk"), None),
            P(("seq", "blk"), None),
            P("blk"),
            P("blk", None),
            P("blk", None),
            P("blk", None),
            P("blk", None),
            P("blk"),
            P("blk", None),
            P("blk", None),
            P("blk", None),
        ),
        check_vma=False,
    )
```

```python
import functools
import math
import types

import jax
import jax.numpy as jnp
import numpy as np
from jax import lax
from jax.experimental import pallas as pl
from jax.experimental.pallas import tpu as pltpu
from jax.sharding import PartitionSpec as P

HEAD_DIM = 64


EPS = 1e-05
THETA = 10000.0
MIX = 0.5
NEG = -1e30


def doc_layout(lengths, index):
    ends = jnp.cumsum(lengths, axis=-1)
    past = (index[:, None] >= ends).astype(jnp.int32)
    return (jnp.sum(past, axis=1), index - jnp.sum(past * lengths, axis=1))


def tables(position):
    half = HEAD_DIM // 2
    freq = THETA ** (-(jnp.arange(half).astype(jnp.float32) * 2.0 / HEAD_DIM))
    angle = position.astype(jnp.float32)[:, None] * freq[None, :]
    return (jnp.cos(angle)[:, None, :], jnp.sin(angle)[:, None, :])


def rotate(values, cosine, sine):
    half = values.shape[-1] // 2
    first = values[..., :half]
    second = values[..., half:]
    return jnp.concatenate(
        [first * cosine - second * sine, second * cosine + first * sine], axis=-1
    )


def by_blocks(step, carry, pieces, start):
    rows = pieces[0].shape[0]
    size = math.gcd(rows, 1024)
    count = rows // size
    if count == 1:
        return step(carry, pieces, start)
    stacked = tuple((piece.reshape((count, size) + piece.shape[1:]) for piece in pieces))
    offsets = jnp.arange(count, dtype=jnp.int32) * size

    def turn(state, inputs):
        return (step(state, inputs[1], start + inputs[0]), None)

    result, unused = lax.scan(turn, carry, (offsets, stacked))
    return result


def outer(left, right):
    return lax.dot_general(
        left, right, (((0,), (0,)), ((), ())), preferred_element_type=jnp.float32
    )


def back(left, weight):
    return lax.dot_general(
        left, weight, (((1,), (1,)), ((), ())), preferred_element_type=jnp.float32
    )


TILE = 256
LANES = 128
GROUP = 16
MESH = pl.DeviceIdType.MESH
F32 = jnp.float32
BF16 = jnp.bfloat16


def remote(src, dst, send, recv, where):
    return pltpu.make_async_remote_copy(
        src_ref=src, dst_ref=dst, send_sem=send, recv_sem=recv, device_id=where, device_id_type=MESH
    )


def span(start, size, unit):
    return pl.ds(pl.multiple_of(start, unit), size)


def times(left, right):
    return jnp.dot(left, right, preferred_element_type=F32)


def iota(shape, dim):
    return lax.broadcasted_iota(jnp.int32, shape, dim)


def loop(low, high, body):
    def turn(index, unused):
        body(index)
        return unused

    lax.fori_loop(low, high, turn, 0)


class Trade:
    def __init__(self, blk, n_blk, phase, send, recv, source, place):
        self.blk, self.n_blk = blk, n_blk
        self.send, self.recv = send.at[phase], recv.at[phase]
        self.source, self.place = source, place

    def start(self, peer):
        src, dst = self.source(peer), self.place(self.blk)

        @pl.when(peer != self.blk)
        def _():
            remote(src, dst, self.send.at[peer], self.recv.at[self.blk], {"blk": peer}).start()

        @pl.when(peer == self.blk)
        def _():
            pltpu.make_async_copy(src, dst, self.recv.at[self.blk]).start()

    def arrived(self, peer):
        src, dst = self.source(peer), self.place(peer)

        @pl.when(peer != self.blk)
        def _():
            remote(src, dst, self.send.at[peer], self.recv.at[peer], {"blk": peer}).wait_recv()

        @pl.when(peer == self.blk)
        def _():
            pltpu.make_async_copy(src, dst, self.recv.at[peer]).wait()

    def all_arrived(self):
        loop(0, self.n_blk, self.arrived)

    def all_left(self):
        def left(peer):
            @pl.when(peer != self.blk)
            def _():
                remote(
                    self.source(peer), self.place(self.blk), self.send.at[peer], self.recv.at[self.blk], {"blk": peer}
                ).wait_send()

        loop(0, self.n_blk, left)


class Gift:
    def __init__(self, seq, n_seq, rows, owner, kind, src, dst, send, recv):
        self.seq, self.n_seq, self.rows, self.owner, self.kind = seq, n_seq, rows, owner, kind
        self.src, self.dst, self.send, self.recv = src, dst, send, recv

    def copy(self, other, send):
        dst = self.dst.at[span(other * self.rows, self.rows, self.rows)]
        return remote(self.src, dst, self.send.at[self.kind, send], self.recv.at[self.kind, other], {"seq": send})

    def own(self):
        dst = self.dst.at[pl.ds(self.owner * self.rows, self.rows)]
        return pltpu.make_async_copy(self.src, dst, self.recv.at[self.kind, self.owner])

    def start(self):
        @pl.when(self.seq != self.owner)
        def _():
            self.copy(self.seq, self.owner).start()

        @pl.when(self.seq == self.owner)
        def _():
            self.own().start()

    def arrived(self):
        for other in range(self.n_seq):
            if other == self.owner:
                self.own().wait()
            else:
                self.copy(other, other).wait_recv()

    def left(self):
        @pl.when(self.seq != self.owner)
        def _():
            self.copy(self.seq, self.owner).wait_send()


class Sum:
    def __init__(self, blk, size, part, cgot, rgot, zgot, total, sems):
        self.blk, self.size = blk, size
        self.core, self.chip = lax.rem(blk, 2), lax.div(blk, 2)
        side = lax.div(self.chip, 2)
        self.far = 2 * (1 - side)
        self.partner = self.chip + 1 - 2 * lax.rem(self.chip, 2)
        self.inner = lax.rem(self.chip, 2) != side
        self.far_inner = 2 - side
        self.part, self.cgot, self.rgot, self.zgot, self.total = part, cgot, rgot, zgot, total
        self.csend, self.crecv, self.rsend, self.rrecv, self.zsend, self.zrecv = sems

    def order(self, step):
        return jnp.where(step < 2, self.far + step, jnp.where(step == 2, self.partner, self.chip))

    def chunk(self, index):
        return self.part.at[span(index * self.size, self.size, 32)]

    def mine(self, chip):
        return self.chunk(2 * chip + self.core)

    def swap(self, chip):
        return remote(
            self.chunk(2 * chip + 1 - self.core),
            self.cgot(chip),
            self.csend.at[chip],
            self.crecv.at[chip],
            {"blk": 2 * self.chip + 1 - self.core},
        )

    def lend(self, index):
        return remote(
            self.mine(self.far + index),
            self.rgot(index),
            self.rsend.at[index],
            self.rrecv.at[index],
            {"blk": 2 * self.partner + self.core},
        )

    def send_far(self, index):
        return remote(
            self.mine(self.far + index),
            self.zgot(1),
            self.zsend.at[index],
            self.zrecv.at[1],
            {"blk": 2 * (self.far + index) + self.core},
        )

    def send_near(self):
        return remote(
            self.mine(self.partner),
            self.zgot(0),
            self.zsend.at[2],
            self.zrecv.at[0],
            {"blk": 2 * self.partner + self.core},
        )

    def add(self, mine, other):
        def group(index):
            at = span(index * 32, 32, 32)
            mine[at, :] = (mine[at, :].astype(F32) + other[at, :].astype(F32)).astype(BF16)

        loop(0, self.size // 32, group)

    def begin(self):
        for index in range(2):
            chip = self.far + index
            self.swap(chip).wait()
            self.add(self.mine(chip), self.cgot(chip))

            @pl.when(jnp.logical_not(self.inner))
            def _(index=index):
                self.lend(index).start()

        self.swap(self.partner).wait()
        self.add(self.mine(self.partner), self.cgot(self.partner))
        self.send_near().start()
        self.swap(self.chip).wait()

    def relay(self):
        @pl.when(self.inner)
        def _():
            for index in range(2):
                self.lend(index).wait_recv()
                self.add(self.mine(self.far + index), self.rgot(index))
                self.send_far(index).start()

    def end(self):
        self.send_near().wait_recv()
        self.send_far(0).wait_recv()
        mine, other = self.mine(self.chip), self.cgot(self.chip)

        def group(index):
            at = span(index * 32, 32, 32)
            value = mine[at, :].astype(F32) + other[at, :].astype(F32)
            value = value + self.zgot(0)[at, :].astype(F32) + self.zgot(1)[at, :].astype(F32)
            self.total[at, :] = value.astype(BF16)

        loop(0, self.size // 32, group)

    def left(self):
        self.send_near().wait_send()

        @pl.when(self.inner)
        def _():
            for index in range(2):
                self.send_far(index).wait_send()

        @pl.when(jnp.logical_not(self.inner))
        def _():
            for index in range(2):
                self.lend(index).wait_send()


class TileGift:
    def __init__(self, seq, n_seq, rows, src, dst, send, recv, owner_of):
        self.seq, self.n_seq, self.rows, self.src, self.dst = seq, n_seq, rows, src, dst
        self.send, self.recv, self.owner_of = send, recv, owner_of

    def place(self, other, slot):
        return self.dst.at[span(other * self.rows, self.rows, self.rows), span(slot * TILE, TILE, TILE)]

    def tile(self, index):
        return self.src.at[:, span(index * TILE, TILE, TILE)]

    def start(self, index):
        owner, slot = self.owner_of(index)
        src, dst, recv = self.tile(index), self.place(self.seq, slot), self.recv.at[slot, self.seq]

        @pl.when(owner != self.seq)
        def _():
            remote(src, dst, self.send.at[index], recv, {"seq": owner}).start()

        @pl.when(owner == self.seq)
        def _():
            pltpu.make_async_copy(src, dst, recv).start()

    def arrived(self, low, high):
        def one(slot):
            def other_one(other):
                dst, recv = self.place(other, slot), self.recv.at[slot, other]

                @pl.when(other != self.seq)
                def _():
                    remote(self.tile(0), dst, self.send.at[0], recv, {"seq": other}).wait_recv()

                @pl.when(other == self.seq)
                def _():
                    pltpu.make_async_copy(self.tile(0), dst, recv).wait()

            loop(0, self.n_seq, other_one)

        loop(low, high, one)

    def left(self, count):
        def one(index):
            owner, slot = self.owner_of(index)

            @pl.when(owner != self.seq)
            def _():
                remote(
                    self.tile(index), self.place(self.seq, slot), self.send.at[index], self.recv.at[slot, self.seq],
                    {"seq": owner},
                ).wait_send()

        loop(0, count, one)


class Spread:
    def __init__(self, seq, owner, kind, src, dst, send, recv, local, on_send, on_recv):
        self.seq, self.owner, self.kind, self.src, self.dst = seq, owner, kind, src, dst
        self.send, self.recv, self.local, self.on_send, self.on_recv = send, recv, local, on_send, on_recv
        self.half = src.shape[0] // 2

    def copy(self, bit):
        return remote(
            self.src, self.dst, self.send.at[self.kind, bit], self.recv.at[self.kind], {"seq": self.owner ^ (bit + 1)}
        )

    def onward(self, bit):
        part = self.dst.at[bit * self.half : (bit + 1) * self.half]
        return remote(
            part, part, self.on_send.at[self.kind, bit], self.on_recv.at[self.kind, bit], {"seq": self.owner ^ 3}
        )

    def own(self):
        return pltpu.make_async_copy(self.src, self.dst, self.local.at[self.kind])

    def start(self):
        @pl.when(self.seq == self.owner)
        def _():
            for bit in range(2):
                self.copy(bit).start()
            self.own().start()

    def pass_on(self):
        for bit in range(2):

            @pl.when(self.seq == self.owner ^ (bit + 1))
            def _(bit=bit):
                self.copy(bit).wait_recv()
                self.onward(bit).start()

    def finish(self):
        @pl.when(self.seq == self.owner)
        def _():
            for bit in range(2):
                self.copy(bit).wait_send()
            self.own().wait()

        for bit in range(2):

            @pl.when(self.seq == self.owner ^ (bit + 1))
            def _(bit=bit):
                self.onward(bit).wait_send()

        @pl.when(self.seq == self.owner ^ 3)
        def _():
            for bit in range(2):
                self.onward(bit).wait_recv()


def turn_over(src, dst):
    def one(index):
        at = span(index * TILE, TILE, TILE)
        dst[at, :] = src[:, at].T

    loop(0, src.shape[1] // TILE, one)


def outer_tiles(turned, rhs, part, chip, tiles, rhs_at, part_at):
    rows = span(chip * TILE, TILE, TILE)

    def tile(index):
        value = times(turned[rows, :], rhs[:, span(rhs_at + index * TILE, TILE, TILE)])
        part[rows, span(part_at + index * TILE, TILE, TILE)] = value.astype(BF16)

    loop(0, tiles, tile)


def layer_kernel(
    sizes,
    freq, tokens, first, lengths, attn_gain, ffn_gain, cot,
    h_query, h_key, h_value, h_out, h_gate, h_up, h_down,
    o_layer, o_tokens, o_first, o_gu, o_down, o_out, o_query, o_key, o_value, o_gain,
    v, sem,
):
    rows, width, ff, n_seq, n_blk, split = sizes
    v, sem = types.SimpleNamespace(**v), types.SimpleNamespace(**sem)
    docs = lengths.shape[1]
    chips = n_blk // 2
    scale = HEAD_DIM ** (-0.5)
    seq, blk = lax.axis_index("seq"), lax.axis_index("blk")
    chip_at = lax.div(blk, 2)

    def turned_chip(step):
        return lax.rem(chip_at + step, chips)

    barrier = pltpu.get_barrier_semaphore()
    for step in range(1, n_seq):
        pl.semaphore_signal(barrier, inc=1, device_id={"seq": lax.rem(seq + step, n_seq)}, device_id_type=MESH)
    for step in range(1, n_blk):
        pl.semaphore_signal(barrier, inc=1, device_id={"blk": lax.rem(blk + step, n_blk)}, device_id_type=MESH)

    def load(index, src, dst):
        copy = pltpu.make_async_copy(src, dst, sem.load.at[index])
        copy.start()
        return copy

    load_query = load(0, h_query, v.w_query)
    load_key = load(1, h_key, v.w_key)
    load_value = load(2, h_value, v.w_value)
    load_out = load(3, h_out, v.w_out)
    load_gate = load(4, h_gate, v.w_gate)
    load_up = load(5, h_up, v.w_up)
    load_down = load(6, h_down, v.w_down)

    def norm(group):
        at = span(group * GROUP, GROUP, GROUP)
        x = tokens[at, :].astype(F32)
        inv = lax.rsqrt(jnp.mean(x * x, axis=-1, keepdims=True) + EPS)
        v.normed[at, :] = (x * inv * attn_gain[...]).astype(BF16)
        v.inv_first[at, :] = jnp.broadcast_to(inv, (GROUP, LANES))

    loop(0, rows // GROUP, norm)

    def doc_start(index):
        start, end = jnp.zeros_like(index), jnp.int32(0)
        for doc in range(docs):
            end = end + lengths[0, doc]
            start = jnp.where(index >= end, end, start)
        return start

    half = HEAD_DIM // 2

    def low_half(count):
        return lax.rem(iota((count, LANES), 1), HEAD_DIM) < half

    def set_tables(start, count, cosine_ref, sine_ref):
        index = start + iota((count, LANES), 0)
        angle = (index - doc_start(index)).astype(F32) * freq[...]
        cosine_ref[...] = jnp.cos(angle)
        sine = jnp.sin(angle)
        sine_ref[...] = jnp.where(low_half(count), -sine, sine)

    def halves_changed(u):
        return jnp.where(low_half(u.shape[0]), pltpu.roll(u, LANES - half, 1), pltpu.roll(u, half, 1))

    set_tables(blk * rows, rows, v.cos, v.sin)

    def rotated(u):
        return u * v.cos[...] + halves_changed(u) * v.sin[...]

    cuts = [0]
    for tiles in split:
        cuts.append(cuts[-1] + tiles * TILE)
    wide = max(split) * TILE

    def gift(owner, kind, src, dst):
        return Gift(seq, n_seq, rows, owner, kind, src, dst, sem.xsend, sem.xrecv)

    gift_cot = gift(3, 0, cot, v.buf_a)
    gifts_two = [gift(owner, 0, v.two, v.buf_a) for owner in range(3)]
    each, hidden = split[0], ff // TILE
    gift_gu = TileGift(
        seq, n_seq, rows, v.gate_up, v.buf_b, sem.gusend, sem.gurecv,
        lambda index: (lax.div(index, each), lax.rem(index, each)),
    )
    gift_act = TileGift(seq, n_seq, rows, v.act, v.buf_b, sem.actsend, sem.actrecv, lambda index: (3, index))
    gift_att = gift(2, 2, v.att, v.buf_att)
    gift_mid = gift(2, 3, v.mid_b, v.buf_mid)
    def trade(phase, source, place):
        return Trade(blk, n_blk, phase, sem.asend, sem.arecv, source, place)

    def block_rows(ref):
        return lambda peer: ref.at[span(peer * rows, rows, rows)]

    def block_columns(ref):
        return lambda peer: ref.at[:, span(peer * LANES, LANES, LANES)]

    give_qkv = trade(0, lambda peer: v.pack.at[peer], lambda peer: v.qkv.at[:, span(peer * rows, rows, rows)])
    give_att = trade(1, block_rows(v.ob), block_columns(v.att))
    give_out = trade(2, lambda peer: v.out_pack.at[peer], block_rows(v.out_grad))
    give_grads = trade(
        3, lambda peer: v.pack.at[peer], lambda peer: v.grads.at[:, :, span(peer * LANES, LANES, LANES)]
    )

    give_tail = trade(4, lambda peer: v.tail_sum.at[peer], lambda peer: v.tail_got.at[peer])
    core = lax.rem(blk, 2)
    mate = blk + 1 - 2 * core

    def block_of(step):
        return 2 * turned_chip(step) + core

    def rows_of(block):
        return v.normed_all.at[span(block * rows, rows, rows)]

    def normed_out(step):
        return remote(
            v.normed, rows_of(blk), sem.nsend.at[step - 1], sem.nrecv.at[step - 1], {"blk": block_of(step)}
        )

    def normed_over(step):
        there = rows_of(block_of(step))
        return remote(there, there, sem.fsend.at[step], sem.frecv.at[step], {"blk": mate})

    def mates_normed(step):
        there = rows_of(2 * turned_chip(step) + 1 - core)
        return remote(there, there, sem.fsend.at[step], sem.frecv.at[step], {"blk": mate})

    pl.semaphore_wait(barrier, n_seq + n_blk - 2)
    gift_cot.start()
    own_normed = pltpu.make_async_copy(v.normed, rows_of(blk), sem.nlocal.at[0])
    own_normed.start()

    for item in (load_query, load_key, load_value):
        item.wait()

    def project(step):
        chip = turned_chip(step)
        at = span(chip * TILE, TILE, TILE)
        left = v.normed[...]
        q, k, val = times(left, v.w_query[:, at]), times(left, v.w_key[:, at]), times(left, v.w_value[:, at])
        old = first[:, at].astype(F32)
        for core in range(2):
            peer = 2 * chip + core
            cols = slice(core * LANES, (core + 1) * LANES)
            v.pack[peer, 0] = (rotated(q[:, cols]) * scale).astype(BF16)
            v.pack[peer, 1] = rotated(k[:, cols]).astype(BF16)
            v.pack[peer, 2] = (MIX * val[:, cols] + MIX * old[:, cols]).astype(BF16)
            give_qkv.start(peer)

    loop(1, chips + 1, project)

    load_down.wait()

    def act_back(tile):
        cols = span(tile * TILE, TILE, TILE)
        v.act_grad[:, cols] = back(cot[...], v.w_down[cols, :])

    loop(0, ff // TILE, act_back)

    first_head = iota((TILE, LANES), 1) < HEAD_DIM

    def stacked(values):
        return jnp.concatenate([jnp.where(first_head, values, 0.0), jnp.where(first_head, 0.0, values)], axis=0)

    def unstacked(values):
        return jnp.where(first_head, values[:TILE], values[TILE:])

    def attend(block):
        for core in range(2):
            give_qkv.arrived(2 * block + core)
        at, both = span(block * TILE, TILE, TILE), span(block * 2 * TILE, 2 * TILE, 2 * TILE)
        queries = stacked(v.qkv[0, at, :].astype(F32)).astype(BF16)
        v.q2[both, :] = queries
        v.q2_turned[:, both] = queries.T
        index = block * TILE + lax.rem(iota((2 * TILE, 1), 0), TILE)
        start = doc_start(index)
        v.top[...] = jnp.full((2 * TILE, LANES), NEG, F32)

        def scores(tile):
            cols = span(tile * TILE, TILE, TILE)
            score = back(v.q2[both, :], v.qkv[1, cols, :])
            key = tile * TILE + iota((2 * TILE, TILE), 1)
            score = jnp.where((key <= index) & (key >= start), score, NEG)
            v.score[:, cols] = score
            v.top[...] = jnp.maximum(v.top[...], jnp.maximum(score[:, :LANES], score[:, LANES:]))

        loop(0, block + 1, scores)
        top = jnp.max(v.top[...], axis=1, keepdims=True)
        v.top[...] = jnp.zeros((2 * TILE, LANES), F32)
        v.o2[...] = jnp.zeros((2 * TILE, LANES), F32)

        def weights(tile):
            cols = span(tile * TILE, TILE, TILE)
            weight = jnp.exp(v.score[:, cols] - top)
            v.top[...] += weight[:, :LANES] + weight[:, LANES:]
            weight = weight.astype(BF16)
            v.prob[both, cols] = weight
            v.o2[...] += times(weight, v.qkv[2, cols, :])

        loop(0, block + 1, weights)
        inv = 1.0 / jnp.sum(v.top[...], axis=1, keepdims=True)
        v.row[both, :] = jnp.broadcast_to(inv, (2 * TILE, LANES))
        attended = unstacked(v.o2[...] * inv)
        v.o32[at, :] = attended
        v.ob[at, :] = attended.astype(BF16)
        for core in range(2):
            give_att.start(2 * block + core)

    loop(0, chips, attend)
    loop(
        0,
        chips,
        lambda block: set_tables(
            block * TILE,
            TILE,
            v.score.at[:TILE, span(block * TILE, LANES, LANES)],
            v.score.at[:TILE, span(block * TILE + LANES, LANES, LANES)],
        ),
    )
    give_att.all_arrived()
    gift_att.start()
    normed_out(1).start()
    normed_out(3).start()

    load_out.wait()

    def middle(tile):
        cols = span(tile * TILE, TILE, TILE)
        value = tokens[:, cols].astype(F32) + times(v.att[...], v.w_out[:, cols])
        v.mid[:, cols] = value

    loop(0, width // TILE, middle)

    def norm_two(group):
        at = span(group * GROUP, GROUP, GROUP)
        x = v.mid[at, :]
        inv = lax.rsqrt(jnp.mean(x * x, axis=-1, keepdims=True) + EPS)
        v.two[at, :] = (x * inv * ffn_gain[...]).astype(BF16)
        v.inv_second[at, :] = jnp.broadcast_to(inv, (GROUP, LANES))

    loop(0, rows // GROUP, norm_two)
    for item in gifts_two:
        item.start()

    for item in (load_gate, load_up):
        item.wait()
    v.two_grad[...] = jnp.zeros((rows, width), F32)

    def feed(step):
        tile = lax.rem(split[0] + step, hidden)
        cols = span(tile * TILE, TILE, TILE)
        gate = times(v.two[...], v.w_gate[:, cols])
        up = times(v.two[...], v.w_up[:, cols])
        act_grad = v.act_grad[:, cols]
        sigma = jax.nn.sigmoid(gate)
        silu = gate * sigma
        act = (silu * up).astype(BF16)
        gate_grad = (act_grad * up * sigma * (1.0 + gate * (1.0 - sigma))).astype(BF16)
        up_grad = (act_grad * silu).astype(BF16)
        v.act[:, cols] = act
        v.gate_up[:, cols] = gate_grad
        v.gate_up[:, span(ff + tile * TILE, TILE, TILE)] = up_grad
        gift_gu.start(tile)
        gift_gu.start(hidden + tile)
        gift_act.start(tile)
        v.two_grad[...] += back(gate_grad, v.w_gate[:, cols]) + back(up_grad, v.w_up[:, cols])

    loop(0, hidden, feed)
    v.gain_rows[...] = jnp.zeros((16, width), F32)

    def norm_two_back(group):
        at = span(group * GROUP, GROUP, GROUP)
        x, grad, inv = v.mid[at, :], v.two_grad[at, :], v.inv_second[at, :1]
        term = grad * x * inv
        v.gain_rows[8:16, :] += term[:8] + term[8:]
        scaled = grad * ffn_gain[...]
        mean = jnp.mean(scaled * x, axis=-1, keepdims=True)
        value = cot[at, :].astype(F32) + inv * scaled - x * (inv * inv * inv * mean)
        v.mid_grad[at, :] = value
        v.mid_b[at, :] = value.astype(BF16)

    loop(0, rows // GROUP, norm_two_back)
    gift_mid.start()

    def out_back(step):
        chip = turned_chip(step)
        value = back(v.mid_b[...], v.w_out[span(chip * TILE, TILE, TILE), :]).astype(BF16)
        for core in range(2):
            v.out_pack[2 * chip + core] = value[:, core * LANES : (core + 1) * LANES]
            give_out.start(2 * chip + core)

    loop(1, chips + 1, out_back)

    def layer_out(tile):
        cols = span(tile * TILE, TILE, TILE)
        o_layer[:, cols] = v.mid[:, cols] + times(v.act[...], v.w_down[:, cols])

    loop(0, width // TILE, layer_out)
    own_normed.wait()
    normed_over(0).start()
    for step in (1, 3):
        normed_out(chips - step).wait_recv()
        normed_over(step).start()

    chunk, down = width // n_blk, ff // n_blk

    def sems_of(index):
        return tuple(
            item.at[index] for item in (sem.csend, sem.crecv, sem.rsend, sem.rrecv, sem.zsend, sem.zrecv)
        )

    def stack_in(ref, top, cols):
        return lambda index: ref.at[span(top + index * chunk, chunk, 32), cols]

    def square_in(ref, more, low, high):
        def place(index):
            index = index + more
            return ref.at[
                span(lax.rem(index, 2) * down, down, 32), span(lax.div(index, 2) * width + low, high - low, LANES)
            ]

        return place

    def piece(index, low, high):
        cols = slice(low, high)
        return Sum(
            blk, chunk, v.w_gate.at[:, cols], stack_in(v.w_up, 0, cols), stack_in(v.w_up, chips * chunk, cols),
            stack_in(v.w_up, (chips + 2) * chunk, cols), v.total.at[:, cols], sems_of(index),
        )

    edges = [0, each // 3, 2 * each // 3, each]
    thirds = [piece(index, edges[index] * TILE, edges[index + 1] * TILE) for index in range(3)]
    last = split[2] * TILE
    halves = [piece(0, 0, last), piece(1, last, last + width)]
    bounds = [0, width // 8, 3 * width // 8, 5 * width // 8, 7 * width // 8, width]
    fifths = [
        Sum(
            blk, down, v.w_down.at[:, low:high], square_in(v.w_up, 0, low, high), square_in(v.w_gate, 0, low, high),
            square_in(v.w_gate, 2, low, high), v.total_down.at[:, low:high], sems_of(index),
        )
        for index, (low, high) in enumerate(zip(bounds[:-1], bounds[1:]))
    ]
    first_two, third_one, fourth = seq < 2, seq == 2, seq == 3

    def spread(owner, kind, src, dst):
        return Spread(
            seq, owner, kind, src, dst, sem.gsend, sem.grecv, sem.glocal, sem.onsend, sem.onrecv
        )

    spreads = [
        [
            spread(
                owner,
                3 * owner + index,
                v.total.at[:, edges[index] * TILE : edges[index + 1] * TILE],
                o_gu.at[:, cuts[owner] + edges[index] * TILE : cuts[owner] + edges[index + 1] * TILE],
            )
            for index in range(3)
        ]
        for owner in range(2)
    ] + [
        [
            spread(2, 6, v.total.at[:, :last], o_gu.at[:, cuts[2] : cuts[3]]),
            spread(2, 7, v.total.at[:, last : last + width], o_out),
        ],
        [
            spread(3, 8 + index, v.total_down.at[:, low:high], o_down.at[:, low:high])
            for index, (low, high) in enumerate(zip(bounds[:-1], bounds[1:]))
        ],
    ]
    def products(item, turned, rhs, tiles, rhs_at, part_at):
        def one(step):
            chip = item.order(step)
            outer_tiles(turned, rhs, v.w_gate, chip, tiles, rhs_at, part_at)

        loop(0, chips, one)

    def swaps(item):
        loop(0, chips, lambda step: item.swap(item.order(step)).start())

    def gate_up_piece(index):
        gift_gu.arrived(edges[index], edges[index + 1])
        at = edges[index] * TILE
        products(thirds[index], v.turned, v.buf_b, edges[index + 1] - edges[index], at, at)

    def down_products(low, high):
        def one(step):
            index = lax.rem(split[0] + step, hidden)
            gift_act.arrived(index, index + 1)
            at = span(index * TILE, TILE, TILE)
            v.turned[:TILE, :] = v.buf_b[:, at].T
            v.w_down[at, :] = times(v.turned[:TILE, :], v.buf_a[...]).astype(BF16)

        loop(low, high, one)

    def down_swaps():
        for item in fifths:
            swaps(item)

    for owner in range(2):

        @pl.when(seq == owner)
        def _(owner=owner):
            gifts_two[owner].arrived()
            turn_over(v.buf_a, v.turned)

    @pl.when(fourth)
    def _():
        gift_cot.arrived()
        down_products(0, hidden // 4)


    def prepare(block):
        at, both = span(block * TILE, TILE, TILE), span(block * 2 * TILE, 2 * TILE, 2 * TILE)
        grad = (stacked(v.out_grad[at, :].astype(F32)) * v.row[both, :]).astype(BF16)
        v.do2[both, :] = grad
        v.do2_turned[:, both] = grad.T
        attended = v.o32[at, :]
        delta = jnp.sum(grad.astype(F32) * jnp.concatenate([attended, attended], axis=0), axis=1, keepdims=True)
        v.row[both, :] = jnp.broadcast_to(delta, (2 * TILE, LANES))
        v.dq[both, :] = jnp.zeros((2 * TILE, LANES), F32)

    for chip in (0, 2, 3, 1):
        for side in range(2):
            give_out.arrived(2 * chip + side)
        if chip == 1:
            normed_out(2).start()
        prepare(chip)
    give_qkv.all_left()

    def key_block(block):
        at = span(block * TILE, TILE, TILE)
        v.dk[...] = jnp.zeros((LANES, TILE), F32)
        v.dv[...] = jnp.zeros((LANES, TILE), F32)

        def query_block(other):
            both = span(other * 2 * TILE, 2 * TILE, 2 * TILE)
            prob = v.prob[both, at]
            grad = back(v.do2[both, :], v.qkv[2, at, :])
            score_grad = (prob.astype(F32) * (grad - v.row[both, :1])).astype(BF16)
            v.dk[...] += times(v.q2_turned[:, both], score_grad)
            v.dv[...] += times(v.do2_turned[:, both], prob)
            v.dq[both, :] += times(score_grad, v.qkv[1, at, :])

        loop(block, chips, query_block)
        cosine = v.score[:TILE, span(block * TILE, LANES, LANES)]
        sine = v.score[:TILE, span(block * TILE + LANES, LANES, LANES)]

        def rotated_back(u):
            u = u.astype(BF16).astype(F32)
            return (u * cosine - halves_changed(u) * sine).astype(BF16)

        dq = rotated_back(unstacked(v.dq[span(block * 2 * TILE, 2 * TILE, 2 * TILE), :]) * scale)
        dk = rotated_back(v.dk[...].T)
        dv = (MIX * v.dv[...].T.astype(BF16).astype(F32)).astype(BF16)
        for index, value in enumerate((dq, dk, dv)):
            v.heads_grad[at, index * LANES : (index + 1) * LANES] = value
            for half_at in range(2):
                v.pack[2 * block + half_at, index] = value[half_at * rows : (half_at + 1) * rows]
        for half_at in range(2):
            give_grads.start(2 * block + half_at)

    loop(0, chips, key_block)

    def when(which, *steps):
        @pl.when(which)
        def _():
            for step in steps:
                step()

    def ended(item, goes):
        def step():
            item.end()
            for other in goes:
                other.start()

        return step

    def first_half():
        gifts_two[2].arrived()
        turn_over(v.buf_a, v.turned)
        gift_gu.arrived(0, split[2])
        products(halves[0], v.turned, v.buf_b, split[2], 0, 0)
        swaps(halves[0])
        halves[0].begin()

    def second_half():
        gift_att.arrived()
        gift_mid.arrived()
        turn_over(v.buf_att, v.turned)
        products(halves[1], v.turned, v.buf_mid, width // TILE, 0, last)
        swaps(halves[1])

    def gate_up_gone(index):
        gate_up_piece(index)
        swaps(thirds[index])

    when(first_two, lambda: gate_up_gone(0), thirds[0].begin, lambda: gate_up_gone(1), thirds[1].begin)
    when(third_one, first_half)
    when(fourth, lambda: down_products(hidden // 4, hidden), down_swaps, fifths[0].begin, fifths[1].begin)

    normed_out(2).wait_recv()
    normed_over(2).start()
    for step in range(chips):
        mates_normed(step).wait_recv()

    def project_back(index):
        value = outer(v.normed_all[:, span(index * TILE, TILE, TILE)], v.heads_grad[...]).astype(BF16)
        v.tail_part[2 * index] = value[:LANES]
        v.tail_part[2 * index + 1] = value[LANES:]

    loop(0, width // TILE, project_back)
    quarter = LANES // n_seq

    def tail_share(step):
        other = lax.rem(seq + step, n_seq)
        return remote(
            v.tail_part.at[:, span(other * quarter, quarter, quarter)],
            v.tail_shares.at[step - 1],
            sem.qsend.at[step - 1],
            sem.qrecv.at[step - 1],
            {"seq": other},
        )

    for step in range(1, n_seq):
        tail_share(step).start()

    when(first_two, thirds[0].relay, lambda: gate_up_gone(2))
    when(third_one, second_half)

    def tail_add(index):
        value = v.tail_part[index, span(seq * quarter, quarter, quarter), :].astype(F32)
        for step in range(1, n_seq):
            value = value + v.tail_shares[step - 1, index].astype(F32)
        v.tail_sum[index] = value.astype(BF16)
        give_tail.start(index)

    for step in range(1, n_seq):
        tail_share(step).wait()
    loop(0, n_blk, tail_add)
    when(first_two, thirds[2].begin)
    when(third_one, halves[1].begin)

    give_grads.all_arrived()

    def gone(index, *owners):
        return [spreads[owner][index] for owner in owners]

    when(fourth, fifths[0].relay, fifths[2].begin)

    def normed_back(tile):
        at = span(tile * TILE, TILE, TILE)
        o_tokens[:, at] = (
            back(v.grads[0], v.w_query[at, :])
            + back(v.grads[1], v.w_key[at, :])
            + back(v.grads[2], v.w_value[at, :])
        )

    loop(0, width // TILE, normed_back)
    o_first[...] = v.grads[2].astype(F32)
    when(first_two, thirds[1].relay, ended(thirds[0], []))
    for item in gone(0, 0, 1):
        item.start()

    def norm_back(group):
        at = span(group * GROUP, GROUP, GROUP)
        x, grad, inv = tokens[at, :].astype(F32), o_tokens[at, :], v.inv_first[at, :1]
        term = grad * x * inv
        v.gain_rows[0:8, :] += term[:8] + term[8:]
        scaled = grad * attn_gain[...]
        mean = jnp.mean(scaled * x, axis=-1, keepdims=True)
        o_tokens[at, :] = v.mid_grad[at, :] + inv * scaled - x * (inv * inv * inv * mean)

    loop(0, rows // GROUP, norm_back)

    for peer in range(n_blk):
        v.gains[peer] = v.gain_rows[:, peer * LANES : (peer + 1) * LANES]

    def gain_copy(step):
        other = lax.rem(blk + step, n_blk)
        return remote(
            v.gains.at[other], v.gain_got.at[step - 1], sem.hsend.at[step - 1], sem.hrecv.at[step - 1],
            {"blk": other},
        )

    for step in range(1, n_blk):
        gain_copy(step).start()
    when(fourth, ended(fifths[0], gone(0, 3)), fifths[1].relay, fifths[3].begin, fifths[4].begin)

    when(first_two, ended(thirds[1], gone(1, 0, 1)))
    when(third_one, halves[0].relay, ended(halves[0], gone(0, 2)))
    when(fourth, ended(fifths[1], gone(1, 3)))

    give_tail.all_arrived()
    for index in range(3):
        for peer in range(n_blk):
            v.tail_done[index, :, peer * LANES : (peer + 1) * LANES] = v.tail_got[
                peer, :, index * LANES : (index + 1) * LANES
            ]

    def tail_spread(index, step, owner):
        at = span(owner * quarter, quarter, quarter)
        return remote(
            v.tail_done.at[index],
            (o_query, o_key, o_value)[index].at[at],
            sem.tsend.at[index, step - 1],
            sem.trecv.at[index, owner],
            {"seq": lax.rem(seq + step, n_seq)},
        )

    def tail_own(index):
        at = span(seq * quarter, quarter, quarter)
        return pltpu.make_async_copy(
            v.tail_done.at[index], (o_query, o_key, o_value)[index].at[at], sem.trecv.at[index, seq]
        )

    for index in range(3):
        tail_own(index).start()
        for step in range(1, n_seq):
            tail_spread(index, step, seq).start()

    def pass_on(*items):
        for item in items:
            item.pass_on()

    pass_on(*gone(0, 0, 1, 3))
    when(first_two, thirds[2].relay, ended(thirds[2], gone(2, 0, 1)))
    when(third_one, halves[1].relay, ended(halves[1], gone(1, 2)))
    when(fourth, fifths[2].relay, fifths[3].relay, ended(fifths[2], gone(2, 3)))
    value = v.gains[blk]
    for step in range(1, n_blk):
        gain_copy(step).wait()
        value = value + v.gain_got[step - 1]
    v.gain_sum[seq] = value
    for step in range(1, n_seq):
        other = lax.rem(seq + step, n_seq)
        mine = v.gain_sum.at[seq]
        remote(mine, mine, sem.isend.at[step - 1], sem.irecv.at[seq], {"seq": other}).start()

    when(fourth, fifths[4].relay, ended(fifths[3], gone(3, 3)), ended(fifths[4], gone(4, 3)))
    pass_on(*gone(0, 2), *gone(1, 3, 0, 1))
    pass_on(*gone(2, 0, 1, 3), *gone(1, 2), *gone(3, 3), *gone(4, 3))

    for step in range(1, n_seq):
        other = lax.rem(seq + step, n_seq)
        theirs = v.gain_sum.at[other]
        remote(theirs, theirs, sem.isend.at[step - 1], sem.irecv.at[other], {"seq": other}).wait()
    value = v.gain_sum[0]
    for group in range(1, n_seq):
        value = value + v.gain_sum[group]
    o_gain[0:8, :] = jnp.broadcast_to(jnp.sum(value[:8], axis=0, keepdims=True), (8, LANES))
    o_gain[8:16, :] = jnp.broadcast_to(jnp.sum(value[8:], axis=0, keepdims=True), (8, LANES))

    for index in range(3):
        tail_own(index).wait()
        for step in range(1, n_seq):
            tail_spread(index, step, seq).wait_send()
            tail_spread(index, step, lax.rem(seq + step, n_seq)).wait_recv()
    for item in sum(spreads, []):
        item.finish()
    for item in [gift_cot, gift_att, gift_mid] + gifts_two:
        item.left()
    gift_gu.left(2 * hidden)
    gift_act.left(hidden)
    for item in (give_att, give_out, give_grads, give_tail):
        item.all_left()
    for step in range(chips):
        normed_over(step).wait_send()
        if step:
            normed_out(step).wait_send()

    @pl.when(first_two)
    def _():
        for item in thirds:
            item.left()

    @pl.when(third_one)
    def _():
        for item in halves:
            item.left()

    @pl.when(fourth)
    def _():
        for item in fifths:
            item.left()


def finish_kernel(
    layer, tokens, first, gu, down, out, query, key, value, gain,
    o_layer, o_tokens, o_first, o_gain, o_gain_two, o_query, o_key, o_value, o_out, o_gate, o_up, o_down,
    kept, small, large, sem_kept_in, sem_kept_out, sem_in, sem_out,
):
    kept_in = [
        pltpu.make_async_copy(src, kept[index], sem_kept_in.at[index])
        for index, src in enumerate((layer, tokens, first))
    ]
    kept_out = [
        pltpu.make_async_copy(kept[index], dst, sem_kept_out.at[index])
        for index, dst in enumerate((o_layer, o_tokens, o_first))
    ]
    ff = o_gate.shape[1]
    sources = [query, key, value, out, down, gu.at[:, :ff], gu.at[:, ff:]]
    targets = [o_query, o_key, o_value, o_out, o_down, o_gate, o_up]
    loads = [pltpu.make_async_copy(src, small[index], sem_in.at[index]) for index, src in enumerate(sources)]
    stores = [pltpu.make_async_copy(large[index], dst, sem_out.at[index]) for index, dst in enumerate(targets)]
    for item in loads + kept_in:
        item.start()
    for index in range(len(sources)):
        loads[index].wait()

        def group(step, index=index):
            at = span(step * GROUP, GROUP, GROUP)
            large[index][at, :] = small[index][at, :].astype(F32)

        loop(0, targets[index].shape[0] // GROUP, group)
        stores[index].start()
    for coming, going in zip(kept_in, kept_out):
        coming.wait()
        going.start()
    o_gain[...] = gain[0:1, :]
    o_gain_two[...] = gain[8:9, :]
    for item in stores + kept_out:
        item.wait()


def finish(layer, tokens, first, gu, down, out, query, key, value, gain):
    hbm, vmem = pl.BlockSpec(memory_space=pl.ANY), pl.BlockSpec(memory_space=pltpu.VMEM)
    shape = jax.ShapeDtypeStruct
    ff = gu.shape[1] // 2
    dims = [query.shape, key.shape, value.shape, out.shape, down.shape, (gu.shape[0], ff), (gu.shape[0], ff)]
    dma = pltpu.SemaphoreType.DMA
    results = pl.pallas_call(
        finish_kernel,
        out_shape=tuple(
            shape(each, F32)
            for each in (
                layer.shape, tokens.shape, first.shape, (1, LANES), (1, LANES), dims[0], dims[1], dims[2], dims[3], dims[5], dims[6], dims[4]
            )
        ),
        in_specs=[hbm] * 9 + [vmem],
        out_specs=(hbm,) * 3 + (vmem,) * 2 + (hbm,) * 7,
        scratch_shapes=(
            [pltpu.VMEM(each.shape, F32) for each in (layer, tokens, first)],
            [pltpu.VMEM(each, BF16) for each in dims],
            [pltpu.VMEM(each, F32) for each in dims],
            dma((3,)), dma((3,)), dma((7,)), dma((7,)),
        ),
        compiler_params=pltpu.CompilerParams(vmem_limit_bytes=63 * 1024 * 1024),
        name="finish",
    )(layer, tokens, first, gu, down, out, query, key, value, gain)
    return results[:3] + (results[3][0],) + results[5:9] + (results[4][0],) + results[9:]


def tile_split(width, ff):
    tiles, more = 2 * ff // TILE, width // TILE
    each = -(-(tiles + more) // 3)
    return (each, each, tiles - 2 * each)


def fits(n_seq, n_blk, rows, width, ff):
    return (
        n_seq == 4
        and n_blk % 2 == 0
        and n_blk * LANES == width
        and rows == LANES
        and ff % TILE == 0
        and (ff // n_blk) % 32 == 0
        and 2 * (ff // n_blk) <= width
        and n_blk == 8
        and width == n_seq * TILE
    )


def local_fast(
    n_seq,
    n_blk,
    tokens,
    first_values,
    doc_lengths,
    attn_gain,
    query_weight,
    key_weight,
    value_weight,
    out_weight,
    ffn_gain,
    gate_weight,
    up_weight,
    down_weight,
    cotangent,
):
    rows, width = tokens.shape
    ff = gate_weight.shape[1]
    split = tile_split(width, ff)
    sizes = (rows, width, ff, n_seq, n_blk, split)
    half = HEAD_DIM // 2
    freq = THETA ** (-(np.arange(half) * 2.0 / HEAD_DIM))
    freq = np.tile(freq, LANES // half)[None, :].astype(np.float32)
    wide = max(split) * TILE
    chunk, down, chips = width // n_blk, ff // n_blk, n_blk // 2
    all_rows, group = n_seq * rows, n_blk * rows
    vmem = pl.BlockSpec(memory_space=pltpu.VMEM)
    hbm = pl.BlockSpec(memory_space=pl.ANY)
    smem = pl.BlockSpec(memory_space=pltpu.SMEM)
    shape = jax.ShapeDtypeStruct

    def half_type(*dims):
        return pltpu.VMEM(dims, BF16)

    def full_type(*dims):
        return pltpu.VMEM(dims, F32)

    scratch = dict(
        w_query=half_type(width, width), w_key=half_type(width, width), w_value=half_type(width, width),
        w_out=half_type(width, width), w_gate=half_type(width, ff), w_up=half_type(width, ff),
        w_down=half_type(ff, width),
        normed=half_type(rows, width), inv_first=full_type(rows, LANES), inv_second=full_type(rows, LANES),
        cos=full_type(rows, LANES), sin=full_type(rows, LANES),
        pack=half_type(n_blk, 3, rows, LANES), qkv=half_type(3, group, LANES),
        q2=half_type(2 * group, LANES), do2=half_type(2 * group, LANES), prob=half_type(2 * group, group),
        score=full_type(2 * TILE, group), top=full_type(2 * TILE, LANES), o2=full_type(2 * TILE, LANES),
        row=full_type(2 * group, LANES), o32=full_type(group, LANES), ob=half_type(group, LANES),
        dq=full_type(2 * group, LANES), dk=full_type(LANES, TILE), dv=full_type(LANES, TILE),
        q2_turned=half_type(LANES, 2 * group), do2_turned=half_type(LANES, 2 * group),
        att=half_type(rows, width), mid=full_type(rows, width), two=half_type(rows, width),
        act=half_type(rows, ff), act_grad=full_type(rows, ff), gate_up=half_type(rows, 2 * ff), two_grad=full_type(rows, width),
        mid_grad=full_type(rows, width), mid_b=half_type(rows, width),
        out_pack=half_type(n_blk, rows, LANES), out_grad=half_type(group, LANES),
        grads=half_type(3, rows, width),
        buf_a=half_type(all_rows, width), buf_b=half_type(all_rows, ff), buf_att=half_type(all_rows, width),
        buf_mid=half_type(all_rows, width), normed_all=half_type(group, width), heads_grad=half_type(group, 3 * LANES),
        tail_part=half_type(n_blk, chunk, 3 * LANES), tail_shares=half_type(n_seq - 1, n_blk, chunk // n_seq, 3 * LANES),
        tail_sum=half_type(n_blk, chunk // n_seq, 3 * LANES), tail_got=half_type(n_blk, chunk // n_seq, 3 * LANES),
        tail_done=half_type(3, chunk // n_seq, width),
        turned=half_type(width, all_rows),
        total=half_type(chunk, wide), total_down=half_type(down, width),
        gain_rows=full_type(16, width), gains=full_type(n_blk, 16, LANES), gain_got=full_type(n_blk - 1, 16, LANES),
        gain_sum=full_type(n_seq, 16, LANES),
    )
    dma = pltpu.SemaphoreType.DMA
    sems = dict(
        load=dma((7,)), asend=dma((5, n_blk)), arecv=dma((5, n_blk)), xsend=dma((4, n_seq)), xrecv=dma((4, n_seq)),
        gusend=dma((2 * ff // TILE,)), gurecv=dma((split[0], n_seq)), actsend=dma((ff // TILE,)),
        actrecv=dma((ff // TILE, n_seq)),
        csend=dma((5, chips)), crecv=dma((5, chips)), rsend=dma((5, 2)), rrecv=dma((5, 2)), zsend=dma((5, 3)),
        zrecv=dma((5, 2)), gsend=dma((13, 2)), grecv=dma((13,)), glocal=dma((13,)), onsend=dma((13, 2)), onrecv=dma((13, 2)),
        nsend=dma((chips - 1,)), nrecv=dma((chips - 1,)), fsend=dma((chips,)), frecv=dma((chips,)), nlocal=dma((1,)),
        qsend=dma((n_seq - 1,)), qrecv=dma((n_seq - 1,)), tsend=dma((3, n_seq - 1)), trecv=dma((3, n_seq)),
        hsend=dma((n_blk - 1,)), hrecv=dma((n_blk - 1,)), isend=dma((n_seq - 1,)), irecv=dma((n_seq,)),
    )
    layer, grad_tokens, grad_first, out_gu, out_down, out_out, out_query, out_key, out_value, out_gain = pl.pallas_call(
        functools.partial(layer_kernel, sizes),
        out_shape=(
            shape((rows, width), F32),
            shape((rows, width), F32),
            shape((rows, width), F32),
            shape((chunk, 2 * ff), BF16),
            shape((down, width), BF16),
            shape((chunk, width), BF16),
            shape((chunk, width), BF16),
            shape((chunk, width), BF16),
            shape((chunk, width), BF16),
            shape((16, LANES), F32),
        ),
        in_specs=[vmem, vmem, vmem, smem, vmem, vmem, vmem] + [hbm] * 7,
        out_specs=(vmem, vmem, vmem) + (hbm,) * 6 + (vmem,),
        scratch_shapes=(scratch, sems),
        compiler_params=pltpu.CompilerParams(
            collective_id=0, has_side_effects=True, vmem_limit_bytes=63 * 1024 * 1024
        ),
        name="layer",
    )(
        freq, tokens, first_values, doc_lengths, attn_gain[None, :], ffn_gain[None, :], cotangent,
        query_weight, key_weight, value_weight, out_weight, gate_weight, up_weight, down_weight,
    )
    return finish(layer, grad_tokens, grad_first, out_gu, out_down, out_out, out_query, out_key, out_value, out_gain)


def local(
    tokens,
    first_values,
    doc_lengths,
    attn_gain,
    query_weight,
    key_weight,
    value_weight,
    out_weight,
    ffn_gain,
    gate_weight,
    up_weight,
    down_weight,
    cotangent,
):
    rows, width = tokens.shape
    heads = width // HEAD_DIM
    scale = HEAD_DIM ** (-0.5)
    shape3 = (rows, heads, HEAD_DIM)
    my_start = lax.axis_index("blk") * rows
    my_index = my_start + jnp.arange(rows, dtype=jnp.int32)
    my_doc, my_pos = doc_layout(doc_lengths, my_index)
    cosine, sine = tables(my_pos)
    source = tokens.astype(jnp.float32)
    inv_first = lax.rsqrt(jnp.mean(source * source, axis=-1, keepdims=True) + EPS)
    normed = (source * inv_first * attn_gain).astype(jnp.bfloat16)
    query_pre = jnp.dot(normed, query_weight, preferred_element_type=jnp.float32)
    key_pre = jnp.dot(normed, key_weight, preferred_element_type=jnp.float32)
    value_pre = jnp.dot(normed, value_weight, preferred_element_type=jnp.float32)
    queries = rotate(query_pre.reshape(shape3), cosine, sine).astype(jnp.bfloat16)
    keys = rotate(key_pre.reshape(shape3), cosine, sine).astype(jnp.bfloat16).reshape(rows, width)
    mixed = (MIX * value_pre + MIX * first_values.astype(jnp.float32)).astype(jnp.bfloat16)
    keys_local = keys.reshape(shape3)
    mixed_local = mixed.reshape(shape3)

    def allowed_mask(query_index, query_doc, key_index, key_doc):
        return (query_doc[:, None] == key_doc[None, :]) & (
            key_index[None, :] <= query_index[:, None]
        )

    def forward_step(state, pieces, start):
        count = pieces[0].shape[0]
        keys_piece = pieces[0].reshape(count, heads, HEAD_DIM)
        values_piece = pieces[1].reshape(count, heads, HEAD_DIM)
        key_index = start + jnp.arange(count, dtype=jnp.int32)

        def forward_compute(state):
            high, total, accum = state
            key_doc, unused = doc_layout(doc_lengths, key_index)
            allowed = allowed_mask(my_index, my_doc, key_index, key_doc)[None]
            score = (
                jnp.einsum("qhd,khd->hqk", queries, keys_piece, preferred_element_type=jnp.float32)
                * scale
            )
            score = jnp.where(allowed, score, NEG)
            new_high = jnp.maximum(high, jnp.max(score, axis=-1))
            weight = jnp.where(allowed, jnp.exp(score - new_high[:, :, None]), 0.0)
            factor = jnp.exp(high - new_high)
            total = total * factor + jnp.sum(weight, axis=-1)
            accum = accum * factor.T[:, :, None] + jnp.einsum(
                "hqk,khd->qhd",
                weight.astype(jnp.bfloat16),
                values_piece,
                preferred_element_type=jnp.float32,
            )
            return (new_high, total, accum)

        return lax.cond(start <= my_index[-1], forward_compute, lambda kept: kept, state)

    def query_grad_step(grad_q, pieces, start):
        count = pieces[0].shape[0]
        keys_piece = pieces[0].reshape(count, heads, HEAD_DIM)
        values_piece = pieces[1].reshape(count, heads, HEAD_DIM)
        key_index = start + jnp.arange(count, dtype=jnp.int32)

        def query_compute(grad_q):
            key_doc, unused = doc_layout(doc_lengths, key_index)
            allowed = allowed_mask(my_index, my_doc, key_index, key_doc)[None]
            score = (
                jnp.einsum("qhd,khd->hqk", queries, keys_piece, preferred_element_type=jnp.float32)
                * scale
            )
            prob = jnp.where(allowed, jnp.exp(score - logsum[:, :, None]), 0.0)
            prob_grad = jnp.einsum(
                "qhd,khd->hqk", outgrad_local, values_piece, preferred_element_type=jnp.float32
            )
            score_grad = (prob * (prob_grad - delta[:, :, None])).astype(jnp.bfloat16)
            return (
                grad_q
                + jnp.einsum(
                    "hqk,khd->qhd", score_grad, keys_piece, preferred_element_type=jnp.float32
                )
                * scale
            )

        return lax.cond(start <= my_index[-1], query_compute, lambda kept: kept, grad_q)

    init = (
        jnp.full((heads, rows), NEG, jnp.float32),
        jnp.zeros((heads, rows), jnp.float32),
        jnp.zeros(shape3, jnp.float32),
    )
    state = by_blocks(
        forward_step,
        init,
        (
            lax.all_gather(keys, "blk", axis=0, tiled=True),
            lax.all_gather(mixed, "blk", axis=0, tiled=True),
        ),
        jnp.int32(0),
    )
    high, total, accum = state
    logsum = high + jnp.log(total)
    attended = accum / total.T[:, :, None]
    attended_b = attended.astype(jnp.bfloat16).reshape(rows, width)
    mid = source + jnp.dot(attended_b, out_weight, preferred_element_type=jnp.float32)
    inv_second = lax.rsqrt(jnp.mean(mid * mid, axis=-1, keepdims=True) + EPS)
    normed_two = (mid * inv_second * ffn_gain).astype(jnp.bfloat16)
    gate = jnp.dot(normed_two, gate_weight, preferred_element_type=jnp.float32)
    up = jnp.dot(normed_two, up_weight, preferred_element_type=jnp.float32)
    act = (jax.nn.silu(gate) * up).astype(jnp.bfloat16)
    layer_output = mid + jnp.dot(act, down_weight, preferred_element_type=jnp.float32)
    cot_float = cotangent.astype(jnp.float32)
    grad_down = outer(act, cotangent)
    act_grad = back(cotangent, down_weight)
    sigma = jax.nn.sigmoid(gate)
    gate_grad = (act_grad * up * sigma * (1.0 + gate * (1.0 - sigma))).astype(jnp.bfloat16)
    up_grad = (act_grad * gate * sigma).astype(jnp.bfloat16)
    grad_gate = outer(normed_two, gate_grad)
    grad_up = outer(normed_two, up_grad)
    normed_two_grad = back(gate_grad, gate_weight) + back(up_grad, up_weight)
    grad_ffn_gain = jnp.sum(normed_two_grad * mid * inv_second, axis=0)
    scaled_two = normed_two_grad * ffn_gain
    mid_grad = (
        cot_float
        + inv_second * scaled_two
        - mid * inv_second**3 * jnp.mean(scaled_two * mid, axis=-1, keepdims=True)
    )
    mid_grad_b = mid_grad.astype(jnp.bfloat16)
    grad_out_weight = outer(attended_b, mid_grad_b)
    attended_grad = back(mid_grad_b, out_weight).astype(jnp.bfloat16)
    outgrad_local = attended_grad.reshape(shape3)
    delta = jnp.sum(outgrad_local.astype(jnp.float32) * attended, axis=-1).T
    zeros3 = jnp.zeros(shape3, jnp.float32)
    grad_q = by_blocks(
        query_grad_step,
        zeros3,
        (
            lax.all_gather(keys, "blk", axis=0, tiled=True),
            lax.all_gather(mixed, "blk", axis=0, tiled=True),
        ),
        jnp.int32(0),
    )
    all_logsum, all_delta = (
        lax.all_gather(logsum.T, "blk", axis=0, tiled=True),
        lax.all_gather(delta.T, "blk", axis=0, tiled=True),
    )

    def key_grad_step(state, pieces, start):
        count = pieces[0].shape[0]
        query_piece = pieces[0].reshape(count, heads, HEAD_DIM)
        outgrad_piece = pieces[1].reshape(count, heads, HEAD_DIM)
        query_index = start + jnp.arange(count, dtype=jnp.int32)

        def key_compute(state):
            grad_k, grad_v = state
            logsum_piece = lax.dynamic_slice_in_dim(all_logsum, start, count, 0).T
            delta_piece = lax.dynamic_slice_in_dim(all_delta, start, count, 0).T
            query_doc, unused = doc_layout(doc_lengths, query_index)
            allowed = allowed_mask(query_index, query_doc, my_index, my_doc)[None]
            score = (
                jnp.einsum(
                    "qhd,khd->hqk", query_piece, keys_local, preferred_element_type=jnp.float32
                )
                * scale
            )
            prob = jnp.where(allowed, jnp.exp(score - logsum_piece[:, :, None]), 0.0)
            grad_v = grad_v + jnp.einsum(
                "hqk,qhd->khd",
                prob.astype(jnp.bfloat16),
                outgrad_piece,
                preferred_element_type=jnp.float32,
            )
            prob_grad = jnp.einsum(
                "qhd,khd->hqk", outgrad_piece, mixed_local, preferred_element_type=jnp.float32
            )
            score_grad = (prob * (prob_grad - delta_piece[:, :, None])).astype(jnp.bfloat16)
            grad_k = (
                grad_k
                + jnp.einsum(
                    "hqk,qhd->khd", score_grad, query_piece, preferred_element_type=jnp.float32
                )
                * scale
            )
            return (grad_k, grad_v)

        return lax.cond(query_index[-1] >= my_start, key_compute, lambda kept: kept, state)

    grad_k, grad_v = by_blocks(
        key_grad_step,
        (zeros3, zeros3),
        (
            lax.all_gather(queries.reshape(rows, width), "blk", axis=0, tiled=True),
            lax.all_gather(attended_grad, "blk", axis=0, tiled=True),
        ),
        jnp.int32(0),
    )
    queries_grad = grad_q.astype(jnp.bfloat16)
    keys_grad = grad_k.astype(jnp.bfloat16)
    mixed_grad = grad_v.astype(jnp.bfloat16).reshape(rows, width)
    q_pre_grad = (
        rotate(queries_grad.astype(jnp.float32), cosine, -sine)
        .astype(jnp.bfloat16)
        .reshape(rows, width)
    )
    k_pre_grad = (
        rotate(keys_grad.astype(jnp.float32), cosine, -sine)
        .astype(jnp.bfloat16)
        .reshape(rows, width)
    )
    grad_first = MIX * mixed_grad.astype(jnp.float32)
    value_grad = grad_first.astype(jnp.bfloat16)
    grad_query = outer(normed, q_pre_grad)
    grad_key = outer(normed, k_pre_grad)
    grad_value = outer(normed, value_grad)
    normed_grad = (
        back(q_pre_grad, query_weight)
        + back(k_pre_grad, key_weight)
        + back(value_grad, value_weight)
    )
    grad_attn_gain = jnp.sum(normed_grad * source * inv_first, axis=0)
    scaled_one = normed_grad * attn_gain
    grad_tokens = (
        mid_grad
        + inv_first * scaled_one
        - source * inv_first**3 * jnp.mean(scaled_one * source, axis=-1, keepdims=True)
    )
    summed = (
        lax.psum_scatter(grad_attn_gain, "blk", scatter_dimension=0, tiled=True),
        lax.psum_scatter(grad_query, "blk", scatter_dimension=0, tiled=True),
        lax.psum_scatter(grad_key, "blk", scatter_dimension=0, tiled=True),
        lax.psum_scatter(grad_value, "blk", scatter_dimension=0, tiled=True),
        lax.psum_scatter(grad_out_weight, "blk", scatter_dimension=0, tiled=True),
        lax.psum_scatter(grad_ffn_gain, "blk", scatter_dimension=0, tiled=True),
        lax.psum_scatter(grad_gate, "blk", scatter_dimension=0, tiled=True),
        lax.psum_scatter(grad_up, "blk", scatter_dimension=0, tiled=True),
        lax.psum_scatter(grad_down, "blk", scatter_dimension=0, tiled=True),
    )
    summed = (
        lax.psum(summed[0].astype(jnp.bfloat16), "seq").astype(jnp.float32),
        lax.psum(summed[1].astype(jnp.bfloat16), "seq").astype(jnp.float32),
        lax.psum(summed[2].astype(jnp.bfloat16), "seq").astype(jnp.float32),
        lax.psum(summed[3].astype(jnp.bfloat16), "seq").astype(jnp.float32),
        lax.psum(summed[4].astype(jnp.bfloat16), "seq").astype(jnp.float32),
        lax.psum(summed[5].astype(jnp.bfloat16), "seq").astype(jnp.float32),
        lax.psum(summed[6].astype(jnp.bfloat16), "seq").astype(jnp.float32),
        lax.psum(summed[7].astype(jnp.bfloat16), "seq").astype(jnp.float32),
        lax.psum(summed[8].astype(jnp.bfloat16), "seq").astype(jnp.float32),
    )
    return (
        layer_output,
        grad_tokens,
        grad_first,
        summed[0],
        summed[1],
        summed[2],
        summed[3],
        summed[4],
        summed[5],
        summed[6],
        summed[7],
        summed[8],
    )


def solution(mesh):
    n_seq, n_blk = mesh.shape["seq"], mesh.shape["blk"]

    def chosen(*args):
        rows, width = args[0].shape
        if fits(n_seq, n_blk, rows, width, args[9].shape[1]):
            return local_fast(n_seq, n_blk, *args)
        return local(*args)

    return jax.shard_map(
        chosen,
        mesh=mesh,
        in_specs=(
            P(("seq", "blk"), None),
            P(("seq", "blk"), None),
            P("seq", None),
            P(),
            P(),
            P(),
            P(),
            P(),
            P(),
            P(),
            P(),
            P(),
            P(("seq", "blk"), None),
        ),
        out_specs=(
            P(("seq", "blk"), None),
            P(("seq", "blk"), None),
            P(("seq", "blk"), None),
            P("blk"),
            P("blk", None),
            P("blk", None),
            P("blk", None),
            P("blk", None),
            P("blk"),
            P("blk", None),
            P("blk", None),
            P("blk", None),
        ),
        check_vma=False,
    )
```

```python
import functools
import math
import types

import jax
import jax.numpy as jnp
import numpy as np
from jax import lax
from jax.experimental import pallas as pl
from jax.experimental.pallas import tpu as pltpu
from jax.sharding import PartitionSpec as P

HEAD_DIM = 64


EPS = 1e-05
THETA = 10000.0
MIX = 0.5
NEG = -1e30


def doc_layout(lengths, index):
    ends = jnp.cumsum(lengths, axis=-1)
    past = (index[:, None] >= ends).astype(jnp.int32)
    return (jnp.sum(past, axis=1), index - jnp.sum(past * lengths, axis=1))


def tables(position):
    half = HEAD_DIM // 2
    freq = THETA ** (-(jnp.arange(half).astype(jnp.float32) * 2.0 / HEAD_DIM))
    angle = position.astype(jnp.float32)[:, None] * freq[None, :]
    return (jnp.cos(angle)[:, None, :], jnp.sin(angle)[:, None, :])


def rotate(values, cosine, sine):
    half = values.shape[-1] // 2
    first = values[..., :half]
    second = values[..., half:]
    return jnp.concatenate(
        [first * cosine - second * sine, second * cosine + first * sine], axis=-1
    )


def by_blocks(step, carry, pieces, start):
    rows = pieces[0].shape[0]
    size = math.gcd(rows, 1024)
    count = rows // size
    if count == 1:
        return step(carry, pieces, start)
    stacked = tuple((piece.reshape((count, size) + piece.shape[1:]) for piece in pieces))
    offsets = jnp.arange(count, dtype=jnp.int32) * size

    def turn(state, inputs):
        return (step(state, inputs[1], start + inputs[0]), None)

    result, unused = lax.scan(turn, carry, (offsets, stacked))
    return result


def outer(left, right):
    return lax.dot_general(
        left, right, (((0,), (0,)), ((), ())), preferred_element_type=jnp.float32
    )


def back(left, weight):
    return lax.dot_general(
        left, weight, (((1,), (1,)), ((), ())), preferred_element_type=jnp.float32
    )


TILE = 256
LANES = 128
GROUP = 16
MESH = pl.DeviceIdType.MESH
F32 = jnp.float32
BF16 = jnp.bfloat16


def remote(src, dst, send, recv, where):
    return pltpu.make_async_remote_copy(
        src_ref=src, dst_ref=dst, send_sem=send, recv_sem=recv, device_id=where, device_id_type=MESH
    )


def span(start, size, unit):
    return pl.ds(pl.multiple_of(start, unit), size)


def times(left, right):
    return jnp.dot(left, right, preferred_element_type=F32)


def iota(shape, dim):
    return lax.broadcasted_iota(jnp.int32, shape, dim)


def loop(low, high, body):
    def turn(index, unused):
        body(index)
        return unused

    lax.fori_loop(low, high, turn, 0)


class Trade:
    def __init__(self, blk, n_blk, phase, send, recv, source, place):
        self.blk, self.n_blk = blk, n_blk
        self.send, self.recv = send.at[phase], recv.at[phase]
        self.source, self.place = source, place

    def start(self, peer):
        src, dst = self.source(peer), self.place(self.blk)

        @pl.when(peer != self.blk)
        def _():
            remote(src, dst, self.send.at[peer], self.recv.at[self.blk], {"blk": peer}).start()

        @pl.when(peer == self.blk)
        def _():
            pltpu.make_async_copy(src, dst, self.recv.at[self.blk]).start()

    def arrived(self, peer):
        src, dst = self.source(peer), self.place(peer)

        @pl.when(peer != self.blk)
        def _():
            remote(src, dst, self.send.at[peer], self.recv.at[peer], {"blk": peer}).wait_recv()

        @pl.when(peer == self.blk)
        def _():
            pltpu.make_async_copy(src, dst, self.recv.at[peer]).wait()

    def all_arrived(self):
        loop(0, self.n_blk, self.arrived)

    def all_left(self):
        def left(peer):
            @pl.when(peer != self.blk)
            def _():
                remote(
                    self.source(peer), self.place(self.blk), self.send.at[peer], self.recv.at[self.blk], {"blk": peer}
                ).wait_send()

        loop(0, self.n_blk, left)


class Gift:
    def __init__(self, seq, n_seq, rows, owner, kind, src, dst, send, recv):
        self.seq, self.n_seq, self.rows, self.owner, self.kind = seq, n_seq, rows, owner, kind
        self.src, self.dst, self.send, self.recv = src, dst, send, recv

    def copy(self, other, send):
        dst = self.dst.at[span(other * self.rows, self.rows, self.rows)]
        return remote(self.src, dst, self.send.at[self.kind, send], self.recv.at[self.kind, other], {"seq": send})

    def own(self):
        dst = self.dst.at[pl.ds(self.owner * self.rows, self.rows)]
        return pltpu.make_async_copy(self.src, dst, self.recv.at[self.kind, self.owner])

    def start(self):
        @pl.when(self.seq != self.owner)
        def _():
            self.copy(self.seq, self.owner).start()

        @pl.when(self.seq == self.owner)
        def _():
            self.own().start()

    def arrived(self):
        for other in range(self.n_seq):
            if other == self.owner:
                self.own().wait()
            else:
                self.copy(other, other).wait_recv()

    def left(self):
        @pl.when(self.seq != self.owner)
        def _():
            self.copy(self.seq, self.owner).wait_send()


class Sum:
    def __init__(self, blk, size, part, cgot, rgot, zgot, total, sems):
        self.blk, self.size = blk, size
        self.core, self.chip = lax.rem(blk, 2), lax.div(blk, 2)
        side = lax.div(self.chip, 2)
        self.far = 2 * (1 - side)
        self.partner = self.chip + 1 - 2 * lax.rem(self.chip, 2)
        self.inner = lax.rem(self.chip, 2) != side
        self.far_inner = 2 - side
        self.part, self.cgot, self.rgot, self.zgot, self.total = part, cgot, rgot, zgot, total
        self.csend, self.crecv, self.rsend, self.rrecv, self.zsend, self.zrecv = sems

    def order(self, step):
        return jnp.where(step < 2, self.far + step, jnp.where(step == 2, self.partner, self.chip))

    def chunk(self, index):
        return self.part.at[span(index * self.size, self.size, 32)]

    def mine(self, chip):
        return self.chunk(2 * chip + self.core)

    def swap(self, chip):
        return remote(
            self.chunk(2 * chip + 1 - self.core),
            self.cgot(chip),
            self.csend.at[chip],
            self.crecv.at[chip],
            {"blk": 2 * self.chip + 1 - self.core},
        )

    def lend(self, index):
        return remote(
            self.mine(self.far + index),
            self.rgot(index),
            self.rsend.at[index],
            self.rrecv.at[index],
            {"blk": 2 * self.partner + self.core},
        )

    def send_far(self, index):
        return remote(
            self.mine(self.far + index),
            self.zgot(1),
            self.zsend.at[index],
            self.zrecv.at[1],
            {"blk": 2 * (self.far + index) + self.core},
        )

    def send_near(self):
        return remote(
            self.mine(self.partner),
            self.zgot(0),
            self.zsend.at[2],
            self.zrecv.at[0],
            {"blk": 2 * self.partner + self.core},
        )

    def add(self, mine, other):
        def group(index):
            at = span(index * 32, 32, 32)
            mine[at, :] = (mine[at, :].astype(F32) + other[at, :].astype(F32)).astype(BF16)

        loop(0, self.size // 32, group)

    def begin(self):
        for index in range(2):
            chip = self.far + index
            self.swap(chip).wait()
            self.add(self.mine(chip), self.cgot(chip))

            @pl.when(jnp.logical_not(self.inner))
            def _(index=index):
                self.lend(index).start()

        self.swap(self.partner).wait()
        self.add(self.mine(self.partner), self.cgot(self.partner))
        self.send_near().start()
        self.swap(self.chip).wait()

    def relay(self):
        @pl.when(self.inner)
        def _():
            for index in range(2):
                self.lend(index).wait_recv()
                self.add(self.mine(self.far + index), self.rgot(index))
                self.send_far(index).start()

    def end(self):
        self.send_near().wait_recv()
        self.send_far(0).wait_recv()
        mine, other = self.mine(self.chip), self.cgot(self.chip)

        def group(index):
            at = span(index * 32, 32, 32)
            value = mine[at, :].astype(F32) + other[at, :].astype(F32)
            value = value + self.zgot(0)[at, :].astype(F32) + self.zgot(1)[at, :].astype(F32)
            self.total[at, :] = value.astype(BF16)

        loop(0, self.size // 32, group)

    def left(self):
        self.send_near().wait_send()

        @pl.when(self.inner)
        def _():
            for index in range(2):
                self.send_far(index).wait_send()

        @pl.when(jnp.logical_not(self.inner))
        def _():
            for index in range(2):
                self.lend(index).wait_send()


class TileGift:
    def __init__(self, seq, n_seq, rows, src, dst, send, recv, owner_of):
        self.seq, self.n_seq, self.rows, self.src, self.dst = seq, n_seq, rows, src, dst
        self.send, self.recv, self.owner_of = send, recv, owner_of

    def place(self, other, slot):
        return self.dst.at[span(other * self.rows, self.rows, self.rows), span(slot * TILE, TILE, TILE)]

    def tile(self, index):
        return self.src.at[:, span(index * TILE, TILE, TILE)]

    def start(self, index):
        owner, slot = self.owner_of(index)
        src, dst, recv = self.tile(index), self.place(self.seq, slot), self.recv.at[slot, self.seq]

        @pl.when(owner != self.seq)
        def _():
            remote(src, dst, self.send.at[index], recv, {"seq": owner}).start()

        @pl.when(owner == self.seq)
        def _():
            pltpu.make_async_copy(src, dst, recv).start()

    def arrived(self, low, high):
        def one(slot):
            def other_one(other):
                dst, recv = self.place(other, slot), self.recv.at[slot, other]

                @pl.when(other != self.seq)
                def _():
                    remote(self.tile(0), dst, self.send.at[0], recv, {"seq": other}).wait_recv()

                @pl.when(other == self.seq)
                def _():
                    pltpu.make_async_copy(self.tile(0), dst, recv).wait()

            loop(0, self.n_seq, other_one)

        loop(low, high, one)

    def left(self, count):
        def one(index):
            owner, slot = self.owner_of(index)

            @pl.when(owner != self.seq)
            def _():
                remote(
                    self.tile(index), self.place(self.seq, slot), self.send.at[index], self.recv.at[slot, self.seq],
                    {"seq": owner},
                ).wait_send()

        loop(0, count, one)


class Spread:
    def __init__(self, seq, owner, kind, src, dst, send, recv, local, on_send, on_recv):
        self.seq, self.owner, self.kind, self.src, self.dst = seq, owner, kind, src, dst
        self.send, self.recv, self.local, self.on_send, self.on_recv = send, recv, local, on_send, on_recv
        self.half = src.shape[0] // 2

    def copy(self, bit):
        return remote(
            self.src, self.dst, self.send.at[self.kind, bit], self.recv.at[self.kind], {"seq": self.owner ^ (bit + 1)}
        )

    def onward(self, bit):
        part = self.dst.at[bit * self.half : (bit + 1) * self.half]
        return remote(
            part, part, self.on_send.at[self.kind, bit], self.on_recv.at[self.kind, bit], {"seq": self.owner ^ 3}
        )

    def own(self):
        return pltpu.make_async_copy(self.src, self.dst, self.local.at[self.kind])

    def start(self):
        @pl.when(self.seq == self.owner)
        def _():
            for bit in range(2):
                self.copy(bit).start()
            self.own().start()

    def pass_on(self):
        for bit in range(2):

            @pl.when(self.seq == self.owner ^ (bit + 1))
            def _(bit=bit):
                self.copy(bit).wait_recv()
                self.onward(bit).start()

    def finish(self):
        @pl.when(self.seq == self.owner)
        def _():
            for bit in range(2):
                self.copy(bit).wait_send()
            self.own().wait()

        for bit in range(2):

            @pl.when(self.seq == self.owner ^ (bit + 1))
            def _(bit=bit):
                self.onward(bit).wait_send()

        @pl.when(self.seq == self.owner ^ 3)
        def _():
            for bit in range(2):
                self.onward(bit).wait_recv()


def turn_over(src, dst):
    def one(index):
        at = span(index * TILE, TILE, TILE)
        dst[at, :] = src[:, at].T

    loop(0, src.shape[1] // TILE, one)


def outer_tiles(turned, rhs, part, chip, tiles, rhs_at, part_at):
    rows = span(chip * TILE, TILE, TILE)

    def tile(index):
        value = times(turned[rows, :], rhs[:, span(rhs_at + index * TILE, TILE, TILE)])
        part[rows, span(part_at + index * TILE, TILE, TILE)] = value.astype(BF16)

    loop(0, tiles, tile)


def layer_kernel(
    sizes,
    freq, tokens, first, lengths, attn_gain, ffn_gain, cot,
    h_query, h_key, h_value, h_out, h_gate, h_up, h_down,
    o_layer, o_tokens, o_first, o_gu, o_down, o_out, o_query, o_key, o_value, o_gain,
    v, sem,
):
    rows, width, ff, n_seq, n_blk, split = sizes
    v, sem = types.SimpleNamespace(**v), types.SimpleNamespace(**sem)
    docs = lengths.shape[1]
    chips = n_blk // 2
    scale = HEAD_DIM ** (-0.5)
    seq, blk = lax.axis_index("seq"), lax.axis_index("blk")
    chip_at = lax.div(blk, 2)

    def turned_chip(step):
        return lax.rem(chip_at + step, chips)

    barrier = pltpu.get_barrier_semaphore()
    for step in range(1, n_seq):
        pl.semaphore_signal(barrier, inc=1, device_id={"seq": lax.rem(seq + step, n_seq)}, device_id_type=MESH)
    for step in range(1, n_blk):
        pl.semaphore_signal(barrier, inc=1, device_id={"blk": lax.rem(blk + step, n_blk)}, device_id_type=MESH)

    def load(index, src, dst):
        copy = pltpu.make_async_copy(src, dst, sem.load.at[index])
        copy.start()
        return copy

    load_query = load(0, h_query, v.w_query)
    load_key = load(1, h_key, v.w_key)
    load_value = load(2, h_value, v.w_value)
    load_out = load(3, h_out, v.w_out)
    load_gate = load(4, h_gate, v.w_gate)
    load_up = load(5, h_up, v.w_up)
    load_down = load(6, h_down, v.w_down)

    def norm(group):
        at = span(group * GROUP, GROUP, GROUP)
        x = tokens[at, :].astype(F32)
        inv = lax.rsqrt(jnp.mean(x * x, axis=-1, keepdims=True) + EPS)
        v.normed[at, :] = (x * inv * attn_gain[...]).astype(BF16)
        v.inv_first[at, :] = jnp.broadcast_to(inv, (GROUP, LANES))

    loop(0, rows // GROUP, norm)

    def doc_start(index):
        start, end = jnp.zeros_like(index), jnp.int32(0)
        for doc in range(docs):
            end = end + lengths[0, doc]
            start = jnp.where(index >= end, end, start)
        return start

    half = HEAD_DIM // 2

    def low_half(count):
        return lax.rem(iota((count, LANES), 1), HEAD_DIM) < half

    def set_tables(start, count, cosine_ref, sine_ref):
        index = start + iota((count, LANES), 0)
        angle = (index - doc_start(index)).astype(F32) * freq[...]
        cosine_ref[...] = jnp.cos(angle)
        sine = jnp.sin(angle)
        sine_ref[...] = jnp.where(low_half(count), -sine, sine)

    def halves_changed(u):
        return jnp.where(low_half(u.shape[0]), pltpu.roll(u, LANES - half, 1), pltpu.roll(u, half, 1))

    set_tables(blk * rows, rows, v.cos, v.sin)

    def rotated(u):
        return u * v.cos[...] + halves_changed(u) * v.sin[...]

    cuts = [0]
    for tiles in split:
        cuts.append(cuts[-1] + tiles * TILE)
    wide = max(split) * TILE

    def gift(owner, kind, src, dst):
        return Gift(seq, n_seq, rows, owner, kind, src, dst, sem.xsend, sem.xrecv)

    gift_cot = gift(3, 0, cot, v.buf_a)
    gifts_two = [gift(owner, 0, v.two, v.buf_a) for owner in range(3)]
    each, hidden = split[0], ff // TILE
    gift_gu = TileGift(
        seq, n_seq, rows, v.gate_up, v.buf_b, sem.gusend, sem.gurecv,
        lambda index: (lax.div(index, each), lax.rem(index, each)),
    )
    gift_act = TileGift(seq, n_seq, rows, v.act, v.buf_b, sem.actsend, sem.actrecv, lambda index: (3, index))
    gift_att = gift(2, 2, v.att, v.buf_att)
    gift_mid = gift(2, 3, v.mid_b, v.buf_mid)
    def trade(phase, source, place):
        return Trade(blk, n_blk, phase, sem.asend, sem.arecv, source, place)

    def block_rows(ref):
        return lambda peer: ref.at[span(peer * rows, rows, rows)]

    def block_columns(ref):
        return lambda peer: ref.at[:, span(peer * LANES, LANES, LANES)]

    give_qkv = trade(0, lambda peer: v.pack.at[peer], lambda peer: v.qkv.at[:, span(peer * rows, rows, rows)])
    give_att = trade(1, block_rows(v.ob), block_columns(v.att))
    give_out = trade(2, lambda peer: v.out_pack.at[peer], block_rows(v.out_grad))
    give_grads = trade(
        3, lambda peer: v.pack.at[peer], lambda peer: v.grads.at[:, :, span(peer * LANES, LANES, LANES)]
    )

    give_tail = trade(4, lambda peer: v.tail_sum.at[peer], lambda peer: v.tail_got.at[peer])
    core = lax.rem(blk, 2)
    mate = blk + 1 - 2 * core

    def block_of(step):
        return 2 * turned_chip(step) + core

    def rows_of(block):
        return v.normed_all.at[span(block * rows, rows, rows)]

    def normed_out(step):
        return remote(
            v.normed, rows_of(blk), sem.nsend.at[step - 1], sem.nrecv.at[step - 1], {"blk": block_of(step)}
        )

    def normed_over(step):
        there = rows_of(block_of(step))
        return remote(there, there, sem.fsend.at[step], sem.frecv.at[step], {"blk": mate})

    def mates_normed(step):
        there = rows_of(2 * turned_chip(step) + 1 - core)
        return remote(there, there, sem.fsend.at[step], sem.frecv.at[step], {"blk": mate})

    pl.semaphore_wait(barrier, n_seq + n_blk - 2)
    gift_cot.start()
    own_normed = pltpu.make_async_copy(v.normed, rows_of(blk), sem.nlocal.at[0])
    own_normed.start()

    for item in (load_query, load_key, load_value):
        item.wait()

    def project(step):
        chip = turned_chip(step)
        at = span(chip * TILE, TILE, TILE)
        left = v.normed[...]
        q, k, val = times(left, v.w_query[:, at]), times(left, v.w_key[:, at]), times(left, v.w_value[:, at])
        old = first[:, at].astype(F32)
        for core in range(2):
            peer = 2 * chip + core
            cols = slice(core * LANES, (core + 1) * LANES)
            v.pack[peer, 0] = (rotated(q[:, cols]) * scale).astype(BF16)
            v.pack[peer, 1] = rotated(k[:, cols]).astype(BF16)
            v.pack[peer, 2] = (MIX * val[:, cols] + MIX * old[:, cols]).astype(BF16)
            give_qkv.start(peer)

    loop(1, chips + 1, project)

    load_down.wait()

    def act_back(tile):
        cols = span(tile * TILE, TILE, TILE)
        v.act_grad[:, cols] = back(cot[...], v.w_down[cols, :])

    loop(0, ff // TILE, act_back)

    first_head = iota((TILE, LANES), 1) < HEAD_DIM

    def stacked(values):
        return jnp.concatenate([jnp.where(first_head, values, 0.0), jnp.where(first_head, 0.0, values)], axis=0)

    def unstacked(values):
        return jnp.where(first_head, values[:TILE], values[TILE:])

    def attend(block):
        for core in range(2):
            give_qkv.arrived(2 * block + core)
        at, both = span(block * TILE, TILE, TILE), span(block * 2 * TILE, 2 * TILE, 2 * TILE)
        queries = stacked(v.qkv[0, at, :].astype(F32)).astype(BF16)
        v.q2[both, :] = queries
        v.q2_turned[:, both] = queries.T
        index = block * TILE + lax.rem(iota((2 * TILE, 1), 0), TILE)
        start = doc_start(index)
        v.top[...] = jnp.full((2 * TILE, LANES), NEG, F32)

        def scores(tile):
            cols = span(tile * TILE, TILE, TILE)
            score = back(v.q2[both, :], v.qkv[1, cols, :])
            key = tile * TILE + iota((2 * TILE, TILE), 1)
            score = jnp.where((key <= index) & (key >= start), score, NEG)
            v.score[:, cols] = score
            v.top[...] = jnp.maximum(v.top[...], jnp.maximum(score[:, :LANES], score[:, LANES:]))

        loop(0, block + 1, scores)
        top = jnp.max(v.top[...], axis=1, keepdims=True)
        v.top[...] = jnp.zeros((2 * TILE, LANES), F32)
        v.o2[...] = jnp.zeros((2 * TILE, LANES), F32)

        def weights(tile):
            cols = span(tile * TILE, TILE, TILE)
            weight = jnp.exp(v.score[:, cols] - top)
            v.top[...] += weight[:, :LANES] + weight[:, LANES:]
            weight = weight.astype(BF16)
            v.prob[both, cols] = weight
            v.o2[...] += times(weight, v.qkv[2, cols, :])

        loop(0, block + 1, weights)
        inv = 1.0 / jnp.sum(v.top[...], axis=1, keepdims=True)
        v.row[both, :] = jnp.broadcast_to(inv, (2 * TILE, LANES))
        attended = unstacked(v.o2[...] * inv)
        v.o32[at, :] = attended
        v.ob[at, :] = attended.astype(BF16)
        for core in range(2):
            give_att.start(2 * block + core)

    loop(0, chips, attend)
    loop(
        0,
        chips,
        lambda block: set_tables(
            block * TILE,
            TILE,
            v.score.at[:TILE, span(block * TILE, LANES, LANES)],
            v.score.at[:TILE, span(block * TILE + LANES, LANES, LANES)],
        ),
    )
    give_att.all_arrived()
    gift_att.start()
    normed_out(1).start()
    normed_out(3).start()

    load_out.wait()

    def middle(tile):
        cols = span(tile * TILE, TILE, TILE)
        value = tokens[:, cols].astype(F32) + times(v.att[...], v.w_out[:, cols])
        v.mid[:, cols] = value

    loop(0, width // TILE, middle)

    def norm_two(group):
        at = span(group * GROUP, GROUP, GROUP)
        x = v.mid[at, :]
        inv = lax.rsqrt(jnp.mean(x * x, axis=-1, keepdims=True) + EPS)
        v.two[at, :] = (x * inv * ffn_gain[...]).astype(BF16)
        v.inv_second[at, :] = jnp.broadcast_to(inv, (GROUP, LANES))

    loop(0, rows // GROUP, norm_two)
    for item in gifts_two:
        item.start()

    for item in (load_gate, load_up):
        item.wait()
    v.two_grad[...] = jnp.zeros((rows, width), F32)

    def feed(step):
        tile = lax.rem(split[0] + step, hidden)
        cols = span(tile * TILE, TILE, TILE)
        gate = times(v.two[...], v.w_gate[:, cols])
        up = times(v.two[...], v.w_up[:, cols])
        act_grad = v.act_grad[:, cols]
        sigma = jax.nn.sigmoid(gate)
        silu = gate * sigma
        act = (silu * up).astype(BF16)
        gate_grad = (act_grad * up * sigma * (1.0 + gate * (1.0 - sigma))).astype(BF16)
        up_grad = (act_grad * silu).astype(BF16)
        v.act[:, cols] = act
        v.gate_up[:, cols] = gate_grad
        v.gate_up[:, span(ff + tile * TILE, TILE, TILE)] = up_grad
        gift_gu.start(tile)
        gift_gu.start(hidden + tile)
        gift_act.start(tile)
        v.two_grad[...] += back(gate_grad, v.w_gate[:, cols]) + back(up_grad, v.w_up[:, cols])

    loop(0, hidden, feed)
    v.gain_rows[...] = jnp.zeros((16, width), F32)

    def norm_two_back(group):
        at = span(group * GROUP, GROUP, GROUP)
        x, grad, inv = v.mid[at, :], v.two_grad[at, :], v.inv_second[at, :1]
        term = grad * x * inv
        v.gain_rows[8:16, :] += term[:8] + term[8:]
        scaled = grad * ffn_gain[...]
        mean = jnp.mean(scaled * x, axis=-1, keepdims=True)
        value = cot[at, :].astype(F32) + inv * scaled - x * (inv * inv * inv * mean)
        v.mid_grad[at, :] = value
        v.mid_b[at, :] = value.astype(BF16)

    loop(0, rows // GROUP, norm_two_back)
    gift_mid.start()

    def out_back(step):
        chip = turned_chip(step)
        value = back(v.mid_b[...], v.w_out[span(chip * TILE, TILE, TILE), :]).astype(BF16)
        for core in range(2):
            v.out_pack[2 * chip + core] = value[:, core * LANES : (core + 1) * LANES]
            give_out.start(2 * chip + core)

    loop(1, chips + 1, out_back)

    def layer_out(tile):
        cols = span(tile * TILE, TILE, TILE)
        o_layer[:, cols] = v.mid[:, cols] + times(v.act[...], v.w_down[:, cols])

    loop(0, width // TILE, layer_out)
    own_normed.wait()
    normed_over(0).start()
    for step in (1, 3):
        normed_out(chips - step).wait_recv()
        normed_over(step).start()

    chunk, down = width // n_blk, ff // n_blk

    def sems_of(index):
        return tuple(
            item.at[index] for item in (sem.csend, sem.crecv, sem.rsend, sem.rrecv, sem.zsend, sem.zrecv)
        )

    def stack_in(ref, top, cols):
        return lambda index: ref.at[span(top + index * chunk, chunk, 32), cols]

    def square_in(ref, more, low, high):
        def place(index):
            index = index + more
            return ref.at[
                span(lax.rem(index, 2) * down, down, 32), span(lax.div(index, 2) * width + low, high - low, LANES)
            ]

        return place

    def piece(index, low, high):
        cols = slice(low, high)
        return Sum(
            blk, chunk, v.w_gate.at[:, cols], stack_in(v.w_up, 0, cols), stack_in(v.w_up, chips * chunk, cols),
            stack_in(v.w_up, (chips + 2) * chunk, cols), v.total.at[:, cols], sems_of(index),
        )

    edges = [0, each // 3, 2 * each // 3, each]
    thirds = [piece(index, edges[index] * TILE, edges[index + 1] * TILE) for index in range(3)]
    last = split[2] * TILE
    half_out = last + width // 2
    halves = [piece(0, 0, last), piece(1, last, half_out), piece(2, half_out, last + width)]
    bounds = [0, width // 8, 3 * width // 8, 5 * width // 8, 7 * width // 8, width]
    fifths = [
        Sum(
            blk, down, v.w_down.at[:, low:high], square_in(v.w_up, 0, low, high), square_in(v.w_gate, 0, low, high),
            square_in(v.w_gate, 2, low, high), v.total_down.at[:, low:high], sems_of(index),
        )
        for index, (low, high) in enumerate(zip(bounds[:-1], bounds[1:]))
    ]
    first_two, third_one, fourth = seq < 2, seq == 2, seq == 3

    def spread(owner, kind, src, dst):
        return Spread(
            seq, owner, kind, src, dst, sem.gsend, sem.grecv, sem.glocal, sem.onsend, sem.onrecv
        )

    spreads = [
        [
            spread(
                owner,
                3 * owner + index,
                v.total.at[:, edges[index] * TILE : edges[index + 1] * TILE],
                o_gu.at[:, cuts[owner] + edges[index] * TILE : cuts[owner] + edges[index + 1] * TILE],
            )
            for index in range(3)
        ]
        for owner in range(2)
    ] + [
        [
            spread(2, 6, v.total.at[:, :last], o_gu.at[:, cuts[2] : cuts[3]]),
            spread(2, 7, v.total.at[:, last:half_out], o_out.at[:, : width // 2]),
            spread(2, 13, v.total.at[:, half_out : last + width], o_out.at[:, width // 2 :]),
        ],
        [
            spread(3, 8 + index, v.total_down.at[:, low:high], o_down.at[:, low:high])
            for index, (low, high) in enumerate(zip(bounds[:-1], bounds[1:]))
        ],
    ]
    def products(item, turned, rhs, tiles, rhs_at, part_at):
        def one(step):
            chip = item.order(step)
            outer_tiles(turned, rhs, v.w_gate, chip, tiles, rhs_at, part_at)

        loop(0, chips, one)

    def swaps(item):
        loop(0, chips, lambda step: item.swap(item.order(step)).start())

    def gate_up_piece(index):
        gift_gu.arrived(edges[index], edges[index + 1])
        at = edges[index] * TILE
        products(thirds[index], v.turned, v.buf_b, edges[index + 1] - edges[index], at, at)

    def down_products(low, high):
        def one(step):
            index = lax.rem(split[0] + step, hidden)
            gift_act.arrived(index, index + 1)
            at = span(index * TILE, TILE, TILE)
            v.turned[:TILE, :] = v.buf_b[:, at].T
            v.w_down[at, :] = times(v.turned[:TILE, :], v.buf_a[...]).astype(BF16)

        loop(low, high, one)

    def down_swaps():
        for item in fifths:
            swaps(item)

    for owner in range(2):

        @pl.when(seq == owner)
        def _(owner=owner):
            gifts_two[owner].arrived()
            turn_over(v.buf_a, v.turned)

    @pl.when(fourth)
    def _():
        gift_cot.arrived()
        down_products(0, hidden // 4)


    def prepare(block):
        at, both = span(block * TILE, TILE, TILE), span(block * 2 * TILE, 2 * TILE, 2 * TILE)
        grad = (stacked(v.out_grad[at, :].astype(F32)) * v.row[both, :]).astype(BF16)
        v.do2[both, :] = grad
        v.do2_turned[:, both] = grad.T
        attended = v.o32[at, :]
        delta = jnp.sum(grad.astype(F32) * jnp.concatenate([attended, attended], axis=0), axis=1, keepdims=True)
        v.row[both, :] = jnp.broadcast_to(delta, (2 * TILE, LANES))
        v.dq[both, :] = jnp.zeros((2 * TILE, LANES), F32)

    for chip in (0, 2, 3, 1):
        for side in range(2):
            give_out.arrived(2 * chip + side)
        if chip == 1:
            normed_out(2).start()
        prepare(chip)
    give_qkv.all_left()

    def key_block(block):
        at = span(block * TILE, TILE, TILE)
        v.dk[...] = jnp.zeros((LANES, TILE), F32)
        v.dv[...] = jnp.zeros((LANES, TILE), F32)

        def query_block(other):
            both = span(other * 2 * TILE, 2 * TILE, 2 * TILE)
            prob = v.prob[both, at]
            grad = back(v.do2[both, :], v.qkv[2, at, :])
            score_grad = (prob.astype(F32) * (grad - v.row[both, :1])).astype(BF16)
            v.dk[...] += times(v.q2_turned[:, both], score_grad)
            v.dv[...] += times(v.do2_turned[:, both], prob)
            v.dq[both, :] += times(score_grad, v.qkv[1, at, :])

        loop(block, chips, query_block)
        cosine = v.score[:TILE, span(block * TILE, LANES, LANES)]
        sine = v.score[:TILE, span(block * TILE + LANES, LANES, LANES)]

        def rotated_back(u):
            u = u.astype(BF16).astype(F32)
            return (u * cosine - halves_changed(u) * sine).astype(BF16)

        dq = rotated_back(unstacked(v.dq[span(block * 2 * TILE, 2 * TILE, 2 * TILE), :]) * scale)
        dk = rotated_back(v.dk[...].T)
        dv = (MIX * v.dv[...].T.astype(BF16).astype(F32)).astype(BF16)
        for index, value in enumerate((dq, dk, dv)):
            v.heads_grad[at, index * LANES : (index + 1) * LANES] = value
            for half_at in range(2):
                v.pack[2 * block + half_at, index] = value[half_at * rows : (half_at + 1) * rows]
        for half_at in range(2):
            give_grads.start(2 * block + half_at)

    loop(0, chips, key_block)

    def when(which, *steps):
        @pl.when(which)
        def _():
            for step in steps:
                step()

    def ended(item, goes):
        def step():
            item.end()
            for other in goes:
                other.start()

        return step

    def first_half():
        gifts_two[2].arrived()
        turn_over(v.buf_a, v.turned)
        gift_gu.arrived(0, split[2])
        products(halves[0], v.turned, v.buf_b, split[2], 0, 0)
        swaps(halves[0])
        halves[0].begin()

    def second_half():
        gift_att.arrived()
        gift_mid.arrived()
        turn_over(v.buf_att, v.turned)
        products(halves[1], v.turned, v.buf_mid, width // 2 // TILE, 0, last)
        swaps(halves[1])
        products(halves[2], v.turned, v.buf_mid, width // 2 // TILE, width // 2, half_out)
        swaps(halves[2])

    def gate_up_gone(index):
        gate_up_piece(index)
        swaps(thirds[index])

    when(first_two, lambda: gate_up_gone(0), thirds[0].begin, lambda: gate_up_gone(1), thirds[1].begin)
    when(third_one, first_half)
    when(fourth, lambda: down_products(hidden // 4, hidden), down_swaps, fifths[0].begin, fifths[1].begin)

    normed_out(2).wait_recv()
    normed_over(2).start()
    for step in range(chips):
        mates_normed(step).wait_recv()

    def project_back(index):
        value = outer(v.normed_all[:, span(index * TILE, TILE, TILE)], v.heads_grad[...]).astype(BF16)
        v.tail_part[2 * index] = value[:LANES]
        v.tail_part[2 * index + 1] = value[LANES:]

    loop(0, width // TILE, project_back)
    quarter = LANES // n_seq

    def tail_share(step):
        other = lax.rem(seq + step, n_seq)
        return remote(
            v.tail_part.at[:, span(other * quarter, quarter, quarter)],
            v.tail_shares.at[step - 1],
            sem.qsend.at[step - 1],
            sem.qrecv.at[step - 1],
            {"seq": other},
        )

    for step in range(1, n_seq):
        tail_share(step).start()

    when(first_two, thirds[0].relay, lambda: gate_up_gone(2))
    when(third_one, second_half)

    def tail_add(index):
        value = v.tail_part[index, span(seq * quarter, quarter, quarter), :].astype(F32)
        for step in range(1, n_seq):
            value = value + v.tail_shares[step - 1, index].astype(F32)
        v.tail_sum[index] = value.astype(BF16)
        give_tail.start(index)

    for step in range(1, n_seq):
        tail_share(step).wait()
    loop(0, n_blk, tail_add)
    when(first_two, thirds[2].begin)
    when(third_one, halves[1].begin, halves[2].begin)

    give_grads.all_arrived()

    def gone(index, *owners):
        return [spreads[owner][index] for owner in owners]

    when(fourth, fifths[0].relay, fifths[2].begin)

    def normed_back(tile):
        at = span(tile * TILE, TILE, TILE)
        o_tokens[:, at] = (
            back(v.grads[0], v.w_query[at, :])
            + back(v.grads[1], v.w_key[at, :])
            + back(v.grads[2], v.w_value[at, :])
        )

    loop(0, width // TILE, normed_back)
    o_first[...] = v.grads[2].astype(F32)
    when(first_two, thirds[1].relay, ended(thirds[0], []))
    for item in gone(0, 0, 1):
        item.start()

    def norm_back(group):
        at = span(group * GROUP, GROUP, GROUP)
        x, grad, inv = tokens[at, :].astype(F32), o_tokens[at, :], v.inv_first[at, :1]
        term = grad * x * inv
        v.gain_rows[0:8, :] += term[:8] + term[8:]
        scaled = grad * attn_gain[...]
        mean = jnp.mean(scaled * x, axis=-1, keepdims=True)
        o_tokens[at, :] = v.mid_grad[at, :] + inv * scaled - x * (inv * inv * inv * mean)

    loop(0, rows // GROUP, norm_back)

    for peer in range(n_blk):
        v.gains[peer] = v.gain_rows[:, peer * LANES : (peer + 1) * LANES]

    def gain_copy(step):
        other = lax.rem(blk + step, n_blk)
        return remote(
            v.gains.at[other], v.gain_got.at[step - 1], sem.hsend.at[step - 1], sem.hrecv.at[step - 1],
            {"blk": other},
        )

    for step in range(1, n_blk):
        gain_copy(step).start()
    when(fourth, ended(fifths[0], gone(0, 3)), fifths[1].relay, fifths[3].begin, fifths[4].begin)

    when(first_two, ended(thirds[1], gone(1, 0, 1)))
    when(third_one, halves[0].relay, ended(halves[0], gone(0, 2)))
    when(fourth, ended(fifths[1], gone(1, 3)))

    give_tail.all_arrived()
    for index in range(3):
        for peer in range(n_blk):
            v.tail_done[index, :, peer * LANES : (peer + 1) * LANES] = v.tail_got[
                peer, :, index * LANES : (index + 1) * LANES
            ]

    def tail_spread(index, step, owner):
        at = span(owner * quarter, quarter, quarter)
        return remote(
            v.tail_done.at[index],
            (o_query, o_key, o_value)[index].at[at],
            sem.tsend.at[index, step - 1],
            sem.trecv.at[index, owner],
            {"seq": lax.rem(seq + step, n_seq)},
        )

    def tail_own(index):
        at = span(seq * quarter, quarter, quarter)
        return pltpu.make_async_copy(
            v.tail_done.at[index], (o_query, o_key, o_value)[index].at[at], sem.trecv.at[index, seq]
        )

    for index in range(3):
        tail_own(index).start()
        for step in range(1, n_seq):
            tail_spread(index, step, seq).start()

    def pass_on(*items):
        for item in items:
            item.pass_on()

    pass_on(*gone(0, 0, 1, 3))
    when(first_two, thirds[2].relay, ended(thirds[2], gone(2, 0, 1)))
    when(
        third_one,
        halves[1].relay,
        ended(halves[1], gone(1, 2)),
        halves[2].relay,
        ended(halves[2], gone(2, 2)),
    )
    when(fourth, fifths[2].relay, fifths[3].relay, ended(fifths[2], gone(2, 3)))
    value = v.gains[blk]
    for step in range(1, n_blk):
        gain_copy(step).wait()
        value = value + v.gain_got[step - 1]
    v.gain_sum[seq] = value
    for step in range(1, n_seq):
        other = lax.rem(seq + step, n_seq)
        mine = v.gain_sum.at[seq]
        remote(mine, mine, sem.isend.at[step - 1], sem.irecv.at[seq], {"seq": other}).start()

    when(fourth, fifths[4].relay, ended(fifths[3], gone(3, 3)), ended(fifths[4], gone(4, 3)))
    pass_on(*gone(0, 2), *gone(1, 3, 0, 1))
    pass_on(*gone(2, 0, 1, 3), *gone(1, 2), *gone(2, 2), *gone(3, 3), *gone(4, 3))

    for step in range(1, n_seq):
        other = lax.rem(seq + step, n_seq)
        theirs = v.gain_sum.at[other]
        remote(theirs, theirs, sem.isend.at[step - 1], sem.irecv.at[other], {"seq": other}).wait()
    value = v.gain_sum[0]
    for group in range(1, n_seq):
        value = value + v.gain_sum[group]
    o_gain[0:8, :] = jnp.broadcast_to(jnp.sum(value[:8], axis=0, keepdims=True), (8, LANES))
    o_gain[8:16, :] = jnp.broadcast_to(jnp.sum(value[8:], axis=0, keepdims=True), (8, LANES))

    for index in range(3):
        tail_own(index).wait()
        for step in range(1, n_seq):
            tail_spread(index, step, seq).wait_send()
            tail_spread(index, step, lax.rem(seq + step, n_seq)).wait_recv()
    for item in sum(spreads, []):
        item.finish()
    for item in [gift_cot, gift_att, gift_mid] + gifts_two:
        item.left()
    gift_gu.left(2 * hidden)
    gift_act.left(hidden)
    for item in (give_att, give_out, give_grads, give_tail):
        item.all_left()
    for step in range(chips):
        normed_over(step).wait_send()
        if step:
            normed_out(step).wait_send()

    @pl.when(first_two)
    def _():
        for item in thirds:
            item.left()

    @pl.when(third_one)
    def _():
        for item in halves:
            item.left()

    @pl.when(fourth)
    def _():
        for item in fifths:
            item.left()


def finish_kernel(
    layer, tokens, first, gu, down, out, query, key, value, gain,
    o_layer, o_tokens, o_first, o_gain, o_gain_two, o_query, o_key, o_value, o_out, o_gate, o_up, o_down,
    kept, small, large, sem_kept_in, sem_kept_out, sem_in, sem_out,
):
    kept_in = [
        pltpu.make_async_copy(src, kept[index], sem_kept_in.at[index])
        for index, src in enumerate((layer, tokens, first))
    ]
    kept_out = [
        pltpu.make_async_copy(kept[index], dst, sem_kept_out.at[index])
        for index, dst in enumerate((o_layer, o_tokens, o_first))
    ]
    ff = o_gate.shape[1]
    sources = [query, key, value, out, down, gu.at[:, :ff], gu.at[:, ff:]]
    targets = [o_query, o_key, o_value, o_out, o_down, o_gate, o_up]
    loads = [pltpu.make_async_copy(src, small[index], sem_in.at[index]) for index, src in enumerate(sources)]
    stores = [pltpu.make_async_copy(large[index], dst, sem_out.at[index]) for index, dst in enumerate(targets)]
    for item in loads + kept_in:
        item.start()
    for index in range(len(sources)):
        loads[index].wait()

        def group(step, index=index):
            at = span(step * GROUP, GROUP, GROUP)
            large[index][at, :] = small[index][at, :].astype(F32)

        loop(0, targets[index].shape[0] // GROUP, group)
        stores[index].start()
    for coming, going in zip(kept_in, kept_out):
        coming.wait()
        going.start()
    o_gain[...] = gain[0:1, :]
    o_gain_two[...] = gain[8:9, :]
    for item in stores + kept_out:
        item.wait()


def finish(layer, tokens, first, gu, down, out, query, key, value, gain):
    hbm, vmem = pl.BlockSpec(memory_space=pl.ANY), pl.BlockSpec(memory_space=pltpu.VMEM)
    shape = jax.ShapeDtypeStruct
    ff = gu.shape[1] // 2
    dims = [query.shape, key.shape, value.shape, out.shape, down.shape, (gu.shape[0], ff), (gu.shape[0], ff)]
    dma = pltpu.SemaphoreType.DMA
    results = pl.pallas_call(
        finish_kernel,
        out_shape=tuple(
            shape(each, F32)
            for each in (
                layer.shape, tokens.shape, first.shape, (1, LANES), (1, LANES), dims[0], dims[1], dims[2], dims[3], dims[5], dims[6], dims[4]
            )
        ),
        in_specs=[hbm] * 9 + [vmem],
        out_specs=(hbm,) * 3 + (vmem,) * 2 + (hbm,) * 7,
        scratch_shapes=(
            [pltpu.VMEM(each.shape, F32) for each in (layer, tokens, first)],
            [pltpu.VMEM(each, BF16) for each in dims],
            [pltpu.VMEM(each, F32) for each in dims],
            dma((3,)), dma((3,)), dma((7,)), dma((7,)),
        ),
        compiler_params=pltpu.CompilerParams(vmem_limit_bytes=63 * 1024 * 1024),
        name="finish",
    )(layer, tokens, first, gu, down, out, query, key, value, gain)
    return results[:3] + (results[3][0],) + results[5:9] + (results[4][0],) + results[9:]


def tile_split(width, ff):
    tiles, more = 2 * ff // TILE, width // TILE
    each = -(-(tiles + more) // 3)
    return (each, each, tiles - 2 * each)


def fits(n_seq, n_blk, rows, width, ff):
    return (
        n_seq == 4
        and n_blk % 2 == 0
        and n_blk * LANES == width
        and rows == LANES
        and ff % TILE == 0
        and (ff // n_blk) % 32 == 0
        and 2 * (ff // n_blk) <= width
        and n_blk == 8
        and width == n_seq * TILE
    )


def local_fast(
    n_seq,
    n_blk,
    tokens,
    first_values,
    doc_lengths,
    attn_gain,
    query_weight,
    key_weight,
    value_weight,
    out_weight,
    ffn_gain,
    gate_weight,
    up_weight,
    down_weight,
    cotangent,
):
    rows, width = tokens.shape
    ff = gate_weight.shape[1]
    split = tile_split(width, ff)
    sizes = (rows, width, ff, n_seq, n_blk, split)
    half = HEAD_DIM // 2
    freq = THETA ** (-(np.arange(half) * 2.0 / HEAD_DIM))
    freq = np.tile(freq, LANES // half)[None, :].astype(np.float32)
    wide = max(split) * TILE
    chunk, down, chips = width // n_blk, ff // n_blk, n_blk // 2
    all_rows, group = n_seq * rows, n_blk * rows
    vmem = pl.BlockSpec(memory_space=pltpu.VMEM)
    hbm = pl.BlockSpec(memory_space=pl.ANY)
    smem = pl.BlockSpec(memory_space=pltpu.SMEM)
    shape = jax.ShapeDtypeStruct

    def half_type(*dims):
        return pltpu.VMEM(dims, BF16)

    def full_type(*dims):
        return pltpu.VMEM(dims, F32)

    scratch = dict(
        w_query=half_type(width, width), w_key=half_type(width, width), w_value=half_type(width, width),
        w_out=half_type(width, width), w_gate=half_type(width, ff), w_up=half_type(width, ff),
        w_down=half_type(ff, width),
        normed=half_type(rows, width), inv_first=full_type(rows, LANES), inv_second=full_type(rows, LANES),
        cos=full_type(rows, LANES), sin=full_type(rows, LANES),
        pack=half_type(n_blk, 3, rows, LANES), qkv=half_type(3, group, LANES),
        q2=half_type(2 * group, LANES), do2=half_type(2 * group, LANES), prob=half_type(2 * group, group),
        score=full_type(2 * TILE, group), top=full_type(2 * TILE, LANES), o2=full_type(2 * TILE, LANES),
        row=full_type(2 * group, LANES), o32=full_type(group, LANES), ob=half_type(group, LANES),
        dq=full_type(2 * group, LANES), dk=full_type(LANES, TILE), dv=full_type(LANES, TILE),
        q2_turned=half_type(LANES, 2 * group), do2_turned=half_type(LANES, 2 * group),
        att=half_type(rows, width), mid=full_type(rows, width), two=half_type(rows, width),
        act=half_type(rows, ff), act_grad=full_type(rows, ff), gate_up=half_type(rows, 2 * ff), two_grad=full_type(rows, width),
        mid_grad=full_type(rows, width), mid_b=half_type(rows, width),
        out_pack=half_type(n_blk, rows, LANES), out_grad=half_type(group, LANES),
        grads=half_type(3, rows, width),
        buf_a=half_type(all_rows, width), buf_b=half_type(all_rows, ff), buf_att=half_type(all_rows, width),
        buf_mid=half_type(all_rows, width), normed_all=half_type(group, width), heads_grad=half_type(group, 3 * LANES),
        tail_part=half_type(n_blk, chunk, 3 * LANES), tail_shares=half_type(n_seq - 1, n_blk, chunk // n_seq, 3 * LANES),
        tail_sum=half_type(n_blk, chunk // n_seq, 3 * LANES), tail_got=half_type(n_blk, chunk // n_seq, 3 * LANES),
        tail_done=half_type(3, chunk // n_seq, width),
        turned=half_type(width, all_rows),
        total=half_type(chunk, wide), total_down=half_type(down, width),
        gain_rows=full_type(16, width), gains=full_type(n_blk, 16, LANES), gain_got=full_type(n_blk - 1, 16, LANES),
        gain_sum=full_type(n_seq, 16, LANES),
    )
    dma = pltpu.SemaphoreType.DMA
    sems = dict(
        load=dma((7,)), asend=dma((5, n_blk)), arecv=dma((5, n_blk)), xsend=dma((4, n_seq)), xrecv=dma((4, n_seq)),
        gusend=dma((2 * ff // TILE,)), gurecv=dma((split[0], n_seq)), actsend=dma((ff // TILE,)),
        actrecv=dma((ff // TILE, n_seq)),
        csend=dma((5, chips)), crecv=dma((5, chips)), rsend=dma((5, 2)), rrecv=dma((5, 2)), zsend=dma((5, 3)),
        zrecv=dma((5, 2)), gsend=dma((14, 2)), grecv=dma((14,)), glocal=dma((14,)), onsend=dma((14, 2)), onrecv=dma((14, 2)),
        nsend=dma((chips - 1,)), nrecv=dma((chips - 1,)), fsend=dma((chips,)), frecv=dma((chips,)), nlocal=dma((1,)),
        qsend=dma((n_seq - 1,)), qrecv=dma((n_seq - 1,)), tsend=dma((3, n_seq - 1)), trecv=dma((3, n_seq)),
        hsend=dma((n_blk - 1,)), hrecv=dma((n_blk - 1,)), isend=dma((n_seq - 1,)), irecv=dma((n_seq,)),
    )
    layer, grad_tokens, grad_first, out_gu, out_down, out_out, out_query, out_key, out_value, out_gain = pl.pallas_call(
        functools.partial(layer_kernel, sizes),
        out_shape=(
            shape((rows, width), F32),
            shape((rows, width), F32),
            shape((rows, width), F32),
            shape((chunk, 2 * ff), BF16),
            shape((down, width), BF16),
            shape((chunk, width), BF16),
            shape((chunk, width), BF16),
            shape((chunk, width), BF16),
            shape((chunk, width), BF16),
            shape((16, LANES), F32),
        ),
        in_specs=[vmem, vmem, vmem, smem, vmem, vmem, vmem] + [hbm] * 7,
        out_specs=(vmem, vmem, vmem) + (hbm,) * 6 + (vmem,),
        scratch_shapes=(scratch, sems),
        compiler_params=pltpu.CompilerParams(
            collective_id=0, has_side_effects=True, vmem_limit_bytes=63 * 1024 * 1024
        ),
        name="layer",
    )(
        freq, tokens, first_values, doc_lengths, attn_gain[None, :], ffn_gain[None, :], cotangent,
        query_weight, key_weight, value_weight, out_weight, gate_weight, up_weight, down_weight,
    )
    return finish(layer, grad_tokens, grad_first, out_gu, out_down, out_out, out_query, out_key, out_value, out_gain)


def local(
    tokens,
    first_values,
    doc_lengths,
    attn_gain,
    query_weight,
    key_weight,
    value_weight,
    out_weight,
    ffn_gain,
    gate_weight,
    up_weight,
    down_weight,
    cotangent,
):
    rows, width = tokens.shape
    heads = width // HEAD_DIM
    scale = HEAD_DIM ** (-0.5)
    shape3 = (rows, heads, HEAD_DIM)
    my_start = lax.axis_index("blk") * rows
    my_index = my_start + jnp.arange(rows, dtype=jnp.int32)
    my_doc, my_pos = doc_layout(doc_lengths, my_index)
    cosine, sine = tables(my_pos)
    source = tokens.astype(jnp.float32)
    inv_first = lax.rsqrt(jnp.mean(source * source, axis=-1, keepdims=True) + EPS)
    normed = (source * inv_first * attn_gain).astype(jnp.bfloat16)
    query_pre = jnp.dot(normed, query_weight, preferred_element_type=jnp.float32)
    key_pre = jnp.dot(normed, key_weight, preferred_element_type=jnp.float32)
    value_pre = jnp.dot(normed, value_weight, preferred_element_type=jnp.float32)
    queries = rotate(query_pre.reshape(shape3), cosine, sine).astype(jnp.bfloat16)
    keys = rotate(key_pre.reshape(shape3), cosine, sine).astype(jnp.bfloat16).reshape(rows, width)
    mixed = (MIX * value_pre + MIX * first_values.astype(jnp.float32)).astype(jnp.bfloat16)
    keys_local = keys.reshape(shape3)
    mixed_local = mixed.reshape(shape3)

    def allowed_mask(query_index, query_doc, key_index, key_doc):
        return (query_doc[:, None] == key_doc[None, :]) & (
            key_index[None, :] <= query_index[:, None]
        )

    def forward_step(state, pieces, start):
        count = pieces[0].shape[0]
        keys_piece = pieces[0].reshape(count, heads, HEAD_DIM)
        values_piece = pieces[1].reshape(count, heads, HEAD_DIM)
        key_index = start + jnp.arange(count, dtype=jnp.int32)

        def forward_compute(state):
            high, total, accum = state
            key_doc, unused = doc_layout(doc_lengths, key_index)
            allowed = allowed_mask(my_index, my_doc, key_index, key_doc)[None]
            score = (
                jnp.einsum("qhd,khd->hqk", queries, keys_piece, preferred_element_type=jnp.float32)
                * scale
            )
            score = jnp.where(allowed, score, NEG)
            new_high = jnp.maximum(high, jnp.max(score, axis=-1))
            weight = jnp.where(allowed, jnp.exp(score - new_high[:, :, None]), 0.0)
            factor = jnp.exp(high - new_high)
            total = total * factor + jnp.sum(weight, axis=-1)
            accum = accum * factor.T[:, :, None] + jnp.einsum(
                "hqk,khd->qhd",
                weight.astype(jnp.bfloat16),
                values_piece,
                preferred_element_type=jnp.float32,
            )
            return (new_high, total, accum)

        return lax.cond(start <= my_index[-1], forward_compute, lambda kept: kept, state)

    def query_grad_step(grad_q, pieces, start):
        count = pieces[0].shape[0]
        keys_piece = pieces[0].reshape(count, heads, HEAD_DIM)
        values_piece = pieces[1].reshape(count, heads, HEAD_DIM)
        key_index = start + jnp.arange(count, dtype=jnp.int32)

        def query_compute(grad_q):
            key_doc, unused = doc_layout(doc_lengths, key_index)
            allowed = allowed_mask(my_index, my_doc, key_index, key_doc)[None]
            score = (
                jnp.einsum("qhd,khd->hqk", queries, keys_piece, preferred_element_type=jnp.float32)
                * scale
            )
            prob = jnp.where(allowed, jnp.exp(score - logsum[:, :, None]), 0.0)
            prob_grad = jnp.einsum(
                "qhd,khd->hqk", outgrad_local, values_piece, preferred_element_type=jnp.float32
            )
            score_grad = (prob * (prob_grad - delta[:, :, None])).astype(jnp.bfloat16)
            return (
                grad_q
                + jnp.einsum(
                    "hqk,khd->qhd", score_grad, keys_piece, preferred_element_type=jnp.float32
                )
                * scale
            )

        return lax.cond(start <= my_index[-1], query_compute, lambda kept: kept, grad_q)

    init = (
        jnp.full((heads, rows), NEG, jnp.float32),
        jnp.zeros((heads, rows), jnp.float32),
        jnp.zeros(shape3, jnp.float32),
    )
    state = by_blocks(
        forward_step,
        init,
        (
            lax.all_gather(keys, "blk", axis=0, tiled=True),
            lax.all_gather(mixed, "blk", axis=0, tiled=True),
        ),
        jnp.int32(0),
    )
    high, total, accum = state
    logsum = high + jnp.log(total)
    attended = accum / total.T[:, :, None]
    attended_b = attended.astype(jnp.bfloat16).reshape(rows, width)
    mid = source + jnp.dot(attended_b, out_weight, preferred_element_type=jnp.float32)
    inv_second = lax.rsqrt(jnp.mean(mid * mid, axis=-1, keepdims=True) + EPS)
    normed_two = (mid * inv_second * ffn_gain).astype(jnp.bfloat16)
    gate = jnp.dot(normed_two, gate_weight, preferred_element_type=jnp.float32)
    up = jnp.dot(normed_two, up_weight, preferred_element_type=jnp.float32)
    act = (jax.nn.silu(gate) * up).astype(jnp.bfloat16)
    layer_output = mid + jnp.dot(act, down_weight, preferred_element_type=jnp.float32)
    cot_float = cotangent.astype(jnp.float32)
    grad_down = outer(act, cotangent)
    act_grad = back(cotangent, down_weight)
    sigma = jax.nn.sigmoid(gate)
    gate_grad = (act_grad * up * sigma * (1.0 + gate * (1.0 - sigma))).astype(jnp.bfloat16)
    up_grad = (act_grad * gate * sigma).astype(jnp.bfloat16)
    grad_gate = outer(normed_two, gate_grad)
    grad_up = outer(normed_two, up_grad)
    normed_two_grad = back(gate_grad, gate_weight) + back(up_grad, up_weight)
    grad_ffn_gain = jnp.sum(normed_two_grad * mid * inv_second, axis=0)
    scaled_two = normed_two_grad * ffn_gain
    mid_grad = (
        cot_float
        + inv_second * scaled_two
        - mid * inv_second**3 * jnp.mean(scaled_two * mid, axis=-1, keepdims=True)
    )
    mid_grad_b = mid_grad.astype(jnp.bfloat16)
    grad_out_weight = outer(attended_b, mid_grad_b)
    attended_grad = back(mid_grad_b, out_weight).astype(jnp.bfloat16)
    outgrad_local = attended_grad.reshape(shape3)
    delta = jnp.sum(outgrad_local.astype(jnp.float32) * attended, axis=-1).T
    zeros3 = jnp.zeros(shape3, jnp.float32)
    grad_q = by_blocks(
        query_grad_step,
        zeros3,
        (
            lax.all_gather(keys, "blk", axis=0, tiled=True),
            lax.all_gather(mixed, "blk", axis=0, tiled=True),
        ),
        jnp.int32(0),
    )
    all_logsum, all_delta = (
        lax.all_gather(logsum.T, "blk", axis=0, tiled=True),
        lax.all_gather(delta.T, "blk", axis=0, tiled=True),
    )

    def key_grad_step(state, pieces, start):
        count = pieces[0].shape[0]
        query_piece = pieces[0].reshape(count, heads, HEAD_DIM)
        outgrad_piece = pieces[1].reshape(count, heads, HEAD_DIM)
        query_index = start + jnp.arange(count, dtype=jnp.int32)

        def key_compute(state):
            grad_k, grad_v = state
            logsum_piece = lax.dynamic_slice_in_dim(all_logsum, start, count, 0).T
            delta_piece = lax.dynamic_slice_in_dim(all_delta, start, count, 0).T
            query_doc, unused = doc_layout(doc_lengths, query_index)
            allowed = allowed_mask(query_index, query_doc, my_index, my_doc)[None]
            score = (
                jnp.einsum(
                    "qhd,khd->hqk", query_piece, keys_local, preferred_element_type=jnp.float32
                )
                * scale
            )
            prob = jnp.where(allowed, jnp.exp(score - logsum_piece[:, :, None]), 0.0)
            grad_v = grad_v + jnp.einsum(
                "hqk,qhd->khd",
                prob.astype(jnp.bfloat16),
                outgrad_piece,
                preferred_element_type=jnp.float32,
            )
            prob_grad = jnp.einsum(
                "qhd,khd->hqk", outgrad_piece, mixed_local, preferred_element_type=jnp.float32
            )
            score_grad = (prob * (prob_grad - delta_piece[:, :, None])).astype(jnp.bfloat16)
            grad_k = (
                grad_k
                + jnp.einsum(
                    "hqk,qhd->khd", score_grad, query_piece, preferred_element_type=jnp.float32
                )
                * scale
            )
            return (grad_k, grad_v)

        return lax.cond(query_index[-1] >= my_start, key_compute, lambda kept: kept, state)

    grad_k, grad_v = by_blocks(
        key_grad_step,
        (zeros3, zeros3),
        (
            lax.all_gather(queries.reshape(rows, width), "blk", axis=0, tiled=True),
            lax.all_gather(attended_grad, "blk", axis=0, tiled=True),
        ),
        jnp.int32(0),
    )
    queries_grad = grad_q.astype(jnp.bfloat16)
    keys_grad = grad_k.astype(jnp.bfloat16)
    mixed_grad = grad_v.astype(jnp.bfloat16).reshape(rows, width)
    q_pre_grad = (
        rotate(queries_grad.astype(jnp.float32), cosine, -sine)
        .astype(jnp.bfloat16)
        .reshape(rows, width)
    )
    k_pre_grad = (
        rotate(keys_grad.astype(jnp.float32), cosine, -sine)
        .astype(jnp.bfloat16)
        .reshape(rows, width)
    )
    grad_first = MIX * mixed_grad.astype(jnp.float32)
    value_grad = grad_first.astype(jnp.bfloat16)
    grad_query = outer(normed, q_pre_grad)
    grad_key = outer(normed, k_pre_grad)
    grad_value = outer(normed, value_grad)
    normed_grad = (
        back(q_pre_grad, query_weight)
        + back(k_pre_grad, key_weight)
        + back(value_grad, value_weight)
    )
    grad_attn_gain = jnp.sum(normed_grad * source * inv_first, axis=0)
    scaled_one = normed_grad * attn_gain
    grad_tokens = (
        mid_grad
        + inv_first * scaled_one
        - source * inv_first**3 * jnp.mean(scaled_one * source, axis=-1, keepdims=True)
    )
    summed = (
        lax.psum_scatter(grad_attn_gain, "blk", scatter_dimension=0, tiled=True),
        lax.psum_scatter(grad_query, "blk", scatter_dimension=0, tiled=True),
        lax.psum_scatter(grad_key, "blk", scatter_dimension=0, tiled=True),
        lax.psum_scatter(grad_value, "blk", scatter_dimension=0, tiled=True),
        lax.psum_scatter(grad_out_weight, "blk", scatter_dimension=0, tiled=True),
        lax.psum_scatter(grad_ffn_gain, "blk", scatter_dimension=0, tiled=True),
        lax.psum_scatter(grad_gate, "blk", scatter_dimension=0, tiled=True),
        lax.psum_scatter(grad_up, "blk", scatter_dimension=0, tiled=True),
        lax.psum_scatter(grad_down, "blk", scatter_dimension=0, tiled=True),
    )
    summed = (
        lax.psum(summed[0].astype(jnp.bfloat16), "seq").astype(jnp.float32),
        lax.psum(summed[1].astype(jnp.bfloat16), "seq").astype(jnp.float32),
        lax.psum(summed[2].astype(jnp.bfloat16), "seq").astype(jnp.float32),
        lax.psum(summed[3].astype(jnp.bfloat16), "seq").astype(jnp.float32),
        lax.psum(summed[4].astype(jnp.bfloat16), "seq").astype(jnp.float32),
        lax.psum(summed[5].astype(jnp.bfloat16), "seq").astype(jnp.float32),
        lax.psum(summed[6].astype(jnp.bfloat16), "seq").astype(jnp.float32),
        lax.psum(summed[7].astype(jnp.bfloat16), "seq").astype(jnp.float32),
        lax.psum(summed[8].astype(jnp.bfloat16), "seq").astype(jnp.float32),
    )
    return (
        layer_output,
        grad_tokens,
        grad_first,
        summed[0],
        summed[1],
        summed[2],
        summed[3],
        summed[4],
        summed[5],
        summed[6],
        summed[7],
        summed[8],
    )


def solution(mesh):
    n_seq, n_blk = mesh.shape["seq"], mesh.shape["blk"]

    def chosen(*args):
        rows, width = args[0].shape
        if fits(n_seq, n_blk, rows, width, args[9].shape[1]):
            return local_fast(n_seq, n_blk, *args)
        return local(*args)

    return jax.shard_map(
        chosen,
        mesh=mesh,
        in_specs=(
            P(("seq", "blk"), None),
            P(("seq", "blk"), None),
            P("seq", None),
            P(),
            P(),
            P(),
            P(),
            P(),
            P(),
            P(),
            P(),
            P(),
            P(("seq", "blk"), None),
        ),
        out_specs=(
            P(("seq", "blk"), None),
            P(("seq", "blk"), None),
            P(("seq", "blk"), None),
            P("blk"),
            P("blk", None),
            P("blk", None),
            P("blk", None),
            P("blk", None),
            P("blk"),
            P("blk", None),
            P("blk", None),
            P("blk", None),
        ),
        check_vma=False,
    )
```
